32 devices in a mesh: rep: 4 (over x, core), fsdp: 8 (over z, y).
Axes of the slice: x: 2, y: 2, z: 4, core: 2. Of those that a mesh axis runs over, the one named last changes fastest.
Arguments:
- hidden_in: bfloat16 [4096, 2048], P(('rep', 'fsdp')), may hold values from -6 to 6
- layer_input: bfloat16 [4096, 256], P(('rep', 'fsdp')), may hold values from -6 to 6
- out_grad: bfloat16 [4096, 2048], P(('rep', 'fsdp')), may hold values from -6 to 6
- seg_lengths: int32 [4, 13], P('rep'), may hold values from 1 to 409, 1024 in all within a row
- seg_parents: int32 [4, 13], P('rep'), may hold values from 0 to 11, as said below
- attn_norm: bfloat16 [2048], P('fsdp'), may hold values from 0.25 to 1.75
- q_proj: bfloat16 [2048, 2048], P('fsdp'), may hold values from -0.125 to 0.125
- k_proj: bfloat16 [2048, 512], P('fsdp'), may hold values from -0.125 to 0.125
- v_proj: bfloat16 [2048, 512], P('fsdp'), may hold values from -0.125 to 0.125
- q_norm: bfloat16 [256], P('fsdp'), may hold values from 0.25 to 1.75
- k_norm: bfloat16 [256], P('fsdp'), may hold values from 0.25 to 1.75
- o_proj: bfloat16 [2048, 2048], P('fsdp'), may hold values from -0.125 to 0.125
- attn_post_norm: bfloat16 [2048], P('fsdp'), may hold values from 0.25 to 1.75
- laurel_left: bfloat16 [2048, 64], P('fsdp'), may hold values from -0.125 to 0.125
- laurel_right: bfloat16 [2048, 64], P('fsdp'), may hold values from -0.75 to 0.75
- laurel_norm: bfloat16 [2048], P('fsdp'), may hold values from 0.25 to 1.75
- ffw_norm: bfloat16 [2048], P('fsdp'), may hold values from 0.25 to 1.75
- gate_proj: bfloat16 [8192, 2048], P('fsdp'), may hold values from -0.125 to 0.125
- up_proj: bfloat16 [8192, 2048], P('fsdp'), may hold values from -0.125 to 0.125
- down_proj: bfloat16 [8192, 2048], P('fsdp'), may hold values from -0.0625 to 0.0625
- ffw_post_norm: bfloat16 [2048], P('fsdp'), may hold values from 0.25 to 1.75
- pl_gate: bfloat16 [2048, 256], P('fsdp'), may hold values from -0.125 to 0.125
- pl_proj: bfloat16 [256, 2048], P('fsdp'), may hold values from -0.375 to 0.375
- pl_post_norm: bfloat16 [2048], P('fsdp'), may hold values from 0.25 to 1.75
Outputs:
- layer_out: bfloat16 [4096, 2048], P(('rep', 'fsdp'))
- input_grad: bfloat16 [4096, 2048], P(('rep', 'fsdp'))
- layer_input_grad: bfloat16 [4096, 256], P(('rep', 'fsdp'))
- attn_norm_grad: float32 [2048], P('fsdp')
- q_proj_grad: float32 [2048, 2048], P('fsdp')
- k_proj_grad: float32 [2048, 512], P('fsdp')
- v_proj_grad: float32 [2048, 512], P('fsdp')
- q_norm_grad: float32 [256], P('fsdp')
- k_norm_grad: float32 [256], P('fsdp')
- o_proj_grad: float32 [2048, 2048], P('fsdp')
- attn_post_norm_grad: float32 [2048], P('fsdp')
- laurel_left_grad: float32 [2048, 64], P('fsdp')
- laurel_right_grad: float32 [2048, 64], P('fsdp')
- laurel_norm_grad: float32 [2048], P('fsdp')
- ffw_norm_grad: float32 [2048], P('fsdp')
- gate_proj_grad: float32 [8192, 2048], P('fsdp')
- up_proj_grad: float32 [8192, 2048], P('fsdp')
- down_proj_grad: float32 [8192, 2048], P('fsdp')
- ffw_post_norm_grad: float32 [2048], P('fsdp')
- pl_gate_grad: float32 [2048, 256], P('fsdp')
- pl_proj_grad: float32 [256, 2048], P('fsdp')
- pl_post_norm_grad: float32 [2048], P('fsdp')
The draws below stay inside these ranges and needn't reach their ends.
Inputs may be any that keep to these rules, and one draw needn't show every extreme that they name: Row r describes the tree of replica group r: segment s covers the next seg_lengths[r, s] of that group's 1024 tokens, in order; each row sums to 1024. seg_parents[r, 0] is 0 and marks the root; for s >= 1, seg_parents[r, s] is a segment below s.
All inputs are finite; a program needn't handle non-finite values.
Results may differ from the reference program's by a relative error of at most 0.025.
Values may be sent and summed in bfloat16 or wider, within the bound.
A program may use at most 704 MiB of HBM per device.

```python
import math
import jax
import jax.numpy as jnp
import numpy as np
from jax import lax

D = 2048
FF = 8192
HEADS = 8
KV_HEADS = 2
HEAD_DIM = 256
RANK = 64
PER_LAYER = 256
SEGS = 13
GROUP_TOK = 1024
TREES = 4
TOKENS = 4096
QWIDTH = 2048
KWIDTH = 512
MOST = 409


def draw_seg_parents(key, part):
    key = jax.random.fold_in(key, 7)
    column = jnp.arange(SEGS, dtype=jnp.int32)
    upper = jnp.broadcast_to(jnp.maximum(column, 1)[None, :], (TREES, SEGS))
    picked = jax.random.randint(key, (TREES, SEGS), 0, upper, dtype=jnp.int32)
    picked = jnp.where(column[None, :] == 0, 0, picked)
    picked = jnp.where(column[None, :] == SEGS - 1, SEGS - 2, picked)
    return picked.astype(jnp.int32)


def levels(own_key, extent, shards, low, high):
    def one(axis_at, shards_of):
        draws = jax.random.uniform(jax.random.fold_in(jax.random.fold_in(own_key, 6), axis_at), (shards_of,), jnp.float32, low / len(shards), high / len(shards))
        return jnp.repeat(jnp.exp(draws), extent[axis_at] // shards_of).reshape((-1,) + (1,) * (len(extent) - axis_at - 1))

    loudness = one(*shards[0])
    for cut in shards[1:]:
        loudness = loudness * one(*cut)
    return loudness


def profile(number_of, total, most, slope):
    weights = [(1 << 20) // math.isqrt(grade ** slope) + 1 for grade in range(2, number_of + 1)]
    rest, holding = total - most - (number_of - 1), [1] * (number_of - 1)
    while rest > 0:
        movable = [i for i in range(number_of - 1) if holding[i] < most]
        pool, left = sum([weights[i] for i in movable]), rest
        for i in movable:
            more = min(most - holding[i], max(1, left * weights[i] // pool), rest)
            holding[i] = holding[i] + more
            rest = rest - more
    return np.array([most] + holding)


def ragged_sizes(stream_key, amount, total, limit, skew):
    if amount == 2:
        one = jax.random.randint(stream_key, (), max(1, total - limit), min(limit, total - 1) + 1)
        return jnp.stack([one, total - one])
    tallies = jnp.asarray(profile(amount, total, limit, skew), jnp.int32)
    twos = (amount - 1) // 2
    source_of, taker = tallies[1:1 + 2 * twos:2], tallies[2:2 + 2 * twos:2]
    room = jnp.minimum(source_of - 1, limit - taker)
    shifted = jax.random.randint(jax.random.fold_in(stream_key, 1), (twos,), 0, 1 << 20) % (room + 1)
    tallies = tallies.at[1:1 + 2 * twos:2].set(source_of - shifted).at[2:2 + 2 * twos:2].set(taker + shifted)
    return tallies[jax.random.permutation(jax.random.fold_in(stream_key, 2), amount)]


def scatter_about(key, shape, width, most, shards=(), held_as=jnp.bfloat16):
    entries = width * jax.random.normal(key, shape, jnp.float32)
    if shards:
        entries = entries * levels(key, shape, shards, -0.22, 0.18)
    return jnp.clip(entries, -most, most).astype(held_as)


def setup_inputs(seed: int = 0) -> dict:
    arg_keys = jax.random.split(jax.random.key(seed), 25)
    hidden_in = scatter_about(arg_keys[0], (TOKENS, D), 1.0, 6.0, ((0, 32),))
    layer_input = scatter_about(arg_keys[1], (TOKENS, PER_LAYER), 1.0, 6.0, ((0, 32),))
    out_grad = scatter_about(arg_keys[2], (TOKENS, D), 1.0, 6.0, ((0, 32),))
    seg_lengths = jax.vmap(lambda own: ragged_sizes(own, SEGS, GROUP_TOK, MOST, 2))(jax.random.split(arg_keys[3], TREES)).reshape((TREES, SEGS)).astype(jnp.int32)
    seg_parents = draw_seg_parents(jax.random.fold_in(arg_keys[24], 71), 0)
    attn_norm = jnp.clip(1.0 + 0.15 * jax.random.normal(arg_keys[5], (D,), jnp.float32), 0.25, 1.75).astype(jnp.bfloat16)
    q_proj = scatter_about(arg_keys[6], (D, QWIDTH), D ** -0.5, 0.125, ((0, 8),))
    k_proj = scatter_about(arg_keys[7], (D, KWIDTH), D ** -0.5, 0.125, ((0, 8),))
    v_proj = scatter_about(arg_keys[8], (D, KWIDTH), D ** -0.5, 0.125, ((0, 8),))
    q_norm = jnp.clip(1.0 + 0.15 * jax.random.normal(arg_keys[9], (HEAD_DIM,), jnp.float32), 0.25, 1.75).astype(jnp.bfloat16)
    k_norm = jnp.clip(1.0 + 0.15 * jax.random.normal(arg_keys[10], (HEAD_DIM,), jnp.float32), 0.25, 1.75).astype(jnp.bfloat16)
    o_proj = scatter_about(arg_keys[11], (QWIDTH, D), QWIDTH ** -0.5, 0.125, ((0, 8),))
    attn_post_norm = jnp.clip(1.0 + 0.15 * jax.random.normal(arg_keys[12], (D,), jnp.float32), 0.25, 1.75).astype(jnp.bfloat16)
    laurel_left = scatter_about(arg_keys[13], (D, RANK), D ** -0.5, 0.125, ((0, 8),))
    laurel_right = scatter_about(arg_keys[14], (D, RANK), RANK ** -0.5, 0.75, ((0, 8),))
    laurel_norm = jnp.clip(1.0 + 0.15 * jax.random.normal(arg_keys[15], (D,), jnp.float32), 0.25, 1.75).astype(jnp.bfloat16)
    ffw_norm = jnp.clip(1.0 + 0.15 * jax.random.normal(arg_keys[16], (D,), jnp.float32), 0.25, 1.75).astype(jnp.bfloat16)
    gate_proj = scatter_about(arg_keys[17], (FF, D), D ** -0.5, 0.125, ((0, 8),))
    up_proj = scatter_about(arg_keys[18], (FF, D), D ** -0.5, 0.125, ((0, 8),))
    down_proj = scatter_about(arg_keys[19], (FF, D), FF ** -0.5, 0.0625, ((0, 8),))
    ffw_post_norm = jnp.clip(1.0 + 0.15 * jax.random.normal(arg_keys[20], (D,), jnp.float32), 0.25, 1.75).astype(jnp.bfloat16)
    pl_gate = scatter_about(arg_keys[21], (D, PER_LAYER), D ** -0.5, 0.125, ((0, 8),))
    pl_proj = scatter_about(arg_keys[22], (PER_LAYER, D), PER_LAYER ** -0.5, 0.375, ((0, 8),))
    pl_post_norm = jnp.clip(1.0 + 0.15 * jax.random.normal(arg_keys[23], (D,), jnp.float32), 0.25, 1.75).astype(jnp.bfloat16)
    return dict(hidden_in=hidden_in, layer_input=layer_input, out_grad=out_grad, seg_lengths=seg_lengths, seg_parents=seg_parents, attn_norm=attn_norm, q_proj=q_proj, k_proj=k_proj, v_proj=v_proj, q_norm=q_norm, k_norm=k_norm, o_proj=o_proj, attn_post_norm=attn_post_norm, laurel_left=laurel_left, laurel_right=laurel_right, laurel_norm=laurel_norm, ffw_norm=ffw_norm, gate_proj=gate_proj, up_proj=up_proj, down_proj=down_proj, ffw_post_norm=ffw_post_norm, pl_gate=pl_gate, pl_proj=pl_proj, pl_post_norm=pl_post_norm)


EPS = 1e-06
ROPE_BASE = 1000000.0
HALF_ROOT = 0.7071067811865476
MASKED = -1e+30
HIGHEST = lax.Precision.HIGHEST

@jax.custom_vjp
def low(v):
    return lax.optimization_barrier(v.astype(jnp.bfloat16)).astype(jnp.float32)

@jax.custom_vjp
def low_back(v):
    return v

def low_keep(v):
    return (low(v), None)

def low_pass(kept, grad):
    return (grad,)

def back_keep(v):
    return (v, None)

def back_low(kept, grad):
    return (low(grad),)
low.defvjp(low_keep, low_pass)
low_back.defvjp(back_keep, back_low)

def matmul(left, right):
    return jnp.dot(left, right, precision=HIGHEST)

def norm_rows(value, gain):
    return value * lax.rsqrt(lax.optimization_barrier(jnp.mean(value * value, axis=-1, keepdims=True)) + EPS) * gain

def rotate(value, position):
    half = value.shape[-1] // 2
    freqs = jnp.exp(jnp.arange(half, dtype=jnp.float32) * (-2.0 * math.log(ROPE_BASE) / value.shape[-1]))
    angle = position[:, None] * freqs[None, :]
    cosine = jnp.cos(angle)[:, None, :]
    sine = jnp.sin(angle)[:, None, :]
    first_half = value[..., :half]
    second_half = value[..., half:]
    return jnp.concatenate([first_half * cosine - second_half * sine, second_half * cosine + first_half * sine], axis=-1)

def tree_tables(lengths, parents, total):
    count = lengths.shape[0]
    labels = jnp.arange(count, dtype=jnp.int32)
    lengths = lengths.astype(jnp.int32)
    ends = jnp.cumsum(lengths).astype(jnp.int32)
    starts = ends - lengths
    tokens = jnp.arange(total, dtype=jnp.int32)
    segment = lax.optimization_barrier(jnp.sum((ends[None, :] <= tokens[:, None]).astype(jnp.int32), axis=1))
    parent_hot = ((parents[:, None] == labels[None, :]) & (labels[:, None] > 0)).astype(jnp.int32)
    identity = (labels[:, None] == labels[None, :]).astype(jnp.int32)
    ancestors = lax.fori_loop(0, count, lambda step, held: jnp.minimum(1, identity + jnp.dot(parent_hot, held)), identity)
    offset = jnp.dot(ancestors - identity, lengths) - starts
    member = (segment[:, None] == labels[None, :]).astype(jnp.int32)
    reach = jnp.dot(member, ancestors)
    position = jnp.dot(member, offset) + tokens
    return (tokens, member, reach, position)

def visible(reach_rows, row_tokens, member, tokens):
    return (jnp.dot(reach_rows, member.T) > 0) & (tokens[None, :] <= row_tokens[:, None])

def attend(q_rot, k_rot, v_heads, member, reach, tokens):
    total = q_rot.shape[0]
    block = 512 if total % 512 == 0 else total
    count = total // block
    scale = HEAD_DIM ** (-0.5)
    queries = q_rot.reshape(count, block, KV_HEADS, HEADS // KV_HEADS, HEAD_DIM)
    reach_blocks = reach.reshape(count, block, reach.shape[1])
    token_blocks = tokens.reshape(count, block)

    @jax.checkpoint
    def one_block(item):
        query, reach_rows, row_tokens = item
        raw = jnp.einsum('qkgd,nkd->kgqn', query, k_rot, precision=HIGHEST)
        scores = low_back(raw) * scale
        seen = visible(reach_rows, row_tokens, member, tokens)
        scores = jnp.where(seen[None, None], scores, MASKED)
        top = lax.optimization_barrier(jnp.max(scores, axis=-1, keepdims=True))
        expo = jnp.exp(scores - top)
        weights = low(expo / lax.optimization_barrier(jnp.sum(expo, axis=-1, keepdims=True)))
        return jnp.einsum('kgqn,nkd->qkgd', weights, v_heads, precision=HIGHEST)
    mixed = lax.map(one_block, (queries, reach_blocks, token_blocks))
    return mixed.reshape(total, HEADS * HEAD_DIM)

def one_tree(item, params):
    source, extra, lengths, parents = item
    attn_norm, q_proj, k_proj, v_proj, q_norm, k_norm, o_proj, attn_post_norm, laurel_left, laurel_right, laurel_norm, ffw_norm, gate_proj, up_proj, down_proj, ffw_post_norm, pl_gate, pl_proj, pl_post_norm = params
    total = source.shape[0]
    tokens, member, reach, position = tree_tables(lengths, parents, total)
    depth = position.astype(jnp.float32)
    normed = norm_rows(source, attn_norm)
    normed_low = low(normed)
    q_raw = low_back(matmul(normed_low, q_proj))
    k_raw = low_back(matmul(normed_low, k_proj))
    v_raw = low(low_back(matmul(normed_low, v_proj)))
    q_rot = low(rotate(norm_rows(q_raw.reshape(total, HEADS, HEAD_DIM), q_norm), depth))
    k_rot = low(rotate(norm_rows(k_raw.reshape(total, KV_HEADS, HEAD_DIM), k_norm), depth))
    v_heads = v_raw.reshape(total, KV_HEADS, HEAD_DIM)
    attended = low(low_back(attend(q_rot, k_rot, v_heads, member, reach, tokens)))
    branch = low_back(matmul(attended, o_proj))
    left_low = low(low_back(matmul(normed_low, laurel_left)))
    low_rank = low_back(matmul(left_low, laurel_right.T))
    first_sum = (source + norm_rows(branch, attn_post_norm) + normed + norm_rows(low_rank, laurel_norm)) * HALF_ROOT
    ffw_low = low(norm_rows(first_sum, ffw_norm))
    gate = low_back(matmul(ffw_low, gate_proj.T))
    up_val = low_back(matmul(ffw_low, up_proj.T))
    inner_low = low(jax.nn.gelu(gate, approximate=True) * up_val)
    ffw_out = low_back(matmul(inner_low, down_proj))
    second_sum = first_sum + norm_rows(ffw_out, ffw_post_norm)
    second_low = low(second_sum)
    pl_pre = low_back(matmul(second_low, pl_gate))
    pl_mix = low(jax.nn.gelu(pl_pre, approximate=True) * extra)
    pl_out = low_back(matmul(pl_mix, pl_proj))
    return second_sum + norm_rows(pl_out, pl_post_norm)

def reference(hidden_in, layer_input, out_grad, seg_lengths, seg_parents, attn_norm, q_proj, k_proj, v_proj, q_norm, k_norm, o_proj, attn_post_norm, laurel_left, laurel_right, laurel_norm, ffw_norm, gate_proj, up_proj, down_proj, ffw_post_norm, pl_gate, pl_proj, pl_post_norm):
    weights = (attn_norm, q_proj, k_proj, v_proj, q_norm, k_norm, o_proj, attn_post_norm, laurel_left, laurel_right, laurel_norm, ffw_norm, gate_proj, up_proj, down_proj, ffw_post_norm, pl_gate, pl_proj, pl_post_norm)
    floats = tuple((item.astype(jnp.float32) for item in weights))

    def forward(source, extra, params):
        blocks = (source.reshape(TREES, GROUP_TOK, D), extra.reshape(TREES, GROUP_TOK, PER_LAYER), seg_lengths, seg_parents)
        tree_step = jax.checkpoint(lambda item: one_tree(item, params))
        return lax.map(tree_step, blocks).reshape(TREES * GROUP_TOK, D)
    result, pull = jax.vjp(forward, hidden_in.astype(jnp.float32), layer_input.astype(jnp.float32), floats)
    d_source, d_extra, d_params = pull(out_grad.astype(jnp.float32))
    return (result.astype(jnp.bfloat16), d_source.astype(jnp.bfloat16), d_extra.astype(jnp.bfloat16), d_params[0], d_params[1], d_params[2], d_params[3], d_params[4], d_params[5], d_params[6], d_params[7], d_params[8], d_params[9], d_params[10], d_params[11], d_params[12], d_params[13], d_params[14], d_params[15], d_params[16], d_params[17], d_params[18])
```

```python
import functools
import math

import jax
import jax.numpy as jnp
from jax import lax
from jax.experimental import pallas as pl
from jax.experimental.pallas import tpu as pltpu
from jax.sharding import PartitionSpec as P

HEADS = 8
KV_HEADS = 2
HEAD_DIM = 256


EPS = 1e-06
ROPE_BASE = 1000000.0
HALF_ROOT = 0.7071067811865476
MASKED = -1e30


def norm_rows(value, gain):
    return value * lax.rsqrt(jnp.mean(value * value, axis=-1, keepdims=True) + EPS) * gain


def norm_back(value, gain, grad):
    unused, pull = jax.vjp(norm_rows, value, gain)
    return pull(grad)


def rotate(value, position):
    half = value.shape[-1] // 2
    freqs = jnp.exp(
        jnp.arange(half, dtype=jnp.float32) * (-2.0 * math.log(ROPE_BASE) / value.shape[-1])
    )
    angle = position[:, None] * freqs[None, :]
    cosine = jnp.cos(angle)[:, None, :]
    sine = jnp.sin(angle)[:, None, :]
    first_half = value[..., :half]
    second_half = value[..., half:]
    return jnp.concatenate(
        [first_half * cosine - second_half * sine, second_half * cosine + first_half * sine],
        axis=-1,
    )


def tree_tables(lengths, parents, total):
    count = lengths.shape[0]
    labels = jnp.arange(count, dtype=jnp.int32)
    ends = jnp.cumsum(lengths)
    starts = ends - lengths
    tokens = jnp.arange(total, dtype=jnp.int32)
    segment = jnp.sum((ends[None, :] <= tokens[:, None]).astype(jnp.int32), axis=1)
    parent_hot = ((parents[:, None] == labels[None, :]) & (labels[:, None] > 0)).astype(jnp.int32)
    identity = (labels[:, None] == labels[None, :]).astype(jnp.int32)
    ancestors = lax.fori_loop(
        0, count, lambda step, held: jnp.minimum(1, identity + jnp.dot(parent_hot, held)), identity
    )
    offset = jnp.dot(ancestors - identity, lengths) - starts
    member = (segment[:, None] == labels[None, :]).astype(jnp.int32)
    reach = jnp.dot(member, ancestors)
    position = jnp.dot(member, offset) + tokens
    return (tokens, member, reach, position)


def outer(left, right):
    return lax.dot_general(
        left, right, (((0,), (0,)), ((), ())), preferred_element_type=jnp.float32
    )


def mul_t(left, right):
    return lax.dot_general(
        left, right, (((1,), (1,)), ((), ())), preferred_element_type=jnp.float32
    )


def gelu_mix(first, second):
    return jax.nn.gelu(first, approximate=True) * second


def mix_back(first, second, grad):
    unused, pull = jax.vjp(gelu_mix, first, second)
    return pull(grad)


MESH = pl.DeviceIdType.MESH
VMEM_BYTES = 48 << 20


def ring_place(index):
    side = lax.rem(index, 2)
    return index // 2 + side * (HEADS - 1 - 2 * (index // 2))


def ring_index(place):
    back = place // (HEADS // 2)
    return (1 - back) * 2 * place + back * (2 * HEADS - 1 - 2 * place)


def ring_ends(place):
    after = {"fsdp": ring_index(lax.rem(place + 1, HEADS))}
    before = {"fsdp": ring_index(lax.rem(place + HEADS - 1, HEADS))}
    return (after, before)


def greet(others):
    barrier = pltpu.get_barrier_semaphore()
    for other in others:
        pl.semaphore_signal(barrier, inc=1, device_id=other, device_id_type=MESH)
    pl.semaphore_wait(barrier, len(others))


def span(start, size):
    return pl.ds(pl.multiple_of(start, size), size)


def gather_kernel(subs, own_ref, all_ref, local_sem, send_sem, recv_sem):
    rows = own_ref.shape[0]
    part = rows // (2 * subs)
    index = lax.axis_index("fsdp")
    place = ring_place(index)
    ends = ring_ends(place)
    greet(ends)
    local = pltpu.make_async_copy(own_ref, all_ref.at[span(index * rows, rows)], local_sem)
    local.start()
    copies = []
    lanes = 2 * subs
    for step in range(HEADS - 1):
        for lane in range(lanes):
            way = lane % 2
            owner = ring_index(lax.rem(place + (step if way else HEADS - step), HEADS))
            offset = lane * part
            there = all_ref.at[span(owner * rows + offset, part)]
            number = step * lanes + lane
            if step:
                copies[number - lanes].wait_recv()
            copy = pltpu.make_async_remote_copy(
                there if step else own_ref.at[pl.ds(offset, part)],
                there,
                send_sem.at[number],
                recv_sem.at[number],
                device_id=ends[way],
                device_id_type=MESH,
            )
            copy.start()
            copies.append(copy)
    for number, copy in enumerate(copies):
        if number >= (HEADS - 2) * lanes:
            copy.wait_recv()
        copy.wait_send()
    local.wait()


def ring_gather(own, number, subs=2):
    steps = (HEADS - 1) * 2 * subs
    return pl.pallas_call(
        functools.partial(gather_kernel, subs),
        out_shape=jax.ShapeDtypeStruct((own.shape[0] * HEADS, own.shape[1]), own.dtype),
        in_specs=[pl.BlockSpec(memory_space=pl.ANY)],
        out_specs=pl.BlockSpec(memory_space=pl.ANY),
        scratch_shapes=[
            pltpu.SemaphoreType.DMA,
            pltpu.SemaphoreType.DMA((steps,)),
            pltpu.SemaphoreType.DMA((steps,)),
        ],
        compiler_params=pltpu.CompilerParams(collective_id=number, has_side_effects=True),
    )(own)


def scatter_kernel(subs, part_ref, sum_ref, held, send_sem, recv_sem):
    rows = sum_ref.shape[0]
    part = rows // (2 * subs)
    index = lax.axis_index("fsdp")
    place = ring_place(index)
    ends = ring_ends(place)
    greet(ends)
    copies = []
    lanes = 2 * subs
    for step in range(HEADS - 1):
        for lane in range(lanes):
            way = lane % 2
            owner = ring_index(lax.rem(place + (step + 1 if way else HEADS - 1 - step), HEADS))
            mine = span(owner * rows + lane * part, part)
            number = step * lanes + lane
            if step:
                copies[number - lanes].wait_recv()
                source = held.at[number - lanes]
                source[...] = (
                    source[...].astype(jnp.float32) + part_ref[mine, :].astype(jnp.float32)
                ).astype(jnp.bfloat16)
            else:
                source = part_ref.at[mine]
            copy = pltpu.make_async_remote_copy(
                source,
                held.at[number],
                send_sem.at[number],
                recv_sem.at[number],
                device_id=ends[way],
                device_id_type=MESH,
            )
            copy.start()
            copies.append(copy)
    for lane in range(lanes):
        number = (HEADS - 2) * lanes + lane
        copies[number].wait_recv()
        mine = span(index * rows + lane * part, part)
        sum_ref[pl.ds(lane * part, part), :] = held[number].astype(jnp.float32) + part_ref[
            mine, :
        ].astype(jnp.float32)
    for copy in copies:
        copy.wait_send()


def ring_scatter(parts, number, subs=2):
    rows = parts.shape[0] // HEADS
    steps = (HEADS - 1) * 2 * subs
    return pl.pallas_call(
        functools.partial(scatter_kernel, subs),
        out_shape=jax.ShapeDtypeStruct((rows, parts.shape[1]), jnp.float32),
        in_specs=[pl.BlockSpec(memory_space=pltpu.VMEM)],
        out_specs=pl.BlockSpec(memory_space=pltpu.VMEM),
        scratch_shapes=[
            pltpu.VMEM((steps, rows // (2 * subs), parts.shape[1]), jnp.bfloat16),
            pltpu.SemaphoreType.DMA((steps,)),
            pltpu.SemaphoreType.DMA((steps,)),
        ],
        compiler_params=pltpu.CompilerParams(
            collective_id=number, has_side_effects=True, vmem_limit_bytes=VMEM_BYTES
        ),
    )(parts)


def swap_kernel(own_ref, all_ref, local_sem, send_sem, recv_sem):
    rows = own_ref.shape[0] // HEADS
    index = lax.axis_index("fsdp")
    others = [lax.rem(index + step, HEADS) for step in range(1, HEADS)]
    greet([{"fsdp": other} for other in others])
    mine = span(index * rows, rows)
    copies = []
    for step, other in enumerate(others):
        copy = pltpu.make_async_remote_copy(
            own_ref.at[span(other * rows, rows)],
            all_ref.at[mine],
            send_sem.at[step],
            recv_sem.at[step],
            device_id={"fsdp": other},
            device_id_type=MESH,
        )
        copy.start()
        copies.append(copy)
    local = pltpu.make_async_copy(own_ref.at[mine], all_ref.at[mine], local_sem)
    local.start()
    for copy in copies:
        copy.wait()
    local.wait()


def swap_blocks(own, number):
    return pl.pallas_call(
        swap_kernel,
        out_shape=jax.ShapeDtypeStruct(own.shape, own.dtype),
        in_specs=[pl.BlockSpec(memory_space=pl.ANY)],
        out_specs=pl.BlockSpec(memory_space=pl.ANY),
        scratch_shapes=[
            pltpu.SemaphoreType.DMA,
            pltpu.SemaphoreType.DMA((HEADS - 1,)),
            pltpu.SemaphoreType.DMA((HEADS - 1,)),
        ],
        compiler_params=pltpu.CompilerParams(collective_id=number, has_side_effects=True),
    )(own)


def dot(left, right):
    return jnp.dot(left, right, preferred_element_type=jnp.float32)


def low(value):
    return value.astype(jnp.bfloat16)


def head_plan(
    hidden_in,
    layer_input,
    out_grad,
    seg_lengths,
    seg_parents,
    attn_norm,
    q_proj,
    k_proj,
    v_proj,
    q_norm,
    k_norm,
    o_proj,
    attn_post_norm,
    laurel_left,
    laurel_right,
    laurel_norm,
    ffw_norm,
    gate_proj,
    up_proj,
    down_proj,
    ffw_post_norm,
    pl_gate,
    pl_proj,
    pl_post_norm,
):
    index = lax.axis_index("fsdp")
    rows, width = hidden_in.shape
    shard = width // HEADS
    total = rows * HEADS
    groups = HEADS // KV_HEADS
    scale = HEAD_DIM ** (-0.5)
    rank = laurel_left.shape[1]
    per_layer = pl_gate.shape[1]
    key_head = index // groups

    gains = (attn_norm, attn_post_norm, laurel_norm, ffw_norm, ffw_post_norm, pl_post_norm)
    packed = jnp.concatenate(gains + (q_norm, k_norm))
    pad = -packed.shape[0] % (32 * 128)
    packed = jnp.pad(packed, (0, pad)).reshape(-1, 128)
    all_gains = ring_gather(packed, 0, 1).reshape(HEADS, -1).astype(jnp.float32)
    wide_gains = [all_gains[:, i * shard : (i + 1) * shard].reshape(-1) for i in range(len(gains))]
    gain_anorm, gain_apost, gain_lnorm, gain_fnorm, gain_fpost, gain_plpost = wide_gains
    at = len(gains) * shard
    piece = HEAD_DIM // HEADS
    gain_qnorm = all_gains[:, at : at + piece].reshape(-1)
    gain_knorm = all_gains[:, at + piece : at + 2 * piece].reshape(-1)

    hidden_all = ring_gather(hidden_in, 1)
    q_blocks = q_proj.reshape(shard, HEADS, HEAD_DIM).transpose(1, 0, 2).reshape(-1, HEAD_DIM)
    q_head = swap_blocks(q_blocks, 2)
    kv_all = ring_gather(jnp.concatenate([k_proj, v_proj], axis=1), 3)
    small_all = ring_gather(jnp.concatenate([pl_gate, laurel_left, laurel_right], axis=1), 4)
    full_plproj = ring_gather(pl_proj, 5, 1)
    k_head = lax.dynamic_slice_in_dim(kv_all, key_head * HEAD_DIM, HEAD_DIM, 1)
    v_head = lax.dynamic_slice_in_dim(kv_all, (KV_HEADS + key_head) * HEAD_DIM, HEAD_DIM, 1)
    full_plgate = small_all[:, :per_layer]
    full_left = small_all[:, per_layer : per_layer + rank]
    full_right = small_all[:, per_layer + rank :]

    tokens, member, reach, position = tree_tables(seg_lengths[0], seg_parents[0], total)
    depth = position.astype(jnp.float32)
    seen = (jnp.dot(reach, member.T) > 0) & (tokens[None, :] <= tokens[:, None])

    normed_all = low(norm_rows(hidden_all.astype(jnp.float32), gain_anorm))
    q_raw = dot(normed_all, q_head)
    k_raw = dot(normed_all, k_head)
    v_low = low(dot(normed_all, v_head))

    def head_path(raw, gain):
        return rotate(norm_rows(raw, gain)[:, None, :], depth)[:, 0, :]

    q_low = low(head_path(q_raw, gain_qnorm))
    k_low = low(head_path(k_raw, gain_knorm))
    scores = jnp.where(seen, mul_t(q_low, k_low) * scale, MASKED)
    top = jnp.max(scores, axis=-1, keepdims=True)
    expo = jnp.exp(scores - top)
    sums = jnp.sum(expo, axis=-1, keepdims=True)
    probs = expo / sums
    probs_low = low(probs)
    attended = dot(probs_low, v_low)
    attended_low = low(attended)
    branch = ring_scatter(low(dot(attended_low, o_proj)), 6)

    source = hidden_in.astype(jnp.float32)
    extra = layer_input.astype(jnp.float32)
    normed = norm_rows(source, gain_anorm)
    normed_low = low(normed)
    left_low = low(dot(normed_low, full_left))
    low_rank = mul_t(left_low, full_right)
    first_sum = (
        source + norm_rows(branch, gain_apost) + normed + norm_rows(low_rank, gain_lnorm)
    ) * HALF_ROOT
    ffw_low = low(norm_rows(first_sum, gain_fnorm))

    ffw_all = ring_gather(ffw_low, 7)
    gate_val = mul_t(ffw_all, gate_proj)
    up_val = mul_t(ffw_all, up_proj)
    inner_low = low(gelu_mix(gate_val, up_val))
    ffw_out = ring_scatter(low(dot(inner_low, down_proj)), 8)

    second_sum = first_sum + norm_rows(ffw_out, gain_fpost)
    second_low = low(second_sum)
    pl_pre = dot(second_low, full_plgate)
    pl_mix = low(gelu_mix(pl_pre, extra))
    pl_out = dot(pl_mix, full_plproj)
    result = second_sum + norm_rows(pl_out, gain_plpost)
    seed = out_grad.astype(jnp.float32)
    d_plout, grad_plpost = norm_back(pl_out, gain_plpost, seed)
    d_plout_low = low(d_plout)
    grad_plproj = outer(pl_mix, d_plout_low)
    d_mix = mul_t(d_plout_low, full_plproj)
    d_pre, d_extra = mix_back(pl_pre, extra, d_mix)
    d_pre_low = low(d_pre)
    grad_plgate = outer(second_low, d_pre_low)
    d_second = seed + mul_t(d_pre_low, full_plgate)
    d_ffwout, grad_fpost = norm_back(ffw_out, gain_fpost, d_second)

    d_ffw_all = ring_gather(low(d_ffwout), 9)
    d_inner = mul_t(d_ffw_all, down_proj)
    d_gate, d_up = mix_back(gate_val, up_val, d_inner)
    d_gate_low = low(d_gate)
    d_up_low = low(d_up)
    d_ffwin = ring_scatter(low(dot(d_gate_low, gate_proj) + dot(d_up_low, up_proj)), 10)
    ffw_grads = [
        low(outer(d_gate_low, ffw_all)),
        low(outer(d_up_low, ffw_all)),
        low(outer(inner_low, d_ffw_all)),
    ]
    sum_gate, sum_up, sum_down = [lax.psum(item, "rep").astype(jnp.float32) for item in ffw_grads]

    d_first_part, grad_fnorm = norm_back(first_sum, gain_fnorm, d_ffwin)
    d_scaled = (d_second + d_first_part) * HALF_ROOT
    d_branch, grad_apost = norm_back(branch, gain_apost, d_scaled)
    d_lowrank, grad_lnorm = norm_back(low_rank, gain_lnorm, d_scaled)
    d_lowrank_low = low(d_lowrank)
    d_branch_all = ring_gather(low(d_branch), 11)
    grad_right = outer(d_lowrank_low, left_low)
    d_left_low = low(dot(d_lowrank_low, full_right))
    grad_left = outer(normed_low, d_left_low)

    d_att_low = low(mul_t(d_branch_all, o_proj))
    grad_o = outer(attended_low, d_branch_all)
    delta = jnp.sum(d_att_low.astype(jnp.float32) * attended, axis=-1, keepdims=True)
    d_probs = mul_t(d_att_low, v_low)
    d_scores = low(probs * (d_probs - delta) * scale)
    d_query = dot(d_scores, k_low)
    d_key = outer(d_scores, q_low)
    d_value = outer(probs_low, d_att_low)
    unused_q, q_pull = jax.vjp(head_path, q_raw, gain_qnorm)
    d_qraw, grad_qnorm = q_pull(d_query)
    unused_k, k_pull = jax.vjp(head_path, k_raw, gain_knorm)
    d_kraw, grad_knorm = k_pull(d_key)
    d_q_low = low(d_qraw)
    d_k_low = low(d_kraw)
    d_v_low = low(d_value)
    d_normed_part = mul_t(d_q_low, q_head) + mul_t(d_k_low, k_head) + mul_t(d_v_low, v_head)
    d_normed = d_scaled + mul_t(d_left_low, full_left) + ring_scatter(low(d_normed_part), 12)
    d_source_part, grad_anorm = norm_back(source, gain_anorm, d_normed)
    d_source = d_scaled + d_source_part

    head_grads = low(outer(normed_all, jnp.concatenate([d_q_low, d_k_low, d_v_low], axis=1)))
    head_grads = swap_blocks(head_grads, 13).reshape(HEADS, shard, 3 * HEAD_DIM)
    q_part = head_grads[:, :, :HEAD_DIM].transpose(1, 0, 2).reshape(shard, -1)
    kv_part = head_grads[:, :, HEAD_DIM:].astype(jnp.float32)
    kv_part = low(jnp.sum(kv_part.reshape(KV_HEADS, groups, shard, -1), axis=1))
    k_part = kv_part[:, :, :HEAD_DIM].transpose(1, 0, 2).reshape(shard, -1)
    v_part = kv_part[:, :, HEAD_DIM:].transpose(1, 0, 2).reshape(shard, -1)

    def scatter(value):
        return lax.psum_scatter(low(value), "fsdp", scatter_dimension=0, tiled=True)

    def over_trees(value):
        return lax.psum(low(value), "rep").astype(jnp.float32)

    small_grads = [grad_anorm, grad_apost, grad_lnorm, grad_fnorm, grad_fpost, grad_plpost]
    small_sums = lax.psum(jnp.concatenate(small_grads + [grad_qnorm, grad_knorm]), ("rep", "fsdp"))

    def own_part(start, size):
        return lax.dynamic_slice_in_dim(small_sums, start + index * size, size)

    own = [own_part(i * width, shard) for i in range(len(small_grads))]
    sum_anorm, sum_apost, sum_lnorm, sum_fnorm, sum_fpost, sum_plpost = own
    sum_qnorm = own_part(len(small_grads) * width, piece)
    sum_knorm = own_part(len(small_grads) * width + HEAD_DIM, piece)
    mixed = scatter(jnp.concatenate([grad_plgate, grad_left, grad_right], axis=1))
    mixed = over_trees(mixed)
    return (
        low(result),
        low(d_source),
        low(d_extra),
        sum_anorm,
        over_trees(q_part),
        over_trees(k_part),
        over_trees(v_part),
        sum_qnorm,
        sum_knorm,
        over_trees(grad_o),
        sum_apost,
        mixed[:, per_layer : per_layer + rank],
        mixed[:, per_layer + rank :],
        sum_lnorm,
        sum_fnorm,
        sum_gate,
        sum_up,
        sum_down,
        sum_fpost,
        mixed[:, :per_layer],
        over_trees(scatter(grad_plproj)),
        sum_plpost,
    )


def gather_plan(
    hidden_in,
    layer_input,
    out_grad,
    seg_lengths,
    seg_parents,
    attn_norm,
    q_proj,
    k_proj,
    v_proj,
    q_norm,
    k_norm,
    o_proj,
    attn_post_norm,
    laurel_left,
    laurel_right,
    laurel_norm,
    ffw_norm,
    gate_proj,
    up_proj,
    down_proj,
    ffw_post_norm,
    pl_gate,
    pl_proj,
    pl_post_norm,
):
    shards = lax.axis_size("fsdp")
    rank_index = lax.axis_index("fsdp")
    rows = hidden_in.shape[0]
    total = rows * shards
    groups = HEADS // KV_HEADS
    scale = HEAD_DIM ** (-0.5)
    tokens, member, reach, position = tree_tables(seg_lengths[0], seg_parents[0], total)
    first_row = rank_index * rows
    my_tokens = first_row + jnp.arange(rows, dtype=jnp.int32)
    my_reach = lax.dynamic_slice_in_dim(reach, first_row, rows, 0)
    my_depth = lax.dynamic_slice_in_dim(position, first_row, rows, 0).astype(jnp.float32)
    seen = (jnp.dot(my_reach, member.T) > 0) & (tokens[None, :] <= my_tokens[:, None])
    (
        full_anorm,
        full_q,
        full_k,
        full_v,
        full_qnorm,
        full_knorm,
        full_o,
        full_apost,
        full_left,
        full_right,
        full_lnorm,
        full_fnorm,
        full_fpost,
        full_plgate,
        full_plproj,
        full_plpost,
    ) = (
        lax.all_gather(attn_norm, "fsdp", axis=0, tiled=True),
        lax.all_gather(q_proj, "fsdp", axis=0, tiled=True),
        lax.all_gather(k_proj, "fsdp", axis=0, tiled=True),
        lax.all_gather(v_proj, "fsdp", axis=0, tiled=True),
        lax.all_gather(q_norm, "fsdp", axis=0, tiled=True),
        lax.all_gather(k_norm, "fsdp", axis=0, tiled=True),
        lax.all_gather(o_proj, "fsdp", axis=0, tiled=True),
        lax.all_gather(attn_post_norm, "fsdp", axis=0, tiled=True),
        lax.all_gather(laurel_left, "fsdp", axis=0, tiled=True),
        lax.all_gather(laurel_right, "fsdp", axis=0, tiled=True),
        lax.all_gather(laurel_norm, "fsdp", axis=0, tiled=True),
        lax.all_gather(ffw_norm, "fsdp", axis=0, tiled=True),
        lax.all_gather(ffw_post_norm, "fsdp", axis=0, tiled=True),
        lax.all_gather(pl_gate, "fsdp", axis=0, tiled=True),
        lax.all_gather(pl_proj, "fsdp", axis=0, tiled=True),
        lax.all_gather(pl_post_norm, "fsdp", axis=0, tiled=True),
    )
    gain_anorm = full_anorm.astype(jnp.float32)
    gain_qnorm = full_qnorm.astype(jnp.float32)
    gain_knorm = full_knorm.astype(jnp.float32)
    gain_apost = full_apost.astype(jnp.float32)
    gain_lnorm = full_lnorm.astype(jnp.float32)
    gain_fnorm = full_fnorm.astype(jnp.float32)
    gain_fpost = full_fpost.astype(jnp.float32)
    gain_plpost = full_plpost.astype(jnp.float32)
    source = hidden_in.astype(jnp.float32)
    extra = layer_input.astype(jnp.float32)
    normed = norm_rows(source, gain_anorm)
    normed_low = normed.astype(jnp.bfloat16)
    q_raw = jnp.dot(normed_low, full_q, preferred_element_type=jnp.float32)
    k_raw = jnp.dot(normed_low, full_k, preferred_element_type=jnp.float32)
    v_raw = jnp.dot(normed_low, full_v, preferred_element_type=jnp.float32)

    def head_path(raw, gain):
        return rotate(norm_rows(raw.reshape(rows, -1, HEAD_DIM), gain), my_depth)

    q_low = head_path(q_raw, gain_qnorm).astype(jnp.bfloat16)
    k_low = head_path(k_raw, gain_knorm).reshape(rows, -1).astype(jnp.bfloat16)
    v_low = v_raw.astype(jnp.bfloat16)
    keys_all, values_all = (
        lax.all_gather(k_low, "fsdp", axis=0, tiled=True),
        lax.all_gather(v_low, "fsdp", axis=0, tiled=True),
    )
    keys_heads = keys_all.reshape(total, KV_HEADS, HEAD_DIM)
    values_heads = values_all.reshape(total, KV_HEADS, HEAD_DIM)
    query_groups = q_low.reshape(rows, KV_HEADS, groups, HEAD_DIM)
    mixed_list = []
    log_list = []
    for head in range(KV_HEADS):
        scores = (
            jnp.einsum(
                "tgd,nd->gtn",
                query_groups[:, head],
                keys_heads[:, head],
                preferred_element_type=jnp.float32,
            )
            * scale
        )
        scores = jnp.where(seen[None], scores, MASKED)
        top = jnp.max(scores, axis=-1, keepdims=True)
        expo = jnp.exp(scores - top)
        sums = jnp.sum(expo, axis=-1, keepdims=True)
        weights = (expo / sums).astype(jnp.bfloat16)
        mixed_list.append(
            jnp.einsum(
                "gtn,nd->tgd", weights, values_heads[:, head], preferred_element_type=jnp.float32
            )
        )
        log_list.append(top[..., 0] + jnp.log(sums[..., 0]))
    attended = jnp.stack(mixed_list, axis=1)
    log_sums = jnp.stack(log_list, axis=0)
    attended_low = attended.reshape(rows, -1).astype(jnp.bfloat16)
    branch = jnp.dot(attended_low, full_o, preferred_element_type=jnp.float32)
    left_low = jnp.dot(normed_low, full_left, preferred_element_type=jnp.float32).astype(
        jnp.bfloat16
    )
    low_rank = mul_t(left_low, full_right)
    first_sum = (
        source + norm_rows(branch, gain_apost) + normed + norm_rows(low_rank, gain_lnorm)
    ) * HALF_ROOT
    ffw_low = norm_rows(first_sum, gain_fnorm).astype(jnp.bfloat16)
    full_gate, full_up, full_down = (
        lax.all_gather(gate_proj, "fsdp", axis=0, tiled=True),
        lax.all_gather(up_proj, "fsdp", axis=0, tiled=True),
        lax.all_gather(down_proj, "fsdp", axis=0, tiled=True),
    )
    gate_val = mul_t(ffw_low, full_gate)
    up_val = mul_t(ffw_low, full_up)
    inner_low = gelu_mix(gate_val, up_val).astype(jnp.bfloat16)
    ffw_out = jnp.dot(inner_low, full_down, preferred_element_type=jnp.float32)
    second_sum = first_sum + norm_rows(ffw_out, gain_fpost)
    second_low = second_sum.astype(jnp.bfloat16)
    pl_pre = jnp.dot(second_low, full_plgate, preferred_element_type=jnp.float32)
    pl_mix = gelu_mix(pl_pre, extra).astype(jnp.bfloat16)
    pl_out = jnp.dot(pl_mix, full_plproj, preferred_element_type=jnp.float32)
    result = second_sum + norm_rows(pl_out, gain_plpost)
    seed = out_grad.astype(jnp.float32)
    d_plout, grad_plpost = norm_back(pl_out, gain_plpost, seed)
    d_plout_low = d_plout.astype(jnp.bfloat16)
    grad_plproj = outer(pl_mix, d_plout_low)
    d_mix = mul_t(d_plout_low, full_plproj)
    d_pre, d_extra = mix_back(pl_pre, extra, d_mix)
    d_pre_low = d_pre.astype(jnp.bfloat16)
    grad_plgate = outer(second_low, d_pre_low)
    d_second = seed + mul_t(d_pre_low, full_plgate)
    d_ffwout, grad_fpost = norm_back(ffw_out, gain_fpost, d_second)
    d_ffw_low = d_ffwout.astype(jnp.bfloat16)
    d_inner = mul_t(d_ffw_low, full_down)
    d_gate, d_up = mix_back(gate_val, up_val, d_inner)
    d_gate_low = d_gate.astype(jnp.bfloat16)
    d_up_low = d_up.astype(jnp.bfloat16)
    d_ffwin = jnp.dot(d_gate_low, full_gate, preferred_element_type=jnp.float32) + jnp.dot(
        d_up_low, full_up, preferred_element_type=jnp.float32
    )
    width = ffw_low.shape[1]
    gate_part = outer(d_gate_low, ffw_low)
    up_part = outer(d_up_low, ffw_low)
    down_part = outer(inner_low, d_ffw_low)
    stacked = lax.psum_scatter(
        jnp.concatenate([gate_part, up_part, down_part], axis=1).astype(jnp.bfloat16),
        "fsdp",
        scatter_dimension=0,
        tiled=True,
    ).astype(jnp.float32)
    grad_gate = stacked[:, :width]
    grad_up = stacked[:, width : 2 * width]
    grad_down = stacked[:, 2 * width :]
    d_first_part, grad_fnorm = norm_back(first_sum, gain_fnorm, d_ffwin)
    d_first = d_second + d_first_part
    d_scaled = d_first * HALF_ROOT
    d_branch, grad_apost = norm_back(branch, gain_apost, d_scaled)
    d_branch_low = d_branch.astype(jnp.bfloat16)
    d_lowrank, grad_lnorm = norm_back(low_rank, gain_lnorm, d_scaled)
    d_lowrank_low = d_lowrank.astype(jnp.bfloat16)
    grad_o = outer(attended_low, d_branch_low)
    d_att_low = mul_t(d_branch_low, full_o).astype(jnp.bfloat16)
    grad_right = outer(d_lowrank_low, left_low)
    d_left_low = jnp.dot(d_lowrank_low, full_right, preferred_element_type=jnp.float32).astype(
        jnp.bfloat16
    )
    grad_left = outer(normed_low, d_left_low)
    d_att_heads = d_att_low.reshape(rows, KV_HEADS, groups, HEAD_DIM)
    delta = jnp.sum(d_att_heads.astype(jnp.float32) * attended, axis=-1).transpose(1, 2, 0)
    block = 512
    count = total // block
    key_blocks = keys_heads.reshape(count, block, KV_HEADS, HEAD_DIM)
    value_blocks = values_heads.reshape(count, block, KV_HEADS, HEAD_DIM)
    seen_blocks = seen.reshape(rows, count, block).transpose(1, 0, 2)

    def key_step(d_query, item):
        keys, values, shown = item
        scores = (
            jnp.einsum("tkgd,nkd->kgtn", query_groups, keys, preferred_element_type=jnp.float32)
            * scale
        )
        scores = jnp.where(shown[None, None], scores, MASKED)
        probs = jnp.exp(scores - log_sums[..., None])
        d_probs = jnp.einsum(
            "tkgd,nkd->kgtn", d_att_heads, values, preferred_element_type=jnp.float32
        )
        d_scores = (probs * (d_probs - delta[..., None]) * scale).astype(jnp.bfloat16)
        d_query = d_query + jnp.einsum(
            "kgtn,nkd->tkgd", d_scores, keys, preferred_element_type=jnp.float32
        )
        d_keys = jnp.einsum(
            "kgtn,tkgd->nkd", d_scores, query_groups, preferred_element_type=jnp.float32
        )
        d_values = jnp.einsum(
            "kgtn,tkgd->nkd",
            probs.astype(jnp.bfloat16),
            d_att_heads,
            preferred_element_type=jnp.float32,
        )
        return (d_query, (d_keys, d_values))

    zero_query = jnp.zeros((rows, KV_HEADS, groups, HEAD_DIM), jnp.float32)
    d_query, (d_key_blocks, d_value_blocks) = lax.scan(
        key_step, zero_query, (key_blocks, value_blocks, seen_blocks)
    )
    my_dkeys, my_dvalues = (
        lax.psum_scatter(
            d_key_blocks.reshape(total, -1).astype(jnp.bfloat16),
            "fsdp",
            scatter_dimension=0,
            tiled=True,
        ).astype(jnp.float32),
        lax.psum_scatter(
            d_value_blocks.reshape(total, -1).astype(jnp.bfloat16),
            "fsdp",
            scatter_dimension=0,
            tiled=True,
        ).astype(jnp.float32),
    )
    unused_q, q_pull = jax.vjp(head_path, q_raw, gain_qnorm)
    d_qraw, grad_qnorm = q_pull(d_query.reshape(rows, HEADS, HEAD_DIM))
    unused_k, k_pull = jax.vjp(head_path, k_raw, gain_knorm)
    d_kraw, grad_knorm = k_pull(my_dkeys.reshape(rows, KV_HEADS, HEAD_DIM))
    d_q_low = d_qraw.astype(jnp.bfloat16)
    d_k_low = d_kraw.astype(jnp.bfloat16)
    d_v_low = my_dvalues.astype(jnp.bfloat16)
    grad_q = outer(normed_low, d_q_low)
    grad_k = outer(normed_low, d_k_low)
    grad_v = outer(normed_low, d_v_low)
    d_normed = (
        d_scaled
        + mul_t(d_q_low, full_q)
        + mul_t(d_k_low, full_k)
        + mul_t(d_v_low, full_v)
        + mul_t(d_left_low, full_left)
    )
    d_source_part, grad_anorm = norm_back(source, gain_anorm, d_normed)
    d_source = d_scaled + d_source_part
    shard_grads = (
        lax.psum_scatter(
            grad_anorm.astype(jnp.bfloat16), "fsdp", scatter_dimension=0, tiled=True
        ).astype(jnp.float32),
        lax.psum_scatter(
            grad_q.astype(jnp.bfloat16), "fsdp", scatter_dimension=0, tiled=True
        ).astype(jnp.float32),
        lax.psum_scatter(
            grad_k.astype(jnp.bfloat16), "fsdp", scatter_dimension=0, tiled=True
        ).astype(jnp.float32),
        lax.psum_scatter(
            grad_v.astype(jnp.bfloat16), "fsdp", scatter_dimension=0, tiled=True
        ).astype(jnp.float32),
        lax.psum_scatter(
            grad_qnorm.astype(jnp.bfloat16), "fsdp", scatter_dimension=0, tiled=True
        ).astype(jnp.float32),
        lax.psum_scatter(
            grad_knorm.astype(jnp.bfloat16), "fsdp", scatter_dimension=0, tiled=True
        ).astype(jnp.float32),
        lax.psum_scatter(
            grad_o.astype(jnp.bfloat16), "fsdp", scatter_dimension=0, tiled=True
        ).astype(jnp.float32),
        lax.psum_scatter(
            grad_apost.astype(jnp.bfloat16), "fsdp", scatter_dimension=0, tiled=True
        ).astype(jnp.float32),
        lax.psum_scatter(
            grad_left.astype(jnp.bfloat16), "fsdp", scatter_dimension=0, tiled=True
        ).astype(jnp.float32),
        lax.psum_scatter(
            grad_right.astype(jnp.bfloat16), "fsdp", scatter_dimension=0, tiled=True
        ).astype(jnp.float32),
        lax.psum_scatter(
            grad_lnorm.astype(jnp.bfloat16), "fsdp", scatter_dimension=0, tiled=True
        ).astype(jnp.float32),
        lax.psum_scatter(
            grad_fnorm.astype(jnp.bfloat16), "fsdp", scatter_dimension=0, tiled=True
        ).astype(jnp.float32),
        lax.psum_scatter(
            grad_fpost.astype(jnp.bfloat16), "fsdp", scatter_dimension=0, tiled=True
        ).astype(jnp.float32),
        lax.psum_scatter(
            grad_plgate.astype(jnp.bfloat16), "fsdp", scatter_dimension=0, tiled=True
        ).astype(jnp.float32),
        lax.psum_scatter(
            grad_plproj.astype(jnp.bfloat16), "fsdp", scatter_dimension=0, tiled=True
        ).astype(jnp.float32),
        lax.psum_scatter(
            grad_plpost.astype(jnp.bfloat16), "fsdp", scatter_dimension=0, tiled=True
        ).astype(jnp.float32),
    )
    (
        sum_anorm,
        sum_q,
        sum_k,
        sum_v,
        sum_qnorm,
        sum_knorm,
        sum_o,
        sum_apost,
        sum_left,
        sum_right,
        sum_lnorm,
        sum_fnorm,
        sum_fpost,
        sum_plgate,
        sum_plproj,
        sum_plpost,
        sum_gate,
        sum_up,
        sum_down,
    ) = (
        lax.psum(shard_grads[0].astype(jnp.bfloat16), "rep").astype(jnp.float32),
        lax.psum(shard_grads[1].astype(jnp.bfloat16), "rep").astype(jnp.float32),
        lax.psum(shard_grads[2].astype(jnp.bfloat16), "rep").astype(jnp.float32),
        lax.psum(shard_grads[3].astype(jnp.bfloat16), "rep").astype(jnp.float32),
        lax.psum(shard_grads[4].astype(jnp.bfloat16), "rep").astype(jnp.float32),
        lax.psum(shard_grads[5].astype(jnp.bfloat16), "rep").astype(jnp.float32),
        lax.psum(shard_grads[6].astype(jnp.bfloat16), "rep").astype(jnp.float32),
        lax.psum(shard_grads[7].astype(jnp.bfloat16), "rep").astype(jnp.float32),
        lax.psum(shard_grads[8].astype(jnp.bfloat16), "rep").astype(jnp.float32),
        lax.psum(shard_grads[9].astype(jnp.bfloat16), "rep").astype(jnp.float32),
        lax.psum(shard_grads[10].astype(jnp.bfloat16), "rep").astype(jnp.float32),
        lax.psum(shard_grads[11].astype(jnp.bfloat16), "rep").astype(jnp.float32),
        lax.psum(shard_grads[12].astype(jnp.bfloat16), "rep").astype(jnp.float32),
        lax.psum(shard_grads[13].astype(jnp.bfloat16), "rep").astype(jnp.float32),
        lax.psum(shard_grads[14].astype(jnp.bfloat16), "rep").astype(jnp.float32),
        lax.psum(shard_grads[15].astype(jnp.bfloat16), "rep").astype(jnp.float32),
        lax.psum(grad_gate.astype(jnp.bfloat16), "rep").astype(jnp.float32),
        lax.psum(grad_up.astype(jnp.bfloat16), "rep").astype(jnp.float32),
        lax.psum(grad_down.astype(jnp.bfloat16), "rep").astype(jnp.float32),
    )
    return (
        result.astype(jnp.bfloat16),
        d_source.astype(jnp.bfloat16),
        d_extra.astype(jnp.bfloat16),
        sum_anorm,
        sum_q,
        sum_k,
        sum_v,
        sum_qnorm,
        sum_knorm,
        sum_o,
        sum_apost,
        sum_left,
        sum_right,
        sum_lnorm,
        sum_fnorm,
        sum_gate,
        sum_up,
        sum_down,
        sum_fpost,
        sum_plgate,
        sum_plproj,
        sum_plpost,
    )


def solution(mesh):
    placed = (
        P(("rep", "fsdp"), None),
        P(("rep", "fsdp"), None),
        P(("rep", "fsdp"), None),
        P("rep", None),
        P("rep", None),
        P("fsdp"),
        P("fsdp", None),
        P("fsdp", None),
        P("fsdp", None),
        P("fsdp"),
        P("fsdp"),
        P("fsdp", None),
        P("fsdp"),
        P("fsdp", None),
        P("fsdp", None),
        P("fsdp"),
        P("fsdp"),
        P("fsdp", None),
        P("fsdp", None),
        P("fsdp", None),
        P("fsdp"),
        P("fsdp", None),
        P("fsdp", None),
        P("fsdp"),
    )
    return jax.shard_map(
        head_plan if mesh.shape["fsdp"] == HEADS else gather_plan,
        mesh=mesh,
        in_specs=placed,
        out_specs=(
            P(("rep", "fsdp"), None),
            P(("rep", "fsdp"), None),
            P(("rep", "fsdp"), None),
            P("fsdp"),
            P("fsdp", None),
            P("fsdp", None),
            P("fsdp", None),
            P("fsdp"),
            P("fsdp"),
            P("fsdp", None),
            P("fsdp"),
            P("fsdp", None),
            P("fsdp", None),
            P("fsdp"),
            P("fsdp"),
            P("fsdp", None),
            P("fsdp", None),
            P("fsdp", None),
            P("fsdp"),
            P("fsdp", None),
            P("fsdp", None),
            P("fsdp"),
        ),
        check_vma=False,
    )
```

```python
import functools
import math

import jax
import jax.numpy as jnp
from jax import lax
from jax.experimental import pallas as pl
from jax.experimental.pallas import tpu as pltpu
from jax.sharding import PartitionSpec as P

HEADS = 8
KV_HEADS = 2
HEAD_DIM = 256


EPS = 1e-06
ROPE_BASE = 1000000.0
HALF_ROOT = 0.7071067811865476
MASKED = -1e30


def norm_rows(value, gain):
    return value * lax.rsqrt(jnp.mean(value * value, axis=-1, keepdims=True) + EPS) * gain


def norm_back(value, gain, grad):
    unused, pull = jax.vjp(norm_rows, value, gain)
    return pull(grad)


def rotate(value, position):
    half = value.shape[-1] // 2
    freqs = jnp.exp(
        jnp.arange(half, dtype=jnp.float32) * (-2.0 * math.log(ROPE_BASE) / value.shape[-1])
    )
    angle = position[:, None] * freqs[None, :]
    cosine = jnp.cos(angle)[:, None, :]
    sine = jnp.sin(angle)[:, None, :]
    first_half = value[..., :half]
    second_half = value[..., half:]
    return jnp.concatenate(
        [first_half * cosine - second_half * sine, second_half * cosine + first_half * sine],
        axis=-1,
    )


def tree_tables(lengths, parents, total):
    count = lengths.shape[0]
    labels = jnp.arange(count, dtype=jnp.int32)
    ends = jnp.cumsum(lengths)
    starts = ends - lengths
    tokens = jnp.arange(total, dtype=jnp.int32)
    segment = jnp.sum((ends[None, :] <= tokens[:, None]).astype(jnp.int32), axis=1)
    parent_hot = ((parents[:, None] == labels[None, :]) & (labels[:, None] > 0)).astype(jnp.int32)
    identity = (labels[:, None] == labels[None, :]).astype(jnp.int32)
    ancestors = lax.fori_loop(
        0, count, lambda step, held: jnp.minimum(1, identity + jnp.dot(parent_hot, held)), identity
    )
    offset = jnp.dot(ancestors - identity, lengths) - starts
    member = (segment[:, None] == labels[None, :]).astype(jnp.int32)
    reach = jnp.dot(member, ancestors)
    position = jnp.dot(member, offset) + tokens
    return (tokens, member, reach, position)


def outer(left, right):
    return lax.dot_general(
        left, right, (((0,), (0,)), ((), ())), preferred_element_type=jnp.float32
    )


def mul_t(left, right):
    return lax.dot_general(
        left, right, (((1,), (1,)), ((), ())), preferred_element_type=jnp.float32
    )


def gelu_mix(first, second):
    return jax.nn.gelu(first, approximate=True) * second


def mix_back(first, second, grad):
    unused, pull = jax.vjp(gelu_mix, first, second)
    return pull(grad)


MESH = pl.DeviceIdType.MESH
VMEM_BYTES = 48 << 20


def ring_place(index):
    side = lax.rem(index, 2)
    return index // 2 + side * (HEADS - 1 - 2 * (index // 2))


def ring_index(place):
    back = place // (HEADS // 2)
    return (1 - back) * 2 * place + back * (2 * HEADS - 1 - 2 * place)


def ring_ends(place):
    after = {"fsdp": ring_index(lax.rem(place + 1, HEADS))}
    before = {"fsdp": ring_index(lax.rem(place + HEADS - 1, HEADS))}
    return (after, before)


def greet(others):
    barrier = pltpu.get_barrier_semaphore()
    for other in others:
        pl.semaphore_signal(barrier, inc=1, device_id=other, device_id_type=MESH)
    pl.semaphore_wait(barrier, len(others))


def span(start, size):
    return pl.ds(pl.multiple_of(start, size), size)


def neighbours():
    rep = lax.axis_index("rep")
    chip = rep // 2
    core = lax.rem(rep, 2)
    return (chip, core, {"rep": 2 * chip + 1 - core}, {"rep": 2 * (1 - chip) + core})


def remote(source, target, sems, number, device):
    copy = pltpu.make_async_remote_copy(
        source,
        target,
        sems[0].at[number],
        sems[1].at[number],
        device_id=device,
        device_id_type=MESH,
    )
    copy.start()
    return copy


class Ring:
    def __init__(self, place, ends, lanes, sems, own, there):
        self.place, self.ends, self.lanes, self.sems = place, ends, lanes, sems
        self.own, self.there = own, there
        self.copies = []

    def owner(self, step, lane):
        ahead = step if lane % 2 else HEADS - step
        return ring_index(lax.rem(self.place + ahead, HEADS))

    def send(self, step):
        for lane in range(self.lanes):
            number = step * self.lanes + lane
            target = self.there(self.owner(step, lane), lane)
            if step:
                self.copies[number - self.lanes].wait_recv()
            source = target if step else self.own(lane)
            self.copies.append(remote(source, target, self.sems, number, self.ends[lane % 2]))

    def arrive(self, step):
        for lane in range(self.lanes):
            self.copies[(step - 1) * self.lanes + lane].wait_recv()

    def sent(self):
        for copy in self.copies:
            copy.wait_send()


class Mirror:
    def __init__(self, count, sems):
        unused_chip, unused_core, self.sibling, self.across = neighbours()
        self.count, self.sems = count, sems
        self.copies = [None] * (3 * count)

    def give(self, number, ref):
        self.copies[number] = remote(ref, ref, self.sems, number, self.sibling)
        self.copies[self.count + number] = remote(
            ref, ref, self.sems, self.count + number, self.across
        )

    def relay(self, number, ref):
        self.copies[self.count + number].wait_recv()
        self.copies[2 * self.count + number] = remote(
            ref, ref, self.sems, 2 * self.count + number, self.sibling
        )

    def finish(self):
        for number, copy in enumerate(self.copies):
            if number // self.count != 1:
                copy.wait_recv()
            copy.wait_send()


RING_STEPS = HEADS - 1
QUARTERS = 4


def start_kernel(
    hidden_ref,
    gains_ref,
    q_ref,
    kv_ref,
    small_ref,
    plproj_ref,
    hidden_all,
    gains_all,
    q_head,
    kv_all,
    small_all,
    plproj_all,
    local_sems,
    *sems,
):
    pairs = [sems[i : i + 2] for i in range(0, len(sems), 2)]
    hidden_sems, gains_sems, q_sems, kv_sems, small_sems, plproj_sems = pairs[:6]
    q_mirror_sems, kv_mirror_sems, small_mirror_sems, plproj_mirror_sems = pairs[6:]
    index = lax.axis_index("fsdp")
    chip, core, sibling, across = neighbours()
    quarter = 2 * chip + core
    other_quarter = 2 * (1 - chip) + core
    place = ring_place(index)
    ends = ring_ends(place)
    others = [lax.rem(index + step, HEADS) for step in range(1, HEADS)]
    greet([{"fsdp": other} for other in others] + [sibling, across])
    rows = hidden_ref.shape[0]
    shard = q_ref.shape[0]
    deep = plproj_ref.shape[0]
    q_rows = shard // QUARTERS
    wide = plproj_ref.shape[1] // QUARTERS

    locals_list = []
    for source, target in (
        (hidden_ref, hidden_all.at[span(index * rows, rows)]),
        (gains_ref, gains_all.at[span(index * gains_ref.shape[0], gains_ref.shape[0])]),
        (
            q_ref.at[:, span(index * HEAD_DIM, HEAD_DIM)],
            q_head.at[span(index * shard, shard)],
        ),
        (kv_ref, kv_all.at[span(index * shard, shard)]),
        (small_ref, small_all.at[span(index * shard, shard)]),
        (plproj_ref, plproj_all.at[span(index * deep, deep)]),
    ):
        copy = pltpu.make_async_copy(source, target, local_sems.at[len(locals_list)])
        copy.start()
        locals_list.append(copy)

    hidden_part = rows // 4
    gains_part = gains_ref.shape[0] // 2
    shard_part = shard // QUARTERS // 2
    wide_part = wide // 2

    def shard_at(ref, part_of):
        return lambda owner, lane: ref.at[
            span(owner * shard + part_of * 2 * shard_part + lane * shard_part, shard_part)
        ]

    def plproj_at(part_of):
        return lambda owner, lane: plproj_all.at[
            span(owner * deep, deep), span(part_of * wide + lane * wide_part, wide_part)
        ]

    hidden = Ring(
        place,
        ends,
        4,
        hidden_sems,
        lambda lane: hidden_ref.at[pl.ds(lane * hidden_part, hidden_part)],
        lambda owner, lane: hidden_all.at[span(owner * rows + lane * hidden_part, hidden_part)],
    )
    gains = Ring(
        place,
        ends,
        2,
        gains_sems,
        lambda lane: gains_ref.at[pl.ds(lane * gains_part, gains_part)],
        lambda owner, lane: gains_all.at[
            span(owner * gains_ref.shape[0] + lane * gains_part, gains_part)
        ],
    )

    def shard_own(ref):
        return lambda lane: ref.at[
            span(quarter * 2 * shard_part + lane * shard_part, shard_part)
        ]

    kv = Ring(place, ends, 2, kv_sems, shard_own(kv_ref), shard_at(kv_all, quarter))
    small = Ring(place, ends, 2, small_sems, shard_own(small_ref), shard_at(small_all, quarter))
    plproj = Ring(
        place,
        ends,
        2,
        plproj_sems,
        lambda lane: plproj_ref.at[:, span(quarter * wide + lane * wide_part, wide_part)],
        plproj_at(quarter),
    )
    mirrored = [
        (kv, Mirror(2 * RING_STEPS, kv_mirror_sems), shard_at(kv_all, other_quarter)),
        (small, Mirror(2 * RING_STEPS, small_mirror_sems), shard_at(small_all, other_quarter)),
        (plproj, Mirror(2 * RING_STEPS, plproj_mirror_sems), plproj_at(other_quarter)),
    ]
    q_mirror = Mirror(HEADS - 1, q_mirror_sems)
    q_copies = []
    q_landing = q_head.at[span(index * shard + quarter * q_rows, q_rows)]
    for step, other in enumerate(others):
        source = q_ref.at[span(quarter * q_rows, q_rows), span(other * HEAD_DIM, HEAD_DIM)]
        q_copies.append(remote(source, q_landing, q_sems, step, {"fsdp": other}))

    def q_at(step, part_of):
        giver = lax.rem(index + HEADS - 1 - step, HEADS)
        return q_head.at[span(giver * shard + part_of * q_rows, q_rows)]

    def pass_on(step):
        for ring, mirror, unused_there in mirrored:
            for lane in range(2):
                mirror.give((step - 1) * 2 + lane, ring.there(ring.owner(step, lane), lane))

    def pass_again(step):
        for ring, mirror, there in mirrored:
            for lane in range(2):
                mirror.relay((step - 1) * 2 + lane, there(ring.owner(step, lane), lane))

    for step in range(RING_STEPS):
        gains.send(step)
        for ring, unused_mirror, unused_there in mirrored:
            ring.send(step)
        hidden.send(step)
        if step >= 1:
            pass_on(step)
        if step >= 2:
            pass_again(step - 1)
        if step == 4:
            for number, copy in enumerate(q_copies):
                copy.wait_recv()
                q_mirror.give(number, q_at(number, quarter))
        if step == 5:
            for number in range(HEADS - 1):
                q_mirror.relay(number, q_at(number, other_quarter))
    for ring, unused_mirror, unused_there in mirrored:
        ring.arrive(RING_STEPS)
    pass_on(RING_STEPS)
    pass_again(RING_STEPS - 1)
    pass_again(RING_STEPS)
    gains.arrive(RING_STEPS)
    hidden.arrive(RING_STEPS)
    for ring, mirror, unused_there in mirrored:
        ring.sent()
        mirror.finish()
    hidden.sent()
    gains.sent()
    for copy in q_copies:
        copy.wait_send()
    q_mirror.finish()
    for copy in locals_list:
        copy.wait()


def start_gather(hidden, gains, q_proj, kv, small, pl_proj, number):
    shard = q_proj.shape[0]
    arrays = (hidden, gains, q_proj, kv, small, pl_proj)

    def grown(item, rows=None, columns=None):
        rows = rows or item.shape[0] * HEADS
        return jax.ShapeDtypeStruct((rows, columns or item.shape[1]), item.dtype)

    counts = [4 * RING_STEPS, 2 * RING_STEPS, RING_STEPS] + [2 * RING_STEPS] * 3
    counts += [3 * RING_STEPS] + [6 * RING_STEPS] * 3
    return pl.pallas_call(
        start_kernel,
        out_shape=[
            grown(hidden),
            grown(gains),
            grown(q_proj, shard * HEADS, HEAD_DIM),
            grown(kv),
            grown(small),
            grown(pl_proj),
        ],
        in_specs=[pl.BlockSpec(memory_space=pl.ANY)] * len(arrays),
        out_specs=[pl.BlockSpec(memory_space=pl.ANY)] * len(arrays),
        scratch_shapes=[pltpu.SemaphoreType.DMA((len(arrays),))]
        + [pltpu.SemaphoreType.DMA((count,)) for count in counts for unused_side in range(2)],
        compiler_params=pltpu.CompilerParams(collective_id=number, has_side_effects=True),
    )(*arrays)


def gather_kernel(own_ref, all_ref, local_sem, send_sem, recv_sem):
    rows = own_ref.shape[0]
    part = rows // 4
    index = lax.axis_index("fsdp")
    place = ring_place(index)
    ends = ring_ends(place)
    greet(ends)
    local = pltpu.make_async_copy(own_ref, all_ref.at[span(index * rows, rows)], local_sem)
    local.start()
    ring = Ring(
        place,
        ends,
        4,
        (send_sem, recv_sem),
        lambda lane: own_ref.at[pl.ds(lane * part, part)],
        lambda owner, lane: all_ref.at[span(owner * rows + lane * part, part)],
    )
    for step in range(RING_STEPS):
        ring.send(step)
    ring.arrive(RING_STEPS)
    ring.sent()
    local.wait()


def ring_gather(own, number):
    spec = pl.BlockSpec(memory_space=pl.ANY)
    return pl.pallas_call(
        gather_kernel,
        out_shape=[jax.ShapeDtypeStruct((own.shape[0] * HEADS, own.shape[1]), own.dtype)],
        in_specs=[spec],
        out_specs=[spec],
        scratch_shapes=[pltpu.SemaphoreType.DMA]
        + [pltpu.SemaphoreType.DMA((4 * RING_STEPS,))] * 2,
        compiler_params=pltpu.CompilerParams(collective_id=number, has_side_effects=True),
    )(own)


def add_low(left, right):
    return (left.astype(jnp.float32) + right.astype(jnp.float32)).astype(jnp.bfloat16)


class RingSum:
    def __init__(self, place, ends, lanes, sems, held, own):
        self.place, self.ends, self.lanes, self.sems = place, ends, lanes, sems
        self.held, self.own = held, own
        self.copies = []

    def send(self, step):
        for lane in range(self.lanes):
            ahead = step + 1 if lane % 2 else HEADS - 1 - step
            owner = ring_index(lax.rem(self.place + ahead, HEADS))
            number = step * self.lanes + lane
            if step:
                slot = number - self.lanes
                self.copies[slot].wait_recv()
                value = self.held[slot].astype(jnp.float32) + self.own(owner, lane)
            else:
                slot = RING_STEPS * self.lanes + lane
                value = self.own(owner, lane)
            self.held[slot] = value.astype(jnp.bfloat16)
            self.copies.append(
                remote(self.held.at[slot], self.held.at[number], self.sems, number, self.ends[lane % 2])
            )

    def last(self, index, lane):
        number = (RING_STEPS - 1) * self.lanes + lane
        self.copies[number].wait_recv()
        return self.held[number].astype(jnp.float32) + self.own(index, lane)

    def sent(self):
        for copy in self.copies:
            copy.wait_send()


def scatter_kernel(part_ref, *refs):
    if len(refs) > 4:
        blocks_ref, sum_ref, block_sum, held, send_sem, recv_sem, block_held, block_send, block_recv = refs
    else:
        blocks_ref = None
        sum_ref, held, send_sem, recv_sem = refs
    rows = sum_ref.shape[0]
    part = rows // 4
    index = lax.axis_index("fsdp")
    place = ring_place(index)
    ends = ring_ends(place)
    greet(ends)

    def own(owner, lane):
        return part_ref[span(owner * rows + lane * part, part), :].astype(jnp.float32)

    rings = [RingSum(place, ends, 4, (send_sem, recv_sem), held, own)]
    if blocks_ref is not None:
        low_rows = block_sum.shape[0] // 2

        def block_own(owner, lane):
            return blocks_ref[owner, pl.ds(lane * low_rows, low_rows), :].astype(jnp.float32)

        rings.append(RingSum(place, ends, 2, (block_send, block_recv), block_held, block_own))
    for step in range(RING_STEPS):
        for ring in rings:
            ring.send(step)
    for lane in range(4):
        sum_ref[pl.ds(lane * part, part), :] = rings[0].last(index, lane)
    if blocks_ref is not None:
        for lane in range(2):
            block_sum[pl.ds(lane * low_rows, low_rows), :] = (
                rings[1].last(index, lane).astype(jnp.bfloat16)
            )
    for ring in rings:
        ring.sent()


def ring_scatter(parts, number, blocks=None):
    rows = parts.shape[0] // HEADS
    near = pl.BlockSpec(memory_space=pltpu.VMEM)
    out_shape = [jax.ShapeDtypeStruct((rows, parts.shape[1]), jnp.float32)]
    steps = 4 * RING_STEPS
    scratch = [pltpu.VMEM((steps + 4, rows // 4, parts.shape[1]), jnp.bfloat16)]
    scratch += [pltpu.SemaphoreType.DMA((steps,))] * 2
    arrays = [parts]
    if blocks is not None:
        arrays.append(blocks)
        out_shape.append(jax.ShapeDtypeStruct(blocks.shape[1:], jnp.bfloat16))
        steps = 2 * RING_STEPS
        shape = (steps + 2, blocks.shape[1] // 2, blocks.shape[2])
        scratch += [pltpu.VMEM(shape, jnp.bfloat16)] + [pltpu.SemaphoreType.DMA((steps,))] * 2
    return pl.pallas_call(
        scatter_kernel,
        out_shape=out_shape,
        in_specs=[near] * len(arrays),
        out_specs=[near] * len(out_shape),
        scratch_shapes=scratch,
        compiler_params=pltpu.CompilerParams(
            collective_id=number, has_side_effects=True, vmem_limit_bytes=VMEM_BYTES
        ),
    )(*arrays)


def lane_offset(lane, rows):
    return (lane % 2) * (rows // 2) + (lane // 2) * (rows // 4)


def tile_loop(count, size, body):
    def step(number, carry):
        body(span(number * size, size))
        return carry

    lax.fori_loop(0, count, step, 0)


class Pair:
    def __init__(self, place, step, rows):
        half = rows // 2
        behind = ring_index(lax.rem(place + HEADS - step, HEADS))
        ahead = ring_index(lax.rem(place + step, HEADS))
        self.half = half
        self.rows = (span(behind * rows, half), span(ahead * rows + half, half))

    def read(self, ref, columns=slice(None)):
        return jnp.concatenate([ref[rows, columns] for rows in self.rows], axis=0)

    def write(self, ref, columns, value):
        for side, rows in enumerate(self.rows):
            ref[rows, columns] = value[side * self.half : (side + 1) * self.half]


GELU_ROOT = math.sqrt(2.0 / math.pi)
GELU_CUBE = 0.044715
TILE = 256


def start_loads(pairs, sems):
    copies = []
    for number, (source, target) in enumerate(pairs):
        copy = pltpu.make_async_copy(source, target, sems.at[number])
        copy.start()
        copies.append(copy)
    return copies


def ffn_kernel(
    own_ref,
    gate_any,
    up_any,
    down_any,
    sum_ref,
    all_ref,
    act_ref,
    slope_ref,
    inner_ref,
    gate,
    up,
    down,
    block,
    inner_block,
    part,
    held,
    load_sems,
    send_sem,
    recv_sem,
    sum_send,
    sum_recv,
):
    rows, width = own_ref.shape
    units = gate.shape[0]
    piece = rows // 4
    index = lax.axis_index("fsdp")
    place = ring_place(index)
    ends = ring_ends(place)
    loads = start_loads(((gate_any, gate), (up_any, up), (down_any, down)), load_sems)
    greet(ends)
    ring = Ring(
        place,
        ends,
        4,
        (send_sem, recv_sem),
        lambda lane: own_ref.at[pl.ds(lane_offset(lane, rows), piece)],
        lambda owner, lane: all_ref.at[span(owner * rows + lane_offset(lane, rows), piece)],
    )

    def own(owner, lane):
        return part[span(owner * rows + lane_offset(lane, rows), piece), :].astype(jnp.float32)

    sums = RingSum(place, ends, 4, (sum_send, sum_recv), held, own)

    def compute(step):
        pair = Pair(place, step, rows)
        block[...] = pair.read(all_ref)

        def into(tile):
            value = mul_t(block[...], gate[tile, :])
            second = mul_t(block[...], up[tile, :])
            square = value * value
            bent = jnp.tanh(GELU_ROOT * value * (1.0 + GELU_CUBE * square))
            share = 0.5 * (1.0 + bent)
            act = value * share
            slope = share + (0.5 * GELU_ROOT) * value * (1.0 - bent * bent) * (
                1.0 + (3.0 * GELU_CUBE) * square
            )
            inner = low(act * second)
            inner_block[:, tile] = inner
            pair.write(act_ref, tile, low(act))
            pair.write(slope_ref, tile, low(slope * second))
            pair.write(inner_ref, tile, inner)

        tile_loop(units // TILE, TILE, into)

        def out(tile):
            pair.write(part, tile, low(dot(inner_block[...], down[:, tile])))

        tile_loop(width // (2 * TILE), 2 * TILE, out)

    ring.send(0)
    all_ref[span(index * rows, rows), :] = own_ref[...]
    for copy in loads:
        copy.wait()
    compute(0)
    for step in range(1, HEADS):
        if step < RING_STEPS:
            ring.send(step)
        else:
            ring.arrive(step)
        compute(step)
        sums.send(step - 1)
    for lane in range(4):
        sum_ref[pl.ds(lane_offset(lane, rows), piece), :] = sums.last(index, lane)
    ring.sent()
    sums.sent()


def ffn_forward(own, gate, up, down, number):
    rows, width = own.shape
    units = gate.shape[0]
    near, anywhere = pl.BlockSpec(memory_space=pltpu.VMEM), pl.BlockSpec(memory_space=pl.ANY)
    total = rows * HEADS
    steps = 4 * RING_STEPS
    bf16 = jnp.bfloat16
    inner = jax.ShapeDtypeStruct((total, units), bf16)
    return pl.pallas_call(
        ffn_kernel,
        out_shape=[
            jax.ShapeDtypeStruct((rows, width), jnp.float32),
            jax.ShapeDtypeStruct((total, width), bf16),
            inner,
            inner,
            inner,
        ],
        in_specs=[near] + [anywhere] * 3,
        out_specs=[near] * 5,
        scratch_shapes=[pltpu.VMEM((units, width), bf16)] * 3
        + [
            pltpu.VMEM((rows, width), bf16),
            pltpu.VMEM((rows, units), bf16),
            pltpu.VMEM((total, width), bf16),
            pltpu.VMEM((steps + 4, rows // 4, width), bf16),
            pltpu.SemaphoreType.DMA((3,)),
        ]
        + [pltpu.SemaphoreType.DMA((steps,))] * 4,
        compiler_params=pltpu.CompilerParams(
            collective_id=number, has_side_effects=True, vmem_limit_bytes=VMEM_BYTES
        ),
    )(own, gate, up, down)


def ffn_back_kernel(
    own_ref,
    all_any,
    act_any,
    slope_any,
    inner_any,
    gate_any,
    up_any,
    down_any,
    blocks_ref,
    sum_ref,
    down_out,
    gate_out,
    up_out,
    far_down,
    block_sum,
    d_all,
    tokens,
    d_up,
    d_gate,
    inner,
    gate,
    up,
    down,
    block,
    inner_block,
    part,
    held,
    turned,
    give,
    keep,
    theirs,
    block_held,
    load_sems,
    store_sems,
    *sems,
):
    ring_sems, sum_sems, fold_sems, block_sems, far_sems = [
        sems[i : i + 2] for i in range(0, 10, 2)
    ]
    rows, width = own_ref.shape
    units = gate.shape[0]
    piece = rows // 4
    index = lax.axis_index("fsdp")
    place = ring_place(index)
    ends = ring_ends(place)
    unused_chip, core, sibling, across = neighbours()
    load_down, load_act, load_slope, load_gate, load_up, load_inner, load_tokens = start_loads(
        (
            (down_any, down),
            (act_any, d_up),
            (slope_any, d_gate),
            (gate_any, gate),
            (up_any, up),
            (inner_any, inner),
            (all_any, tokens),
        ),
        load_sems,
    )
    greet(ends + (sibling, across))
    ring = Ring(
        place,
        ends,
        4,
        ring_sems,
        lambda lane: own_ref.at[pl.ds(lane_offset(lane, rows), piece)],
        lambda owner, lane: d_all.at[span(owner * rows + lane_offset(lane, rows), piece)],
    )

    def own(owner, lane):
        return part[span(owner * rows + lane_offset(lane, rows), piece), :].astype(jnp.float32)

    low_rows = block_sum.shape[0] // 2

    def block_own(owner, lane):
        return blocks_ref[owner, pl.ds(lane * low_rows, low_rows), :].astype(jnp.float32)

    sums = RingSum(place, ends, 4, sum_sems, held, own)
    block_sums = RingSum(place, ends, 2, block_sems, block_held, block_own)

    def compute(step):
        pair = Pair(place, step, rows)
        block[...] = pair.read(d_all)

        def into(tile):
            grad = mul_t(block[...], down[tile, :])
            first = low(grad * pair.read(d_gate, tile).astype(jnp.float32))
            second = low(grad * pair.read(d_up, tile).astype(jnp.float32))
            pair.write(d_gate, tile, first)
            pair.write(d_up, tile, second)
            inner_block[0, :, tile] = first
            inner_block[1, :, tile] = second

        tile_loop(units // TILE, TILE, into)
        if step == 0:
            load_gate.wait()
            load_up.wait()

        def out(tile):
            total = dot(inner_block[0], gate[:, tile]) + dot(inner_block[1], up[:, tile])
            pair.write(part, tile, low(total))

        tile_loop(width // (2 * TILE), 2 * TILE, out)

    half = units // 2
    folds, stores, swaps = [], [], []
    jobs = (
        (inner, d_all, down_out),
        (d_gate, tokens, gate_out),
        (d_up, tokens, up_out),
    )

    def outer_half(number, side, target):
        left, right, unused_out = jobs[number]
        turned[...] = left[:, span(side * half, half)].T

        def tile_step(tile):
            target[:, tile] = low(dot(turned[...], right[:, tile]))

        tile_loop(width // (2 * TILE), 2 * TILE, tile_step)

    def grads_give(number):
        if number:
            folds[number - 1].wait_send()
        outer_half(number, 1 - core, give)
        folds.append(remote(give, theirs.at[number], fold_sems, number, sibling))

    def grads_keep(number):
        if number > 1:
            stores[number - 1].wait()
        outer_half(number, core, keep)
        folds[number].wait_recv()

        def add(tile):
            keep[tile, :] = add_low(keep[tile, :], theirs[number, tile, :])

        tile_loop(half // 64, 64, add)
        store = pltpu.make_async_copy(keep, jobs[number][2], store_sems.at[number])
        store.start()
        stores.append(store)
        if not number:
            store.wait()
            swaps.append(remote(down_out, far_down, far_sems, 0, across))

    ring.send(0)
    d_all[span(index * rows, rows), :] = own_ref[...]
    for copy in (load_down, load_act, load_slope):
        copy.wait()
    compute(0)
    for step in range(1, HEADS):
        if step < RING_STEPS:
            ring.send(step)
        else:
            ring.arrive(step)
        if step >= RING_STEPS - 1:
            sums.send(step - RING_STEPS + 1)
        compute(step)
    load_inner.wait()
    load_tokens.wait()
    for step in range(RING_STEPS):
        if step >= 2:
            sums.send(step)
        block_sums.send(step)
        if step < 6:
            if step % 2:
                grads_keep(step // 2)
            else:
                grads_give(step // 2)
    for lane in range(4):
        sum_ref[pl.ds(lane_offset(lane, rows), piece), :] = sums.last(index, lane)
    for lane in range(2):
        block_sum[pl.ds(lane * low_rows, low_rows), :] = low(block_sums.last(index, lane))
    for item in (ring, sums, block_sums):
        item.sent()
    folds[-1].wait_send()
    stores[-1].wait()
    swaps[0].wait()


def ffn_back(own, arrays, weights, blocks, number):
    rows, width = own.shape
    units = weights[0].shape[0]
    near, anywhere = pl.BlockSpec(memory_space=pltpu.VMEM), pl.BlockSpec(memory_space=pl.ANY)
    total = rows * HEADS
    steps = 4 * RING_STEPS
    bf16 = jnp.bfloat16
    counts = [steps, steps, 3, 2 * RING_STEPS, 1]
    half = (units // 2, width)
    low_rows = blocks.shape[1] // 2
    return pl.pallas_call(
        ffn_back_kernel,
        out_shape=[jax.ShapeDtypeStruct((rows, width), jnp.float32)]
        + [jax.ShapeDtypeStruct(half, bf16)] * 4
        + [jax.ShapeDtypeStruct(blocks.shape[1:], bf16)],
        in_specs=[near] + [anywhere] * 7 + [near],
        out_specs=[near] + [anywhere] * 4 + [near],
        scratch_shapes=[pltpu.VMEM((total, width), bf16)] * 2
        + [pltpu.VMEM((total, units), bf16)] * 3
        + [pltpu.VMEM((units, width), bf16)] * 3
        + [
            pltpu.VMEM((rows, width), bf16),
            pltpu.VMEM((2, rows, units), bf16),
            pltpu.VMEM((total, width), bf16),
            pltpu.VMEM((steps + 4, rows // 4, width), bf16),
            pltpu.VMEM((units // 2, total), bf16),
            pltpu.VMEM(half, bf16),
            pltpu.VMEM(half, bf16),
            pltpu.VMEM((3,) + half, bf16),
            pltpu.VMEM((2 * RING_STEPS + 2, low_rows, blocks.shape[2]), bf16),
            pltpu.SemaphoreType.DMA((7,)),
            pltpu.SemaphoreType.DMA((3,)),
        ]
        + [pltpu.SemaphoreType.DMA((count,)) for count in counts for unused_side in range(2)],
        compiler_params=pltpu.CompilerParams(
            collective_id=number, has_side_effects=True, vmem_limit_bytes=56 << 20
        ),
    )(own, *arrays, *weights, blocks)


ACROSS = ((0, 2), (2, 0), (1, 3), (3, 1))
SIBLING = ((0, 1), (1, 0), (2, 3), (3, 2))


def tail_kernel(
    grads_ref,
    weights_ref,
    blocks_ref,
    early_ref,
    sum_ref,
    owned_ref,
    early_all,
    held,
    part,
    keep,
    folded,
    far,
    near_sum,
    key_held,
    *sems,
):
    ring_sems, fold_sems, far_sems, swap_sems, key_sems, mirror_sems, early_sems = [
        sems[i : i + 2] for i in range(0, 14, 2)
    ]
    load_sem = sems[14]
    rows = sum_ref.shape[0]
    half = rows // 2
    piece = rows // 4
    lanes = 4
    index = lax.axis_index("fsdp")
    chip, core, sibling, across = neighbours()
    place = ring_place(index)
    ends = ring_ends(place)
    others = [lax.rem(index + step, HEADS) for step in range(1, HEADS)]
    greet([{"fsdp": other} for other in others] + [sibling, across])
    quarter_rows = blocks_ref.shape[2]
    folds, loads = [], []
    for side in range(2):
        folds.append(
            remote(blocks_ref.at[:, 2 * side + 1 - core], folded.at[side], fold_sems, side, sibling)
        )
        load = pltpu.make_async_copy(
            blocks_ref.at[:, 2 * side + core], keep.at[side], load_sem.at[side]
        )
        load.start()
        loads.append(load)

    quarter = 2 * chip + core
    own_rows = span(quarter * quarter_rows, quarter_rows)
    other_rows = span((2 * (1 - chip) + core) * quarter_rows, quarter_rows)
    early_all[own_rows, :] = early_ref[...]
    early = Mirror(1, early_sems)
    early.give(0, early_all.at[own_rows])

    def owner_at(step, way):
        return ring_index(lax.rem(place + (step + 1 if way else HEADS - 1 - step), HEADS))

    def compute(step):
        tops = [
            grads_ref[span(owner_at(step, way) * rows + way * half, half), :] for way in range(2)
        ]
        part[...] = mul_t(jnp.concatenate(tops, axis=0), weights_ref[...])

    def lane_rows(lane):
        return pl.ds((lane % 2) * half + (lane // 2) * piece, piece)

    across_sends, swaps, key_swaps = [], [], []
    mirror = Mirror(1, mirror_sems)
    rest = blocks_ref.shape[3] - HEAD_DIM
    q_columns = HEADS * HEAD_DIM

    def fold_step():
        for side in range(2):
            folds[side].wait_recv()
            loads[side].wait()
        for block in range(HEADS):
            keep[1 - chip, block] = add_low(keep[1 - chip, block], folded[1 - chip, block])
        across_sends.append(remote(keep.at[1 - chip], far, far_sems, 0, across))
        for block in range(HEADS):
            keep[chip, block] = add_low(keep[chip, block], folded[chip, block])

    def swap_step():
        across_sends[0].wait_recv()
        for block in range(HEADS):
            near_sum[block] = add_low(keep[chip, block], far[block])
        mine = span(index * HEAD_DIM, HEAD_DIM)
        for step, other in enumerate(others):
            swaps.append(
                remote(
                    near_sum.at[other, :, pl.ds(0, HEAD_DIM)],
                    owned_ref.at[own_rows, mine],
                    swap_sems,
                    step,
                    {"fsdp": other},
                )
            )
            key_swaps.append(
                remote(
                    near_sum.at[other, :, pl.ds(HEAD_DIM, rest)],
                    key_held.at[index],
                    key_sems,
                    step,
                    {"fsdp": other},
                )
            )
        owned_ref[own_rows, mine] = near_sum[index, :, :HEAD_DIM]
        key_held[index] = near_sum[index, :, HEAD_DIM:]

    copies = []
    for step in range(RING_STEPS):
        compute(step)
        for lane in range(lanes):
            number = step * lanes + lane
            if step:
                copies[number - lanes].wait_recv()
                held[number - lanes] = (
                    held[number - lanes].astype(jnp.float32) + part[lane_rows(lane), :]
                ).astype(jnp.bfloat16)
                source = held.at[number - lanes]
            else:
                source = held.at[RING_STEPS * lanes + lane]
                source[...] = part[lane_rows(lane), :].astype(jnp.bfloat16)
            copies.append(remote(source, held.at[number], ring_sems, number, ends[lane % 2]))
        if step == 1:
            fold_step()
        if step == 3:
            early.relay(0, early_all.at[other_rows])
        if step == 4:
            swap_step()
    tops = grads_ref[span(index * rows, rows), :]
    part[...] = mul_t(tops, weights_ref[...])
    for lane in range(lanes):
        number = (RING_STEPS - 1) * lanes + lane
        copies[number].wait_recv()
        sum_ref[lane_rows(lane), :] = held[number].astype(jnp.float32) + part[lane_rows(lane), :]
    for copy in swaps + key_swaps:
        copy.wait_recv()
    groups = HEADS // KV_HEADS
    for head in range(KV_HEADS):
        total = key_held[head * groups].astype(jnp.float32)
        for step in range(1, groups):
            total = total + key_held[head * groups + step].astype(jnp.float32)
        total = total.astype(jnp.bfloat16)
        for side in range(2):
            base = q_columns + (side * KV_HEADS + head) * HEAD_DIM
            owned_ref[own_rows, pl.ds(base, HEAD_DIM)] = total[
                :, side * HEAD_DIM : (side + 1) * HEAD_DIM
            ]
    extra = key_held[0, :, 2 * HEAD_DIM :].astype(jnp.float32)
    for step in range(1, HEADS):
        extra = extra + key_held[step, :, 2 * HEAD_DIM :].astype(jnp.float32)
    base = q_columns + 2 * KV_HEADS * HEAD_DIM
    owned_ref[own_rows, pl.ds(base, rest - 2 * HEAD_DIM)] = extra.astype(jnp.bfloat16)
    mirror.give(0, owned_ref.at[own_rows])
    mirror.relay(0, owned_ref.at[other_rows])
    mirror.finish()
    early.finish()
    for copy in copies + folds + across_sends + swaps + key_swaps:
        copy.wait_send()


def tail_scatter(grads, weights, blocks, early, number):
    rows = grads.shape[0] // HEADS
    width = weights.shape[0]
    shard = width // HEADS
    steps = 4 * RING_STEPS
    quarter = shard // QUARTERS
    across = blocks.shape[1]
    rest = across - HEAD_DIM
    blocks = blocks.reshape(HEADS, QUARTERS, quarter, across)
    near = pl.BlockSpec(memory_space=pltpu.VMEM)
    bf16 = jnp.bfloat16
    counts = [steps, 2, 1, HEADS - 1, HEADS - 1, 3, 3]
    owned = (HEADS + 2 * KV_HEADS) * HEAD_DIM + rest - 2 * HEAD_DIM
    return pl.pallas_call(
        tail_kernel,
        out_shape=[
            jax.ShapeDtypeStruct((rows, width), jnp.float32),
            jax.ShapeDtypeStruct((shard, owned), bf16),
            jax.ShapeDtypeStruct((shard, early.shape[1]), bf16),
        ],
        in_specs=[near, near, pl.BlockSpec(memory_space=pl.ANY), near],
        out_specs=[near] * 3,
        scratch_shapes=[
            pltpu.VMEM((steps + 4, rows // 4, width), bf16),
            pltpu.VMEM((rows, width), jnp.float32),
            pltpu.VMEM((2, HEADS, quarter, across), bf16),
            pltpu.VMEM((2, HEADS, quarter, across), bf16),
            pltpu.VMEM((HEADS, quarter, across), bf16),
            pltpu.VMEM((HEADS, quarter, across), bf16),
            pltpu.VMEM((HEADS, quarter, rest), bf16),
        ]
        + [pltpu.SemaphoreType.DMA((count,)) for count in counts for unused_side in range(2)]
        + [pltpu.SemaphoreType.DMA((2,))],
        compiler_params=pltpu.CompilerParams(
            collective_id=number, has_side_effects=True, vmem_limit_bytes=VMEM_BYTES
        ),
    )(grads, weights, blocks, early)


def gains_kernel(parts_ref, sum_ref, landed, totals, send_sem, recv_sem, rep_send, rep_recv):
    index = lax.axis_index("fsdp")
    rep = lax.axis_index("rep")
    others = [lax.rem(index + step, HEADS) for step in range(1, HEADS)]
    twins = [lax.rem(rep + step, QUARTERS) for step in range(1, QUARTERS)]
    greet([{"fsdp": other} for other in others] + [{"rep": twin} for twin in twins])
    sends = [
        remote(parts_ref.at[other], landed.at[index], (send_sem, recv_sem), step, {"fsdp": other})
        for step, other in enumerate(others)
    ]
    landed[index] = parts_ref[index]
    for copy in sends:
        copy.wait_recv()
    total = landed[0]
    for step in range(1, HEADS):
        total = total + landed[step]
    totals[rep] = total
    twin_sends = [
        remote(totals.at[rep], totals.at[rep], (rep_send, rep_recv), step, {"rep": twin})
        for step, twin in enumerate(twins)
    ]
    for copy in twin_sends:
        copy.wait_recv()
    total = totals[0]
    for step in range(1, QUARTERS):
        total = total + totals[step]
    sum_ref[...] = total
    for copy in sends + twin_sends:
        copy.wait_send()


def gains_sum(parts, number):
    near = pl.BlockSpec(memory_space=pltpu.VMEM)
    return pl.pallas_call(
        gains_kernel,
        out_shape=jax.ShapeDtypeStruct(parts.shape[1:], parts.dtype),
        in_specs=[near],
        out_specs=near,
        scratch_shapes=[
            pltpu.VMEM(parts.shape, parts.dtype),
            pltpu.VMEM((QUARTERS,) + parts.shape[1:], parts.dtype),
        ]
        + [pltpu.SemaphoreType.DMA((HEADS - 1,))] * 2
        + [pltpu.SemaphoreType.DMA((QUARTERS - 1,))] * 2,
        compiler_params=pltpu.CompilerParams(collective_id=number, has_side_effects=True),
    )(parts)


def core_fold(value, axis):
    half = value.shape[axis] // 2
    core = lax.rem(lax.axis_index("rep"), 2)
    give = lax.dynamic_slice_in_dim(value, (1 - core) * half, half, axis)
    keep = lax.dynamic_slice_in_dim(value, core * half, half, axis)
    return add_low(keep, lax.ppermute(give, "rep", SIBLING))


def chip_fold(value, axis):
    half = value.shape[axis] // 2
    chip = lax.axis_index("rep") // 2
    give = lax.dynamic_slice_in_dim(value, (1 - chip) * half, half, axis)
    keep = lax.dynamic_slice_in_dim(value, chip * half, half, axis)
    return add_low(keep, lax.ppermute(give, "rep", ACROSS))


def quarter_fold(value):
    value = value.reshape(value.shape[:-3] + (2, 2) + value.shape[-2:])
    axis = value.ndim - 4
    value = chip_fold(core_fold(value, axis + 1), axis)
    return value.reshape(value.shape[:axis] + value.shape[axis + 2 :])


def dot(left, right):
    return jnp.dot(left, right, preferred_element_type=jnp.float32)


def low(value):
    return value.astype(jnp.bfloat16)


def tree_places(lengths, parents, total):
    count = lengths.shape[0]
    labels = jnp.arange(count, dtype=jnp.int32)
    ends = jnp.sum(jnp.where(labels[:, None] <= labels[None, :], lengths[:, None], 0), axis=0)
    starts = ends - lengths
    tokens = jnp.arange(total, dtype=jnp.int32)
    segment = jnp.sum((ends[None, :] <= tokens[:, None]).astype(jnp.int32), axis=1)
    parent_hot = (parents[:, None] == labels[None, :]) & (labels[:, None] > 0)
    identity = labels[:, None] == labels[None, :]
    reached = parent_hot | identity
    for unused_step in range((count - 1).bit_length()):
        reached = jnp.any(reached[:, :, None] & reached[None, :, :], axis=1)
    offset = jnp.sum(jnp.where(reached & ~identity, lengths[None, :], 0), axis=1) - starts
    member = segment[:, None] == labels[None, :]
    reach = jnp.any(member[:, :, None] & reached[None, :, :], axis=1)
    position = jnp.sum(jnp.where(member, offset[None, :], 0), axis=1) + tokens
    return (tokens, member.astype(jnp.bfloat16), reach.astype(jnp.bfloat16), position)


def head_plan(
    hidden_in,
    layer_input,
    out_grad,
    seg_lengths,
    seg_parents,
    attn_norm,
    q_proj,
    k_proj,
    v_proj,
    q_norm,
    k_norm,
    o_proj,
    attn_post_norm,
    laurel_left,
    laurel_right,
    laurel_norm,
    ffw_norm,
    gate_proj,
    up_proj,
    down_proj,
    ffw_post_norm,
    pl_gate,
    pl_proj,
    pl_post_norm,
):
    index = lax.axis_index("fsdp")
    rows, width = hidden_in.shape
    shard = width // HEADS
    total = rows * HEADS
    groups = HEADS // KV_HEADS
    scale = HEAD_DIM ** (-0.5)
    rank = laurel_left.shape[1]
    per_layer = pl_gate.shape[1]
    key_head = index // groups

    gains = (attn_norm, attn_post_norm, laurel_norm, ffw_norm, ffw_post_norm, pl_post_norm)
    packed = jnp.concatenate(gains + (q_norm, k_norm))
    pad = -packed.shape[0] % (32 * 128)
    packed = jnp.pad(packed, (0, pad)).reshape(-1, 128)
    hidden_all, gains_held, q_head, kv_all, small_all, full_plproj = start_gather(
        hidden_in,
        packed,
        q_proj,
        jnp.concatenate([k_proj, v_proj], axis=1),
        jnp.concatenate([pl_gate, laurel_left, laurel_right], axis=1),
        pl_proj,
        0,
    )
    all_gains = gains_held.reshape(HEADS, -1).astype(jnp.float32)
    wide_gains = [all_gains[:, i * shard : (i + 1) * shard].reshape(-1) for i in range(len(gains))]
    gain_anorm, gain_apost, gain_lnorm, gain_fnorm, gain_fpost, gain_plpost = wide_gains
    at = len(gains) * shard
    piece = HEAD_DIM // HEADS
    gain_qnorm = all_gains[:, at : at + piece].reshape(-1)
    gain_knorm = all_gains[:, at + piece : at + 2 * piece].reshape(-1)

    k_head = lax.dynamic_slice_in_dim(kv_all, key_head * HEAD_DIM, HEAD_DIM, 1)
    v_head = lax.dynamic_slice_in_dim(kv_all, (KV_HEADS + key_head) * HEAD_DIM, HEAD_DIM, 1)
    full_plgate = small_all[:, :per_layer]
    full_left = small_all[:, per_layer : per_layer + rank]
    full_right = small_all[:, per_layer + rank :]

    tokens, member, reach, position = tree_places(seg_lengths[0], seg_parents[0], total)
    depth = position.astype(jnp.float32)
    seen = (mul_t(reach, member) > 0) & (tokens[None, :] <= tokens[:, None])

    normed_all = low(norm_rows(hidden_all.astype(jnp.float32), gain_anorm))
    q_raw = dot(normed_all, q_head)
    k_raw = dot(normed_all, k_head)
    v_low = low(dot(normed_all, v_head))

    def head_path(raw, gain):
        return rotate(norm_rows(raw, gain)[:, None, :], depth)[:, 0, :]

    q_low = low(head_path(q_raw, gain_qnorm))
    k_low = low(head_path(k_raw, gain_knorm))
    scores = jnp.where(seen, mul_t(q_low, k_low) * scale, MASKED)
    top = jnp.max(scores, axis=-1, keepdims=True)
    expo = jnp.exp(scores - top)
    sums = jnp.sum(expo, axis=-1, keepdims=True)
    probs = expo / sums
    probs_low = low(probs)
    attended = dot(probs_low, v_low)
    attended_low = low(attended)
    (branch,) = ring_scatter(low(dot(attended_low, o_proj)), 6)

    source = hidden_in.astype(jnp.float32)
    extra = layer_input.astype(jnp.float32)
    normed = norm_rows(source, gain_anorm)
    normed_low = low(normed)
    left_low = low(dot(normed_low, full_left))
    low_rank = mul_t(left_low, full_right)
    first_sum = (
        source + norm_rows(branch, gain_apost) + normed + norm_rows(low_rank, gain_lnorm)
    ) * HALF_ROOT
    ffw_low = low(norm_rows(first_sum, gain_fnorm))

    ffw_out, ffw_all, act, slope, inner_low = ffn_forward(
        ffw_low, gate_proj, up_proj, down_proj, 7
    )
    second_sum = first_sum + norm_rows(ffw_out, gain_fpost)
    second_low = low(second_sum)
    pl_pre = dot(second_low, full_plgate)
    pl_mix = low(gelu_mix(pl_pre, extra))
    pl_out = dot(pl_mix, full_plproj)
    result = second_sum + norm_rows(pl_out, gain_plpost)
    seed = out_grad.astype(jnp.float32)
    d_plout, grad_plpost = norm_back(pl_out, gain_plpost, seed)
    d_plout_low = low(d_plout)
    grad_plproj = outer(pl_mix, d_plout_low)
    d_mix = mul_t(d_plout_low, full_plproj)
    d_pre, d_extra = mix_back(pl_pre, extra, d_mix)
    d_pre_low = low(d_pre)
    grad_plgate = outer(second_low, d_pre_low)
    d_second = seed + mul_t(d_pre_low, full_plgate)
    pl_blocks = jnp.concatenate(
        [
            low(grad_plgate).reshape(HEADS, shard, per_layer),
            low(grad_plproj).reshape(HEADS, shard, per_layer),
        ],
        axis=-1,
    )
    pl_blocks = quarter_fold(pl_blocks.reshape(HEADS, QUARTERS, -1, 2 * per_layer))
    d_ffwout, grad_fpost = norm_back(ffw_out, gain_fpost, d_second)

    d_ffwin, *rest = ffn_back(
        low(d_ffwout),
        (ffw_all, act, slope, inner_low),
        (gate_proj, up_proj, down_proj),
        pl_blocks,
        9,
    )
    chip_grads, far_down, pl_sum = rest[:3], rest[3], rest[4]
    late = chip_grads[2].shape[0] * 3 // 4
    far_gate, far_up, far_last = [
        lax.ppermute(item, "rep", ACROSS)
        for item in (chip_grads[1], chip_grads[2][:late], chip_grads[2][late:])
    ]

    d_first_part, grad_fnorm = norm_back(first_sum, gain_fnorm, d_ffwin)
    d_scaled = (d_second + d_first_part) * HALF_ROOT
    d_branch, grad_apost = norm_back(branch, gain_apost, d_scaled)
    d_lowrank, grad_lnorm = norm_back(low_rank, gain_lnorm, d_scaled)
    d_lowrank_low = low(d_lowrank)
    (d_branch_all,) = ring_gather(low(d_branch), 11)
    grad_right = outer(d_lowrank_low, left_low)
    d_left_low = low(dot(d_lowrank_low, full_right))
    grad_left = outer(normed_low, d_left_low)

    d_att_low = low(mul_t(d_branch_all, o_proj))
    grad_o = outer(attended_low, d_branch_all)
    o_quarter = quarter_fold(low(grad_o).reshape(QUARTERS, -1, width))
    delta = jnp.sum(d_att_low.astype(jnp.float32) * attended, axis=-1, keepdims=True)
    d_probs = mul_t(d_att_low, v_low)
    d_scores = low(probs * (d_probs - delta) * scale)
    d_query = dot(d_scores, k_low)
    d_key = outer(d_scores, q_low)
    d_value = outer(probs_low, d_att_low)
    unused_q, q_pull = jax.vjp(head_path, q_raw, gain_qnorm)
    d_qraw, grad_qnorm = q_pull(d_query)
    unused_k, k_pull = jax.vjp(head_path, k_raw, gain_knorm)
    d_kraw, grad_knorm = k_pull(d_key)
    d_q_low = low(d_qraw)
    d_k_low = low(d_kraw)
    d_v_low = low(d_value)
    d_qkv = jnp.concatenate([d_q_low, d_k_low, d_v_low], axis=1)
    qkv_head = jnp.concatenate([q_head, k_head, v_head], axis=1)
    d_qkv, far_gate, far_up = lax.optimization_barrier((d_qkv, far_gate, far_up))
    blocks = jnp.concatenate(
        [low(outer(normed_all, d_qkv)), low(grad_left), low(grad_right)], axis=1
    )
    d_normed_sum, owned, early = tail_scatter(
        d_qkv, qkv_head, blocks, jnp.concatenate([o_quarter, pl_sum], axis=1), 12
    )
    owned = owned.astype(jnp.float32)
    early = early.astype(jnp.float32)
    key_at = width
    value_at = key_at + KV_HEADS * HEAD_DIM
    left_at = value_at + KV_HEADS * HEAD_DIM
    d_normed = d_scaled + mul_t(d_left_low, full_left) + d_normed_sum
    d_source_part, grad_anorm = norm_back(source, gain_anorm, d_normed)
    d_source = d_scaled + d_source_part

    far_grads = [far_down, far_gate, jnp.concatenate([far_up, far_last], axis=0)]
    sums = []
    core = lax.rem(lax.axis_index("rep"), 2)
    for item, far in zip(chip_grads, far_grads):
        both = add_low(item, far)
        other = lax.ppermute(both, "rep", SIBLING)
        halves = [jnp.where(core == 0, both, other), jnp.where(core == 0, other, both)]
        sums.append(jnp.concatenate(halves, axis=0).astype(jnp.float32))
    sum_down, sum_gate, sum_up = sums
    small_grads = [grad_anorm, grad_apost, grad_lnorm, grad_fnorm, grad_fpost, grad_plpost]
    parts = [item.reshape(HEADS, shard) for item in small_grads]
    parts += [item.reshape(HEADS, piece) for item in (grad_qnorm, grad_knorm)]
    parts = jnp.concatenate(parts, axis=1)
    parts = jnp.pad(parts, ((0, 0), (0, -parts.shape[1] % 1024))).reshape(HEADS, -1, 128)
    small_sums = gains_sum(parts, 13).reshape(-1)
    own = [small_sums[i * shard : (i + 1) * shard] for i in range(len(small_grads))]
    sum_anorm, sum_apost, sum_lnorm, sum_fnorm, sum_fpost, sum_plpost = own
    sum_qnorm = small_sums[at : at + piece]
    sum_knorm = small_sums[at + piece : at + 2 * piece]
    return (
        low(result),
        low(d_source),
        low(d_extra),
        sum_anorm,
        owned[:, :width],
        owned[:, key_at:value_at],
        owned[:, value_at:left_at],
        sum_qnorm,
        sum_knorm,
        early[:, :width],
        sum_apost,
        owned[:, left_at : left_at + rank],
        owned[:, left_at + rank :],
        sum_lnorm,
        sum_fnorm,
        sum_gate,
        sum_up,
        sum_down,
        sum_fpost,
        early[:, width : width + per_layer],
        early[:, width + per_layer :].reshape(pl_proj.shape),
        sum_plpost,
    )


def gather_plan(
    hidden_in,
    layer_input,
    out_grad,
    seg_lengths,
    seg_parents,
    attn_norm,
    q_proj,
    k_proj,
    v_proj,
    q_norm,
    k_norm,
    o_proj,
    attn_post_norm,
    laurel_left,
    laurel_right,
    laurel_norm,
    ffw_norm,
    gate_proj,
    up_proj,
    down_proj,
    ffw_post_norm,
    pl_gate,
    pl_proj,
    pl_post_norm,
):
    shards = lax.axis_size("fsdp")
    rank_index = lax.axis_index("fsdp")
    rows = hidden_in.shape[0]
    total = rows * shards
    groups = HEADS // KV_HEADS
    scale = HEAD_DIM ** (-0.5)
    tokens, member, reach, position = tree_tables(seg_lengths[0], seg_parents[0], total)
    first_row = rank_index * rows
    my_tokens = first_row + jnp.arange(rows, dtype=jnp.int32)
    my_reach = lax.dynamic_slice_in_dim(reach, first_row, rows, 0)
    my_depth = lax.dynamic_slice_in_dim(position, first_row, rows, 0).astype(jnp.float32)
    seen = (jnp.dot(my_reach, member.T) > 0) & (tokens[None, :] <= my_tokens[:, None])
    (
        full_anorm,
        full_q,
        full_k,
        full_v,
        full_qnorm,
        full_knorm,
        full_o,
        full_apost,
        full_left,
        full_right,
        full_lnorm,
        full_fnorm,
        full_fpost,
        full_plgate,
        full_plproj,
        full_plpost,
    ) = (
        lax.all_gather(attn_norm, "fsdp", axis=0, tiled=True),
        lax.all_gather(q_proj, "fsdp", axis=0, tiled=True),
        lax.all_gather(k_proj, "fsdp", axis=0, tiled=True),
        lax.all_gather(v_proj, "fsdp", axis=0, tiled=True),
        lax.all_gather(q_norm, "fsdp", axis=0, tiled=True),
        lax.all_gather(k_norm, "fsdp", axis=0, tiled=True),
        lax.all_gather(o_proj, "fsdp", axis=0, tiled=True),
        lax.all_gather(attn_post_norm, "fsdp", axis=0, tiled=True),
        lax.all_gather(laurel_left, "fsdp", axis=0, tiled=True),
        lax.all_gather(laurel_right, "fsdp", axis=0, tiled=True),
        lax.all_gather(laurel_norm, "fsdp", axis=0, tiled=True),
        lax.all_gather(ffw_norm, "fsdp", axis=0, tiled=True),
        lax.all_gather(ffw_post_norm, "fsdp", axis=0, tiled=True),
        lax.all_gather(pl_gate, "fsdp", axis=0, tiled=True),
        lax.all_gather(pl_proj, "fsdp", axis=0, tiled=True),
        lax.all_gather(pl_post_norm, "fsdp", axis=0, tiled=True),
    )
    gain_anorm = full_anorm.astype(jnp.float32)
    gain_qnorm = full_qnorm.astype(jnp.float32)
    gain_knorm = full_knorm.astype(jnp.float32)
    gain_apost = full_apost.astype(jnp.float32)
    gain_lnorm = full_lnorm.astype(jnp.float32)
    gain_fnorm = full_fnorm.astype(jnp.float32)
    gain_fpost = full_fpost.astype(jnp.float32)
    gain_plpost = full_plpost.astype(jnp.float32)
    source = hidden_in.astype(jnp.float32)
    extra = layer_input.astype(jnp.float32)
    normed = norm_rows(source, gain_anorm)
    normed_low = normed.astype(jnp.bfloat16)
    q_raw = jnp.dot(normed_low, full_q, preferred_element_type=jnp.float32)
    k_raw = jnp.dot(normed_low, full_k, preferred_element_type=jnp.float32)
    v_raw = jnp.dot(normed_low, full_v, preferred_element_type=jnp.float32)

    def head_path(raw, gain):
        return rotate(norm_rows(raw.reshape(rows, -1, HEAD_DIM), gain), my_depth)

    q_low = head_path(q_raw, gain_qnorm).astype(jnp.bfloat16)
    k_low = head_path(k_raw, gain_knorm).reshape(rows, -1).astype(jnp.bfloat16)
    v_low = v_raw.astype(jnp.bfloat16)
    keys_all, values_all = (
        lax.all_gather(k_low, "fsdp", axis=0, tiled=True),
        lax.all_gather(v_low, "fsdp", axis=0, tiled=True),
    )
    keys_heads = keys_all.reshape(total, KV_HEADS, HEAD_DIM)
    values_heads = values_all.reshape(total, KV_HEADS, HEAD_DIM)
    query_groups = q_low.reshape(rows, KV_HEADS, groups, HEAD_DIM)
    mixed_list = []
    log_list = []
    for head in range(KV_HEADS):
        scores = (
            jnp.einsum(
                "tgd,nd->gtn",
                query_groups[:, head],
                keys_heads[:, head],
                preferred_element_type=jnp.float32,
            )
            * scale
        )
        scores = jnp.where(seen[None], scores, MASKED)
        top = jnp.max(scores, axis=-1, keepdims=True)
        expo = jnp.exp(scores - top)
        sums = jnp.sum(expo, axis=-1, keepdims=True)
        weights = (expo / sums).astype(jnp.bfloat16)
        mixed_list.append(
            jnp.einsum(
                "gtn,nd->tgd", weights, values_heads[:, head], preferred_element_type=jnp.float32
            )
        )
        log_list.append(top[..., 0] + jnp.log(sums[..., 0]))
    attended = jnp.stack(mixed_list, axis=1)
    log_sums = jnp.stack(log_list, axis=0)
    attended_low = attended.reshape(rows, -1).astype(jnp.bfloat16)
    branch = jnp.dot(attended_low, full_o, preferred_element_type=jnp.float32)
    left_low = jnp.dot(normed_low, full_left, preferred_element_type=jnp.float32).astype(
        jnp.bfloat16
    )
    low_rank = mul_t(left_low, full_right)
    first_sum = (
        source + norm_rows(branch, gain_apost) + normed + norm_rows(low_rank, gain_lnorm)
    ) * HALF_ROOT
    ffw_low = norm_rows(first_sum, gain_fnorm).astype(jnp.bfloat16)
    full_gate, full_up, full_down = (
        lax.all_gather(gate_proj, "fsdp", axis=0, tiled=True),
        lax.all_gather(up_proj, "fsdp", axis=0, tiled=True),
        lax.all_gather(down_proj, "fsdp", axis=0, tiled=True),
    )
    gate_val = mul_t(ffw_low, full_gate)
    up_val = mul_t(ffw_low, full_up)
    inner_low = gelu_mix(gate_val, up_val).astype(jnp.bfloat16)
    ffw_out = jnp.dot(inner_low, full_down, preferred_element_type=jnp.float32)
    second_sum = first_sum + norm_rows(ffw_out, gain_fpost)
    second_low = second_sum.astype(jnp.bfloat16)
    pl_pre = jnp.dot(second_low, full_plgate, preferred_element_type=jnp.float32)
    pl_mix = gelu_mix(pl_pre, extra).astype(jnp.bfloat16)
    pl_out = jnp.dot(pl_mix, full_plproj, preferred_element_type=jnp.float32)
    result = second_sum + norm_rows(pl_out, gain_plpost)
    seed = out_grad.astype(jnp.float32)
    d_plout, grad_plpost = norm_back(pl_out, gain_plpost, seed)
    d_plout_low = d_plout.astype(jnp.bfloat16)
    grad_plproj = outer(pl_mix, d_plout_low)
    d_mix = mul_t(d_plout_low, full_plproj)
    d_pre, d_extra = mix_back(pl_pre, extra, d_mix)
    d_pre_low = d_pre.astype(jnp.bfloat16)
    grad_plgate = outer(second_low, d_pre_low)
    d_second = seed + mul_t(d_pre_low, full_plgate)
    d_ffwout, grad_fpost = norm_back(ffw_out, gain_fpost, d_second)
    d_ffw_low = d_ffwout.astype(jnp.bfloat16)
    d_inner = mul_t(d_ffw_low, full_down)
    d_gate, d_up = mix_back(gate_val, up_val, d_inner)
    d_gate_low = d_gate.astype(jnp.bfloat16)
    d_up_low = d_up.astype(jnp.bfloat16)
    d_ffwin = jnp.dot(d_gate_low, full_gate, preferred_element_type=jnp.float32) + jnp.dot(
        d_up_low, full_up, preferred_element_type=jnp.float32
    )
    width = ffw_low.shape[1]
    gate_part = outer(d_gate_low, ffw_low)
    up_part = outer(d_up_low, ffw_low)
    down_part = outer(inner_low, d_ffw_low)
    stacked = lax.psum_scatter(
        jnp.concatenate([gate_part, up_part, down_part], axis=1).astype(jnp.bfloat16),
        "fsdp",
        scatter_dimension=0,
        tiled=True,
    ).astype(jnp.float32)
    grad_gate = stacked[:, :width]
    grad_up = stacked[:, width : 2 * width]
    grad_down = stacked[:, 2 * width :]
    d_first_part, grad_fnorm = norm_back(first_sum, gain_fnorm, d_ffwin)
    d_first = d_second + d_first_part
    d_scaled = d_first * HALF_ROOT
    d_branch, grad_apost = norm_back(branch, gain_apost, d_scaled)
    d_branch_low = d_branch.astype(jnp.bfloat16)
    d_lowrank, grad_lnorm = norm_back(low_rank, gain_lnorm, d_scaled)
    d_lowrank_low = d_lowrank.astype(jnp.bfloat16)
    grad_o = outer(attended_low, d_branch_low)
    d_att_low = mul_t(d_branch_low, full_o).astype(jnp.bfloat16)
    grad_right = outer(d_lowrank_low, left_low)
    d_left_low = jnp.dot(d_lowrank_low, full_right, preferred_element_type=jnp.float32).astype(
        jnp.bfloat16
    )
    grad_left = outer(normed_low, d_left_low)
    d_att_heads = d_att_low.reshape(rows, KV_HEADS, groups, HEAD_DIM)
    delta = jnp.sum(d_att_heads.astype(jnp.float32) * attended, axis=-1).transpose(1, 2, 0)
    block = 512
    count = total // block
    key_blocks = keys_heads.reshape(count, block, KV_HEADS, HEAD_DIM)
    value_blocks = values_heads.reshape(count, block, KV_HEADS, HEAD_DIM)
    seen_blocks = seen.reshape(rows, count, block).transpose(1, 0, 2)

    def key_step(d_query, item):
        keys, values, shown = item
        scores = (
            jnp.einsum("tkgd,nkd->kgtn", query_groups, keys, preferred_element_type=jnp.float32)
            * scale
        )
        scores = jnp.where(shown[None, None], scores, MASKED)
        probs = jnp.exp(scores - log_sums[..., None])
        d_probs = jnp.einsum(
            "tkgd,nkd->kgtn", d_att_heads, values, preferred_element_type=jnp.float32
        )
        d_scores = (probs * (d_probs - delta[..., None]) * scale).astype(jnp.bfloat16)
        d_query = d_query + jnp.einsum(
            "kgtn,nkd->tkgd", d_scores, keys, preferred_element_type=jnp.float32
        )
        d_keys = jnp.einsum(
            "kgtn,tkgd->nkd", d_scores, query_groups, preferred_element_type=jnp.float32
        )
        d_values = jnp.einsum(
            "kgtn,tkgd->nkd",
            probs.astype(jnp.bfloat16),
            d_att_heads,
            preferred_element_type=jnp.float32,
        )
        return (d_query, (d_keys, d_values))

    zero_query = jnp.zeros((rows, KV_HEADS, groups, HEAD_DIM), jnp.float32)
    d_query, (d_key_blocks, d_value_blocks) = lax.scan(
        key_step, zero_query, (key_blocks, value_blocks, seen_blocks)
    )
    my_dkeys, my_dvalues = (
        lax.psum_scatter(
            d_key_blocks.reshape(total, -1).astype(jnp.bfloat16),
            "fsdp",
            scatter_dimension=0,
            tiled=True,
        ).astype(jnp.float32),
        lax.psum_scatter(
            d_value_blocks.reshape(total, -1).astype(jnp.bfloat16),
            "fsdp",
            scatter_dimension=0,
            tiled=True,
        ).astype(jnp.float32),
    )
    unused_q, q_pull = jax.vjp(head_path, q_raw, gain_qnorm)
    d_qraw, grad_qnorm = q_pull(d_query.reshape(rows, HEADS, HEAD_DIM))
    unused_k, k_pull = jax.vjp(head_path, k_raw, gain_knorm)
    d_kraw, grad_knorm = k_pull(my_dkeys.reshape(rows, KV_HEADS, HEAD_DIM))
    d_q_low = d_qraw.astype(jnp.bfloat16)
    d_k_low = d_kraw.astype(jnp.bfloat16)
    d_v_low = my_dvalues.astype(jnp.bfloat16)
    grad_q = outer(normed_low, d_q_low)
    grad_k = outer(normed_low, d_k_low)
    grad_v = outer(normed_low, d_v_low)
    d_normed = (
        d_scaled
        + mul_t(d_q_low, full_q)
        + mul_t(d_k_low, full_k)
        + mul_t(d_v_low, full_v)
        + mul_t(d_left_low, full_left)
    )
    d_source_part, grad_anorm = norm_back(source, gain_anorm, d_normed)
    d_source = d_scaled + d_source_part
    shard_grads = (
        lax.psum_scatter(
            grad_anorm.astype(jnp.bfloat16), "fsdp", scatter_dimension=0, tiled=True
        ).astype(jnp.float32),
        lax.psum_scatter(
            grad_q.astype(jnp.bfloat16), "fsdp", scatter_dimension=0, tiled=True
        ).astype(jnp.float32),
        lax.psum_scatter(
            grad_k.astype(jnp.bfloat16), "fsdp", scatter_dimension=0, tiled=True
        ).astype(jnp.float32),
        lax.psum_scatter(
            grad_v.astype(jnp.bfloat16), "fsdp", scatter_dimension=0, tiled=True
        ).astype(jnp.float32),
        lax.psum_scatter(
            grad_qnorm.astype(jnp.bfloat16), "fsdp", scatter_dimension=0, tiled=True
        ).astype(jnp.float32),
        lax.psum_scatter(
            grad_knorm.astype(jnp.bfloat16), "fsdp", scatter_dimension=0, tiled=True
        ).astype(jnp.float32),
        lax.psum_scatter(
            grad_o.astype(jnp.bfloat16), "fsdp", scatter_dimension=0, tiled=True
        ).astype(jnp.float32),
        lax.psum_scatter(
            grad_apost.astype(jnp.bfloat16), "fsdp", scatter_dimension=0, tiled=True
        ).astype(jnp.float32),
        lax.psum_scatter(
            grad_left.astype(jnp.bfloat16), "fsdp", scatter_dimension=0, tiled=True
        ).astype(jnp.float32),
        lax.psum_scatter(
            grad_right.astype(jnp.bfloat16), "fsdp", scatter_dimension=0, tiled=True
        ).astype(jnp.float32),
        lax.psum_scatter(
            grad_lnorm.astype(jnp.bfloat16), "fsdp", scatter_dimension=0, tiled=True
        ).astype(jnp.float32),
        lax.psum_scatter(
            grad_fnorm.astype(jnp.bfloat16), "fsdp", scatter_dimension=0, tiled=True
        ).astype(jnp.float32),
        lax.psum_scatter(
            grad_fpost.astype(jnp.bfloat16), "fsdp", scatter_dimension=0, tiled=True
        ).astype(jnp.float32),
        lax.psum_scatter(
            grad_plgate.astype(jnp.bfloat16), "fsdp", scatter_dimension=0, tiled=True
        ).astype(jnp.float32),
        lax.psum_scatter(
            grad_plproj.astype(jnp.bfloat16), "fsdp", scatter_dimension=0, tiled=True
        ).astype(jnp.float32),
        lax.psum_scatter(
            grad_plpost.astype(jnp.bfloat16), "fsdp", scatter_dimension=0, tiled=True
        ).astype(jnp.float32),
    )
    (
        sum_anorm,
        sum_q,
        sum_k,
        sum_v,
        sum_qnorm,
        sum_knorm,
        sum_o,
        sum_apost,
        sum_left,
        sum_right,
        sum_lnorm,
        sum_fnorm,
        sum_fpost,
        sum_plgate,
        sum_plproj,
        sum_plpost,
        sum_gate,
        sum_up,
        sum_down,
    ) = (
        lax.psum(shard_grads[0].astype(jnp.bfloat16), "rep").astype(jnp.float32),
        lax.psum(shard_grads[1].astype(jnp.bfloat16), "rep").astype(jnp.float32),
        lax.psum(shard_grads[2].astype(jnp.bfloat16), "rep").astype(jnp.float32),
        lax.psum(shard_grads[3].astype(jnp.bfloat16), "rep").astype(jnp.float32),
        lax.psum(shard_grads[4].astype(jnp.bfloat16), "rep").astype(jnp.float32),
        lax.psum(shard_grads[5].astype(jnp.bfloat16), "rep").astype(jnp.float32),
        lax.psum(shard_grads[6].astype(jnp.bfloat16), "rep").astype(jnp.float32),
        lax.psum(shard_grads[7].astype(jnp.bfloat16), "rep").astype(jnp.float32),
        lax.psum(shard_grads[8].astype(jnp.bfloat16), "rep").astype(jnp.float32),
        lax.psum(shard_grads[9].astype(jnp.bfloat16), "rep").astype(jnp.float32),
        lax.psum(shard_grads[10].astype(jnp.bfloat16), "rep").astype(jnp.float32),
        lax.psum(shard_grads[11].astype(jnp.bfloat16), "rep").astype(jnp.float32),
        lax.psum(shard_grads[12].astype(jnp.bfloat16), "rep").astype(jnp.float32),
        lax.psum(shard_grads[13].astype(jnp.bfloat16), "rep").astype(jnp.float32),
        lax.psum(shard_grads[14].astype(jnp.bfloat16), "rep").astype(jnp.float32),
        lax.psum(shard_grads[15].astype(jnp.bfloat16), "rep").astype(jnp.float32),
        lax.psum(grad_gate.astype(jnp.bfloat16), "rep").astype(jnp.float32),
        lax.psum(grad_up.astype(jnp.bfloat16), "rep").astype(jnp.float32),
        lax.psum(grad_down.astype(jnp.bfloat16), "rep").astype(jnp.float32),
    )
    return (
        result.astype(jnp.bfloat16),
        d_source.astype(jnp.bfloat16),
        d_extra.astype(jnp.bfloat16),
        sum_anorm,
        sum_q,
        sum_k,
        sum_v,
        sum_qnorm,
        sum_knorm,
        sum_o,
        sum_apost,
        sum_left,
        sum_right,
        sum_lnorm,
        sum_fnorm,
        sum_gate,
        sum_up,
        sum_down,
        sum_fpost,
        sum_plgate,
        sum_plproj,
        sum_plpost,
    )


def solution(mesh):
    placed = (
        P(("rep", "fsdp"), None),
        P(("rep", "fsdp"), None),
        P(("rep", "fsdp"), None),
        P("rep", None),
        P("rep", None),
        P("fsdp"),
        P("fsdp", None),
        P("fsdp", None),
        P("fsdp", None),
        P("fsdp"),
        P("fsdp"),
        P("fsdp", None),
        P("fsdp"),
        P("fsdp", None),
        P("fsdp", None),
        P("fsdp"),
        P("fsdp"),
        P("fsdp", None),
        P("fsdp", None),
        P("fsdp", None),
        P("fsdp"),
        P("fsdp", None),
        P("fsdp", None),
        P("fsdp"),
    )
    return jax.shard_map(
        head_plan if mesh.shape["fsdp"] == HEADS else gather_plan,
        mesh=mesh,
        in_specs=placed,
        out_specs=(
            P(("rep", "fsdp"), None),
            P(("rep", "fsdp"), None),
            P(("rep", "fsdp"), None),
            P("fsdp"),
            P("fsdp", None),
            P("fsdp", None),
            P("fsdp", None),
            P("fsdp"),
            P("fsdp"),
            P("fsdp", None),
            P("fsdp"),
            P("fsdp", None),
            P("fsdp", None),
            P("fsdp"),
            P("fsdp"),
            P("fsdp", None),
            P("fsdp", None),
            P("fsdp", None),
            P("fsdp"),
            P("fsdp", None),
            P("fsdp", None),
            P("fsdp"),
        ),
        check_vma=False,
    )
```

```python
import functools
import math

import jax
import jax.numpy as jnp
from jax import lax
from jax.experimental import pallas as pl
from jax.experimental.pallas import tpu as pltpu
from jax.sharding import PartitionSpec as P

HEADS = 8
KV_HEADS = 2
HEAD_DIM = 256


EPS = 1e-06
ROPE_BASE = 1000000.0
HALF_ROOT = 0.7071067811865476
MASKED = -1e30


def norm_rows(value, gain):
    return value * lax.rsqrt(jnp.mean(value * value, axis=-1, keepdims=True) + EPS) * gain


def norm_back(value, gain, grad):
    unused, pull = jax.vjp(norm_rows, value, gain)
    return pull(grad)


def rotate(value, position):
    half = value.shape[-1] // 2
    freqs = jnp.exp(
        jnp.arange(half, dtype=jnp.float32) * (-2.0 * math.log(ROPE_BASE) / value.shape[-1])
    )
    angle = position[:, None] * freqs[None, :]
    cosine = jnp.cos(angle)[:, None, :]
    sine = jnp.sin(angle)[:, None, :]
    first_half = value[..., :half]
    second_half = value[..., half:]
    return jnp.concatenate(
        [first_half * cosine - second_half * sine, second_half * cosine + first_half * sine],
        axis=-1,
    )


def tree_tables(lengths, parents, total):
    count = lengths.shape[0]
    labels = jnp.arange(count, dtype=jnp.int32)
    ends = jnp.cumsum(lengths)
    starts = ends - lengths
    tokens = jnp.arange(total, dtype=jnp.int32)
    segment = jnp.sum((ends[None, :] <= tokens[:, None]).astype(jnp.int32), axis=1)
    parent_hot = ((parents[:, None] == labels[None, :]) & (labels[:, None] > 0)).astype(jnp.int32)
    identity = (labels[:, None] == labels[None, :]).astype(jnp.int32)
    ancestors = lax.fori_loop(
        0, count, lambda step, held: jnp.minimum(1, identity + jnp.dot(parent_hot, held)), identity
    )
    offset = jnp.dot(ancestors - identity, lengths) - starts
    member = (segment[:, None] == labels[None, :]).astype(jnp.int32)
    reach = jnp.dot(member, ancestors)
    position = jnp.dot(member, offset) + tokens
    return (tokens, member, reach, position)


def outer(left, right):
    return lax.dot_general(
        left, right, (((0,), (0,)), ((), ())), preferred_element_type=jnp.float32
    )


def mul_t(left, right):
    return lax.dot_general(
        left, right, (((1,), (1,)), ((), ())), preferred_element_type=jnp.float32
    )


def gelu_mix(first, second):
    return jax.nn.gelu(first, approximate=True) * second


def mix_back(first, second, grad):
    unused, pull = jax.vjp(gelu_mix, first, second)
    return pull(grad)


MESH = pl.DeviceIdType.MESH
VMEM_BYTES = 48 << 20


def ring_place(index):
    side = lax.rem(index, 2)
    return index // 2 + side * (HEADS - 1 - 2 * (index // 2))


def ring_index(place):
    back = place // (HEADS // 2)
    return (1 - back) * 2 * place + back * (2 * HEADS - 1 - 2 * place)


def ring_ends(place):
    after = {"fsdp": ring_index(lax.rem(place + 1, HEADS))}
    before = {"fsdp": ring_index(lax.rem(place + HEADS - 1, HEADS))}
    return (after, before)


def greet(others):
    barrier = pltpu.get_barrier_semaphore()
    for other in others:
        pl.semaphore_signal(barrier, inc=1, device_id=other, device_id_type=MESH)
    pl.semaphore_wait(barrier, len(others))


def span(start, size):
    return pl.ds(pl.multiple_of(start, size), size)


def neighbours():
    rep = lax.axis_index("rep")
    chip = rep // 2
    core = lax.rem(rep, 2)
    return (chip, core, {"rep": 2 * chip + 1 - core}, {"rep": 2 * (1 - chip) + core})


def remote(source, target, sems, number, device):
    copy = pltpu.make_async_remote_copy(
        source,
        target,
        sems[0].at[number],
        sems[1].at[number],
        device_id=device,
        device_id_type=MESH,
    )
    copy.start()
    return copy


class Ring:
    def __init__(self, place, ends, lanes, sems, own, there):
        self.place, self.ends, self.lanes, self.sems = place, ends, lanes, sems
        self.own, self.there = own, there
        self.copies = []

    def owner(self, step, lane):
        ahead = step if lane % 2 else HEADS - step
        return ring_index(lax.rem(self.place + ahead, HEADS))

    def send(self, step):
        for lane in range(self.lanes):
            number = step * self.lanes + lane
            target = self.there(self.owner(step, lane), lane)
            if step:
                self.copies[number - self.lanes].wait_recv()
            source = target if step else self.own(lane)
            self.copies.append(remote(source, target, self.sems, number, self.ends[lane % 2]))

    def arrive(self, step):
        for lane in range(self.lanes):
            self.copies[(step - 1) * self.lanes + lane].wait_recv()

    def sent(self):
        for copy in self.copies:
            copy.wait_send()


class Mirror:
    def __init__(self, count, sems):
        unused_chip, unused_core, self.sibling, self.across = neighbours()
        self.count, self.sems = count, sems
        self.copies = [None] * (3 * count)

    def give(self, number, ref):
        self.copies[number] = remote(ref, ref, self.sems, number, self.sibling)
        self.copies[self.count + number] = remote(
            ref, ref, self.sems, self.count + number, self.across
        )

    def relay(self, number, ref):
        self.copies[self.count + number].wait_recv()
        self.copies[2 * self.count + number] = remote(
            ref, ref, self.sems, 2 * self.count + number, self.sibling
        )

    def finish(self):
        for number, copy in enumerate(self.copies):
            if number // self.count != 1:
                copy.wait_recv()
            copy.wait_send()


RING_STEPS = HEADS - 1
QUARTERS = 4


def start_kernel(
    hidden_ref,
    gains_ref,
    q_ref,
    kv_ref,
    small_ref,
    plproj_ref,
    hidden_all,
    gains_all,
    q_head,
    kv_all,
    small_all,
    plproj_all,
    local_sems,
    *sems,
):
    pairs = [sems[i : i + 2] for i in range(0, len(sems), 2)]
    hidden_sems, gains_sems, q_sems, kv_sems, small_sems, plproj_sems = pairs[:6]
    q_mirror_sems, kv_mirror_sems, small_mirror_sems, plproj_mirror_sems = pairs[6:]
    index = lax.axis_index("fsdp")
    chip, core, sibling, across = neighbours()
    quarter = 2 * chip + core
    other_quarter = 2 * (1 - chip) + core
    place = ring_place(index)
    ends = ring_ends(place)
    others = [lax.rem(index + step, HEADS) for step in range(1, HEADS)]
    greet([{"fsdp": other} for other in others] + [sibling, across])
    rows = hidden_ref.shape[0]
    shard = q_ref.shape[0]
    deep = plproj_ref.shape[0]
    q_rows = shard // QUARTERS
    wide = plproj_ref.shape[1] // QUARTERS

    locals_list = []
    for source, target in (
        (hidden_ref, hidden_all.at[span(index * rows, rows)]),
        (gains_ref, gains_all.at[span(index * gains_ref.shape[0], gains_ref.shape[0])]),
        (
            q_ref.at[:, span(index * HEAD_DIM, HEAD_DIM)],
            q_head.at[span(index * shard, shard)],
        ),
        (kv_ref, kv_all.at[span(index * shard, shard)]),
        (small_ref, small_all.at[span(index * shard, shard)]),
        (plproj_ref, plproj_all.at[span(index * deep, deep)]),
    ):
        copy = pltpu.make_async_copy(source, target, local_sems.at[len(locals_list)])
        copy.start()
        locals_list.append(copy)

    hidden_part = rows // 4
    gains_part = gains_ref.shape[0] // 2
    shard_part = shard // QUARTERS // 2
    wide_part = wide // 2

    def shard_at(ref, part_of):
        return lambda owner, lane: ref.at[
            span(owner * shard + part_of * 2 * shard_part + lane * shard_part, shard_part)
        ]

    def plproj_at(part_of):
        return lambda owner, lane: plproj_all.at[
            span(owner * deep, deep), span(part_of * wide + lane * wide_part, wide_part)
        ]

    hidden = Ring(
        place,
        ends,
        4,
        hidden_sems,
        lambda lane: hidden_ref.at[pl.ds(lane * hidden_part, hidden_part)],
        lambda owner, lane: hidden_all.at[span(owner * rows + lane * hidden_part, hidden_part)],
    )
    gains = Ring(
        place,
        ends,
        2,
        gains_sems,
        lambda lane: gains_ref.at[pl.ds(lane * gains_part, gains_part)],
        lambda owner, lane: gains_all.at[
            span(owner * gains_ref.shape[0] + lane * gains_part, gains_part)
        ],
    )

    def shard_own(ref):
        return lambda lane: ref.at[
            span(quarter * 2 * shard_part + lane * shard_part, shard_part)
        ]

    kv = Ring(place, ends, 2, kv_sems, shard_own(kv_ref), shard_at(kv_all, quarter))
    small = Ring(place, ends, 2, small_sems, shard_own(small_ref), shard_at(small_all, quarter))
    plproj = Ring(
        place,
        ends,
        2,
        plproj_sems,
        lambda lane: plproj_ref.at[:, span(quarter * wide + lane * wide_part, wide_part)],
        plproj_at(quarter),
    )
    mirrored = [
        (kv, Mirror(2 * RING_STEPS, kv_mirror_sems), shard_at(kv_all, other_quarter)),
        (small, Mirror(2 * RING_STEPS, small_mirror_sems), shard_at(small_all, other_quarter)),
        (plproj, Mirror(2 * RING_STEPS, plproj_mirror_sems), plproj_at(other_quarter)),
    ]
    q_mirror = Mirror(HEADS - 1, q_mirror_sems)
    q_copies = []
    q_landing = q_head.at[span(index * shard + quarter * q_rows, q_rows)]
    for step, other in enumerate(others):
        source = q_ref.at[span(quarter * q_rows, q_rows), span(other * HEAD_DIM, HEAD_DIM)]
        q_copies.append(remote(source, q_landing, q_sems, step, {"fsdp": other}))

    def q_at(step, part_of):
        giver = lax.rem(index + HEADS - 1 - step, HEADS)
        return q_head.at[span(giver * shard + part_of * q_rows, q_rows)]

    def pass_on(step):
        for ring, mirror, unused_there in mirrored:
            for lane in range(2):
                mirror.give((step - 1) * 2 + lane, ring.there(ring.owner(step, lane), lane))

    def pass_again(step):
        for ring, mirror, there in mirrored:
            for lane in range(2):
                mirror.relay((step - 1) * 2 + lane, there(ring.owner(step, lane), lane))

    for step in range(RING_STEPS):
        gains.send(step)
        for ring, unused_mirror, unused_there in mirrored:
            ring.send(step)
        hidden.send(step)
        if step >= 1:
            pass_on(step)
        if step >= 2:
            pass_again(step - 1)
        if step == 4:
            for number, copy in enumerate(q_copies):
                copy.wait_recv()
                q_mirror.give(number, q_at(number, quarter))
        if step == 5:
            for number in range(HEADS - 1):
                q_mirror.relay(number, q_at(number, other_quarter))
    for ring, unused_mirror, unused_there in mirrored:
        ring.arrive(RING_STEPS)
    pass_on(RING_STEPS)
    pass_again(RING_STEPS - 1)
    pass_again(RING_STEPS)
    gains.arrive(RING_STEPS)
    hidden.arrive(RING_STEPS)
    for ring, mirror, unused_there in mirrored:
        ring.sent()
        mirror.finish()
    hidden.sent()
    gains.sent()
    for copy in q_copies:
        copy.wait_send()
    q_mirror.finish()
    for copy in locals_list:
        copy.wait()


def start_gather(hidden, gains, q_proj, kv, small, pl_proj, number):
    shard = q_proj.shape[0]
    arrays = (hidden, gains, q_proj, kv, small, pl_proj)

    def grown(item, rows=None, columns=None):
        rows = rows or item.shape[0] * HEADS
        return jax.ShapeDtypeStruct((rows, columns or item.shape[1]), item.dtype)

    counts = [4 * RING_STEPS, 2 * RING_STEPS, RING_STEPS] + [2 * RING_STEPS] * 3
    counts += [3 * RING_STEPS] + [6 * RING_STEPS] * 3
    return pl.pallas_call(
        start_kernel,
        out_shape=[
            grown(hidden),
            grown(gains),
            grown(q_proj, shard * HEADS, HEAD_DIM),
            grown(kv),
            grown(small),
            grown(pl_proj),
        ],
        in_specs=[pl.BlockSpec(memory_space=pl.ANY)] * len(arrays),
        out_specs=[pl.BlockSpec(memory_space=pl.ANY)] * len(arrays),
        scratch_shapes=[pltpu.SemaphoreType.DMA((len(arrays),))]
        + [pltpu.SemaphoreType.DMA((count,)) for count in counts for unused_side in range(2)],
        compiler_params=pltpu.CompilerParams(collective_id=number, has_side_effects=True),
    )(*arrays)


def gather_kernel(own_ref, all_ref, local_sem, send_sem, recv_sem):
    rows = own_ref.shape[0]
    part = rows // 4
    index = lax.axis_index("fsdp")
    place = ring_place(index)
    ends = ring_ends(place)
    greet(ends)
    local = pltpu.make_async_copy(own_ref, all_ref.at[span(index * rows, rows)], local_sem)
    local.start()
    ring = Ring(
        place,
        ends,
        4,
        (send_sem, recv_sem),
        lambda lane: own_ref.at[pl.ds(lane * part, part)],
        lambda owner, lane: all_ref.at[span(owner * rows + lane * part, part)],
    )
    for step in range(RING_STEPS):
        ring.send(step)
    ring.arrive(RING_STEPS)
    ring.sent()
    local.wait()


def ring_gather(own, number):
    spec = pl.BlockSpec(memory_space=pl.ANY)
    return pl.pallas_call(
        gather_kernel,
        out_shape=[jax.ShapeDtypeStruct((own.shape[0] * HEADS, own.shape[1]), own.dtype)],
        in_specs=[spec],
        out_specs=[spec],
        scratch_shapes=[pltpu.SemaphoreType.DMA]
        + [pltpu.SemaphoreType.DMA((4 * RING_STEPS,))] * 2,
        compiler_params=pltpu.CompilerParams(collective_id=number, has_side_effects=True),
    )(own)


def add_low(left, right):
    return (left.astype(jnp.float32) + right.astype(jnp.float32)).astype(jnp.bfloat16)


class RingSum:
    def __init__(self, place, ends, lanes, sems, held, own):
        self.place, self.ends, self.lanes, self.sems = place, ends, lanes, sems
        self.held, self.own = held, own
        self.copies = []

    def send(self, step):
        for lane in range(self.lanes):
            ahead = step + 1 if lane % 2 else HEADS - 1 - step
            owner = ring_index(lax.rem(self.place + ahead, HEADS))
            number = step * self.lanes + lane
            if step:
                slot = number - self.lanes
                self.copies[slot].wait_recv()
                value = self.held[slot].astype(jnp.float32) + self.own(owner, lane)
            else:
                slot = RING_STEPS * self.lanes + lane
                value = self.own(owner, lane)
            self.held[slot] = value.astype(jnp.bfloat16)
            self.copies.append(
                remote(self.held.at[slot], self.held.at[number], self.sems, number, self.ends[lane % 2])
            )

    def last(self, index, lane):
        number = (RING_STEPS - 1) * self.lanes + lane
        self.copies[number].wait_recv()
        return self.held[number].astype(jnp.float32) + self.own(index, lane)

    def sent(self):
        for copy in self.copies:
            copy.wait_send()


def scatter_kernel(part_ref, *refs):
    if len(refs) > 4:
        blocks_ref, sum_ref, block_sum, held, send_sem, recv_sem, block_held, block_send, block_recv = refs
    else:
        blocks_ref = None
        sum_ref, held, send_sem, recv_sem = refs
    rows = sum_ref.shape[0]
    part = rows // 4
    index = lax.axis_index("fsdp")
    place = ring_place(index)
    ends = ring_ends(place)
    greet(ends)

    def own(owner, lane):
        return part_ref[span(owner * rows + lane * part, part), :].astype(jnp.float32)

    rings = [RingSum(place, ends, 4, (send_sem, recv_sem), held, own)]
    if blocks_ref is not None:
        low_rows = block_sum.shape[0] // 2

        def block_own(owner, lane):
            return blocks_ref[owner, pl.ds(lane * low_rows, low_rows), :].astype(jnp.float32)

        rings.append(RingSum(place, ends, 2, (block_send, block_recv), block_held, block_own))
    for step in range(RING_STEPS):
        for ring in rings:
            ring.send(step)
    for lane in range(4):
        sum_ref[pl.ds(lane * part, part), :] = rings[0].last(index, lane)
    if blocks_ref is not None:
        for lane in range(2):
            block_sum[pl.ds(lane * low_rows, low_rows), :] = (
                rings[1].last(index, lane).astype(jnp.bfloat16)
            )
    for ring in rings:
        ring.sent()


def ring_scatter(parts, number, blocks=None):
    rows = parts.shape[0] // HEADS
    near = pl.BlockSpec(memory_space=pltpu.VMEM)
    out_shape = [jax.ShapeDtypeStruct((rows, parts.shape[1]), jnp.float32)]
    steps = 4 * RING_STEPS
    scratch = [pltpu.VMEM((steps + 4, rows // 4, parts.shape[1]), jnp.bfloat16)]
    scratch += [pltpu.SemaphoreType.DMA((steps,))] * 2
    arrays = [parts]
    if blocks is not None:
        arrays.append(blocks)
        out_shape.append(jax.ShapeDtypeStruct(blocks.shape[1:], jnp.bfloat16))
        steps = 2 * RING_STEPS
        shape = (steps + 2, blocks.shape[1] // 2, blocks.shape[2])
        scratch += [pltpu.VMEM(shape, jnp.bfloat16)] + [pltpu.SemaphoreType.DMA((steps,))] * 2
    return pl.pallas_call(
        scatter_kernel,
        out_shape=out_shape,
        in_specs=[near] * len(arrays),
        out_specs=[near] * len(out_shape),
        scratch_shapes=scratch,
        compiler_params=pltpu.CompilerParams(
            collective_id=number, has_side_effects=True, vmem_limit_bytes=VMEM_BYTES
        ),
    )(*arrays)


def lane_offset(lane, rows):
    return (lane % 2) * (rows // 2) + (lane // 2) * (rows // 4)


def tile_loop(count, size, body):
    def step(number, carry):
        body(span(number * size, size))
        return carry

    lax.fori_loop(0, count, step, 0)


class Pair:
    def __init__(self, place, step, rows):
        half = rows // 2
        behind = ring_index(lax.rem(place + HEADS - step, HEADS))
        ahead = ring_index(lax.rem(place + step, HEADS))
        self.half = half
        self.rows = (span(behind * rows, half), span(ahead * rows + half, half))

    def read(self, ref, columns=slice(None)):
        return jnp.concatenate([ref[rows, columns] for rows in self.rows], axis=0)

    def write(self, ref, columns, value):
        for side, rows in enumerate(self.rows):
            ref[rows, columns] = value[side * self.half : (side + 1) * self.half]


GELU_ROOT = math.sqrt(2.0 / math.pi)
GELU_CUBE = 0.044715
TILE = 256


def start_loads(pairs, sems):
    copies = []
    for number, (source, target) in enumerate(pairs):
        copy = pltpu.make_async_copy(source, target, sems.at[number])
        copy.start()
        copies.append(copy)
    return copies


def ffn_kernel(
    own_ref,
    gate_any,
    up_any,
    down_any,
    sum_ref,
    all_ref,
    act_ref,
    slope_ref,
    inner_ref,
    gate,
    up,
    down,
    block,
    inner_block,
    part,
    held,
    load_sems,
    send_sem,
    recv_sem,
    sum_send,
    sum_recv,
):
    rows, width = own_ref.shape
    units = gate.shape[0]
    piece = rows // 4
    index = lax.axis_index("fsdp")
    place = ring_place(index)
    ends = ring_ends(place)
    loads = start_loads(((gate_any, gate), (up_any, up), (down_any, down)), load_sems)
    greet(ends)
    ring = Ring(
        place,
        ends,
        4,
        (send_sem, recv_sem),
        lambda lane: own_ref.at[pl.ds(lane_offset(lane, rows), piece)],
        lambda owner, lane: all_ref.at[span(owner * rows + lane_offset(lane, rows), piece)],
    )

    def own(owner, lane):
        return part[span(owner * rows + lane_offset(lane, rows), piece), :].astype(jnp.float32)

    sums = RingSum(place, ends, 4, (sum_send, sum_recv), held, own)

    def compute(step):
        pair = Pair(place, step, rows)
        block[...] = pair.read(all_ref)

        def into(tile):
            value = mul_t(block[...], gate[tile, :])
            second = mul_t(block[...], up[tile, :])
            square = value * value
            bent = jnp.tanh(GELU_ROOT * value * (1.0 + GELU_CUBE * square))
            share = 0.5 * (1.0 + bent)
            act = value * share
            slope = share + (0.5 * GELU_ROOT) * value * (1.0 - bent * bent) * (
                1.0 + (3.0 * GELU_CUBE) * square
            )
            inner = low(act * second)
            inner_block[:, tile] = inner
            pair.write(act_ref, tile, low(act))
            pair.write(slope_ref, tile, low(slope * second))
            pair.write(inner_ref, tile, inner)

        tile_loop(units // TILE, TILE, into)

        def out(tile):
            pair.write(part, tile, low(dot(inner_block[...], down[:, tile])))

        tile_loop(width // (2 * TILE), 2 * TILE, out)

    ring.send(0)
    all_ref[span(index * rows, rows), :] = own_ref[...]
    for copy in loads:
        copy.wait()
    compute(0)
    for step in range(1, HEADS):
        if step < RING_STEPS:
            ring.send(step)
        else:
            ring.arrive(step)
        compute(step)
        sums.send(step - 1)
    for lane in range(4):
        sum_ref[pl.ds(lane_offset(lane, rows), piece), :] = sums.last(index, lane)
    ring.sent()
    sums.sent()


def ffn_forward(own, gate, up, down, number):
    rows, width = own.shape
    units = gate.shape[0]
    near, anywhere = pl.BlockSpec(memory_space=pltpu.VMEM), pl.BlockSpec(memory_space=pl.ANY)
    total = rows * HEADS
    steps = 4 * RING_STEPS
    bf16 = jnp.bfloat16
    inner = jax.ShapeDtypeStruct((total, units), bf16)
    return pl.pallas_call(
        ffn_kernel,
        out_shape=[
            jax.ShapeDtypeStruct((rows, width), jnp.float32),
            jax.ShapeDtypeStruct((total, width), bf16),
            inner,
            inner,
            inner,
        ],
        in_specs=[near] + [anywhere] * 3,
        out_specs=[near] * 5,
        scratch_shapes=[pltpu.VMEM((units, width), bf16)] * 3
        + [
            pltpu.VMEM((rows, width), bf16),
            pltpu.VMEM((rows, units), bf16),
            pltpu.VMEM((total, width), bf16),
            pltpu.VMEM((steps + 4, rows // 4, width), bf16),
            pltpu.SemaphoreType.DMA((3,)),
        ]
        + [pltpu.SemaphoreType.DMA((steps,))] * 4,
        compiler_params=pltpu.CompilerParams(
            collective_id=number, has_side_effects=True, vmem_limit_bytes=VMEM_BYTES
        ),
    )(own, gate, up, down)


def ffn_back_kernel(
    own_ref,
    all_any,
    act_any,
    slope_any,
    inner_any,
    gate_any,
    up_any,
    down_any,
    blocks_ref,
    sum_ref,
    down_out,
    gate_out,
    up_out,
    far_down,
    block_sum,
    d_all,
    tokens,
    d_up,
    d_gate,
    inner,
    gate,
    up,
    down,
    block,
    inner_block,
    part,
    held,
    turned,
    give,
    keep,
    theirs,
    block_held,
    load_sems,
    store_sems,
    *sems,
):
    ring_sems, sum_sems, fold_sems, block_sems, far_sems = [
        sems[i : i + 2] for i in range(0, 10, 2)
    ]
    rows, width = own_ref.shape
    units = gate.shape[0]
    piece = rows // 4
    index = lax.axis_index("fsdp")
    place = ring_place(index)
    ends = ring_ends(place)
    unused_chip, core, sibling, across = neighbours()
    load_down, load_act, load_slope, load_gate, load_up, load_inner, load_tokens = start_loads(
        (
            (down_any, down),
            (act_any, d_up),
            (slope_any, d_gate),
            (gate_any, gate),
            (up_any, up),
            (inner_any, inner),
            (all_any, tokens),
        ),
        load_sems,
    )
    greet(ends + (sibling, across))
    ring = Ring(
        place,
        ends,
        4,
        ring_sems,
        lambda lane: own_ref.at[pl.ds(lane_offset(lane, rows), piece)],
        lambda owner, lane: d_all.at[span(owner * rows + lane_offset(lane, rows), piece)],
    )

    def own(owner, lane):
        return part[span(owner * rows + lane_offset(lane, rows), piece), :].astype(jnp.float32)

    low_rows = block_sum.shape[0] // 2

    def block_own(owner, lane):
        return blocks_ref[owner, pl.ds(lane * low_rows, low_rows), :].astype(jnp.float32)

    sums = RingSum(place, ends, 4, sum_sems, held, own)
    block_sums = RingSum(place, ends, 2, block_sems, block_held, block_own)

    def compute(step):
        pair = Pair(place, step, rows)
        block[...] = pair.read(d_all)

        def into(tile):
            grad = mul_t(block[...], down[tile, :])
            first = low(grad * pair.read(d_gate, tile).astype(jnp.float32))
            second = low(grad * pair.read(d_up, tile).astype(jnp.float32))
            pair.write(d_gate, tile, first)
            pair.write(d_up, tile, second)
            inner_block[0, :, tile] = first
            inner_block[1, :, tile] = second

        tile_loop(units // TILE, TILE, into)
        if step == 0:
            load_gate.wait()
            load_up.wait()

        def out(tile):
            total = dot(inner_block[0], gate[:, tile]) + dot(inner_block[1], up[:, tile])
            pair.write(part, tile, low(total))

        tile_loop(width // (2 * TILE), 2 * TILE, out)

    half = units // 2
    folds, stores, swaps = [], [], []
    jobs = (
        (inner, d_all, down_out),
        (d_gate, tokens, gate_out),
        (d_up, tokens, up_out),
    )

    def outer_half(number, side, target):
        left, right, unused_out = jobs[number]
        turned[...] = left[:, span(side * half, half)].T

        def tile_step(tile):
            target[:, tile] = low(dot(turned[...], right[:, tile]))

        tile_loop(width // (2 * TILE), 2 * TILE, tile_step)

    def grads_give(number):
        if number:
            folds[number - 1].wait_send()
        outer_half(number, 1 - core, give)
        folds.append(remote(give, theirs.at[number], fold_sems, number, sibling))

    def grads_keep(number):
        if number > 1:
            stores[number - 1].wait()
        outer_half(number, core, keep)
        folds[number].wait_recv()

        def add(tile):
            keep[tile, :] = add_low(keep[tile, :], theirs[number, tile, :])

        tile_loop(half // 64, 64, add)
        store = pltpu.make_async_copy(keep, jobs[number][2], store_sems.at[number])
        store.start()
        stores.append(store)
        if not number:
            store.wait()
            swaps.append(remote(down_out, far_down, far_sems, 0, across))

    ring.send(0)
    d_all[span(index * rows, rows), :] = own_ref[...]
    for copy in (load_down, load_act, load_slope):
        copy.wait()
    compute(0)
    for step in range(1, HEADS):
        if step < RING_STEPS:
            ring.send(step)
        else:
            ring.arrive(step)
        if step >= RING_STEPS - 1:
            sums.send(step - RING_STEPS + 1)
        compute(step)
    load_inner.wait()
    load_tokens.wait()
    for step in range(RING_STEPS):
        if step >= 2:
            sums.send(step)
        block_sums.send(step)
        if step < 6:
            if step % 2:
                grads_keep(step // 2)
            else:
                grads_give(step // 2)
    for lane in range(4):
        sum_ref[pl.ds(lane_offset(lane, rows), piece), :] = sums.last(index, lane)
    for lane in range(2):
        block_sum[pl.ds(lane * low_rows, low_rows), :] = low(block_sums.last(index, lane))
    for item in (ring, sums, block_sums):
        item.sent()
    folds[-1].wait_send()
    stores[-1].wait()
    swaps[0].wait()


def ffn_back(own, arrays, weights, blocks, number):
    rows, width = own.shape
    units = weights[0].shape[0]
    near, anywhere = pl.BlockSpec(memory_space=pltpu.VMEM), pl.BlockSpec(memory_space=pl.ANY)
    total = rows * HEADS
    steps = 4 * RING_STEPS
    bf16 = jnp.bfloat16
    counts = [steps, steps, 3, 2 * RING_STEPS, 1]
    half = (units // 2, width)
    low_rows = blocks.shape[1] // 2
    return pl.pallas_call(
        ffn_back_kernel,
        out_shape=[jax.ShapeDtypeStruct((rows, width), jnp.float32)]
        + [jax.ShapeDtypeStruct(half, bf16)] * 4
        + [jax.ShapeDtypeStruct(blocks.shape[1:], bf16)],
        in_specs=[near] + [anywhere] * 7 + [near],
        out_specs=[near] + [anywhere] * 4 + [near],
        scratch_shapes=[pltpu.VMEM((total, width), bf16)] * 2
        + [pltpu.VMEM((total, units), bf16)] * 3
        + [pltpu.VMEM((units, width), bf16)] * 3
        + [
            pltpu.VMEM((rows, width), bf16),
            pltpu.VMEM((2, rows, units), bf16),
            pltpu.VMEM((total, width), bf16),
            pltpu.VMEM((steps + 4, rows // 4, width), bf16),
            pltpu.VMEM((units // 2, total), bf16),
            pltpu.VMEM(half, bf16),
            pltpu.VMEM(half, bf16),
            pltpu.VMEM((3,) + half, bf16),
            pltpu.VMEM((2 * RING_STEPS + 2, low_rows, blocks.shape[2]), bf16),
            pltpu.SemaphoreType.DMA((7,)),
            pltpu.SemaphoreType.DMA((3,)),
        ]
        + [pltpu.SemaphoreType.DMA((count,)) for count in counts for unused_side in range(2)],
        compiler_params=pltpu.CompilerParams(
            collective_id=number, has_side_effects=True, vmem_limit_bytes=56 << 20
        ),
    )(own, *arrays, *weights, blocks)


ACROSS = ((0, 2), (2, 0), (1, 3), (3, 1))
SIBLING = ((0, 1), (1, 0), (2, 3), (3, 2))


def head_back(grad, raw, gain, cosine, sine):
    half = raw.shape[1] // 2
    first, second = grad[:, :half], grad[:, half:]
    turned = jnp.concatenate(
        [first * cosine + second * sine, second * cosine - first * sine], axis=1
    )
    root = lax.rsqrt(jnp.mean(raw * raw, axis=1, keepdims=True) + EPS)
    gain_grad = jnp.sum(turned * raw * root, axis=0, keepdims=True)
    turned = turned * gain
    along = jnp.mean(turned * raw, axis=1, keepdims=True)
    return (root * turned - raw * (root * root * root * along), gain_grad)


def attention_back_kernel(
    own_ref,
    o_any,
    q_any,
    k_any,
    v_any,
    att_any,
    probs_any,
    normed_any,
    weights_any,
    q_raw_any,
    k_raw_any,
    cosine_any,
    sine_any,
    laurel_any,
    gains_ref,
    pl_ref,
    own_down,
    far_down,
    own_gate,
    own_up,
    sum_ref,
    owned_ref,
    early_ref,
    gain_grads,
    total_down,
    total_gate,
    total_up,
    far_gate,
    far_up,
    o_proj,
    q_low,
    k_low,
    v_low,
    att,
    probs,
    normed,
    weights,
    q_raw,
    k_raw,
    cosine,
    sine,
    d_all,
    block,
    att_block,
    q_block,
    dq_block,
    d_q,
    d_k,
    d_v,
    d_qkv,
    turned,
    part,
    held,
    blocks,
    folded,
    far,
    near_sum,
    key_held,
    o_grad,
    o_folded,
    o_far,
    sum_own,
    sum_far,
    load_sems,
    final_sems,
    *sems,
):
    pairs = [sems[i : i + 2] for i in range(0, len(sems), 2)]
    ring_sems, sum_sems, fold_sems, far_sems, swap_sems, key_sems = pairs[:6]
    mirror_sems, early_sems, o_fold_sems, o_far_sems, cross_sems, total_sems = pairs[6:]
    rows, width = own_ref.shape
    total_rows = rows * HEADS
    half = rows // 2
    piece = rows // 4
    index = lax.axis_index("fsdp")
    chip, core, sibling, across = neighbours()
    place = ring_place(index)
    ends = ring_ends(place)
    others = [lax.rem(index + step, HEADS) for step in range(1, HEADS)]
    quarter = 2 * chip + core
    quarter_rows = blocks.shape[2]
    own_rows = span(quarter * quarter_rows, quarter_rows)
    other_rows = span((2 * (1 - chip) + core) * quarter_rows, quarter_rows)
    groups = HEADS // KV_HEADS
    scale = HEAD_DIM ** (-0.5)
    head_columns = 3 * HEAD_DIM
    loads = start_loads(
        (
            (o_any, o_proj),
            (q_any, q_low),
            (k_any, k_low),
            (v_any, v_low),
            (att_any, att),
            (probs_any, probs),
            (q_raw_any, q_raw),
            (k_raw_any, k_raw),
            (cosine_any, cosine),
            (sine_any, sine),
            (weights_any, weights),
            (normed_any, normed),
            (laurel_any, blocks.at[:, :, :, pl.ds(head_columns, laurel_any.shape[3])]),
        ),
        load_sems,
    )
    greet([{"fsdp": other} for other in others] + [sibling, across])
    early_rows = far_up.shape[0] // 4
    late_rows = far_up.shape[0] - early_rows
    crossings = [
        remote(own_gate, far_gate, cross_sems, 0, across),
        remote(
            own_up.at[pl.ds(0, early_rows)], far_up.at[pl.ds(0, early_rows)], cross_sems, 1, across
        ),
    ]
    ring = Ring(
        place,
        ends,
        4,
        ring_sems,
        lambda lane: own_ref.at[pl.ds(lane_offset(lane, rows), piece)],
        lambda owner, lane: d_all.at[span(owner * rows + lane_offset(lane, rows), piece)],
    )
    sums = RingSum(
        place,
        ends,
        4,
        sum_sems,
        held,
        lambda owner, lane: part[pl.ds(lane_offset(lane, rows), piece), :],
    )
    key_tiles = total_rows // TILE

    def compute(step):
        pair = Pair(place, step, rows)
        block[...] = pair.read(d_all)
        d_att = low(mul_t(block[...], o_proj[...]))
        att_block[...] = d_att
        q_block[...] = pair.read(q_low)
        delta = jnp.sum(
            d_att.astype(jnp.float32) * pair.read(att).astype(jnp.float32), axis=1, keepdims=True
        )
        dq_block[...] = jnp.zeros_like(dq_block)

        def keys(tile):
            chance = pair.read(probs, tile)
            d_chance = mul_t(att_block[...], v_low[tile, :])
            d_score = low(chance.astype(jnp.float32) * (d_chance - delta) * scale)
            dq_block[...] += dot(d_score, k_low[tile, :])
            d_k[tile, :] += dot(d_score.T, q_block[...])
            d_v[tile, :] += dot(chance.T, att_block[...])

        tile_loop(key_tiles, TILE, keys)
        pair.write(d_q, slice(None), dq_block[...])

    finals = (
        (own_down, far_down, total_down),
        (own_gate, far_gate, total_gate),
        (own_up, far_up, total_up),
    )
    final_loads, final_sends, final_stores = [], [], []
    half_units = far_up.shape[0]

    def load_final(number):
        if number:
            final_sends[number - 1].wait_send()
            final_stores[number - 1].wait()
        for side, (ref, target) in enumerate(zip(finals[number], (sum_own, sum_far))):
            copy = pltpu.make_async_copy(ref, target, final_sems.at[side])
            copy.start()
            final_loads.append(copy)

    def add_final(number):
        for copy in final_loads[2 * number :]:
            copy.wait()

        def add(tile):
            sum_own[tile, :] = add_low(sum_own[tile, :], sum_far[tile, :])

        tile_loop(half_units // 64, 64, add)
        target = finals[number][2].at[span(core * half_units, half_units)]
        final_sends.append(remote(sum_own, target, total_sems, number, sibling))
        store = pltpu.make_async_copy(sum_own, target, final_sems.at[2])
        store.start()
        final_stores.append(store)

    d_k[...] = jnp.zeros_like(d_k)
    d_v[...] = jnp.zeros_like(d_v)
    gain_grads[...] = jnp.zeros_like(gain_grads)
    ring.send(0)
    d_all[span(index * rows, rows), :] = own_ref[...]
    for copy in loads[:6]:
        copy.wait()
    compute(0)
    for step in range(1, HEADS):
        if step < RING_STEPS:
            ring.send(step)
        else:
            ring.arrive(step)
        compute(step)
        if step == 2:
            load_final(0)
        if step == 4:
            add_final(0)
    for copy in loads[6:]:
        copy.wait()

    def raw_tile(tile):
        for side, (grad, raw) in enumerate(((d_q, q_raw), (d_k, k_raw))):
            value, gain_grad = head_back(
                grad[tile, :],
                raw[tile, :],
                gains_ref[side : side + 1, :],
                cosine[tile, :],
                sine[tile, :],
            )
            d_qkv[tile, side * HEAD_DIM : (side + 1) * HEAD_DIM] = low(value)
            gain_grads[side : side + 1, :] += gain_grad
        d_qkv[tile, 2 * HEAD_DIM :] = low(d_v[tile, :])

    tile_loop(total_rows // 128, 128, raw_tile)

    def owner_at(step, way):
        return ring_index(lax.rem(place + (step + 1 if way else HEADS - 1 - step), HEADS))

    def part_of(step):
        tops = [
            d_qkv[span(owner_at(step, way) * rows + way * half, half), :] for way in range(2)
        ]
        part[...] = mul_t(jnp.concatenate(tops, axis=0), weights[...])

    def head_grads(number, carry):
        turned[...] = normed[:, span(number * TILE, TILE)].T
        value = low(dot(turned[...], d_qkv[...]))
        for step in range(QUARTERS):
            blocks[number, step, :, :head_columns] = value[
                step * quarter_rows : (step + 1) * quarter_rows
            ]
        return carry

    def o_tile(tile):
        value = low(dot(turned[...], d_all[:, tile]))
        for step in range(QUARTERS):
            o_grad[step, :, tile] = value[step * quarter_rows : (step + 1) * quarter_rows]

    part_of(0)
    sums.send(0)
    lax.fori_loop(0, width // TILE, head_grads, 0)
    folds, o_folds, across_sends, swaps, key_swaps = [], [], [], [], []
    for side in range(2):
        folds.append(
            remote(blocks.at[:, 2 * side + 1 - core], folded.at[side], fold_sems, side, sibling)
        )
    part_of(1)
    sums.send(1)
    turned[...] = att[...].T
    tile_loop(width // (2 * TILE), 2 * TILE, o_tile)
    for side in range(2):
        o_folds.append(
            remote(o_grad.at[2 * side + 1 - core], o_folded.at[side], o_fold_sems, side, sibling)
        )
    mirror, early = Mirror(1, mirror_sems), Mirror(1, early_sems)
    rest = blocks.shape[3] - HEAD_DIM
    q_columns = HEADS * HEAD_DIM
    mine, yours = 2 * chip + core, 2 * (1 - chip) + core

    def fold_step():
        for side in range(2):
            folds[side].wait_recv()
            o_folds[side].wait_recv()
        for number in range(HEADS):
            blocks[number, yours] = add_low(blocks[number, yours], folded[1 - chip, number])
        across_sends.append(remote(blocks.at[:, yours], far, far_sems, 0, across))
        o_grad[yours] = add_low(o_grad[yours], o_folded[1 - chip])
        across_sends.append(remote(o_grad.at[yours], o_far, o_far_sems, 0, across))
        crossings.append(
            remote(
                own_up.at[pl.ds(early_rows, late_rows)],
                far_up.at[pl.ds(early_rows, late_rows)],
                cross_sems,
                2,
                across,
            )
        )
        for number in range(HEADS):
            blocks[number, mine] = add_low(blocks[number, mine], folded[chip, number])
        o_grad[mine] = add_low(o_grad[mine], o_folded[chip])

    def swap_step():
        across_sends[0].wait_recv()
        for number in range(HEADS):
            near_sum[number] = add_low(blocks[number, mine], far[number])
        here = span(index * HEAD_DIM, HEAD_DIM)
        for step, other in enumerate(others):
            swaps.append(
                remote(
                    near_sum.at[other, :, pl.ds(0, HEAD_DIM)],
                    owned_ref.at[own_rows, here],
                    swap_sems,
                    step,
                    {"fsdp": other},
                )
            )
            key_swaps.append(
                remote(
                    near_sum.at[other, :, pl.ds(HEAD_DIM, rest)],
                    key_held.at[index],
                    key_sems,
                    step,
                    {"fsdp": other},
                )
            )
        owned_ref[own_rows, here] = near_sum[index, :, :HEAD_DIM]
        key_held[index] = near_sum[index, :, HEAD_DIM:]
        across_sends[1].wait_recv()
        early_ref[own_rows, :width] = add_low(o_grad[mine], o_far[...])
        early_ref[own_rows, width:] = pl_ref[...]
        early.give(0, early_ref.at[own_rows])

    for step in range(2, RING_STEPS):
        part_of(step)
        sums.send(step)
        if step == 2:
            fold_step()
        if step == 3:
            crossings[0].wait_recv()
            load_final(1)
        if step == 4:
            swap_step()
        if step == 5:
            add_final(1)
        if step == 6:
            early.relay(0, early_ref.at[other_rows])
    part[...] = mul_t(d_qkv[span(index * rows, rows), :], weights[...])
    for lane in range(4):
        sum_ref[pl.ds(lane_offset(lane, rows), piece), :] = sums.last(index, lane)
    for copy in swaps + key_swaps:
        copy.wait_recv()
    for head in range(KV_HEADS):
        total = key_held[head * groups].astype(jnp.float32)
        for step in range(1, groups):
            total = total + key_held[head * groups + step].astype(jnp.float32)
        total = low(total)
        for side in range(2):
            base = q_columns + (side * KV_HEADS + head) * HEAD_DIM
            owned_ref[own_rows, pl.ds(base, HEAD_DIM)] = total[
                :, side * HEAD_DIM : (side + 1) * HEAD_DIM
            ]
    extra = key_held[0, :, 2 * HEAD_DIM :].astype(jnp.float32)
    for step in range(1, HEADS):
        extra = extra + key_held[step, :, 2 * HEAD_DIM :].astype(jnp.float32)
    base = q_columns + 2 * KV_HEADS * HEAD_DIM
    owned_ref[own_rows, pl.ds(base, rest - 2 * HEAD_DIM)] = low(extra)
    mirror.give(0, owned_ref.at[own_rows])
    crossings[1].wait_recv()
    crossings[2].wait_recv()
    load_final(2)
    mirror.relay(0, owned_ref.at[other_rows])
    add_final(2)
    mirror.finish()
    early.finish()
    ring.sent()
    sums.sent()
    for copy in folds + o_folds + across_sends + swaps + key_swaps + crossings:
        copy.wait_send()
    final_sends[2].wait_send()
    final_stores[2].wait()
    for copy in final_sends:
        copy.wait_recv()


def attention_back(own, arrays, laurel, gains, pl_sum, chip_grads, far_down, number):
    rows, width = own.shape
    total = rows * HEADS
    shard = width // HEADS
    quarter = shard // QUARTERS
    steps = 4 * RING_STEPS
    columns = 3 * HEAD_DIM + laurel.shape[1]
    laurel = laurel.reshape(HEADS, QUARTERS, quarter, -1)
    half = chip_grads[0].shape
    near, anywhere = pl.BlockSpec(memory_space=pltpu.VMEM), pl.BlockSpec(memory_space=pl.ANY)
    bf16, f32 = jnp.bfloat16, jnp.float32
    owned = (HEADS + 2 * KV_HEADS) * HEAD_DIM + laurel.shape[3]
    counts = [steps, steps, 2, 1, HEADS - 1, HEADS - 1, 3, 3, 2, 1, 3, 3]
    down, gate, up = chip_grads
    whole = jax.ShapeDtypeStruct((2 * half[0], half[1]), bf16)
    part = jax.ShapeDtypeStruct(half, bf16)
    return pl.pallas_call(
        attention_back_kernel,
        out_shape=[
            jax.ShapeDtypeStruct((rows, width), f32),
            jax.ShapeDtypeStruct((shard, owned), bf16),
            jax.ShapeDtypeStruct((shard, width + pl_sum.shape[1]), bf16),
            jax.ShapeDtypeStruct(gains.shape, f32),
            whole,
            whole,
            whole,
            part,
            part,
        ],
        in_specs=[near] + [anywhere] * (len(arrays) + 1) + [near] * 2 + [anywhere] * 4,
        out_specs=[near] * 4 + [anywhere] * 5,
        scratch_shapes=[pltpu.VMEM(item.shape, item.dtype) for item in arrays]
        + [
            pltpu.VMEM((total, width), bf16),
            pltpu.VMEM((rows, width), bf16),
            pltpu.VMEM((rows, HEAD_DIM), bf16),
            pltpu.VMEM((rows, HEAD_DIM), bf16),
            pltpu.VMEM((rows, HEAD_DIM), f32),
            pltpu.VMEM((total, HEAD_DIM), f32),
            pltpu.VMEM((total, HEAD_DIM), f32),
            pltpu.VMEM((total, HEAD_DIM), f32),
            pltpu.VMEM((total, 3 * HEAD_DIM), bf16),
            pltpu.VMEM((HEAD_DIM, total), bf16),
            pltpu.VMEM((rows, width), f32),
            pltpu.VMEM((steps + 4, rows // 4, width), bf16),
            pltpu.VMEM((HEADS, QUARTERS, quarter, columns), bf16),
            pltpu.VMEM((2, HEADS, quarter, columns), bf16),
            pltpu.VMEM((HEADS, quarter, columns), bf16),
            pltpu.VMEM((HEADS, quarter, columns), bf16),
            pltpu.VMEM((HEADS, quarter, columns - HEAD_DIM), bf16),
            pltpu.VMEM((QUARTERS, quarter, width), bf16),
            pltpu.VMEM((2, quarter, width), bf16),
            pltpu.VMEM((quarter, width), bf16),
            pltpu.VMEM(half, bf16),
            pltpu.VMEM(half, bf16),
            pltpu.SemaphoreType.DMA((len(arrays) + 1,)),
            pltpu.SemaphoreType.DMA((3,)),
        ]
        + [pltpu.SemaphoreType.DMA((count,)) for count in counts for unused_side in range(2)],
        compiler_params=pltpu.CompilerParams(
            collective_id=number, has_side_effects=True, vmem_limit_bytes=56 << 20
        ),
    )(own, *arrays, laurel, gains, pl_sum, down, far_down, gate, up)


def gains_kernel(parts_ref, sum_ref, landed, totals, send_sem, recv_sem, rep_send, rep_recv):
    index = lax.axis_index("fsdp")
    rep = lax.axis_index("rep")
    others = [lax.rem(index + step, HEADS) for step in range(1, HEADS)]
    twins = [lax.rem(rep + step, QUARTERS) for step in range(1, QUARTERS)]
    greet([{"fsdp": other} for other in others] + [{"rep": twin} for twin in twins])
    sends = [
        remote(parts_ref.at[other], landed.at[index], (send_sem, recv_sem), step, {"fsdp": other})
        for step, other in enumerate(others)
    ]
    landed[index] = parts_ref[index]
    for copy in sends:
        copy.wait_recv()
    total = landed[0]
    for step in range(1, HEADS):
        total = total + landed[step]
    totals[rep] = total
    twin_sends = [
        remote(totals.at[rep], totals.at[rep], (rep_send, rep_recv), step, {"rep": twin})
        for step, twin in enumerate(twins)
    ]
    for copy in twin_sends:
        copy.wait_recv()
    total = totals[0]
    for step in range(1, QUARTERS):
        total = total + totals[step]
    sum_ref[...] = total
    for copy in sends + twin_sends:
        copy.wait_send()


def gains_sum(parts, number):
    near = pl.BlockSpec(memory_space=pltpu.VMEM)
    return pl.pallas_call(
        gains_kernel,
        out_shape=jax.ShapeDtypeStruct(parts.shape[1:], parts.dtype),
        in_specs=[near],
        out_specs=near,
        scratch_shapes=[
            pltpu.VMEM(parts.shape, parts.dtype),
            pltpu.VMEM((QUARTERS,) + parts.shape[1:], parts.dtype),
        ]
        + [pltpu.SemaphoreType.DMA((HEADS - 1,))] * 2
        + [pltpu.SemaphoreType.DMA((QUARTERS - 1,))] * 2,
        compiler_params=pltpu.CompilerParams(collective_id=number, has_side_effects=True),
    )(parts)


def core_fold(value, axis):
    half = value.shape[axis] // 2
    core = lax.rem(lax.axis_index("rep"), 2)
    give = lax.dynamic_slice_in_dim(value, (1 - core) * half, half, axis)
    keep = lax.dynamic_slice_in_dim(value, core * half, half, axis)
    return add_low(keep, lax.ppermute(give, "rep", SIBLING))


def chip_fold(value, axis):
    half = value.shape[axis] // 2
    chip = lax.axis_index("rep") // 2
    give = lax.dynamic_slice_in_dim(value, (1 - chip) * half, half, axis)
    keep = lax.dynamic_slice_in_dim(value, chip * half, half, axis)
    return add_low(keep, lax.ppermute(give, "rep", ACROSS))


def quarter_fold(value):
    value = value.reshape(value.shape[:-3] + (2, 2) + value.shape[-2:])
    axis = value.ndim - 4
    value = chip_fold(core_fold(value, axis + 1), axis)
    return value.reshape(value.shape[:axis] + value.shape[axis + 2 :])


def dot(left, right):
    return jnp.dot(left, right, preferred_element_type=jnp.float32)


def low(value):
    return value.astype(jnp.bfloat16)


def tree_places(lengths, parents, total):
    count = lengths.shape[0]
    labels = jnp.arange(count, dtype=jnp.int32)
    ends = jnp.sum(jnp.where(labels[:, None] <= labels[None, :], lengths[:, None], 0), axis=0)
    starts = ends - lengths
    tokens = jnp.arange(total, dtype=jnp.int32)
    segment = jnp.sum((ends[None, :] <= tokens[:, None]).astype(jnp.int32), axis=1)
    parent_hot = (parents[:, None] == labels[None, :]) & (labels[:, None] > 0)
    identity = labels[:, None] == labels[None, :]
    reached = parent_hot | identity
    for unused_step in range((count - 1).bit_length()):
        reached = jnp.any(reached[:, :, None] & reached[None, :, :], axis=1)
    offset = jnp.sum(jnp.where(reached & ~identity, lengths[None, :], 0), axis=1) - starts
    member = segment[:, None] == labels[None, :]
    reach = jnp.any(member[:, :, None] & reached[None, :, :], axis=1)
    position = jnp.sum(jnp.where(member, offset[None, :], 0), axis=1) + tokens
    return (tokens, member.astype(jnp.bfloat16), reach.astype(jnp.bfloat16), position)


def head_plan(
    hidden_in,
    layer_input,
    out_grad,
    seg_lengths,
    seg_parents,
    attn_norm,
    q_proj,
    k_proj,
    v_proj,
    q_norm,
    k_norm,
    o_proj,
    attn_post_norm,
    laurel_left,
    laurel_right,
    laurel_norm,
    ffw_norm,
    gate_proj,
    up_proj,
    down_proj,
    ffw_post_norm,
    pl_gate,
    pl_proj,
    pl_post_norm,
):
    index = lax.axis_index("fsdp")
    rows, width = hidden_in.shape
    shard = width // HEADS
    total = rows * HEADS
    groups = HEADS // KV_HEADS
    scale = HEAD_DIM ** (-0.5)
    rank = laurel_left.shape[1]
    per_layer = pl_gate.shape[1]
    key_head = index // groups

    gains = (attn_norm, attn_post_norm, laurel_norm, ffw_norm, ffw_post_norm, pl_post_norm)
    packed = jnp.concatenate(gains + (q_norm, k_norm))
    pad = -packed.shape[0] % (32 * 128)
    packed = jnp.pad(packed, (0, pad)).reshape(-1, 128)
    hidden_all, gains_held, q_head, kv_all, small_all, full_plproj = start_gather(
        hidden_in,
        packed,
        q_proj,
        jnp.concatenate([k_proj, v_proj], axis=1),
        jnp.concatenate([pl_gate, laurel_left, laurel_right], axis=1),
        pl_proj,
        0,
    )
    all_gains = gains_held.reshape(HEADS, -1).astype(jnp.float32)
    wide_gains = [all_gains[:, i * shard : (i + 1) * shard].reshape(-1) for i in range(len(gains))]
    gain_anorm, gain_apost, gain_lnorm, gain_fnorm, gain_fpost, gain_plpost = wide_gains
    at = len(gains) * shard
    piece = HEAD_DIM // HEADS
    gain_qnorm = all_gains[:, at : at + piece].reshape(-1)
    gain_knorm = all_gains[:, at + piece : at + 2 * piece].reshape(-1)

    k_head = lax.dynamic_slice_in_dim(kv_all, key_head * HEAD_DIM, HEAD_DIM, 1)
    v_head = lax.dynamic_slice_in_dim(kv_all, (KV_HEADS + key_head) * HEAD_DIM, HEAD_DIM, 1)
    full_plgate = small_all[:, :per_layer]
    full_left = small_all[:, per_layer : per_layer + rank]
    full_right = small_all[:, per_layer + rank :]

    tokens, member, reach, position = tree_places(seg_lengths[0], seg_parents[0], total)
    depth = position.astype(jnp.float32)
    seen = (mul_t(reach, member) > 0) & (tokens[None, :] <= tokens[:, None])

    normed_all = low(norm_rows(hidden_all.astype(jnp.float32), gain_anorm))
    q_raw = dot(normed_all, q_head)
    k_raw = dot(normed_all, k_head)
    v_low = low(dot(normed_all, v_head))

    half = HEAD_DIM // 2
    freqs = jnp.exp(
        jnp.arange(half, dtype=jnp.float32) * (-2.0 * math.log(ROPE_BASE) / HEAD_DIM)
    )
    angle = depth[:, None] * freqs[None, :]
    cosine, sine = jnp.cos(angle), jnp.sin(angle)

    def head_path(raw, gain):
        value = norm_rows(raw, gain)
        first, second = value[:, :half], value[:, half:]
        return jnp.concatenate(
            [first * cosine - second * sine, second * cosine + first * sine], axis=1
        )

    q_low = low(head_path(q_raw, gain_qnorm))
    k_low = low(head_path(k_raw, gain_knorm))
    scores = jnp.where(seen, mul_t(q_low, k_low) * scale, MASKED)
    top = jnp.max(scores, axis=-1, keepdims=True)
    expo = jnp.exp(scores - top)
    sums = jnp.sum(expo, axis=-1, keepdims=True)
    probs = expo / sums
    probs_low = low(probs)
    attended = dot(probs_low, v_low)
    attended_low = low(attended)
    (branch,) = ring_scatter(low(dot(attended_low, o_proj)), 6)

    source = hidden_in.astype(jnp.float32)
    extra = layer_input.astype(jnp.float32)
    normed = norm_rows(source, gain_anorm)
    normed_low = low(normed)
    left_low = low(dot(normed_low, full_left))
    low_rank = mul_t(left_low, full_right)
    first_sum = (
        source + norm_rows(branch, gain_apost) + normed + norm_rows(low_rank, gain_lnorm)
    ) * HALF_ROOT
    ffw_low = low(norm_rows(first_sum, gain_fnorm))

    ffw_out, ffw_all, act, slope, inner_low = ffn_forward(
        ffw_low, gate_proj, up_proj, down_proj, 7
    )
    second_sum = first_sum + norm_rows(ffw_out, gain_fpost)
    second_low = low(second_sum)
    pl_pre = dot(second_low, full_plgate)
    pl_mix = low(gelu_mix(pl_pre, extra))
    pl_out = dot(pl_mix, full_plproj)
    result = second_sum + norm_rows(pl_out, gain_plpost)
    seed = out_grad.astype(jnp.float32)
    d_plout, grad_plpost = norm_back(pl_out, gain_plpost, seed)
    d_plout_low = low(d_plout)
    grad_plproj = outer(pl_mix, d_plout_low)
    d_mix = mul_t(d_plout_low, full_plproj)
    d_pre, d_extra = mix_back(pl_pre, extra, d_mix)
    d_pre_low = low(d_pre)
    grad_plgate = outer(second_low, d_pre_low)
    d_second = seed + mul_t(d_pre_low, full_plgate)
    pl_blocks = jnp.concatenate(
        [
            low(grad_plgate).reshape(HEADS, shard, per_layer),
            low(grad_plproj).reshape(HEADS, shard, per_layer),
        ],
        axis=-1,
    )
    pl_blocks = quarter_fold(pl_blocks.reshape(HEADS, QUARTERS, -1, 2 * per_layer))
    d_ffwout, grad_fpost = norm_back(ffw_out, gain_fpost, d_second)

    d_ffwin, *rest = ffn_back(
        low(d_ffwout),
        (ffw_all, act, slope, inner_low),
        (gate_proj, up_proj, down_proj),
        pl_blocks,
        9,
    )
    chip_grads, far_down, pl_sum = rest[:3], rest[3], rest[4]
    d_first_part, grad_fnorm = norm_back(first_sum, gain_fnorm, d_ffwin)
    d_scaled = (d_second + d_first_part) * HALF_ROOT
    d_branch, grad_apost = norm_back(branch, gain_apost, d_scaled)
    d_lowrank, grad_lnorm = norm_back(low_rank, gain_lnorm, d_scaled)
    d_lowrank_low = low(d_lowrank)
    grad_right = outer(d_lowrank_low, left_low)
    d_left_low = low(dot(d_lowrank_low, full_right))
    grad_left = outer(normed_low, d_left_low)

    d_normed_sum, owned, early, head_gains, *totals = attention_back(
        low(d_branch),
        (
            o_proj,
            q_low,
            k_low,
            v_low,
            attended_low,
            probs_low,
            normed_all,
            jnp.concatenate([q_head, k_head, v_head], axis=1),
            q_raw,
            k_raw,
            cosine,
            sine,
        ),
        low(jnp.concatenate([grad_left, grad_right], axis=1)),
        jnp.stack([gain_qnorm, gain_knorm]),
        pl_sum,
        chip_grads,
        far_down,
        12,
    )
    grad_qnorm, grad_knorm = head_gains
    sum_down, sum_gate, sum_up = [item.astype(jnp.float32) for item in totals[:3]]
    owned = owned.astype(jnp.float32)
    early = early.astype(jnp.float32)
    key_at = width
    value_at = key_at + KV_HEADS * HEAD_DIM
    left_at = value_at + KV_HEADS * HEAD_DIM
    d_normed = d_scaled + mul_t(d_left_low, full_left) + d_normed_sum
    d_source_part, grad_anorm = norm_back(source, gain_anorm, d_normed)
    d_source = d_scaled + d_source_part

    small_grads = [grad_anorm, grad_apost, grad_lnorm, grad_fnorm, grad_fpost, grad_plpost]
    parts = [item.reshape(HEADS, shard) for item in small_grads]
    parts += [item.reshape(HEADS, piece) for item in (grad_qnorm, grad_knorm)]
    parts = jnp.concatenate(parts, axis=1)
    parts = jnp.pad(parts, ((0, 0), (0, -parts.shape[1] % 1024))).reshape(HEADS, -1, 128)
    small_sums = gains_sum(parts, 13).reshape(-1)
    own = [small_sums[i * shard : (i + 1) * shard] for i in range(len(small_grads))]
    sum_anorm, sum_apost, sum_lnorm, sum_fnorm, sum_fpost, sum_plpost = own
    sum_qnorm = small_sums[at : at + piece]
    sum_knorm = small_sums[at + piece : at + 2 * piece]
    return (
        low(result),
        low(d_source),
        low(d_extra),
        sum_anorm,
        owned[:, :width],
        owned[:, key_at:value_at],
        owned[:, value_at:left_at],
        sum_qnorm,
        sum_knorm,
        early[:, :width],
        sum_apost,
        owned[:, left_at : left_at + rank],
        owned[:, left_at + rank :],
        sum_lnorm,
        sum_fnorm,
        sum_gate,
        sum_up,
        sum_down,
        sum_fpost,
        early[:, width : width + per_layer],
        early[:, width + per_layer :].reshape(pl_proj.shape),
        sum_plpost,
    )


def gather_plan(
    hidden_in,
    layer_input,
    out_grad,
    seg_lengths,
    seg_parents,
    attn_norm,
    q_proj,
    k_proj,
    v_proj,
    q_norm,
    k_norm,
    o_proj,
    attn_post_norm,
    laurel_left,
    laurel_right,
    laurel_norm,
    ffw_norm,
    gate_proj,
    up_proj,
    down_proj,
    ffw_post_norm,
    pl_gate,
    pl_proj,
    pl_post_norm,
):
    shards = lax.axis_size("fsdp")
    rank_index = lax.axis_index("fsdp")
    rows = hidden_in.shape[0]
    total = rows * shards
    groups = HEADS // KV_HEADS
    scale = HEAD_DIM ** (-0.5)
    tokens, member, reach, position = tree_tables(seg_lengths[0], seg_parents[0], total)
    first_row = rank_index * rows
    my_tokens = first_row + jnp.arange(rows, dtype=jnp.int32)
    my_reach = lax.dynamic_slice_in_dim(reach, first_row, rows, 0)
    my_depth = lax.dynamic_slice_in_dim(position, first_row, rows, 0).astype(jnp.float32)
    seen = (jnp.dot(my_reach, member.T) > 0) & (tokens[None, :] <= my_tokens[:, None])
    (
        full_anorm,
        full_q,
        full_k,
        full_v,
        full_qnorm,
        full_knorm,
        full_o,
        full_apost,
        full_left,
        full_right,
        full_lnorm,
        full_fnorm,
        full_fpost,
        full_plgate,
        full_plproj,
        full_plpost,
    ) = (
        lax.all_gather(attn_norm, "fsdp", axis=0, tiled=True),
        lax.all_gather(q_proj, "fsdp", axis=0, tiled=True),
        lax.all_gather(k_proj, "fsdp", axis=0, tiled=True),
        lax.all_gather(v_proj, "fsdp", axis=0, tiled=True),
        lax.all_gather(q_norm, "fsdp", axis=0, tiled=True),
        lax.all_gather(k_norm, "fsdp", axis=0, tiled=True),
        lax.all_gather(o_proj, "fsdp", axis=0, tiled=True),
        lax.all_gather(attn_post_norm, "fsdp", axis=0, tiled=True),
        lax.all_gather(laurel_left, "fsdp", axis=0, tiled=True),
        lax.all_gather(laurel_right, "fsdp", axis=0, tiled=True),
        lax.all_gather(laurel_norm, "fsdp", axis=0, tiled=True),
        lax.all_gather(ffw_norm, "fsdp", axis=0, tiled=True),
        lax.all_gather(ffw_post_norm, "fsdp", axis=0, tiled=True),
        lax.all_gather(pl_gate, "fsdp", axis=0, tiled=True),
        lax.all_gather(pl_proj, "fsdp", axis=0, tiled=True),
        lax.all_gather(pl_post_norm, "fsdp", axis=0, tiled=True),
    )
    gain_anorm = full_anorm.astype(jnp.float32)
    gain_qnorm = full_qnorm.astype(jnp.float32)
    gain_knorm = full_knorm.astype(jnp.float32)
    gain_apost = full_apost.astype(jnp.float32)
    gain_lnorm = full_lnorm.astype(jnp.float32)
    gain_fnorm = full_fnorm.astype(jnp.float32)
    gain_fpost = full_fpost.astype(jnp.float32)
    gain_plpost = full_plpost.astype(jnp.float32)
    source = hidden_in.astype(jnp.float32)
    extra = layer_input.astype(jnp.float32)
    normed = norm_rows(source, gain_anorm)
    normed_low = normed.astype(jnp.bfloat16)
    q_raw = jnp.dot(normed_low, full_q, preferred_element_type=jnp.float32)
    k_raw = jnp.dot(normed_low, full_k, preferred_element_type=jnp.float32)
    v_raw = jnp.dot(normed_low, full_v, preferred_element_type=jnp.float32)

    def head_path(raw, gain):
        return rotate(norm_rows(raw.reshape(rows, -1, HEAD_DIM), gain), my_depth)

    q_low = head_path(q_raw, gain_qnorm).astype(jnp.bfloat16)
    k_low = head_path(k_raw, gain_knorm).reshape(rows, -1).astype(jnp.bfloat16)
    v_low = v_raw.astype(jnp.bfloat16)
    keys_all, values_all = (
        lax.all_gather(k_low, "fsdp", axis=0, tiled=True),
        lax.all_gather(v_low, "fsdp", axis=0, tiled=True),
    )
    keys_heads = keys_all.reshape(total, KV_HEADS, HEAD_DIM)
    values_heads = values_all.reshape(total, KV_HEADS, HEAD_DIM)
    query_groups = q_low.reshape(rows, KV_HEADS, groups, HEAD_DIM)
    mixed_list = []
    log_list = []
    for head in range(KV_HEADS):
        scores = (
            jnp.einsum(
                "tgd,nd->gtn",
                query_groups[:, head],
                keys_heads[:, head],
                preferred_element_type=jnp.float32,
            )
            * scale
        )
        scores = jnp.where(seen[None], scores, MASKED)
        top = jnp.max(scores, axis=-1, keepdims=True)
        expo = jnp.exp(scores - top)
        sums = jnp.sum(expo, axis=-1, keepdims=True)
        weights = (expo / sums).astype(jnp.bfloat16)
        mixed_list.append(
            jnp.einsum(
                "gtn,nd->tgd", weights, values_heads[:, head], preferred_element_type=jnp.float32
            )
        )
        log_list.append(top[..., 0] + jnp.log(sums[..., 0]))
    attended = jnp.stack(mixed_list, axis=1)
    log_sums = jnp.stack(log_list, axis=0)
    attended_low = attended.reshape(rows, -1).astype(jnp.bfloat16)
    branch = jnp.dot(attended_low, full_o, preferred_element_type=jnp.float32)
    left_low = jnp.dot(normed_low, full_left, preferred_element_type=jnp.float32).astype(
        jnp.bfloat16
    )
    low_rank = mul_t(left_low, full_right)
    first_sum = (
        source + norm_rows(branch, gain_apost) + normed + norm_rows(low_rank, gain_lnorm)
    ) * HALF_ROOT
    ffw_low = norm_rows(first_sum, gain_fnorm).astype(jnp.bfloat16)
    full_gate, full_up, full_down = (
        lax.all_gather(gate_proj, "fsdp", axis=0, tiled=True),
        lax.all_gather(up_proj, "fsdp", axis=0, tiled=True),
        lax.all_gather(down_proj, "fsdp", axis=0, tiled=True),
    )
    gate_val = mul_t(ffw_low, full_gate)
    up_val = mul_t(ffw_low, full_up)
    inner_low = gelu_mix(gate_val, up_val).astype(jnp.bfloat16)
    ffw_out = jnp.dot(inner_low, full_down, preferred_element_type=jnp.float32)
    second_sum = first_sum + norm_rows(ffw_out, gain_fpost)
    second_low = second_sum.astype(jnp.bfloat16)
    pl_pre = jnp.dot(second_low, full_plgate, preferred_element_type=jnp.float32)
    pl_mix = gelu_mix(pl_pre, extra).astype(jnp.bfloat16)
    pl_out = jnp.dot(pl_mix, full_plproj, preferred_element_type=jnp.float32)
    result = second_sum + norm_rows(pl_out, gain_plpost)
    seed = out_grad.astype(jnp.float32)
    d_plout, grad_plpost = norm_back(pl_out, gain_plpost, seed)
    d_plout_low = d_plout.astype(jnp.bfloat16)
    grad_plproj = outer(pl_mix, d_plout_low)
    d_mix = mul_t(d_plout_low, full_plproj)
    d_pre, d_extra = mix_back(pl_pre, extra, d_mix)
    d_pre_low = d_pre.astype(jnp.bfloat16)
    grad_plgate = outer(second_low, d_pre_low)
    d_second = seed + mul_t(d_pre_low, full_plgate)
    d_ffwout, grad_fpost = norm_back(ffw_out, gain_fpost, d_second)
    d_ffw_low = d_ffwout.astype(jnp.bfloat16)
    d_inner = mul_t(d_ffw_low, full_down)
    d_gate, d_up = mix_back(gate_val, up_val, d_inner)
    d_gate_low = d_gate.astype(jnp.bfloat16)
    d_up_low = d_up.astype(jnp.bfloat16)
    d_ffwin = jnp.dot(d_gate_low, full_gate, preferred_element_type=jnp.float32) + jnp.dot(
        d_up_low, full_up, preferred_element_type=jnp.float32
    )
    width = ffw_low.shape[1]
    gate_part = outer(d_gate_low, ffw_low)
    up_part = outer(d_up_low, ffw_low)
    down_part = outer(inner_low, d_ffw_low)
    stacked = lax.psum_scatter(
        jnp.concatenate([gate_part, up_part, down_part], axis=1).astype(jnp.bfloat16),
        "fsdp",
        scatter_dimension=0,
        tiled=True,
    ).astype(jnp.float32)
    grad_gate = stacked[:, :width]
    grad_up = stacked[:, width : 2 * width]
    grad_down = stacked[:, 2 * width :]
    d_first_part, grad_fnorm = norm_back(first_sum, gain_fnorm, d_ffwin)
    d_first = d_second + d_first_part
    d_scaled = d_first * HALF_ROOT
    d_branch, grad_apost = norm_back(branch, gain_apost, d_scaled)
    d_branch_low = d_branch.astype(jnp.bfloat16)
    d_lowrank, grad_lnorm = norm_back(low_rank, gain_lnorm, d_scaled)
    d_lowrank_low = d_lowrank.astype(jnp.bfloat16)
    grad_o = outer(attended_low, d_branch_low)
    d_att_low = mul_t(d_branch_low, full_o).astype(jnp.bfloat16)
    grad_right = outer(d_lowrank_low, left_low)
    d_left_low = jnp.dot(d_lowrank_low, full_right, preferred_element_type=jnp.float32).astype(
        jnp.bfloat16
    )
    grad_left = outer(normed_low, d_left_low)
    d_att_heads = d_att_low.reshape(rows, KV_HEADS, groups, HEAD_DIM)
    delta = jnp.sum(d_att_heads.astype(jnp.float32) * attended, axis=-1).transpose(1, 2, 0)
    block = 512
    count = total // block
    key_blocks = keys_heads.reshape(count, block, KV_HEADS, HEAD_DIM)
    value_blocks = values_heads.reshape(count, block, KV_HEADS, HEAD_DIM)
    seen_blocks = seen.reshape(rows, count, block).transpose(1, 0, 2)

    def key_step(d_query, item):
        keys, values, shown = item
        scores = (
            jnp.einsum("tkgd,nkd->kgtn", query_groups, keys, preferred_element_type=jnp.float32)
            * scale
        )
        scores = jnp.where(shown[None, None], scores, MASKED)
        probs = jnp.exp(scores - log_sums[..., None])
        d_probs = jnp.einsum(
            "tkgd,nkd->kgtn", d_att_heads, values, preferred_element_type=jnp.float32
        )
        d_scores = (probs * (d_probs - delta[..., None]) * scale).astype(jnp.bfloat16)
        d_query = d_query + jnp.einsum(
            "kgtn,nkd->tkgd", d_scores, keys, preferred_element_type=jnp.float32
        )
        d_keys = jnp.einsum(
            "kgtn,tkgd->nkd", d_scores, query_groups, preferred_element_type=jnp.float32
        )
        d_values = jnp.einsum(
            "kgtn,tkgd->nkd",
            probs.astype(jnp.bfloat16),
            d_att_heads,
            preferred_element_type=jnp.float32,
        )
        return (d_query, (d_keys, d_values))

    zero_query = jnp.zeros((rows, KV_HEADS, groups, HEAD_DIM), jnp.float32)
    d_query, (d_key_blocks, d_value_blocks) = lax.scan(
        key_step, zero_query, (key_blocks, value_blocks, seen_blocks)
    )
    my_dkeys, my_dvalues = (
        lax.psum_scatter(
            d_key_blocks.reshape(total, -1).astype(jnp.bfloat16),
            "fsdp",
            scatter_dimension=0,
            tiled=True,
        ).astype(jnp.float32),
        lax.psum_scatter(
            d_value_blocks.reshape(total, -1).astype(jnp.bfloat16),
            "fsdp",
            scatter_dimension=0,
            tiled=True,
        ).astype(jnp.float32),
    )
    unused_q, q_pull = jax.vjp(head_path, q_raw, gain_qnorm)
    d_qraw, grad_qnorm = q_pull(d_query.reshape(rows, HEADS, HEAD_DIM))
    unused_k, k_pull = jax.vjp(head_path, k_raw, gain_knorm)
    d_kraw, grad_knorm = k_pull(my_dkeys.reshape(rows, KV_HEADS, HEAD_DIM))
    d_q_low = d_qraw.astype(jnp.bfloat16)
    d_k_low = d_kraw.astype(jnp.bfloat16)
    d_v_low = my_dvalues.astype(jnp.bfloat16)
    grad_q = outer(normed_low, d_q_low)
    grad_k = outer(normed_low, d_k_low)
    grad_v = outer(normed_low, d_v_low)
    d_normed = (
        d_scaled
        + mul_t(d_q_low, full_q)
        + mul_t(d_k_low, full_k)
        + mul_t(d_v_low, full_v)
        + mul_t(d_left_low, full_left)
    )
    d_source_part, grad_anorm = norm_back(source, gain_anorm, d_normed)
    d_source = d_scaled + d_source_part
    shard_grads = (
        lax.psum_scatter(
            grad_anorm.astype(jnp.bfloat16), "fsdp", scatter_dimension=0, tiled=True
        ).astype(jnp.float32),
        lax.psum_scatter(
            grad_q.astype(jnp.bfloat16), "fsdp", scatter_dimension=0, tiled=True
        ).astype(jnp.float32),
        lax.psum_scatter(
            grad_k.astype(jnp.bfloat16), "fsdp", scatter_dimension=0, tiled=True
        ).astype(jnp.float32),
        lax.psum_scatter(
            grad_v.astype(jnp.bfloat16), "fsdp", scatter_dimension=0, tiled=True
        ).astype(jnp.float32),
        lax.psum_scatter(
            grad_qnorm.astype(jnp.bfloat16), "fsdp", scatter_dimension=0, tiled=True
        ).astype(jnp.float32),
        lax.psum_scatter(
            grad_knorm.astype(jnp.bfloat16), "fsdp", scatter_dimension=0, tiled=True
        ).astype(jnp.float32),
        lax.psum_scatter(
            grad_o.astype(jnp.bfloat16), "fsdp", scatter_dimension=0, tiled=True
        ).astype(jnp.float32),
        lax.psum_scatter(
            grad_apost.astype(jnp.bfloat16), "fsdp", scatter_dimension=0, tiled=True
        ).astype(jnp.float32),
        lax.psum_scatter(
            grad_left.astype(jnp.bfloat16), "fsdp", scatter_dimension=0, tiled=True
        ).astype(jnp.float32),
        lax.psum_scatter(
            grad_right.astype(jnp.bfloat16), "fsdp", scatter_dimension=0, tiled=True
        ).astype(jnp.float32),
        lax.psum_scatter(
            grad_lnorm.astype(jnp.bfloat16), "fsdp", scatter_dimension=0, tiled=True
        ).astype(jnp.float32),
        lax.psum_scatter(
            grad_fnorm.astype(jnp.bfloat16), "fsdp", scatter_dimension=0, tiled=True
        ).astype(jnp.float32),
        lax.psum_scatter(
            grad_fpost.astype(jnp.bfloat16), "fsdp", scatter_dimension=0, tiled=True
        ).astype(jnp.float32),
        lax.psum_scatter(
            grad_plgate.astype(jnp.bfloat16), "fsdp", scatter_dimension=0, tiled=True
        ).astype(jnp.float32),
        lax.psum_scatter(
            grad_plproj.astype(jnp.bfloat16), "fsdp", scatter_dimension=0, tiled=True
        ).astype(jnp.float32),
        lax.psum_scatter(
            grad_plpost.astype(jnp.bfloat16), "fsdp", scatter_dimension=0, tiled=True
        ).astype(jnp.float32),
    )
    (
        sum_anorm,
        sum_q,
        sum_k,
        sum_v,
        sum_qnorm,
        sum_knorm,
        sum_o,
        sum_apost,
        sum_left,
        sum_right,
        sum_lnorm,
        sum_fnorm,
        sum_fpost,
        sum_plgate,
        sum_plproj,
        sum_plpost,
        sum_gate,
        sum_up,
        sum_down,
    ) = (
        lax.psum(shard_grads[0].astype(jnp.bfloat16), "rep").astype(jnp.float32),
        lax.psum(shard_grads[1].astype(jnp.bfloat16), "rep").astype(jnp.float32),
        lax.psum(shard_grads[2].astype(jnp.bfloat16), "rep").astype(jnp.float32),
        lax.psum(shard_grads[3].astype(jnp.bfloat16), "rep").astype(jnp.float32),
        lax.psum(shard_grads[4].astype(jnp.bfloat16), "rep").astype(jnp.float32),
        lax.psum(shard_grads[5].astype(jnp.bfloat16), "rep").astype(jnp.float32),
        lax.psum(shard_grads[6].astype(jnp.bfloat16), "rep").astype(jnp.float32),
        lax.psum(shard_grads[7].astype(jnp.bfloat16), "rep").astype(jnp.float32),
        lax.psum(shard_grads[8].astype(jnp.bfloat16), "rep").astype(jnp.float32),
        lax.psum(shard_grads[9].astype(jnp.bfloat16), "rep").astype(jnp.float32),
        lax.psum(shard_grads[10].astype(jnp.bfloat16), "rep").astype(jnp.float32),
        lax.psum(shard_grads[11].astype(jnp.bfloat16), "rep").astype(jnp.float32),
        lax.psum(shard_grads[12].astype(jnp.bfloat16), "rep").astype(jnp.float32),
        lax.psum(shard_grads[13].astype(jnp.bfloat16), "rep").astype(jnp.float32),
        lax.psum(shard_grads[14].astype(jnp.bfloat16), "rep").astype(jnp.float32),
        lax.psum(shard_grads[15].astype(jnp.bfloat16), "rep").astype(jnp.float32),
        lax.psum(grad_gate.astype(jnp.bfloat16), "rep").astype(jnp.float32),
        lax.psum(grad_up.astype(jnp.bfloat16), "rep").astype(jnp.float32),
        lax.psum(grad_down.astype(jnp.bfloat16), "rep").astype(jnp.float32),
    )
    return (
        result.astype(jnp.bfloat16),
        d_source.astype(jnp.bfloat16),
        d_extra.astype(jnp.bfloat16),
        sum_anorm,
        sum_q,
        sum_k,
        sum_v,
        sum_qnorm,
        sum_knorm,
        sum_o,
        sum_apost,
        sum_left,
        sum_right,
        sum_lnorm,
        sum_fnorm,
        sum_gate,
        sum_up,
        sum_down,
        sum_fpost,
        sum_plgate,
        sum_plproj,
        sum_plpost,
    )


def solution(mesh):
    placed = (
        P(("rep", "fsdp"), None),
        P(("rep", "fsdp"), None),
        P(("rep", "fsdp"), None),
        P("rep", None),
        P("rep", None),
        P("fsdp"),
        P("fsdp", None),
        P("fsdp", None),
        P("fsdp", None),
        P("fsdp"),
        P("fsdp"),
        P("fsdp", None),
        P("fsdp"),
        P("fsdp", None),
        P("fsdp", None),
        P("fsdp"),
        P("fsdp"),
        P("fsdp", None),
        P("fsdp", None),
        P("fsdp", None),
        P("fsdp"),
        P("fsdp", None),
        P("fsdp", None),
        P("fsdp"),
    )
    return jax.shard_map(
        head_plan if mesh.shape["fsdp"] == HEADS else gather_plan,
        mesh=mesh,
        in_specs=placed,
        out_specs=(
            P(("rep", "fsdp"), None),
            P(("rep", "fsdp"), None),
            P(("rep", "fsdp"), None),
            P("fsdp"),
            P("fsdp", None),
            P("fsdp", None),
            P("fsdp", None),
            P("fsdp"),
            P("fsdp"),
            P("fsdp", None),
            P("fsdp"),
            P("fsdp", None),
            P("fsdp", None),
            P("fsdp"),
            P("fsdp"),
            P("fsdp", None),
            P("fsdp", None),
            P("fsdp", None),
            P("fsdp"),
            P("fsdp", None),
            P("fsdp", None),
            P("fsdp"),
        ),
        check_vma=False,
    )
```

```python
import functools
import math

import jax
import jax.numpy as jnp
from jax import lax
from jax.experimental import pallas as pl
from jax.experimental.pallas import tpu as pltpu
from jax.sharding import PartitionSpec as P

HEADS = 8
KV_HEADS = 2
HEAD_DIM = 256


EPS = 1e-06
ROPE_BASE = 1000000.0
HALF_ROOT = 0.7071067811865476
MASKED = -1e30


def norm_rows(value, gain):
    return value * lax.rsqrt(jnp.mean(value * value, axis=-1, keepdims=True) + EPS) * gain


def norm_back(value, gain, grad):
    unused, pull = jax.vjp(norm_rows, value, gain)
    return pull(grad)


def rotate(value, position):
    half = value.shape[-1] // 2
    freqs = jnp.exp(
        jnp.arange(half, dtype=jnp.float32) * (-2.0 * math.log(ROPE_BASE) / value.shape[-1])
    )
    angle = position[:, None] * freqs[None, :]
    cosine = jnp.cos(angle)[:, None, :]
    sine = jnp.sin(angle)[:, None, :]
    first_half = value[..., :half]
    second_half = value[..., half:]
    return jnp.concatenate(
        [first_half * cosine - second_half * sine, second_half * cosine + first_half * sine],
        axis=-1,
    )


def tree_tables(lengths, parents, total):
    count = lengths.shape[0]
    labels = jnp.arange(count, dtype=jnp.int32)
    ends = jnp.cumsum(lengths)
    starts = ends - lengths
    tokens = jnp.arange(total, dtype=jnp.int32)
    segment = jnp.sum((ends[None, :] <= tokens[:, None]).astype(jnp.int32), axis=1)
    parent_hot = ((parents[:, None] == labels[None, :]) & (labels[:, None] > 0)).astype(jnp.int32)
    identity = (labels[:, None] == labels[None, :]).astype(jnp.int32)
    ancestors = lax.fori_loop(
        0, count, lambda step, held: jnp.minimum(1, identity + jnp.dot(parent_hot, held)), identity
    )
    offset = jnp.dot(ancestors - identity, lengths) - starts
    member = (segment[:, None] == labels[None, :]).astype(jnp.int32)
    reach = jnp.dot(member, ancestors)
    position = jnp.dot(member, offset) + tokens
    return (tokens, member, reach, position)


def outer(left, right):
    return lax.dot_general(
        left, right, (((0,), (0,)), ((), ())), preferred_element_type=jnp.float32
    )


def mul_t(left, right):
    return lax.dot_general(
        left, right, (((1,), (1,)), ((), ())), preferred_element_type=jnp.float32
    )


def gelu_mix(first, second):
    return jax.nn.gelu(first, approximate=True) * second


def mix_back(first, second, grad):
    unused, pull = jax.vjp(gelu_mix, first, second)
    return pull(grad)


MESH = pl.DeviceIdType.MESH
VMEM_BYTES = 48 << 20


def ring_place(index):
    side = lax.rem(index, 2)
    return index // 2 + side * (HEADS - 1 - 2 * (index // 2))


def ring_index(place):
    back = place // (HEADS // 2)
    return (1 - back) * 2 * place + back * (2 * HEADS - 1 - 2 * place)


def ring_ends(place):
    after = {"fsdp": ring_index(lax.rem(place + 1, HEADS))}
    before = {"fsdp": ring_index(lax.rem(place + HEADS - 1, HEADS))}
    return (after, before)


def greet(others):
    barrier = pltpu.get_barrier_semaphore()
    for other in others:
        pl.semaphore_signal(barrier, inc=1, device_id=other, device_id_type=MESH)
    pl.semaphore_wait(barrier, len(others))


def span(start, size):
    return pl.ds(pl.multiple_of(start, size), size)


def neighbours():
    rep = lax.axis_index("rep")
    chip = rep // 2
    core = lax.rem(rep, 2)
    return (chip, core, {"rep": 2 * chip + 1 - core}, {"rep": 2 * (1 - chip) + core})


def remote(source, target, sems, number, device):
    copy = pltpu.make_async_remote_copy(
        source,
        target,
        sems[0].at[number],
        sems[1].at[number],
        device_id=device,
        device_id_type=MESH,
    )
    copy.start()
    return copy


class Ring:
    def __init__(self, place, ends, lanes, sems, own, there):
        self.place, self.ends, self.lanes, self.sems = place, ends, lanes, sems
        self.own, self.there = own, there
        self.copies = []

    def owner(self, step, lane):
        ahead = step if lane % 2 else HEADS - step
        return ring_index(lax.rem(self.place + ahead, HEADS))

    def send(self, step):
        for lane in range(self.lanes):
            number = step * self.lanes + lane
            target = self.there(self.owner(step, lane), lane)
            if step:
                self.copies[number - self.lanes].wait_recv()
            source = target if step else self.own(lane)
            self.copies.append(remote(source, target, self.sems, number, self.ends[lane % 2]))

    def arrive(self, step):
        for lane in range(self.lanes):
            self.copies[(step - 1) * self.lanes + lane].wait_recv()

    def sent(self):
        for copy in self.copies:
            copy.wait_send()


class Mirror:
    def __init__(self, count, sems):
        unused_chip, unused_core, self.sibling, self.across = neighbours()
        self.count, self.sems = count, sems
        self.copies = [None] * (3 * count)

    def give(self, number, ref):
        self.copies[number] = remote(ref, ref, self.sems, number, self.sibling)
        self.copies[self.count + number] = remote(
            ref, ref, self.sems, self.count + number, self.across
        )

    def relay(self, number, ref):
        self.copies[self.count + number].wait_recv()
        self.copies[2 * self.count + number] = remote(
            ref, ref, self.sems, 2 * self.count + number, self.sibling
        )

    def finish(self):
        for number, copy in enumerate(self.copies):
            if number // self.count != 1:
                copy.wait_recv()
            copy.wait_send()


RING_STEPS = HEADS - 1
QUARTERS = 4


def start_kernel(
    hidden_ref,
    gains_ref,
    q_ref,
    kv_ref,
    small_ref,
    plproj_ref,
    hidden_all,
    gains_all,
    q_head,
    kv_all,
    small_all,
    plproj_all,
    local_sems,
    *sems,
):
    pairs = [sems[i : i + 2] for i in range(0, len(sems), 2)]
    hidden_sems, gains_sems, q_sems, kv_sems, small_sems, plproj_sems = pairs[:6]
    q_mirror_sems, kv_mirror_sems, small_mirror_sems, plproj_mirror_sems = pairs[6:]
    index = lax.axis_index("fsdp")
    chip, core, sibling, across = neighbours()
    quarter = 2 * chip + core
    other_quarter = 2 * (1 - chip) + core
    place = ring_place(index)
    ends = ring_ends(place)
    others = [lax.rem(index + step, HEADS) for step in range(1, HEADS)]
    greet([{"fsdp": other} for other in others] + [sibling, across])
    rows = hidden_ref.shape[0]
    shard = q_ref.shape[0]
    deep = plproj_ref.shape[0]
    q_rows = shard // QUARTERS
    wide = plproj_ref.shape[1] // QUARTERS

    locals_list = []
    for source, target in (
        (hidden_ref, hidden_all.at[span(index * rows, rows)]),
        (gains_ref, gains_all.at[span(index * gains_ref.shape[0], gains_ref.shape[0])]),
        (
            q_ref.at[:, span(index * HEAD_DIM, HEAD_DIM)],
            q_head.at[span(index * shard, shard)],
        ),
        (kv_ref, kv_all.at[span(index * shard, shard)]),
        (small_ref, small_all.at[span(index * shard, shard)]),
        (plproj_ref, plproj_all.at[span(index * deep, deep)]),
    ):
        copy = pltpu.make_async_copy(source, target, local_sems.at[len(locals_list)])
        copy.start()
        locals_list.append(copy)

    hidden_part = rows // 4
    gains_part = gains_ref.shape[0] // 2
    shard_part = shard // QUARTERS // 2
    wide_part = wide // 2

    def shard_at(ref, part_of):
        return lambda owner, lane: ref.at[
            span(owner * shard + part_of * 2 * shard_part + lane * shard_part, shard_part)
        ]

    def plproj_at(part_of):
        return lambda owner, lane: plproj_all.at[
            span(owner * deep, deep), span(part_of * wide + lane * wide_part, wide_part)
        ]

    hidden = Ring(
        place,
        ends,
        4,
        hidden_sems,
        lambda lane: hidden_ref.at[pl.ds(lane * hidden_part, hidden_part)],
        lambda owner, lane: hidden_all.at[span(owner * rows + lane * hidden_part, hidden_part)],
    )
    gains = Ring(
        place,
        ends,
        2,
        gains_sems,
        lambda lane: gains_ref.at[pl.ds(lane * gains_part, gains_part)],
        lambda owner, lane: gains_all.at[
            span(owner * gains_ref.shape[0] + lane * gains_part, gains_part)
        ],
    )

    def shard_own(ref):
        return lambda lane: ref.at[
            span(quarter * 2 * shard_part + lane * shard_part, shard_part)
        ]

    kv = Ring(place, ends, 2, kv_sems, shard_own(kv_ref), shard_at(kv_all, quarter))
    small = Ring(place, ends, 2, small_sems, shard_own(small_ref), shard_at(small_all, quarter))
    plproj = Ring(
        place,
        ends,
        2,
        plproj_sems,
        lambda lane: plproj_ref.at[:, span(quarter * wide + lane * wide_part, wide_part)],
        plproj_at(quarter),
    )
    mirrored = [
        (kv, Mirror(2 * RING_STEPS, kv_mirror_sems), shard_at(kv_all, other_quarter)),
        (small, Mirror(2 * RING_STEPS, small_mirror_sems), shard_at(small_all, other_quarter)),
        (plproj, Mirror(2 * RING_STEPS, plproj_mirror_sems), plproj_at(other_quarter)),
    ]
    q_mirror = Mirror(HEADS - 1, q_mirror_sems)
    q_copies = []
    q_landing = q_head.at[span(index * shard + quarter * q_rows, q_rows)]
    for step, other in enumerate(others):
        source = q_ref.at[span(quarter * q_rows, q_rows), span(other * HEAD_DIM, HEAD_DIM)]
        q_copies.append(remote(source, q_landing, q_sems, step, {"fsdp": other}))

    def q_at(step, part_of):
        giver = lax.rem(index + HEADS - 1 - step, HEADS)
        return q_head.at[span(giver * shard + part_of * q_rows, q_rows)]

    def pass_on(step):
        for ring, mirror, unused_there in mirrored:
            for lane in range(2):
                mirror.give((step - 1) * 2 + lane, ring.there(ring.owner(step, lane), lane))

    def pass_again(step):
        for ring, mirror, there in mirrored:
            for lane in range(2):
                mirror.relay((step - 1) * 2 + lane, there(ring.owner(step, lane), lane))

    for step in range(RING_STEPS):
        gains.send(step)
        for ring, unused_mirror, unused_there in mirrored:
            ring.send(step)
        hidden.send(step)
        if step >= 1:
            pass_on(step)
        if step >= 2:
            pass_again(step - 1)
        if step == 4:
            for number, copy in enumerate(q_copies):
                copy.wait_recv()
                q_mirror.give(number, q_at(number, quarter))
        if step == 5:
            for number in range(HEADS - 1):
                q_mirror.relay(number, q_at(number, other_quarter))
    for ring, unused_mirror, unused_there in mirrored:
        ring.arrive(RING_STEPS)
    pass_on(RING_STEPS)
    pass_again(RING_STEPS - 1)
    pass_again(RING_STEPS)
    gains.arrive(RING_STEPS)
    hidden.arrive(RING_STEPS)
    for ring, mirror, unused_there in mirrored:
        ring.sent()
        mirror.finish()
    hidden.sent()
    gains.sent()
    for copy in q_copies:
        copy.wait_send()
    q_mirror.finish()
    for copy in locals_list:
        copy.wait()


def start_gather(hidden, gains, q_proj, kv, small, pl_proj, number):
    shard = q_proj.shape[0]
    arrays = (hidden, gains, q_proj, kv, small, pl_proj)

    def grown(item, rows=None, columns=None):
        rows = rows or item.shape[0] * HEADS
        return jax.ShapeDtypeStruct((rows, columns or item.shape[1]), item.dtype)

    counts = [4 * RING_STEPS, 2 * RING_STEPS, RING_STEPS] + [2 * RING_STEPS] * 3
    counts += [3 * RING_STEPS] + [6 * RING_STEPS] * 3
    return pl.pallas_call(
        start_kernel,
        out_shape=[
            grown(hidden),
            grown(gains),
            grown(q_proj, shard * HEADS, HEAD_DIM),
            grown(kv),
            grown(small),
            grown(pl_proj),
        ],
        in_specs=[pl.BlockSpec(memory_space=pl.ANY)] * len(arrays),
        out_specs=[pl.BlockSpec(memory_space=pl.ANY)] * len(arrays),
        scratch_shapes=[pltpu.SemaphoreType.DMA((len(arrays),))]
        + [pltpu.SemaphoreType.DMA((count,)) for count in counts for unused_side in range(2)],
        compiler_params=pltpu.CompilerParams(collective_id=number, has_side_effects=True),
    )(*arrays)


def add_low(left, right):
    return (left.astype(jnp.float32) + right.astype(jnp.float32)).astype(jnp.bfloat16)


class RingSum:
    def __init__(self, place, ends, lanes, sems, held, own):
        self.place, self.ends, self.lanes, self.sems = place, ends, lanes, sems
        self.held, self.own = held, own
        self.copies = []

    def send(self, step):
        for lane in range(self.lanes):
            ahead = step + 1 if lane % 2 else HEADS - 1 - step
            owner = ring_index(lax.rem(self.place + ahead, HEADS))
            number = step * self.lanes + lane
            if step:
                slot = number - self.lanes
                self.copies[slot].wait_recv()
                value = self.held[slot].astype(jnp.float32) + self.own(owner, lane)
            else:
                slot = RING_STEPS * self.lanes + lane
                value = self.own(owner, lane)
            self.held[slot] = value.astype(jnp.bfloat16)
            self.copies.append(
                remote(self.held.at[slot], self.held.at[number], self.sems, number, self.ends[lane % 2])
            )

    def last(self, index, lane):
        number = (RING_STEPS - 1) * self.lanes + lane
        self.copies[number].wait_recv()
        return self.held[number].astype(jnp.float32) + self.own(index, lane)

    def sent(self):
        for copy in self.copies:
            copy.wait_send()


def lane_offset(lane, rows):
    return (lane % 2) * (rows // 2) + (lane // 2) * (rows // 4)


def tile_loop(count, size, body):
    def step(number, carry):
        body(span(number * size, size))
        return carry

    lax.fori_loop(0, count, step, 0)


class Pair:
    def __init__(self, place, step, rows):
        half = rows // 2
        behind = ring_index(lax.rem(place + HEADS - step, HEADS))
        ahead = ring_index(lax.rem(place + step, HEADS))
        self.half = half
        self.rows = (span(behind * rows, half), span(ahead * rows + half, half))

    def read(self, ref, columns=slice(None)):
        return jnp.concatenate([ref[rows, columns] for rows in self.rows], axis=0)

    def write(self, ref, columns, value):
        for side, rows in enumerate(self.rows):
            ref[rows, columns] = value[side * self.half : (side + 1) * self.half]


GELU_ROOT = math.sqrt(2.0 / math.pi)
GELU_CUBE = 0.044715
TILE = 256


def start_loads(pairs, sems):
    copies = []
    for number, (source, target) in enumerate(pairs):
        copy = pltpu.make_async_copy(source, target, sems.at[number])
        copy.start()
        copies.append(copy)
    return copies


def root_of(value):
    return lax.rsqrt(jnp.mean(value * value, axis=1, keepdims=True) + EPS)


def norm_pull(value, gain, grad):
    root = root_of(value)
    gain_grad = jnp.sum(grad * value * root, axis=0, keepdims=True)
    grad = grad * gain
    along = jnp.mean(grad * value, axis=1, keepdims=True)
    return (root * grad - value * (root * root * root * along), gain_grad)


def gelu_parts(value):
    square = value * value
    bent = jnp.tanh(GELU_ROOT * value * (1.0 + GELU_CUBE * square))
    share = 0.5 * (1.0 + bent)
    slope = share + (0.5 * GELU_ROOT) * value * (1.0 - bent * bent) * (
        1.0 + (3.0 * GELU_CUBE) * square
    )
    return (value * share, slope)


def attention_kernel(
    hidden_any,
    q_any,
    kv_any,
    o_any,
    norm_ref,
    gains_ref,
    cosine_ref,
    sine_ref,
    reach_ref,
    member_ref,
    sum_ref,
    normed_any,
    weights_any,
    q_raw_any,
    k_raw_any,
    q_low_any,
    k_low_any,
    v_low_any,
    att_any,
    probs_any,
    hidden,
    o_proj,
    normed,
    weights,
    q_raw,
    k_raw,
    q_low,
    k_low,
    v_low,
    att,
    probs,
    part,
    held,
    load_sems,
    store_sems,
    send_sem,
    recv_sem,
):
    rows, width = sum_ref.shape
    total_rows = rows * HEADS
    half = rows // 2
    index = lax.axis_index("fsdp")
    place = ring_place(index)
    ends = ring_ends(place)
    key_at = (index // (HEADS // KV_HEADS)) * HEAD_DIM
    loads = start_loads(
        (
            (q_any, weights.at[:, pl.ds(0, HEAD_DIM)]),
            (kv_any.at[:, span(key_at, HEAD_DIM)], weights.at[:, pl.ds(HEAD_DIM, HEAD_DIM)]),
            (
                kv_any.at[:, span(key_at + KV_HEADS * HEAD_DIM, HEAD_DIM)],
                weights.at[:, pl.ds(2 * HEAD_DIM, HEAD_DIM)],
            ),
            (hidden_any, hidden),
            (o_any, o_proj),
        ),
        load_sems,
    )
    greet(ends)
    for copy in loads:
        copy.wait()

    def project(tile):
        source = hidden[tile, :].astype(jnp.float32)
        value = low(source * root_of(source) * norm_ref[...])
        normed[tile, :] = value
        raw = dot(value, weights[...])
        cosine, sine = cosine_ref[tile, :], sine_ref[tile, :]
        for side, (raw_ref, low_ref) in enumerate(((q_raw, q_low), (k_raw, k_low))):
            item = raw[:, side * HEAD_DIM : (side + 1) * HEAD_DIM]
            raw_ref[tile, :] = item
            item = item * root_of(item) * gains_ref[side : side + 1, :]
            first, second = item[:, : HEAD_DIM // 2], item[:, HEAD_DIM // 2 :]
            low_ref[tile, :] = low(
                jnp.concatenate(
                    [first * cosine - second * sine, second * cosine + first * sine], axis=1
                )
            )
        v_low[tile, :] = low(raw[:, 2 * HEAD_DIM :])

    tile_loop(total_rows // 128, 128, project)
    stores = start_loads(
        (
            (normed, normed_any),
            (weights, weights_any),
            (q_raw, q_raw_any),
            (k_raw, k_raw_any),
            (q_low, q_low_any),
            (k_low, k_low_any),
            (v_low, v_low_any),
        ),
        store_sems,
    )
    scale = HEAD_DIM ** (-0.5)

    def attend(first_owner, second_owner):
        starts = (first_owner * rows, second_owner * rows + half)
        spans = [span(start, half) for start in starts]

        def read(ref):
            return jnp.concatenate([ref[rows_of, :] for rows_of in spans], axis=0)

        query = lax.broadcasted_iota(jnp.int32, (half, total_rows), 0)
        query = jnp.concatenate([query + start for start in starts], axis=0)
        key = lax.broadcasted_iota(jnp.int32, (rows, total_rows), 1)
        scores = mul_t(read(q_low), k_low[...]) * scale
        seen = (mul_t(read(reach_ref), member_ref[...]) > 0.5) & (key <= query)
        scores = jnp.where(seen, scores, MASKED)
        expo = jnp.exp(scores - jnp.max(scores, axis=1, keepdims=True))
        chance = low(expo / jnp.sum(expo, axis=1, keepdims=True))
        mixed = low(dot(chance, v_low[...]))
        for side, rows_of in enumerate(spans):
            probs[rows_of, :] = chance[side * half : (side + 1) * half]
            att[rows_of, :] = mixed[side * half : (side + 1) * half]
        part[...] = dot(mixed, o_proj[...])

    piece = rows // 4
    sums = RingSum(
        place,
        ends,
        4,
        (send_sem, recv_sem),
        held,
        lambda owner, lane: part[pl.ds(lane_offset(lane, rows), piece), :],
    )
    for step in range(RING_STEPS):
        attend(
            ring_index(lax.rem(place + HEADS - 1 - step, HEADS)),
            ring_index(lax.rem(place + step + 1, HEADS)),
        )
        sums.send(step)
    attend(index, index)
    stores += start_loads(((att, att_any), (probs, probs_any)), store_sems.at[pl.ds(7, 2)])
    for lane in range(4):
        sum_ref[pl.ds(lane_offset(lane, rows), piece), :] = sums.last(index, lane)
    sums.sent()
    for copy in stores:
        copy.wait()


def attention_forward(hidden, q_head, kv_all, o_proj, norm, gains, cosine, sine, reach, member, number):
    total, width = hidden.shape
    rows = total // HEADS
    steps = 4 * RING_STEPS
    near, anywhere = pl.BlockSpec(memory_space=pltpu.VMEM), pl.BlockSpec(memory_space=pl.ANY)
    bf16, f32 = jnp.bfloat16, jnp.float32
    head = (total, HEAD_DIM)
    kept = [
        ((total, width), bf16),
        ((width, 3 * HEAD_DIM), bf16),
        (head, f32),
        (head, f32),
        (head, bf16),
        (head, bf16),
        (head, bf16),
        (head, bf16),
        ((total, total), bf16),
    ]
    return pl.pallas_call(
        attention_kernel,
        out_shape=[jax.ShapeDtypeStruct((rows, width), f32)]
        + [jax.ShapeDtypeStruct(shape, dtype) for shape, dtype in kept],
        in_specs=[anywhere] * 4 + [near] * 6,
        out_specs=[near] + [anywhere] * len(kept),
        scratch_shapes=[pltpu.VMEM((total, width), bf16), pltpu.VMEM(o_proj.shape, bf16)]
        + [pltpu.VMEM(shape, dtype) for shape, dtype in kept]
        + [
            pltpu.VMEM((rows, width), f32),
            pltpu.VMEM((steps + 4, rows // 4, width), bf16),
            pltpu.SemaphoreType.DMA((5,)),
            pltpu.SemaphoreType.DMA((9,)),
            pltpu.SemaphoreType.DMA((steps,)),
            pltpu.SemaphoreType.DMA((steps,)),
        ],
        compiler_params=pltpu.CompilerParams(
            collective_id=number, has_side_effects=True, vmem_limit_bytes=VMEM_BYTES
        ),
    )(hidden, q_head, kv_all, o_proj, norm, gains, cosine, sine, reach, member)


def ffn_kernel(
    own_ref,
    gate_any,
    up_any,
    down_any,
    sum_ref,
    all_ref,
    act_ref,
    slope_ref,
    inner_ref,
    gate,
    up,
    down,
    block,
    inner_block,
    part,
    held,
    load_sems,
    send_sem,
    recv_sem,
    sum_send,
    sum_recv,
):
    rows, width = own_ref.shape
    units = gate.shape[0]
    piece = rows // 4
    index = lax.axis_index("fsdp")
    place = ring_place(index)
    ends = ring_ends(place)
    loads = start_loads(((gate_any, gate), (up_any, up), (down_any, down)), load_sems)
    greet(ends)
    ring = Ring(
        place,
        ends,
        4,
        (send_sem, recv_sem),
        lambda lane: own_ref.at[pl.ds(lane_offset(lane, rows), piece)],
        lambda owner, lane: all_ref.at[span(owner * rows + lane_offset(lane, rows), piece)],
    )

    def own(owner, lane):
        return part[span(owner * rows + lane_offset(lane, rows), piece), :].astype(jnp.float32)

    sums = RingSum(place, ends, 4, (sum_send, sum_recv), held, own)

    def compute(step):
        pair = Pair(place, step, rows)
        block[...] = pair.read(all_ref)

        def into(tile):
            value = mul_t(block[...], gate[tile, :])
            second = mul_t(block[...], up[tile, :])
            act, slope = gelu_parts(value)
            inner = low(act * second)
            inner_block[:, tile] = inner
            pair.write(act_ref, tile, low(act))
            pair.write(slope_ref, tile, low(slope * second))
            pair.write(inner_ref, tile, inner)

        tile_loop(units // TILE, TILE, into)

        def out(tile):
            pair.write(part, tile, low(dot(inner_block[...], down[:, tile])))

        tile_loop(width // (2 * TILE), 2 * TILE, out)

    ring.send(0)
    all_ref[span(index * rows, rows), :] = own_ref[...]
    for copy in loads:
        copy.wait()
    compute(0)
    for step in range(1, HEADS):
        if step < RING_STEPS:
            ring.send(step)
        else:
            ring.arrive(step)
        compute(step)
        sums.send(step - 1)
    for lane in range(4):
        sum_ref[pl.ds(lane_offset(lane, rows), piece), :] = sums.last(index, lane)
    ring.sent()
    sums.sent()


def ffn_forward(own, gate, up, down, number):
    rows, width = own.shape
    units = gate.shape[0]
    near, anywhere = pl.BlockSpec(memory_space=pltpu.VMEM), pl.BlockSpec(memory_space=pl.ANY)
    total = rows * HEADS
    steps = 4 * RING_STEPS
    bf16 = jnp.bfloat16
    inner = jax.ShapeDtypeStruct((total, units), bf16)
    return pl.pallas_call(
        ffn_kernel,
        out_shape=[
            jax.ShapeDtypeStruct((rows, width), jnp.float32),
            jax.ShapeDtypeStruct((total, width), bf16),
            inner,
            inner,
            inner,
        ],
        in_specs=[near] + [anywhere] * 3,
        out_specs=[near] * 5,
        scratch_shapes=[pltpu.VMEM((units, width), bf16)] * 3
        + [
            pltpu.VMEM((rows, width), bf16),
            pltpu.VMEM((rows, units), bf16),
            pltpu.VMEM((total, width), bf16),
            pltpu.VMEM((steps + 4, rows // 4, width), bf16),
            pltpu.SemaphoreType.DMA((3,)),
        ]
        + [pltpu.SemaphoreType.DMA((steps,))] * 4,
        compiler_params=pltpu.CompilerParams(
            collective_id=number, has_side_effects=True, vmem_limit_bytes=VMEM_BYTES
        ),
    )(own, gate, up, down)


def ffn_back_kernel(
    first_ref,
    ffw_ref,
    extra_ref,
    seed_ref,
    gains_ref,
    small_any,
    pl_proj_any,
    all_any,
    act_any,
    slope_any,
    inner_any,
    gate_any,
    up_any,
    down_any,
    sum_ref,
    result_ref,
    d_extra_ref,
    d_second_ref,
    gain_grads,
    down_out,
    gate_out,
    up_out,
    far_down,
    theirs_any,
    gate_sum,
    proj_sum,
    d_all,
    tokens,
    d_up,
    d_gate,
    inner,
    gate,
    up,
    down,
    block,
    inner_block,
    part,
    held,
    turned,
    give,
    keep,
    theirs,
    own_ref,
    pl_gate,
    pl_proj,
    gate_blocks,
    gate_folded,
    gate_far,
    gate_held,
    proj_blocks,
    proj_folded,
    proj_far,
    proj_held,
    load_sems,
    store_sems,
    *sems,
):
    ring_sems, sum_sems, fold_sems, far_sems, gate_sems, proj_sems, pl_fold_sems, pl_far_sems = [
        sems[i : i + 2] for i in range(0, 16, 2)
    ]
    rows, width = first_ref.shape
    units = gate.shape[0]
    piece = rows // 4
    index = lax.axis_index("fsdp")
    place = ring_place(index)
    ends = ring_ends(place)
    unused_chip, core, sibling, across = neighbours()
    per_layer = pl_gate.shape[1]
    (
        load_pl_gate,
        load_pl_proj,
        load_down,
        load_act,
        load_slope,
        load_gate,
        load_up,
        load_inner,
        load_tokens,
    ) = start_loads(
        (
            (small_any.at[:, pl.ds(0, per_layer)], pl_gate),
            (pl_proj_any, pl_proj),
            (down_any, down),
            (act_any, d_up),
            (slope_any, d_gate),
            (gate_any, gate),
            (up_any, up),
            (inner_any, inner),
            (all_any, tokens),
        ),
        load_sems,
    )
    greet(ends + (sibling, across))
    ring = Ring(
        place,
        ends,
        4,
        ring_sems,
        lambda lane: own_ref.at[pl.ds(lane_offset(lane, rows), piece)],
        lambda owner, lane: d_all.at[span(owner * rows + lane_offset(lane, rows), piece)],
    )

    def own(owner, lane):
        return part[span(owner * rows + lane_offset(lane, rows), piece), :].astype(jnp.float32)

    chip = neighbours()[0]
    mine, yours = 2 * chip + core, 2 * (1 - chip) + core

    def block_ring(block_sems, block_held, blocks):
        low_rows = blocks.shape[2] // 2
        return RingSum(
            place,
            ends,
            2,
            block_sems,
            block_held,
            lambda owner, lane: blocks[owner, mine, pl.ds(lane * low_rows, low_rows), :].astype(
                jnp.float32
            ),
        )

    sums = RingSum(place, ends, 4, sum_sems, held, own)
    pl_rings = (
        block_ring(gate_sems, gate_held, gate_blocks),
        block_ring(proj_sems, proj_held, proj_blocks),
    )
    pl_arrays = (
        (gate_blocks, gate_folded, gate_far),
        (proj_blocks, proj_folded, proj_far),
    )
    pl_folds, pl_sends = [], []

    def per_layer_branch():
        def after_ffw(tile):
            value = ffw_ref[tile, :]
            total = first_ref[tile, :] + value * root_of(value) * gains_ref[0:1, :]
            sum_ref[tile, :] = total
            block[tile, :] = low(total)

        tile_loop(rows // 32, 32, after_ffw)
        load_pl_gate.wait()
        load_pl_proj.wait()
        extra = extra_ref[...].astype(jnp.float32)
        act, slope = gelu_parts(dot(block[...], pl_gate[...]))
        mix = low(act * extra)
        d_second_ref[...] = dot(mix, pl_proj[...])

        def back_out(tile):
            value = d_second_ref[tile, :]
            result_ref[tile, :] = low(sum_ref[tile, :] + value * root_of(value) * gains_ref[1:2, :])
            grad, gain_grad = norm_pull(
                value, gains_ref[1:2, :], seed_ref[tile, :].astype(jnp.float32)
            )
            own_ref[tile, :] = low(grad)
            gain_grads[1:2, :] += gain_grad

        tile_loop(rows // 32, 32, back_out)
        d_mix = mul_t(own_ref[...], pl_proj[...])
        d_extra_ref[...] = low(d_mix * act)
        d_pre = low(d_mix * extra * slope)
        turned_mix = mix.T
        deep = proj_blocks.shape[2]
        for step in range(QUARTERS):
            wide = proj_blocks.shape[3]
            value = low(dot(turned_mix, own_ref[:, step * wide : (step + 1) * wide]))
            for owner in range(HEADS):
                proj_blocks[owner, step] = value[owner * deep : (owner + 1) * deep]
        shard = width // HEADS
        for owner in range(HEADS):
            value = low(dot(block[:, owner * shard : (owner + 1) * shard].T, d_pre))
            for step in range(QUARTERS):
                gate_blocks[owner, step] = value[
                    step * (shard // QUARTERS) : (step + 1) * (shard // QUARTERS)
                ]
        d_second_ref[...] = mul_t(d_pre, pl_gate[...])

        def back_ffw(tile):
            grad = seed_ref[tile, :].astype(jnp.float32) + d_second_ref[tile, :]
            d_second_ref[tile, :] = grad
            grad, gain_grad = norm_pull(ffw_ref[tile, :], gains_ref[0:1, :], grad)
            own_ref[tile, :] = low(grad)
            gain_grads[0:1, :] += gain_grad

        tile_loop(rows // 32, 32, back_ffw)

    def pl_fold():
        for number, (blocks, folded, far) in enumerate(pl_arrays):
            for side in range(2):
                pl_folds[2 * number + side].wait_recv()
            for owner in range(HEADS):
                blocks[owner, yours] = add_low(blocks[owner, yours], folded[1 - chip, owner])
            pl_sends.append(remote(blocks.at[:, yours], far, pl_far_sems, number, across))
            for owner in range(HEADS):
                blocks[owner, mine] = add_low(blocks[owner, mine], folded[chip, owner])

    def pl_join():
        for number, (blocks, folded, far) in enumerate(pl_arrays):
            pl_sends[number].wait_recv()
            for owner in range(HEADS):
                blocks[owner, mine] = add_low(blocks[owner, mine], far[owner])

    def compute(step):
        pair = Pair(place, step, rows)
        block[...] = pair.read(d_all)

        def into(tile):
            grad = mul_t(block[...], down[tile, :])
            first = low(grad * pair.read(d_gate, tile).astype(jnp.float32))
            second = low(grad * pair.read(d_up, tile).astype(jnp.float32))
            pair.write(d_gate, tile, first)
            pair.write(d_up, tile, second)
            inner_block[0, :, tile] = first
            inner_block[1, :, tile] = second

        tile_loop(units // TILE, TILE, into)
        if step == 0:
            load_gate.wait()
            load_up.wait()

        def out(tile):
            total = dot(inner_block[0], gate[:, tile]) + dot(inner_block[1], up[:, tile])
            pair.write(part, tile, low(total))

        tile_loop(width // (2 * TILE), 2 * TILE, out)

    half = units // 2
    folds, stores, swaps = [], [], []
    jobs = (
        (inner, d_all, down_out),
        (d_gate, tokens, gate_out),
        (d_up, tokens, up_out),
    )

    def outer_half(number, side, target):
        left, right, unused_out = jobs[number]
        turned[...] = left[:, span(side * half, half)].T

        def tile_step(tile):
            target[:, tile] = low(dot(turned[...], right[:, tile]))

        tile_loop(width // (2 * TILE), 2 * TILE, tile_step)

    def grads_give(number):
        if number:
            folds[number - 1].wait_send()
        outer_half(number, 1 - core, give)
        folds.append(remote(give, theirs_any.at[number], fold_sems, number, sibling))

    def grads_keep(number):
        if number > 1:
            stores[number - 1].wait()
        outer_half(number, core, keep)
        folds[number].wait_recv()
        load = pltpu.make_async_copy(theirs_any.at[number], theirs, load_sems.at[9])
        load.start()
        load.wait()

        def add(tile):
            keep[tile, :] = add_low(keep[tile, :], theirs[tile, :])

        tile_loop(half // 64, 64, add)
        store = pltpu.make_async_copy(keep, jobs[number][2], store_sems.at[number])
        store.start()
        stores.append(store)
        if not number:
            store.wait()
            swaps.append(remote(down_out, far_down, far_sems, 0, across))

    gain_grads[...] = jnp.zeros_like(gain_grads)
    per_layer_branch()
    ring.send(0)
    for number, (blocks, folded, unused_far) in enumerate(pl_arrays):
        for side in range(2):
            pl_folds.append(
                remote(
                    blocks.at[:, 2 * side + 1 - core],
                    folded.at[side],
                    pl_fold_sems,
                    2 * number + side,
                    sibling,
                )
            )
    d_all[span(index * rows, rows), :] = own_ref[...]
    for copy in (load_down, load_act, load_slope):
        copy.wait()
    compute(0)
    for step in range(1, HEADS):
        if step < RING_STEPS:
            ring.send(step)
        else:
            ring.arrive(step)
        if step >= RING_STEPS - 1:
            sums.send(step - RING_STEPS + 1)
        compute(step)
        if step == 2:
            pl_fold()
        if step == 4:
            pl_join()
    load_inner.wait()
    load_tokens.wait()
    for step in range(RING_STEPS):
        if step >= 2:
            sums.send(step)
        for item in pl_rings:
            item.send(step)
        if step < 6:
            if step % 2:
                grads_keep(step // 2)
            else:
                grads_give(step // 2)
    for lane in range(4):
        sum_ref[pl.ds(lane_offset(lane, rows), piece), :] = sums.last(index, lane)
    for item, target in zip(pl_rings, (gate_sum, proj_sum)):
        low_rows = target.shape[0] // 2
        for lane in range(2):
            target[pl.ds(lane * low_rows, low_rows), :] = low(item.last(index, lane))
    for item in (ring, sums) + pl_rings:
        item.sent()
    for copy in pl_folds + pl_sends:
        copy.wait_send()
    folds[-1].wait_send()
    stores[-1].wait()
    swaps[0].wait()


def ffn_back(local, gains, small, pl_proj, arrays, weights, number):
    rows, width = local[0].shape
    units = weights[0].shape[0]
    near, anywhere = pl.BlockSpec(memory_space=pltpu.VMEM), pl.BlockSpec(memory_space=pl.ANY)
    total = rows * HEADS
    steps = 4 * RING_STEPS
    bf16, f32 = jnp.bfloat16, jnp.float32
    low_steps = 2 * RING_STEPS
    counts = [steps, steps, 3, 1, low_steps, low_steps, 4, 2]
    half = (units // 2, width)
    deep, per_layer = pl_proj.shape[0] // HEADS, local[2].shape[1]
    gate_block = (width // HEADS // QUARTERS, per_layer)
    proj_block = (deep, width // QUARTERS)

    def block_scratch(shape):
        return [
            pltpu.VMEM((HEADS, QUARTERS) + shape, bf16),
            pltpu.VMEM((2, HEADS) + shape, bf16),
            pltpu.VMEM((HEADS,) + shape, bf16),
            pltpu.VMEM((low_steps + 2, shape[0] // 2, shape[1]), bf16),
        ]

    return pl.pallas_call(
        ffn_back_kernel,
        out_shape=[
            jax.ShapeDtypeStruct((rows, width), f32),
            jax.ShapeDtypeStruct((rows, width), bf16),
            jax.ShapeDtypeStruct((rows, per_layer), bf16),
            jax.ShapeDtypeStruct((rows, width), f32),
            jax.ShapeDtypeStruct(gains.shape, f32),
        ]
        + [jax.ShapeDtypeStruct(half, bf16)] * 4
        + [jax.ShapeDtypeStruct((3,) + half, bf16)]
        + [jax.ShapeDtypeStruct(gate_block, bf16), jax.ShapeDtypeStruct(proj_block, bf16)],
        in_specs=[near] * 5 + [anywhere] * 9,
        out_specs=[near] * 5 + [anywhere] * 5 + [near] * 2,
        scratch_shapes=[pltpu.VMEM((total, width), bf16)] * 2
        + [pltpu.VMEM((total, units), bf16)] * 3
        + [pltpu.VMEM((units, width), bf16)] * 3
        + [
            pltpu.VMEM((rows, width), bf16),
            pltpu.VMEM((2, rows, units), bf16),
            pltpu.VMEM((total, width), bf16),
            pltpu.VMEM((steps + 4, rows // 4, width), bf16),
            pltpu.VMEM((units // 2, total), bf16),
            pltpu.VMEM(half, bf16),
            pltpu.VMEM(half, bf16),
            pltpu.VMEM(half, bf16),
            pltpu.VMEM((rows, width), bf16),
            pltpu.VMEM((width, per_layer), bf16),
            pltpu.VMEM(pl_proj.shape, bf16),
        ]
        + block_scratch(gate_block)
        + block_scratch(proj_block)
        + [pltpu.SemaphoreType.DMA((10,)), pltpu.SemaphoreType.DMA((3,))]
        + [pltpu.SemaphoreType.DMA((count,)) for count in counts for unused_side in range(2)],
        compiler_params=pltpu.CompilerParams(
            collective_id=number, has_side_effects=True, vmem_limit_bytes=58 << 20
        ),
    )(*local, gains, small, pl_proj, *arrays, *weights)


def head_back(grad, raw, gain, cosine, sine):
    half = raw.shape[1] // 2
    first, second = grad[:, :half], grad[:, half:]
    turned = jnp.concatenate(
        [first * cosine + second * sine, second * cosine - first * sine], axis=1
    )
    root = lax.rsqrt(jnp.mean(raw * raw, axis=1, keepdims=True) + EPS)
    gain_grad = jnp.sum(turned * raw * root, axis=0, keepdims=True)
    turned = turned * gain
    along = jnp.mean(turned * raw, axis=1, keepdims=True)
    return (root * turned - raw * (root * root * root * along), gain_grad)


def attention_back_kernel(
    own_ref,
    o_any,
    q_any,
    k_any,
    v_any,
    att_any,
    probs_any,
    normed_any,
    weights_any,
    q_raw_any,
    k_raw_any,
    cosine_any,
    sine_any,
    laurel_any,
    gains_ref,
    pl_gate_ref,
    pl_proj_ref,
    own_down,
    far_down,
    own_gate,
    own_up,
    sum_ref,
    owned_ref,
    early_ref,
    pl_proj_all,
    gain_grads,
    total_down,
    total_gate,
    total_up,
    far_gate,
    far_up,
    o_proj,
    q_low,
    k_low,
    v_low,
    att,
    probs,
    normed,
    weights,
    q_raw,
    k_raw,
    cosine,
    sine,
    d_all,
    block,
    att_block,
    q_block,
    dq_block,
    d_q,
    d_k,
    d_v,
    d_qkv,
    turned,
    part,
    held,
    blocks,
    folded,
    far,
    near_sum,
    key_held,
    o_grad,
    o_folded,
    o_far,
    sum_own,
    sum_far,
    load_sems,
    final_sems,
    *sems,
):
    pairs = [sems[i : i + 2] for i in range(0, len(sems), 2)]
    ring_sems, sum_sems, fold_sems, far_sems, swap_sems, key_sems = pairs[:6]
    mirror_sems, early_sems, o_fold_sems, o_far_sems, cross_sems, total_sems, proj_sems = pairs[6:]
    rows, width = own_ref.shape
    total_rows = rows * HEADS
    half = rows // 2
    piece = rows // 4
    index = lax.axis_index("fsdp")
    chip, core, sibling, across = neighbours()
    place = ring_place(index)
    ends = ring_ends(place)
    others = [lax.rem(index + step, HEADS) for step in range(1, HEADS)]
    quarter = 2 * chip + core
    quarter_rows = blocks.shape[2]
    own_rows = span(quarter * quarter_rows, quarter_rows)
    other_rows = span((2 * (1 - chip) + core) * quarter_rows, quarter_rows)
    groups = HEADS // KV_HEADS
    scale = HEAD_DIM ** (-0.5)
    head_columns = 3 * HEAD_DIM
    loads = start_loads(
        (
            (o_any, o_proj),
            (q_any, q_low),
            (k_any, k_low),
            (v_any, v_low),
            (att_any, att),
            (probs_any, probs),
            (q_raw_any, q_raw),
            (k_raw_any, k_raw),
            (cosine_any, cosine),
            (sine_any, sine),
            (weights_any, weights),
            (normed_any, normed),
            (laurel_any, blocks.at[:, :, :, pl.ds(head_columns, laurel_any.shape[3])]),
        ),
        load_sems,
    )
    greet([{"fsdp": other} for other in others] + [sibling, across])
    early_rows = far_up.shape[0] // 4
    late_rows = far_up.shape[0] - early_rows
    crossings = [
        remote(own_gate, far_gate, cross_sems, 0, across),
        remote(
            own_up.at[pl.ds(0, early_rows)], far_up.at[pl.ds(0, early_rows)], cross_sems, 1, across
        ),
    ]
    ring = Ring(
        place,
        ends,
        4,
        ring_sems,
        lambda lane: own_ref.at[pl.ds(lane_offset(lane, rows), piece)],
        lambda owner, lane: d_all.at[span(owner * rows + lane_offset(lane, rows), piece)],
    )
    sums = RingSum(
        place,
        ends,
        4,
        sum_sems,
        held,
        lambda owner, lane: part[pl.ds(lane_offset(lane, rows), piece), :],
    )
    key_tiles = total_rows // TILE

    def compute(step):
        pair = Pair(place, step, rows)
        block[...] = pair.read(d_all)
        d_att = low(mul_t(block[...], o_proj[...]))
        att_block[...] = d_att
        q_block[...] = pair.read(q_low)
        delta = jnp.sum(
            d_att.astype(jnp.float32) * pair.read(att).astype(jnp.float32), axis=1, keepdims=True
        )
        dq_block[...] = jnp.zeros_like(dq_block)

        def keys(tile):
            chance = pair.read(probs, tile)
            d_chance = mul_t(att_block[...], v_low[tile, :])
            d_score = low(chance.astype(jnp.float32) * (d_chance - delta) * scale)
            dq_block[...] += dot(d_score, k_low[tile, :])
            d_k[tile, :] += dot(d_score.T, q_block[...])
            d_v[tile, :] += dot(chance.T, att_block[...])

        tile_loop(key_tiles, TILE, keys)
        pair.write(d_q, slice(None), dq_block[...])

    finals = (
        (own_down, far_down, total_down),
        (own_gate, far_gate, total_gate),
        (own_up, far_up, total_up),
    )
    final_loads, final_sends, final_stores = [], [], []
    half_units = far_up.shape[0]

    def load_final(number):
        if number:
            final_sends[number - 1].wait_send()
            final_stores[number - 1].wait()
        for side, (ref, target) in enumerate(zip(finals[number], (sum_own, sum_far))):
            copy = pltpu.make_async_copy(ref, target, final_sems.at[side])
            copy.start()
            final_loads.append(copy)

    def add_final(number):
        for copy in final_loads[2 * number :]:
            copy.wait()

        def add(tile):
            sum_own[tile, :] = add_low(sum_own[tile, :], sum_far[tile, :])

        tile_loop(half_units // 64, 64, add)
        target = finals[number][2].at[span(core * half_units, half_units)]
        final_sends.append(remote(sum_own, target, total_sems, number, sibling))
        store = pltpu.make_async_copy(sum_own, target, final_sems.at[2])
        store.start()
        final_stores.append(store)

    d_k[...] = jnp.zeros_like(d_k)
    d_v[...] = jnp.zeros_like(d_v)
    gain_grads[...] = jnp.zeros_like(gain_grads)
    ring.send(0)
    d_all[span(index * rows, rows), :] = own_ref[...]
    for copy in loads[:6]:
        copy.wait()
    compute(0)
    for step in range(1, HEADS):
        if step < RING_STEPS:
            ring.send(step)
        else:
            ring.arrive(step)
        compute(step)
        if step == 2:
            load_final(0)
        if step == 4:
            add_final(0)
    for copy in loads[6:]:
        copy.wait()

    def raw_tile(tile):
        for side, (grad, raw) in enumerate(((d_q, q_raw), (d_k, k_raw))):
            value, gain_grad = head_back(
                grad[tile, :],
                raw[tile, :],
                gains_ref[side : side + 1, :],
                cosine[tile, :],
                sine[tile, :],
            )
            d_qkv[tile, side * HEAD_DIM : (side + 1) * HEAD_DIM] = low(value)
            gain_grads[side : side + 1, :] += gain_grad
        d_qkv[tile, 2 * HEAD_DIM :] = low(d_v[tile, :])

    tile_loop(total_rows // 128, 128, raw_tile)

    def owner_at(step, way):
        return ring_index(lax.rem(place + (step + 1 if way else HEADS - 1 - step), HEADS))

    def part_of(step):
        tops = [
            d_qkv[span(owner_at(step, way) * rows + way * half, half), :] for way in range(2)
        ]
        part[...] = mul_t(jnp.concatenate(tops, axis=0), weights[...])

    def head_grads(number, carry):
        turned[...] = normed[:, span(number * TILE, TILE)].T
        value = low(dot(turned[...], d_qkv[...]))
        for step in range(QUARTERS):
            blocks[number, step, :, :head_columns] = value[
                step * quarter_rows : (step + 1) * quarter_rows
            ]
        return carry

    def o_tile(tile):
        value = low(dot(turned[...], d_all[:, tile]))
        for step in range(QUARTERS):
            o_grad[step, :, tile] = value[step * quarter_rows : (step + 1) * quarter_rows]

    part_of(0)
    sums.send(0)
    lax.fori_loop(0, width // TILE, head_grads, 0)
    folds, o_folds, across_sends, swaps, key_swaps = [], [], [], [], []
    for side in range(2):
        folds.append(
            remote(blocks.at[:, 2 * side + 1 - core], folded.at[side], fold_sems, side, sibling)
        )
    part_of(1)
    sums.send(1)
    turned[...] = att[...].T
    tile_loop(width // (2 * TILE), 2 * TILE, o_tile)
    for side in range(2):
        o_folds.append(
            remote(o_grad.at[2 * side + 1 - core], o_folded.at[side], o_fold_sems, side, sibling)
        )
    mirror, early, pl_mirror = Mirror(1, mirror_sems), Mirror(1, early_sems), Mirror(1, proj_sems)
    wide = pl_proj_ref.shape[1]
    own_columns = span(quarter * wide, wide)
    other_columns = span((2 * (1 - chip) + core) * wide, wide)
    rest = blocks.shape[3] - HEAD_DIM
    q_columns = HEADS * HEAD_DIM
    mine, yours = 2 * chip + core, 2 * (1 - chip) + core

    def fold_step():
        for side in range(2):
            folds[side].wait_recv()
            o_folds[side].wait_recv()
        for number in range(HEADS):
            blocks[number, yours] = add_low(blocks[number, yours], folded[1 - chip, number])
        across_sends.append(remote(blocks.at[:, yours], far, far_sems, 0, across))
        o_grad[yours] = add_low(o_grad[yours], o_folded[1 - chip])
        across_sends.append(remote(o_grad.at[yours], o_far, o_far_sems, 0, across))
        crossings.append(
            remote(
                own_up.at[pl.ds(early_rows, late_rows)],
                far_up.at[pl.ds(early_rows, late_rows)],
                cross_sems,
                2,
                across,
            )
        )
        for number in range(HEADS):
            blocks[number, mine] = add_low(blocks[number, mine], folded[chip, number])
        o_grad[mine] = add_low(o_grad[mine], o_folded[chip])

    def swap_step():
        across_sends[0].wait_recv()
        for number in range(HEADS):
            near_sum[number] = add_low(blocks[number, mine], far[number])
        here = span(index * HEAD_DIM, HEAD_DIM)
        for step, other in enumerate(others):
            swaps.append(
                remote(
                    near_sum.at[other, :, pl.ds(0, HEAD_DIM)],
                    owned_ref.at[own_rows, here],
                    swap_sems,
                    step,
                    {"fsdp": other},
                )
            )
            key_swaps.append(
                remote(
                    near_sum.at[other, :, pl.ds(HEAD_DIM, rest)],
                    key_held.at[index],
                    key_sems,
                    step,
                    {"fsdp": other},
                )
            )
        owned_ref[own_rows, here] = near_sum[index, :, :HEAD_DIM]
        key_held[index] = near_sum[index, :, HEAD_DIM:]
        across_sends[1].wait_recv()
        early_ref[own_rows, :width] = add_low(o_grad[mine], o_far[...])
        early_ref[own_rows, width:] = pl_gate_ref[...]
        early.give(0, early_ref.at[own_rows])
        pl_proj_all[:, own_columns] = pl_proj_ref[...]
        pl_mirror.give(0, pl_proj_all.at[:, own_columns])

    for step in range(2, RING_STEPS):
        part_of(step)
        sums.send(step)
        if step == 2:
            fold_step()
        if step == 3:
            crossings[0].wait_recv()
            load_final(1)
        if step == 4:
            swap_step()
        if step == 5:
            add_final(1)
        if step == 6:
            early.relay(0, early_ref.at[other_rows])
            pl_mirror.relay(0, pl_proj_all.at[:, other_columns])
    part[...] = mul_t(d_qkv[span(index * rows, rows), :], weights[...])
    for lane in range(4):
        sum_ref[pl.ds(lane_offset(lane, rows), piece), :] = sums.last(index, lane)
    for copy in swaps + key_swaps:
        copy.wait_recv()
    for head in range(KV_HEADS):
        total = key_held[head * groups].astype(jnp.float32)
        for step in range(1, groups):
            total = total + key_held[head * groups + step].astype(jnp.float32)
        total = low(total)
        for side in range(2):
            base = q_columns + (side * KV_HEADS + head) * HEAD_DIM
            owned_ref[own_rows, pl.ds(base, HEAD_DIM)] = total[
                :, side * HEAD_DIM : (side + 1) * HEAD_DIM
            ]
    extra = key_held[0, :, 2 * HEAD_DIM :].astype(jnp.float32)
    for step in range(1, HEADS):
        extra = extra + key_held[step, :, 2 * HEAD_DIM :].astype(jnp.float32)
    base = q_columns + 2 * KV_HEADS * HEAD_DIM
    owned_ref[own_rows, pl.ds(base, rest - 2 * HEAD_DIM)] = low(extra)
    mirror.give(0, owned_ref.at[own_rows])
    crossings[1].wait_recv()
    crossings[2].wait_recv()
    load_final(2)
    mirror.relay(0, owned_ref.at[other_rows])
    add_final(2)
    mirror.finish()
    early.finish()
    pl_mirror.finish()
    ring.sent()
    sums.sent()
    for copy in folds + o_folds + across_sends + swaps + key_swaps + crossings:
        copy.wait_send()
    final_sends[2].wait_send()
    final_stores[2].wait()
    for copy in final_sends:
        copy.wait_recv()


def attention_back(own, arrays, laurel, gains, pl_sums, chip_grads, far_down, number):
    rows, width = own.shape
    total = rows * HEADS
    shard = width // HEADS
    quarter = shard // QUARTERS
    steps = 4 * RING_STEPS
    columns = 3 * HEAD_DIM + laurel.shape[1]
    laurel = laurel.reshape(HEADS, QUARTERS, quarter, -1)
    half = chip_grads[0].shape
    near, anywhere = pl.BlockSpec(memory_space=pltpu.VMEM), pl.BlockSpec(memory_space=pl.ANY)
    bf16, f32 = jnp.bfloat16, jnp.float32
    owned = (HEADS + 2 * KV_HEADS) * HEAD_DIM + laurel.shape[3]
    counts = [steps, steps, 2, 1, HEADS - 1, HEADS - 1, 3, 3, 2, 1, 3, 3, 3]
    pl_gate, pl_proj = pl_sums
    down, gate, up = chip_grads
    whole = jax.ShapeDtypeStruct((2 * half[0], half[1]), bf16)
    part = jax.ShapeDtypeStruct(half, bf16)
    return pl.pallas_call(
        attention_back_kernel,
        out_shape=[
            jax.ShapeDtypeStruct((rows, width), f32),
            jax.ShapeDtypeStruct((shard, owned), bf16),
            jax.ShapeDtypeStruct((shard, width + pl_gate.shape[1]), bf16),
            jax.ShapeDtypeStruct((pl_proj.shape[0], width), bf16),
            jax.ShapeDtypeStruct(gains.shape, f32),
            whole,
            whole,
            whole,
            part,
            part,
        ],
        in_specs=[near] + [anywhere] * (len(arrays) + 1) + [near] * 3 + [anywhere] * 4,
        out_specs=[near] * 5 + [anywhere] * 5,
        scratch_shapes=[pltpu.VMEM(item.shape, item.dtype) for item in arrays]
        + [
            pltpu.VMEM((total, width), bf16),
            pltpu.VMEM((rows, width), bf16),
            pltpu.VMEM((rows, HEAD_DIM), bf16),
            pltpu.VMEM((rows, HEAD_DIM), bf16),
            pltpu.VMEM((rows, HEAD_DIM), f32),
            pltpu.VMEM((total, HEAD_DIM), f32),
            pltpu.VMEM((total, HEAD_DIM), f32),
            pltpu.VMEM((total, HEAD_DIM), f32),
            pltpu.VMEM((total, 3 * HEAD_DIM), bf16),
            pltpu.VMEM((HEAD_DIM, total), bf16),
            pltpu.VMEM((rows, width), f32),
            pltpu.VMEM((steps + 4, rows // 4, width), bf16),
            pltpu.VMEM((HEADS, QUARTERS, quarter, columns), bf16),
            pltpu.VMEM((2, HEADS, quarter, columns), bf16),
            pltpu.VMEM((HEADS, quarter, columns), bf16),
            pltpu.VMEM((HEADS, quarter, columns), bf16),
            pltpu.VMEM((HEADS, quarter, columns - HEAD_DIM), bf16),
            pltpu.VMEM((QUARTERS, quarter, width), bf16),
            pltpu.VMEM((2, quarter, width), bf16),
            pltpu.VMEM((quarter, width), bf16),
            pltpu.VMEM(half, bf16),
            pltpu.VMEM(half, bf16),
            pltpu.SemaphoreType.DMA((len(arrays) + 1,)),
            pltpu.SemaphoreType.DMA((3,)),
        ]
        + [pltpu.SemaphoreType.DMA((count,)) for count in counts for unused_side in range(2)],
        compiler_params=pltpu.CompilerParams(
            collective_id=number, has_side_effects=True, vmem_limit_bytes=56 << 20
        ),
    )(own, *arrays, laurel, gains, pl_gate, pl_proj, down, far_down, gate, up)


def gains_kernel(parts_ref, sum_ref, landed, totals, send_sem, recv_sem, rep_send, rep_recv):
    index = lax.axis_index("fsdp")
    rep = lax.axis_index("rep")
    others = [lax.rem(index + step, HEADS) for step in range(1, HEADS)]
    twins = [lax.rem(rep + step, QUARTERS) for step in range(1, QUARTERS)]
    greet([{"fsdp": other} for other in others] + [{"rep": twin} for twin in twins])
    sends = [
        remote(parts_ref.at[other], landed.at[index], (send_sem, recv_sem), step, {"fsdp": other})
        for step, other in enumerate(others)
    ]
    landed[index] = parts_ref[index]
    for copy in sends:
        copy.wait_recv()
    total = landed[0]
    for step in range(1, HEADS):
        total = total + landed[step]
    totals[rep] = total
    twin_sends = [
        remote(totals.at[rep], totals.at[rep], (rep_send, rep_recv), step, {"rep": twin})
        for step, twin in enumerate(twins)
    ]
    for copy in twin_sends:
        copy.wait_recv()
    total = totals[0]
    for step in range(1, QUARTERS):
        total = total + totals[step]
    sum_ref[...] = total
    for copy in sends + twin_sends:
        copy.wait_send()


def gains_sum(parts, number):
    near = pl.BlockSpec(memory_space=pltpu.VMEM)
    return pl.pallas_call(
        gains_kernel,
        out_shape=jax.ShapeDtypeStruct(parts.shape[1:], parts.dtype),
        in_specs=[near],
        out_specs=near,
        scratch_shapes=[
            pltpu.VMEM(parts.shape, parts.dtype),
            pltpu.VMEM((QUARTERS,) + parts.shape[1:], parts.dtype),
        ]
        + [pltpu.SemaphoreType.DMA((HEADS - 1,))] * 2
        + [pltpu.SemaphoreType.DMA((QUARTERS - 1,))] * 2,
        compiler_params=pltpu.CompilerParams(collective_id=number, has_side_effects=True),
    )(parts)


def dot(left, right):
    return jnp.dot(left, right, preferred_element_type=jnp.float32)


def low(value):
    return value.astype(jnp.bfloat16)


def tree_places(lengths, parents, total):
    count = lengths.shape[0]
    labels = jnp.arange(count, dtype=jnp.int32)
    ends = jnp.sum(jnp.where(labels[:, None] <= labels[None, :], lengths[:, None], 0), axis=0)
    starts = ends - lengths
    tokens = jnp.arange(total, dtype=jnp.int32)
    segment = jnp.sum((ends[None, :] <= tokens[:, None]).astype(jnp.int32), axis=1)
    parent_hot = (parents[:, None] == labels[None, :]) & (labels[:, None] > 0)
    identity = labels[:, None] == labels[None, :]
    reached = parent_hot | identity
    for unused_step in range((count - 1).bit_length()):
        reached = jnp.any(reached[:, :, None] & reached[None, :, :], axis=1)
    offset = jnp.sum(jnp.where(reached & ~identity, lengths[None, :], 0), axis=1) - starts
    member = segment[:, None] == labels[None, :]
    reach = jnp.any(member[:, :, None] & reached[None, :, :], axis=1)
    position = jnp.sum(jnp.where(member, offset[None, :], 0), axis=1) + tokens
    return (tokens, member.astype(jnp.bfloat16), reach.astype(jnp.bfloat16), position)


def head_plan(
    hidden_in,
    layer_input,
    out_grad,
    seg_lengths,
    seg_parents,
    attn_norm,
    q_proj,
    k_proj,
    v_proj,
    q_norm,
    k_norm,
    o_proj,
    attn_post_norm,
    laurel_left,
    laurel_right,
    laurel_norm,
    ffw_norm,
    gate_proj,
    up_proj,
    down_proj,
    ffw_post_norm,
    pl_gate,
    pl_proj,
    pl_post_norm,
):
    index = lax.axis_index("fsdp")
    rows, width = hidden_in.shape
    shard = width // HEADS
    total = rows * HEADS
    rank = laurel_left.shape[1]
    per_layer = pl_gate.shape[1]

    gains = (attn_norm, attn_post_norm, laurel_norm, ffw_norm, ffw_post_norm, pl_post_norm)
    packed = jnp.concatenate(gains + (q_norm, k_norm))
    pad = -packed.shape[0] % (32 * 128)
    packed = jnp.pad(packed, (0, pad)).reshape(-1, 128)
    hidden_all, gains_held, q_head, kv_all, small_all, full_plproj = start_gather(
        hidden_in,
        packed,
        q_proj,
        jnp.concatenate([k_proj, v_proj], axis=1),
        jnp.concatenate([pl_gate, laurel_left, laurel_right], axis=1),
        pl_proj,
        0,
    )
    all_gains = gains_held.reshape(HEADS, -1).astype(jnp.float32)
    wide_gains = [all_gains[:, i * shard : (i + 1) * shard].reshape(-1) for i in range(len(gains))]
    gain_anorm, gain_apost, gain_lnorm, gain_fnorm, gain_fpost, gain_plpost = wide_gains
    at = len(gains) * shard
    piece = HEAD_DIM // HEADS
    gain_qnorm = all_gains[:, at : at + piece].reshape(-1)
    gain_knorm = all_gains[:, at + piece : at + 2 * piece].reshape(-1)

    full_left = small_all[:, per_layer : per_layer + rank]
    full_right = small_all[:, per_layer + rank :]

    tokens, member, reach, position = tree_places(seg_lengths[0], seg_parents[0], total)
    depth = position.astype(jnp.float32)
    half = HEAD_DIM // 2
    freqs = jnp.exp(
        jnp.arange(half, dtype=jnp.float32) * (-2.0 * math.log(ROPE_BASE) / HEAD_DIM)
    )
    angle = depth[:, None] * freqs[None, :]
    cosine, sine = jnp.cos(angle), jnp.sin(angle)

    def padded(item):
        return jnp.pad(item, ((0, 0), (0, 128 - item.shape[1])))

    head_gain = jnp.stack([gain_qnorm, gain_knorm])
    (
        branch,
        normed_all,
        qkv_head,
        q_raw,
        k_raw,
        q_low,
        k_low,
        v_low,
        attended_low,
        probs_low,
    ) = attention_forward(
        hidden_all,
        q_head,
        kv_all,
        o_proj,
        gain_anorm[None, :],
        head_gain,
        cosine,
        sine,
        padded(reach),
        padded(member),
        6,
    )

    source = hidden_in.astype(jnp.float32)
    normed = norm_rows(source, gain_anorm)
    normed_low = low(normed)
    left_low = low(dot(normed_low, full_left))
    low_rank = mul_t(left_low, full_right)
    first_sum = (
        source + norm_rows(branch, gain_apost) + normed + norm_rows(low_rank, gain_lnorm)
    ) * HALF_ROOT
    ffw_low = low(norm_rows(first_sum, gain_fnorm))

    ffw_out, ffw_all, act, slope, inner_low = ffn_forward(
        ffw_low, gate_proj, up_proj, down_proj, 7
    )
    d_ffwin, result, d_extra, d_second, ffw_gains, *rest = ffn_back(
        (first_sum, ffw_out, layer_input, out_grad),
        jnp.stack([gain_fpost, gain_plpost]),
        small_all,
        full_plproj,
        (ffw_all, act, slope, inner_low),
        (gate_proj, up_proj, down_proj),
        9,
    )
    grad_fpost, grad_plpost = ffw_gains
    chip_grads, far_down, pl_sums = rest[:3], rest[3], rest[5:]

    d_first_part, grad_fnorm = norm_back(first_sum, gain_fnorm, d_ffwin)
    d_scaled = (d_second + d_first_part) * HALF_ROOT
    d_branch, grad_apost = norm_back(branch, gain_apost, d_scaled)
    d_lowrank, grad_lnorm = norm_back(low_rank, gain_lnorm, d_scaled)
    d_lowrank_low = low(d_lowrank)
    grad_right = outer(d_lowrank_low, left_low)
    d_left_low = low(dot(d_lowrank_low, full_right))
    grad_left = outer(normed_low, d_left_low)

    d_normed_sum, owned, early, sum_plproj, head_gains, *totals = attention_back(
        low(d_branch),
        (
            o_proj,
            q_low,
            k_low,
            v_low,
            attended_low,
            probs_low,
            normed_all,
            qkv_head,
            q_raw,
            k_raw,
            cosine,
            sine,
        ),
        low(jnp.concatenate([grad_left, grad_right], axis=1)),
        head_gain,
        pl_sums,
        chip_grads,
        far_down,
        12,
    )
    grad_qnorm, grad_knorm = head_gains
    sum_down, sum_gate, sum_up = [item.astype(jnp.float32) for item in totals[:3]]
    owned = owned.astype(jnp.float32)
    early = early.astype(jnp.float32)
    key_at = width
    value_at = key_at + KV_HEADS * HEAD_DIM
    left_at = value_at + KV_HEADS * HEAD_DIM
    d_normed = d_scaled + mul_t(d_left_low, full_left) + d_normed_sum
    d_source_part, grad_anorm = norm_back(source, gain_anorm, d_normed)
    d_source = d_scaled + d_source_part

    small_grads = [grad_anorm, grad_apost, grad_lnorm, grad_fnorm, grad_fpost, grad_plpost]
    parts = [item.reshape(HEADS, shard) for item in small_grads]
    parts += [item.reshape(HEADS, piece) for item in (grad_qnorm, grad_knorm)]
    parts = jnp.concatenate(parts, axis=1)
    parts = jnp.pad(parts, ((0, 0), (0, -parts.shape[1] % 1024))).reshape(HEADS, -1, 128)
    small_sums = gains_sum(parts, 13).reshape(-1)
    own = [small_sums[i * shard : (i + 1) * shard] for i in range(len(small_grads))]
    sum_anorm, sum_apost, sum_lnorm, sum_fnorm, sum_fpost, sum_plpost = own
    sum_qnorm = small_sums[at : at + piece]
    sum_knorm = small_sums[at + piece : at + 2 * piece]
    return (
        result,
        low(d_source),
        d_extra,
        sum_anorm,
        owned[:, :width],
        owned[:, key_at:value_at],
        owned[:, value_at:left_at],
        sum_qnorm,
        sum_knorm,
        early[:, :width],
        sum_apost,
        owned[:, left_at : left_at + rank],
        owned[:, left_at + rank :],
        sum_lnorm,
        sum_fnorm,
        sum_gate,
        sum_up,
        sum_down,
        sum_fpost,
        early[:, width:],
        sum_plproj.astype(jnp.float32),
        sum_plpost,
    )


def gather_plan(
    hidden_in,
    layer_input,
    out_grad,
    seg_lengths,
    seg_parents,
    attn_norm,
    q_proj,
    k_proj,
    v_proj,
    q_norm,
    k_norm,
    o_proj,
    attn_post_norm,
    laurel_left,
    laurel_right,
    laurel_norm,
    ffw_norm,
    gate_proj,
    up_proj,
    down_proj,
    ffw_post_norm,
    pl_gate,
    pl_proj,
    pl_post_norm,
):
    shards = lax.axis_size("fsdp")
    rank_index = lax.axis_index("fsdp")
    rows = hidden_in.shape[0]
    total = rows * shards
    groups = HEADS // KV_HEADS
    scale = HEAD_DIM ** (-0.5)
    tokens, member, reach, position = tree_tables(seg_lengths[0], seg_parents[0], total)
    first_row = rank_index * rows
    my_tokens = first_row + jnp.arange(rows, dtype=jnp.int32)
    my_reach = lax.dynamic_slice_in_dim(reach, first_row, rows, 0)
    my_depth = lax.dynamic_slice_in_dim(position, first_row, rows, 0).astype(jnp.float32)
    seen = (jnp.dot(my_reach, member.T) > 0) & (tokens[None, :] <= my_tokens[:, None])
    (
        full_anorm,
        full_q,
        full_k,
        full_v,
        full_qnorm,
        full_knorm,
        full_o,
        full_apost,
        full_left,
        full_right,
        full_lnorm,
        full_fnorm,
        full_fpost,
        full_plgate,
        full_plproj,
        full_plpost,
    ) = (
        lax.all_gather(attn_norm, "fsdp", axis=0, tiled=True),
        lax.all_gather(q_proj, "fsdp", axis=0, tiled=True),
        lax.all_gather(k_proj, "fsdp", axis=0, tiled=True),
        lax.all_gather(v_proj, "fsdp", axis=0, tiled=True),
        lax.all_gather(q_norm, "fsdp", axis=0, tiled=True),
        lax.all_gather(k_norm, "fsdp", axis=0, tiled=True),
        lax.all_gather(o_proj, "fsdp", axis=0, tiled=True),
        lax.all_gather(attn_post_norm, "fsdp", axis=0, tiled=True),
        lax.all_gather(laurel_left, "fsdp", axis=0, tiled=True),
        lax.all_gather(laurel_right, "fsdp", axis=0, tiled=True),
        lax.all_gather(laurel_norm, "fsdp", axis=0, tiled=True),
        lax.all_gather(ffw_norm, "fsdp", axis=0, tiled=True),
        lax.all_gather(ffw_post_norm, "fsdp", axis=0, tiled=True),
        lax.all_gather(pl_gate, "fsdp", axis=0, tiled=True),
        lax.all_gather(pl_proj, "fsdp", axis=0, tiled=True),
        lax.all_gather(pl_post_norm, "fsdp", axis=0, tiled=True),
    )
    gain_anorm = full_anorm.astype(jnp.float32)
    gain_qnorm = full_qnorm.astype(jnp.float32)
    gain_knorm = full_knorm.astype(jnp.float32)
    gain_apost = full_apost.astype(jnp.float32)
    gain_lnorm = full_lnorm.astype(jnp.float32)
    gain_fnorm = full_fnorm.astype(jnp.float32)
    gain_fpost = full_fpost.astype(jnp.float32)
    gain_plpost = full_plpost.astype(jnp.float32)
    source = hidden_in.astype(jnp.float32)
    extra = layer_input.astype(jnp.float32)
    normed = norm_rows(source, gain_anorm)
    normed_low = normed.astype(jnp.bfloat16)
    q_raw = jnp.dot(normed_low, full_q, preferred_element_type=jnp.float32)
    k_raw = jnp.dot(normed_low, full_k, preferred_element_type=jnp.float32)
    v_raw = jnp.dot(normed_low, full_v, preferred_element_type=jnp.float32)

    def head_path(raw, gain):
        return rotate(norm_rows(raw.reshape(rows, -1, HEAD_DIM), gain), my_depth)

    q_low = head_path(q_raw, gain_qnorm).astype(jnp.bfloat16)
    k_low = head_path(k_raw, gain_knorm).reshape(rows, -1).astype(jnp.bfloat16)
    v_low = v_raw.astype(jnp.bfloat16)
    keys_all, values_all = (
        lax.all_gather(k_low, "fsdp", axis=0, tiled=True),
        lax.all_gather(v_low, "fsdp", axis=0, tiled=True),
    )
    keys_heads = keys_all.reshape(total, KV_HEADS, HEAD_DIM)
    values_heads = values_all.reshape(total, KV_HEADS, HEAD_DIM)
    query_groups = q_low.reshape(rows, KV_HEADS, groups, HEAD_DIM)
    mixed_list = []
    log_list = []
    for head in range(KV_HEADS):
        scores = (
            jnp.einsum(
                "tgd,nd->gtn",
                query_groups[:, head],
                keys_heads[:, head],
                preferred_element_type=jnp.float32,
            )
            * scale
        )
        scores = jnp.where(seen[None], scores, MASKED)
        top = jnp.max(scores, axis=-1, keepdims=True)
        expo = jnp.exp(scores - top)
        sums = jnp.sum(expo, axis=-1, keepdims=True)
        weights = (expo / sums).astype(jnp.bfloat16)
        mixed_list.append(
            jnp.einsum(
                "gtn,nd->tgd", weights, values_heads[:, head], preferred_element_type=jnp.float32
            )
        )
        log_list.append(top[..., 0] + jnp.log(sums[..., 0]))
    attended = jnp.stack(mixed_list, axis=1)
    log_sums = jnp.stack(log_list, axis=0)
    attended_low = attended.reshape(rows, -1).astype(jnp.bfloat16)
    branch = jnp.dot(attended_low, full_o, preferred_element_type=jnp.float32)
    left_low = jnp.dot(normed_low, full_left, preferred_element_type=jnp.float32).astype(
        jnp.bfloat16
    )
    low_rank = mul_t(left_low, full_right)
    first_sum = (
        source + norm_rows(branch, gain_apost) + normed + norm_rows(low_rank, gain_lnorm)
    ) * HALF_ROOT
    ffw_low = norm_rows(first_sum, gain_fnorm).astype(jnp.bfloat16)
    full_gate, full_up, full_down = (
        lax.all_gather(gate_proj, "fsdp", axis=0, tiled=True),
        lax.all_gather(up_proj, "fsdp", axis=0, tiled=True),
        lax.all_gather(down_proj, "fsdp", axis=0, tiled=True),
    )
    gate_val = mul_t(ffw_low, full_gate)
    up_val = mul_t(ffw_low, full_up)
    inner_low = gelu_mix(gate_val, up_val).astype(jnp.bfloat16)
    ffw_out = jnp.dot(inner_low, full_down, preferred_element_type=jnp.float32)
    second_sum = first_sum + norm_rows(ffw_out, gain_fpost)
    second_low = second_sum.astype(jnp.bfloat16)
    pl_pre = jnp.dot(second_low, full_plgate, preferred_element_type=jnp.float32)
    pl_mix = gelu_mix(pl_pre, extra).astype(jnp.bfloat16)
    pl_out = jnp.dot(pl_mix, full_plproj, preferred_element_type=jnp.float32)
    result = second_sum + norm_rows(pl_out, gain_plpost)
    seed = out_grad.astype(jnp.float32)
    d_plout, grad_plpost = norm_back(pl_out, gain_plpost, seed)
    d_plout_low = d_plout.astype(jnp.bfloat16)
    grad_plproj = outer(pl_mix, d_plout_low)
    d_mix = mul_t(d_plout_low, full_plproj)
    d_pre, d_extra = mix_back(pl_pre, extra, d_mix)
    d_pre_low = d_pre.astype(jnp.bfloat16)
    grad_plgate = outer(second_low, d_pre_low)
    d_second = seed + mul_t(d_pre_low, full_plgate)
    d_ffwout, grad_fpost = norm_back(ffw_out, gain_fpost, d_second)
    d_ffw_low = d_ffwout.astype(jnp.bfloat16)
    d_inner = mul_t(d_ffw_low, full_down)
    d_gate, d_up = mix_back(gate_val, up_val, d_inner)
    d_gate_low = d_gate.astype(jnp.bfloat16)
    d_up_low = d_up.astype(jnp.bfloat16)
    d_ffwin = jnp.dot(d_gate_low, full_gate, preferred_element_type=jnp.float32) + jnp.dot(
        d_up_low, full_up, preferred_element_type=jnp.float32
    )
    width = ffw_low.shape[1]
    gate_part = outer(d_gate_low, ffw_low)
    up_part = outer(d_up_low, ffw_low)
    down_part = outer(inner_low, d_ffw_low)
    stacked = lax.psum_scatter(
        jnp.concatenate([gate_part, up_part, down_part], axis=1).astype(jnp.bfloat16),
        "fsdp",
        scatter_dimension=0,
        tiled=True,
    ).astype(jnp.float32)
    grad_gate = stacked[:, :width]
    grad_up = stacked[:, width : 2 * width]
    grad_down = stacked[:, 2 * width :]
    d_first_part, grad_fnorm = norm_back(first_sum, gain_fnorm, d_ffwin)
    d_first = d_second + d_first_part
    d_scaled = d_first * HALF_ROOT
    d_branch, grad_apost = norm_back(branch, gain_apost, d_scaled)
    d_branch_low = d_branch.astype(jnp.bfloat16)
    d_lowrank, grad_lnorm = norm_back(low_rank, gain_lnorm, d_scaled)
    d_lowrank_low = d_lowrank.astype(jnp.bfloat16)
    grad_o = outer(attended_low, d_branch_low)
    d_att_low = mul_t(d_branch_low, full_o).astype(jnp.bfloat16)
    grad_right = outer(d_lowrank_low, left_low)
    d_left_low = jnp.dot(d_lowrank_low, full_right, preferred_element_type=jnp.float32).astype(
        jnp.bfloat16
    )
    grad_left = outer(normed_low, d_left_low)
    d_att_heads = d_att_low.reshape(rows, KV_HEADS, groups, HEAD_DIM)
    delta = jnp.sum(d_att_heads.astype(jnp.float32) * attended, axis=-1).transpose(1, 2, 0)
    block = 512
    count = total // block
    key_blocks = keys_heads.reshape(count, block, KV_HEADS, HEAD_DIM)
    value_blocks = values_heads.reshape(count, block, KV_HEADS, HEAD_DIM)
    seen_blocks = seen.reshape(rows, count, block).transpose(1, 0, 2)

    def key_step(d_query, item):
        keys, values, shown = item
        scores = (
            jnp.einsum("tkgd,nkd->kgtn", query_groups, keys, preferred_element_type=jnp.float32)
            * scale
        )
        scores = jnp.where(shown[None, None], scores, MASKED)
        probs = jnp.exp(scores - log_sums[..., None])
        d_probs = jnp.einsum(
            "tkgd,nkd->kgtn", d_att_heads, values, preferred_element_type=jnp.float32
        )
        d_scores = (probs * (d_probs - delta[..., None]) * scale).astype(jnp.bfloat16)
        d_query = d_query + jnp.einsum(
            "kgtn,nkd->tkgd", d_scores, keys, preferred_element_type=jnp.float32
        )
        d_keys = jnp.einsum(
            "kgtn,tkgd->nkd", d_scores, query_groups, preferred_element_type=jnp.float32
        )
        d_values = jnp.einsum(
            "kgtn,tkgd->nkd",
            probs.astype(jnp.bfloat16),
            d_att_heads,
            preferred_element_type=jnp.float32,
        )
        return (d_query, (d_keys, d_values))

    zero_query = jnp.zeros((rows, KV_HEADS, groups, HEAD_DIM), jnp.float32)
    d_query, (d_key_blocks, d_value_blocks) = lax.scan(
        key_step, zero_query, (key_blocks, value_blocks, seen_blocks)
    )
    my_dkeys, my_dvalues = (
        lax.psum_scatter(
            d_key_blocks.reshape(total, -1).astype(jnp.bfloat16),
            "fsdp",
            scatter_dimension=0,
            tiled=True,
        ).astype(jnp.float32),
        lax.psum_scatter(
            d_value_blocks.reshape(total, -1).astype(jnp.bfloat16),
            "fsdp",
            scatter_dimension=0,
            tiled=True,
        ).astype(jnp.float32),
    )
    unused_q, q_pull = jax.vjp(head_path, q_raw, gain_qnorm)
    d_qraw, grad_qnorm = q_pull(d_query.reshape(rows, HEADS, HEAD_DIM))
    unused_k, k_pull = jax.vjp(head_path, k_raw, gain_knorm)
    d_kraw, grad_knorm = k_pull(my_dkeys.reshape(rows, KV_HEADS, HEAD_DIM))
    d_q_low = d_qraw.astype(jnp.bfloat16)
    d_k_low = d_kraw.astype(jnp.bfloat16)
    d_v_low = my_dvalues.astype(jnp.bfloat16)
    grad_q = outer(normed_low, d_q_low)
    grad_k = outer(normed_low, d_k_low)
    grad_v = outer(normed_low, d_v_low)
    d_normed = (
        d_scaled
        + mul_t(d_q_low, full_q)
        + mul_t(d_k_low, full_k)
        + mul_t(d_v_low, full_v)
        + mul_t(d_left_low, full_left)
    )
    d_source_part, grad_anorm = norm_back(source, gain_anorm, d_normed)
    d_source = d_scaled + d_source_part
    shard_grads = (
        lax.psum_scatter(
            grad_anorm.astype(jnp.bfloat16), "fsdp", scatter_dimension=0, tiled=True
        ).astype(jnp.float32),
        lax.psum_scatter(
            grad_q.astype(jnp.bfloat16), "fsdp", scatter_dimension=0, tiled=True
        ).astype(jnp.float32),
        lax.psum_scatter(
            grad_k.astype(jnp.bfloat16), "fsdp", scatter_dimension=0, tiled=True
        ).astype(jnp.float32),
        lax.psum_scatter(
            grad_v.astype(jnp.bfloat16), "fsdp", scatter_dimension=0, tiled=True
        ).astype(jnp.float32),
        lax.psum_scatter(
            grad_qnorm.astype(jnp.bfloat16), "fsdp", scatter_dimension=0, tiled=True
        ).astype(jnp.float32),
        lax.psum_scatter(
            grad_knorm.astype(jnp.bfloat16), "fsdp", scatter_dimension=0, tiled=True
        ).astype(jnp.float32),
        lax.psum_scatter(
            grad_o.astype(jnp.bfloat16), "fsdp", scatter_dimension=0, tiled=True
        ).astype(jnp.float32),
        lax.psum_scatter(
            grad_apost.astype(jnp.bfloat16), "fsdp", scatter_dimension=0, tiled=True
        ).astype(jnp.float32),
        lax.psum_scatter(
            grad_left.astype(jnp.bfloat16), "fsdp", scatter_dimension=0, tiled=True
        ).astype(jnp.float32),
        lax.psum_scatter(
            grad_right.astype(jnp.bfloat16), "fsdp", scatter_dimension=0, tiled=True
        ).astype(jnp.float32),
        lax.psum_scatter(
            grad_lnorm.astype(jnp.bfloat16), "fsdp", scatter_dimension=0, tiled=True
        ).astype(jnp.float32),
        lax.psum_scatter(
            grad_fnorm.astype(jnp.bfloat16), "fsdp", scatter_dimension=0, tiled=True
        ).astype(jnp.float32),
        lax.psum_scatter(
            grad_fpost.astype(jnp.bfloat16), "fsdp", scatter_dimension=0, tiled=True
        ).astype(jnp.float32),
        lax.psum_scatter(
            grad_plgate.astype(jnp.bfloat16), "fsdp", scatter_dimension=0, tiled=True
        ).astype(jnp.float32),
        lax.psum_scatter(
            grad_plproj.astype(jnp.bfloat16), "fsdp", scatter_dimension=0, tiled=True
        ).astype(jnp.float32),
        lax.psum_scatter(
            grad_plpost.astype(jnp.bfloat16), "fsdp", scatter_dimension=0, tiled=True
        ).astype(jnp.float32),
    )
    (
        sum_anorm,
        sum_q,
        sum_k,
        sum_v,
        sum_qnorm,
        sum_knorm,
        sum_o,
        sum_apost,
        sum_left,
        sum_right,
        sum_lnorm,
        sum_fnorm,
        sum_fpost,
        sum_plgate,
        sum_plproj,
        sum_plpost,
        sum_gate,
        sum_up,
        sum_down,
    ) = (
        lax.psum(shard_grads[0].astype(jnp.bfloat16), "rep").astype(jnp.float32),
        lax.psum(shard_grads[1].astype(jnp.bfloat16), "rep").astype(jnp.float32),
        lax.psum(shard_grads[2].astype(jnp.bfloat16), "rep").astype(jnp.float32),
        lax.psum(shard_grads[3].astype(jnp.bfloat16), "rep").astype(jnp.float32),
        lax.psum(shard_grads[4].astype(jnp.bfloat16), "rep").astype(jnp.float32),
        lax.psum(shard_grads[5].astype(jnp.bfloat16), "rep").astype(jnp.float32),
        lax.psum(shard_grads[6].astype(jnp.bfloat16), "rep").astype(jnp.float32),
        lax.psum(shard_grads[7].astype(jnp.bfloat16), "rep").astype(jnp.float32),
        lax.psum(shard_grads[8].astype(jnp.bfloat16), "rep").astype(jnp.float32),
        lax.psum(shard_grads[9].astype(jnp.bfloat16), "rep").astype(jnp.float32),
        lax.psum(shard_grads[10].astype(jnp.bfloat16), "rep").astype(jnp.float32),
        lax.psum(shard_grads[11].astype(jnp.bfloat16), "rep").astype(jnp.float32),
        lax.psum(shard_grads[12].astype(jnp.bfloat16), "rep").astype(jnp.float32),
        lax.psum(shard_grads[13].astype(jnp.bfloat16), "rep").astype(jnp.float32),
        lax.psum(shard_grads[14].astype(jnp.bfloat16), "rep").astype(jnp.float32),
        lax.psum(shard_grads[15].astype(jnp.bfloat16), "rep").astype(jnp.float32),
        lax.psum(grad_gate.astype(jnp.bfloat16), "rep").astype(jnp.float32),
        lax.psum(grad_up.astype(jnp.bfloat16), "rep").astype(jnp.float32),
        lax.psum(grad_down.astype(jnp.bfloat16), "rep").astype(jnp.float32),
    )
    return (
        result.astype(jnp.bfloat16),
        d_source.astype(jnp.bfloat16),
        d_extra.astype(jnp.bfloat16),
        sum_anorm,
        sum_q,
        sum_k,
        sum_v,
        sum_qnorm,
        sum_knorm,
        sum_o,
        sum_apost,
        sum_left,
        sum_right,
        sum_lnorm,
        sum_fnorm,
        sum_gate,
        sum_up,
        sum_down,
        sum_fpost,
        sum_plgate,
        sum_plproj,
        sum_plpost,
    )


def solution(mesh):
    placed = (
        P(("rep", "fsdp"), None),
        P(("rep", "fsdp"), None),
        P(("rep", "fsdp"), None),
        P("rep", None),
        P("rep", None),
        P("fsdp"),
        P("fsdp", None),
        P("fsdp", None),
        P("fsdp", None),
        P("fsdp"),
        P("fsdp"),
        P("fsdp", None),
        P("fsdp"),
        P("fsdp", None),
        P("fsdp", None),
        P("fsdp"),
        P("fsdp"),
        P("fsdp", None),
        P("fsdp", None),
        P("fsdp", None),
        P("fsdp"),
        P("fsdp", None),
        P("fsdp", None),
        P("fsdp"),
    )
    return jax.shard_map(
        head_plan if mesh.shape["fsdp"] == HEADS else gather_plan,
        mesh=mesh,
        in_specs=placed,
        out_specs=(
            P(("rep", "fsdp"), None),
            P(("rep", "fsdp"), None),
            P(("rep", "fsdp"), None),
            P("fsdp"),
            P("fsdp", None),
            P("fsdp", None),
            P("fsdp", None),
            P("fsdp"),
            P("fsdp"),
            P("fsdp", None),
            P("fsdp"),
            P("fsdp", None),
            P("fsdp", None),
            P("fsdp"),
            P("fsdp"),
            P("fsdp", None),
            P("fsdp", None),
            P("fsdp", None),
            P("fsdp"),
            P("fsdp", None),
            P("fsdp", None),
            P("fsdp"),
        ),
        check_vma=False,
    )
```

```python
import functools
import math

import jax
import jax.numpy as jnp
from jax import lax
from jax.experimental import pallas as pl
from jax.experimental.pallas import tpu as pltpu
from jax.sharding import PartitionSpec as P

HEADS = 8
KV_HEADS = 2
HEAD_DIM = 256


EPS = 1e-06
ROPE_BASE = 1000000.0
HALF_ROOT = 0.7071067811865476
MASKED = -1e30


def norm_rows(value, gain):
    return value * lax.rsqrt(jnp.mean(value * value, axis=-1, keepdims=True) + EPS) * gain


def norm_back(value, gain, grad):
    unused, pull = jax.vjp(norm_rows, value, gain)
    return pull(grad)


def rotate(value, position):
    half = value.shape[-1] // 2
    freqs = jnp.exp(
        jnp.arange(half, dtype=jnp.float32) * (-2.0 * math.log(ROPE_BASE) / value.shape[-1])
    )
    angle = position[:, None] * freqs[None, :]
    cosine = jnp.cos(angle)[:, None, :]
    sine = jnp.sin(angle)[:, None, :]
    first_half = value[..., :half]
    second_half = value[..., half:]
    return jnp.concatenate(
        [first_half * cosine - second_half * sine, second_half * cosine + first_half * sine],
        axis=-1,
    )


def tree_tables(lengths, parents, total):
    count = lengths.shape[0]
    labels = jnp.arange(count, dtype=jnp.int32)
    ends = jnp.cumsum(lengths)
    starts = ends - lengths
    tokens = jnp.arange(total, dtype=jnp.int32)
    segment = jnp.sum((ends[None, :] <= tokens[:, None]).astype(jnp.int32), axis=1)
    parent_hot = ((parents[:, None] == labels[None, :]) & (labels[:, None] > 0)).astype(jnp.int32)
    identity = (labels[:, None] == labels[None, :]).astype(jnp.int32)
    ancestors = lax.fori_loop(
        0, count, lambda step, held: jnp.minimum(1, identity + jnp.dot(parent_hot, held)), identity
    )
    offset = jnp.dot(ancestors - identity, lengths) - starts
    member = (segment[:, None] == labels[None, :]).astype(jnp.int32)
    reach = jnp.dot(member, ancestors)
    position = jnp.dot(member, offset) + tokens
    return (tokens, member, reach, position)


def outer(left, right):
    return lax.dot_general(
        left, right, (((0,), (0,)), ((), ())), preferred_element_type=jnp.float32
    )


def mul_t(left, right):
    return lax.dot_general(
        left, right, (((1,), (1,)), ((), ())), preferred_element_type=jnp.float32
    )


def gelu_mix(first, second):
    return jax.nn.gelu(first, approximate=True) * second


def mix_back(first, second, grad):
    unused, pull = jax.vjp(gelu_mix, first, second)
    return pull(grad)


MESH = pl.DeviceIdType.MESH
VMEM_BYTES = 48 << 20


def ring_place(index):
    side = lax.rem(index, 2)
    return index // 2 + side * (HEADS - 1 - 2 * (index // 2))


def ring_index(place):
    back = place // (HEADS // 2)
    return (1 - back) * 2 * place + back * (2 * HEADS - 1 - 2 * place)


def ring_ends(place):
    after = {"fsdp": ring_index(lax.rem(place + 1, HEADS))}
    before = {"fsdp": ring_index(lax.rem(place + HEADS - 1, HEADS))}
    return (after, before)


def greet(others):
    barrier = pltpu.get_barrier_semaphore()
    for other in others:
        pl.semaphore_signal(barrier, inc=1, device_id=other, device_id_type=MESH)
    pl.semaphore_wait(barrier, len(others))


def span(start, size):
    return pl.ds(pl.multiple_of(start, size), size)


def neighbours():
    rep = lax.axis_index("rep")
    chip = rep // 2
    core = lax.rem(rep, 2)
    return (chip, core, {"rep": 2 * chip + 1 - core}, {"rep": 2 * (1 - chip) + core})


def remote(source, target, sems, number, device):
    copy = pltpu.make_async_remote_copy(
        source,
        target,
        sems[0].at[number],
        sems[1].at[number],
        device_id=device,
        device_id_type=MESH,
    )
    copy.start()
    return copy


class Ring:
    def __init__(self, place, ends, lanes, sems, own, there):
        self.place, self.ends, self.lanes, self.sems = place, ends, lanes, sems
        self.own, self.there = own, there
        self.copies = []

    def owner(self, step, lane):
        ahead = step if lane % 2 else HEADS - step
        return ring_index(lax.rem(self.place + ahead, HEADS))

    def send(self, step):
        for lane in range(self.lanes):
            number = step * self.lanes + lane
            target = self.there(self.owner(step, lane), lane)
            if step:
                self.copies[number - self.lanes].wait_recv()
            source = target if step else self.own(lane)
            self.copies.append(remote(source, target, self.sems, number, self.ends[lane % 2]))

    def arrive(self, step):
        for lane in range(self.lanes):
            self.copies[(step - 1) * self.lanes + lane].wait_recv()

    def sent(self):
        for copy in self.copies:
            copy.wait_send()


class Mirror:
    def __init__(self, count, sems):
        unused_chip, unused_core, self.sibling, self.across = neighbours()
        self.count, self.sems = count, sems
        self.copies = [None] * (3 * count)

    def give(self, number, ref):
        self.copies[number] = remote(ref, ref, self.sems, number, self.sibling)
        self.copies[self.count + number] = remote(
            ref, ref, self.sems, self.count + number, self.across
        )

    def relay(self, number, ref):
        self.copies[self.count + number].wait_recv()
        self.copies[2 * self.count + number] = remote(
            ref, ref, self.sems, 2 * self.count + number, self.sibling
        )

    def arrive(self):
        for number, copy in enumerate(self.copies):
            if number // self.count != 1:
                copy.wait_recv()

    def sent(self):
        for copy in self.copies:
            copy.wait_send()

    def finish(self):
        self.arrive()
        self.sent()


RING_STEPS = HEADS - 1
QUARTERS = 4


def dot(left, right):
    return jnp.dot(left, right, preferred_element_type=jnp.float32)


def low(value):
    return value.astype(jnp.bfloat16)


def add_low(left, right):
    return (left.astype(jnp.float32) + right.astype(jnp.float32)).astype(jnp.bfloat16)


class RingSum:
    def __init__(self, place, ends, lanes, sems, held, own):
        self.place, self.ends, self.lanes, self.sems = place, ends, lanes, sems
        self.held, self.own = held, own
        self.copies = []

    def send(self, step):
        for lane in range(self.lanes):
            ahead = step + 1 if lane % 2 else HEADS - 1 - step
            owner = ring_index(lax.rem(self.place + ahead, HEADS))
            number = step * self.lanes + lane
            if step:
                slot = number - self.lanes
                self.copies[slot].wait_recv()
                value = self.held[slot].astype(jnp.float32) + self.own(owner, lane)
            else:
                slot = RING_STEPS * self.lanes + lane
                value = self.own(owner, lane)
            self.held[slot] = value.astype(jnp.bfloat16)
            self.copies.append(
                remote(self.held.at[slot], self.held.at[number], self.sems, number, self.ends[lane % 2])
            )

    def last(self, index, lane):
        number = (RING_STEPS - 1) * self.lanes + lane
        self.copies[number].wait_recv()
        return self.held[number].astype(jnp.float32) + self.own(index, lane)

    def sent(self):
        for copy in self.copies:
            copy.wait_send()


def lane_offset(lane, rows):
    return (lane % 2) * (rows // 2) + (lane // 2) * (rows // 4)


def tile_loop(count, size, body):
    def step(number, carry):
        body(span(number * size, size))
        return carry

    lax.fori_loop(0, count, step, 0)


class Pair:
    def __init__(self, place, step, rows):
        half = rows // 2
        behind = ring_index(lax.rem(place + HEADS - step, HEADS))
        ahead = ring_index(lax.rem(place + step, HEADS))
        self.half = half
        self.rows = (span(behind * rows, half), span(ahead * rows + half, half))

    def read(self, ref, columns=slice(None)):
        return jnp.concatenate([ref[rows, columns] for rows in self.rows], axis=0)

    def write(self, ref, columns, value):
        for side, rows in enumerate(self.rows):
            ref[rows, columns] = value[side * self.half : (side + 1) * self.half]


GELU_ROOT = math.sqrt(2.0 / math.pi)
GELU_CUBE = 0.044715
TILE = 256


def start_loads(pairs, sems):
    copies = []
    for number, (source, target) in enumerate(pairs):
        copy = pltpu.make_async_copy(source, target, sems.at[number])
        copy.start()
        copies.append(copy)
    return copies


def root_of(value):
    return lax.rsqrt(jnp.mean(value * value, axis=1, keepdims=True) + EPS)


def norm_pull(value, gain, grad):
    root = root_of(value)
    gain_grad = jnp.sum(grad * value * root, axis=0, keepdims=True)
    grad = grad * gain
    along = jnp.mean(grad * value, axis=1, keepdims=True)
    return (root * grad - value * (root * root * root * along), gain_grad)


def gelu_parts(value):
    square = value * value
    bent = jnp.tanh(GELU_ROOT * value * (1.0 + GELU_CUBE * square))
    share = 0.5 * (1.0 + bent)
    slope = share + (0.5 * GELU_ROOT) * value * (1.0 - bent * bent) * (
        1.0 + (3.0 * GELU_CUBE) * square
    )
    return (value * share, slope)


def tree_tables_near(segments, count, tables):
    member, reach, cosine, sine = tables
    lengths, parents = segments[0:1, :], segments[1:2, :]
    size = lengths.shape[1]
    row = lax.broadcasted_iota(jnp.int32, (size, size), 0)
    column = lax.broadcasted_iota(jnp.int32, (size, size), 1)
    same = row == column

    def upright(value):
        return jnp.sum(jnp.where(same, value, 0.0), axis=1, keepdims=True)

    parent = upright(parents) == column.astype(jnp.float32)
    reached = jnp.where(same | (parent & (row > 0)), 1.0, 0.0)
    for unused_step in range((count - 1).bit_length()):
        reached = jnp.where(dot(low(reached), low(reached)) > 0.5, 1.0, 0.0)
    ends = jnp.sum(jnp.where(row <= column, upright(lengths), 0.0), axis=0, keepdims=True)
    starts = ends - lengths
    above = jnp.sum(jnp.where(same, 0.0, reached * lengths), axis=1, keepdims=True)
    offset = jnp.sum(jnp.where(same, above, 0.0), axis=0, keepdims=True) - starts
    reached = low(reached)
    half = cosine.shape[1]
    place = lax.broadcasted_iota(jnp.int32, (1, half), 1).astype(jnp.float32)
    freqs = jnp.exp(place * (-math.log(ROPE_BASE) / half))

    def token_tile(number, carry):
        tile = span(number * size, size)
        token = (row + number * size).astype(jnp.float32)
        inside = jnp.where((token >= starts) & (token < ends), 1.0, 0.0)
        position = jnp.sum(inside * offset, axis=1, keepdims=True) + token[:, :1]
        angle = position * freqs
        cosine[tile, :] = jnp.cos(angle)
        sine[tile, :] = jnp.sin(angle)
        member[tile, :] = low(inside)
        reach[tile, :] = low(dot(low(inside), reached))
        return carry

    lax.fori_loop(0, member.shape[0] // size, token_tile, 0)


def attention_kernel(
    count,
    hidden_ref,
    packed_ref,
    segments_ref,
    q_ref,
    kv_ref,
    small_ref,
    pl_proj_ref,
    o_any,
    sum_ref,
    gains_ref,
    small_all,
    pl_proj_all,
    normed_any,
    weights_any,
    q_raw_any,
    k_raw_any,
    q_low_any,
    k_low_any,
    v_low_any,
    att_any,
    probs_any,
    cosine_any,
    sine_any,
    normed,
    weights,
    q_raw,
    k_raw,
    q_low,
    k_low,
    v_low,
    att,
    probs,
    cosine,
    sine,
    hidden_all,
    kv_all,
    gains_all,
    o_proj,
    member,
    reach,
    part,
    held,
    load_sems,
    store_sems,
    *sems,
):
    pairs = [sems[i : i + 2] for i in range(0, len(sems), 2)]
    hidden_sems, gains_sems, q_sems, kv_sems, small_sems, pl_proj_sems, sum_sems = pairs[:7]
    q_mirror_sems, kv_mirror_sems, small_mirror_sems, pl_proj_mirror_sems = pairs[7:]
    rows, width = hidden_ref.shape
    total_rows = rows * HEADS
    half = rows // 2
    piece = rows // 4
    shard = q_ref.shape[0]
    deep = pl_proj_ref.shape[0]
    q_rows = shard // QUARTERS
    shard_part = q_rows // 2
    wide = pl_proj_ref.shape[1] // QUARTERS
    wide_part = wide // 2
    index = lax.axis_index("fsdp")
    chip, core, sibling, across = neighbours()
    quarter, other_quarter = 2 * chip + core, 2 * (1 - chip) + core
    place = ring_place(index)
    ends = ring_ends(place)
    others = [lax.rem(index + step, HEADS) for step in range(1, HEADS)]
    own_shard = span(index * shard, shard)
    loads = start_loads(
        (
            (q_ref.at[:, span(index * HEAD_DIM, HEAD_DIM)], weights.at[own_shard, pl.ds(0, HEAD_DIM)]),
            (kv_ref, kv_all.at[own_shard]),
            (o_any, o_proj),
            (small_ref, small_all.at[own_shard]),
            (pl_proj_ref, pl_proj_all.at[span(index * deep, deep)]),
        ),
        load_sems,
    )
    greet([{"fsdp": other} for other in others] + [sibling, across])
    gain_copies = [
        remote(packed_ref, gains_all.at[index], gains_sems, step, {"fsdp": other})
        for step, other in enumerate(others)
    ]

    def shard_at(ref, part_of):
        return lambda owner, lane: ref.at[
            span(owner * shard + part_of * q_rows + lane * shard_part, shard_part)
        ]

    def pl_proj_at(part_of):
        return lambda owner, lane: pl_proj_all.at[
            span(owner * deep, deep), span(part_of * wide + lane * wide_part, wide_part)
        ]

    def shard_own(ref):
        return lambda lane: ref.at[span(quarter * q_rows + lane * shard_part, shard_part)]

    hidden = Ring(
        place,
        ends,
        4,
        hidden_sems,
        lambda lane: hidden_ref.at[pl.ds(lane_offset(lane, rows), piece)],
        lambda owner, lane: hidden_all.at[span(owner * rows + lane_offset(lane, rows), piece)],
    )
    kv = Ring(place, ends, 2, kv_sems, shard_own(kv_ref), shard_at(kv_all, quarter))
    small = Ring(place, ends, 2, small_sems, shard_own(small_ref), shard_at(small_all, quarter))
    pl_proj = Ring(
        place,
        ends,
        2,
        pl_proj_sems,
        lambda lane: pl_proj_ref.at[:, span(quarter * wide + lane * wide_part, wide_part)],
        pl_proj_at(quarter),
    )
    lanes = 2 * RING_STEPS
    kv_mirror = Mirror(lanes, kv_mirror_sems)
    q_mirror = Mirror(HEADS - 1, q_mirror_sems)
    late = (
        (small, Mirror(lanes, small_mirror_sems), shard_at(small_all, other_quarter)),
        (pl_proj, Mirror(lanes, pl_proj_mirror_sems), pl_proj_at(other_quarter)),
    )
    kv_other = shard_at(kv_all, other_quarter)

    def pass_on(ring, mirror, step):
        for lane in range(2):
            mirror.give((step - 1) * 2 + lane, ring.there(ring.owner(step, lane), lane))

    def pass_again(ring, mirror, there, step):
        for lane in range(2):
            mirror.relay((step - 1) * 2 + lane, there(ring.owner(step, lane), lane))

    def late_step(step):
        for ring, mirror, there in late:
            if step < RING_STEPS:
                ring.send(step)
            elif step == RING_STEPS:
                ring.arrive(step)
            if 1 <= step <= RING_STEPS:
                pass_on(ring, mirror, step)
            if step >= 2:
                pass_again(ring, mirror, there, step - 1)

    def q_at(step, part_of):
        giver = lax.rem(index + HEADS - 1 - step, HEADS)
        return weights.at[span(giver * shard + part_of * q_rows, q_rows), pl.ds(0, HEAD_DIM)]

    kv.send(0)
    q_landing = weights.at[span(index * shard + quarter * q_rows, q_rows), pl.ds(0, HEAD_DIM)]
    q_copies = [
        remote(
            q_ref.at[span(quarter * q_rows, q_rows), span(other * HEAD_DIM, HEAD_DIM)],
            q_landing,
            q_sems,
            step,
            {"fsdp": other},
        )
        for step, other in enumerate(others)
    ]
    hidden.send(0)
    hidden_all[span(index * rows, rows), :] = hidden_ref[...]
    gains_all[index] = packed_ref[...]
    tree_tables_near(segments_ref, count, (member, reach, cosine, sine))

    def project(step):
        pair = Pair(place, step, rows)
        source = pair.read(hidden_all).astype(jnp.float32)
        value = low(source * root_of(source) * gains_ref[0:1, :])
        pair.write(normed, slice(None), value)
        raw = dot(value, weights[...])
        cos_rows, sin_rows = pair.read(cosine), pair.read(sine)
        for side, (raw_ref, low_ref) in enumerate(((q_raw, q_low), (k_raw, k_low))):
            item = raw[:, side * HEAD_DIM : (side + 1) * HEAD_DIM]
            pair.write(raw_ref, slice(None), item)
            item = item * root_of(item) * gains_ref[6 + side : 7 + side, :HEAD_DIM]
            first, second = item[:, : HEAD_DIM // 2], item[:, HEAD_DIM // 2 :]
            turned = jnp.concatenate(
                [first * cos_rows - second * sin_rows, second * cos_rows + first * sin_rows],
                axis=1,
            )
            pair.write(low_ref, slice(None), low(turned))
        pair.write(v_low, slice(None), low(raw[:, 2 * HEAD_DIM :]))

    for step in range(1, RING_STEPS):
        if step <= 3:
            for kv_step in (2 * step - 1, 2 * step):
                kv.send(kv_step)
                pass_on(kv, kv_mirror, kv_step)
        hidden.send(step)
        if step in (2, 3):
            for kv_step in (2 * step - 3, 2 * step - 2):
                pass_again(kv, kv_mirror, kv_other, kv_step)
        if step == 2:
            for number, copy in enumerate(q_copies):
                copy.wait_recv()
                q_mirror.give(number, q_at(number, quarter))
        if step == 3:
            for number in range(HEADS - 1):
                q_mirror.relay(number, q_at(number, other_quarter))
        if step == 4:
            kv.arrive(RING_STEPS)
            pass_on(kv, kv_mirror, RING_STEPS)
            for kv_step in (5, 6, 7):
                pass_again(kv, kv_mirror, kv_other, kv_step)
            for copy in gain_copies:
                copy.wait_recv()
            for owner in range(HEADS):
                gains_ref[:, owner * shard : (owner + 1) * shard] = gains_all[owner]
            total = gains_all[0, 6:, :]
            for owner in range(1, HEADS):
                total = total + gains_all[owner, 6:, :]
            gains_ref[6:, :shard] = total
        if step == 5:
            late_step(0)
            kv_mirror.arrive()
            q_mirror.arrive()
            loads[0].wait()
            loads[1].wait()
            key_at = (index // (HEADS // KV_HEADS)) * HEAD_DIM
            turns = start_loads(
                [
                    (
                        kv_all.at[:, span(key_at + side * KV_HEADS * HEAD_DIM, HEAD_DIM)],
                        weights.at[:, pl.ds((1 + side) * HEAD_DIM, HEAD_DIM)],
                    )
                    for side in range(2)
                ],
                load_sems.at[pl.ds(5, 2)],
            )
            for copy in turns:
                copy.wait()
            for number in range(3):
                project(number)
        if step == 6:
            late_step(1)
            for number in range(3, 6):
                project(number)
    late_step(2)
    project(6)
    hidden.arrive(RING_STEPS)
    project(7)
    stores = start_loads(
        (
            (normed, normed_any),
            (weights, weights_any),
            (q_raw, q_raw_any),
            (k_raw, k_raw_any),
            (q_low, q_low_any),
            (k_low, k_low_any),
            (v_low, v_low_any),
            (cosine, cosine_any),
            (sine, sine_any),
        ),
        store_sems,
    )
    loads[2].wait()
    scale = HEAD_DIM ** (-0.5)

    def attend(first_owner, second_owner):
        starts = (first_owner * rows, second_owner * rows + half)
        spans = [span(start, half) for start in starts]

        def read(ref):
            return jnp.concatenate([ref[rows_of, :] for rows_of in spans], axis=0)

        query = lax.broadcasted_iota(jnp.int32, (half, total_rows), 0)
        query = jnp.concatenate([query + start for start in starts], axis=0)
        key = lax.broadcasted_iota(jnp.int32, (rows, total_rows), 1)
        scores = mul_t(read(q_low), k_low[...]) * scale
        seen = (mul_t(read(reach), member[...]) > 0.5) & (key <= query)
        scores = jnp.where(seen, scores, MASKED)
        expo = jnp.exp(scores - jnp.max(scores, axis=1, keepdims=True))
        chance = low(expo / jnp.sum(expo, axis=1, keepdims=True))
        mixed = low(dot(chance, v_low[...]))
        for side, rows_of in enumerate(spans):
            probs[rows_of, :] = chance[side * half : (side + 1) * half]
            att[rows_of, :] = mixed[side * half : (side + 1) * half]
        part[...] = dot(mixed, o_proj[...])

    sums = RingSum(
        place,
        ends,
        4,
        sum_sems,
        held,
        lambda owner, lane: part[pl.ds(lane_offset(lane, rows), piece), :],
    )
    for step in range(RING_STEPS):
        attend(
            ring_index(lax.rem(place + HEADS - 1 - step, HEADS)),
            ring_index(lax.rem(place + step + 1, HEADS)),
        )
        sums.send(step)
        if step + 3 <= HEADS:
            late_step(step + 3)
    attend(index, index)
    stores += start_loads(((att, att_any), (probs, probs_any)), store_sems.at[pl.ds(9, 2)])
    for lane in range(4):
        sum_ref[pl.ds(lane_offset(lane, rows), piece), :] = sums.last(index, lane)
    for item in (hidden, kv, small, pl_proj, sums, kv_mirror, q_mirror):
        item.sent()
    for unused_ring, mirror, unused_there in late:
        mirror.finish()
    for copy in q_copies + gain_copies:
        copy.wait_send()
    for copy in loads[3:] + stores:
        copy.wait()


def attention_forward(hidden, packed, segments, count, q_proj, kv, small, pl_proj, o_proj, number):
    rows, width = hidden.shape
    total = rows * HEADS
    shard = q_proj.shape[0]
    steps = 4 * RING_STEPS
    near, anywhere = pl.BlockSpec(memory_space=pltpu.VMEM), pl.BlockSpec(memory_space=pl.ANY)
    bf16, f32 = jnp.bfloat16, jnp.float32
    head = (total, HEAD_DIM)
    table = (total, HEAD_DIM // 2)
    kept = [
        ((total, width), bf16),
        ((width, 3 * HEAD_DIM), bf16),
        (head, f32),
        (head, f32),
        (head, bf16),
        (head, bf16),
        (head, bf16),
        (head, bf16),
        ((total, total), bf16),
        (table, f32),
        (table, f32),
    ]
    grown = [((shard * HEADS, small.shape[1]), bf16), ((pl_proj.shape[0] * HEADS, width), bf16)]
    low_steps = 2 * RING_STEPS
    counts = [steps, HEADS - 1, HEADS - 1] + [low_steps] * 3 + [steps]
    counts += [3 * (HEADS - 1)] + [3 * low_steps] * 3
    return pl.pallas_call(
        functools.partial(attention_kernel, count),
        out_shape=[
            jax.ShapeDtypeStruct((rows, width), f32),
            jax.ShapeDtypeStruct((8, width), f32),
        ]
        + [jax.ShapeDtypeStruct(shape, dtype) for shape, dtype in grown + kept],
        in_specs=[near] * 3 + [anywhere] * 5,
        out_specs=[near] * 2 + [anywhere] * (len(grown) + len(kept)),
        scratch_shapes=[pltpu.VMEM(shape, dtype) for shape, dtype in kept]
        + [
            pltpu.VMEM((total, width), bf16),
            pltpu.VMEM((width, kv.shape[1]), bf16),
            pltpu.VMEM((HEADS,) + packed.shape, f32),
            pltpu.VMEM(o_proj.shape, bf16),
            pltpu.VMEM((total, segments.shape[1]), bf16),
            pltpu.VMEM((total, segments.shape[1]), bf16),
            pltpu.VMEM((rows, width), f32),
            pltpu.VMEM((steps + 4, rows // 4, width), bf16),
            pltpu.SemaphoreType.DMA((7,)),
            pltpu.SemaphoreType.DMA((11,)),
        ]
        + [pltpu.SemaphoreType.DMA((item,)) for item in counts for unused_side in range(2)],
        compiler_params=pltpu.CompilerParams(
            collective_id=number, has_side_effects=True, vmem_limit_bytes=VMEM_BYTES
        ),
    )(hidden, packed, segments, q_proj, kv, small, pl_proj, o_proj)


def ffn_kernel(
    own_ref,
    gate_any,
    up_any,
    down_any,
    sum_ref,
    all_ref,
    act_ref,
    slope_ref,
    inner_ref,
    gate,
    up,
    down,
    block,
    inner_block,
    part,
    held,
    load_sems,
    send_sem,
    recv_sem,
    sum_send,
    sum_recv,
):
    rows, width = own_ref.shape
    units = gate.shape[0]
    piece = rows // 4
    index = lax.axis_index("fsdp")
    place = ring_place(index)
    ends = ring_ends(place)
    loads = start_loads(((gate_any, gate), (up_any, up), (down_any, down)), load_sems)
    greet(ends)
    ring = Ring(
        place,
        ends,
        4,
        (send_sem, recv_sem),
        lambda lane: own_ref.at[pl.ds(lane_offset(lane, rows), piece)],
        lambda owner, lane: all_ref.at[span(owner * rows + lane_offset(lane, rows), piece)],
    )

    def own(owner, lane):
        return part[span(owner * rows + lane_offset(lane, rows), piece), :].astype(jnp.float32)

    sums = RingSum(place, ends, 4, (sum_send, sum_recv), held, own)

    def compute(step):
        pair = Pair(place, step, rows)
        block[...] = pair.read(all_ref)

        def into(tile):
            value = mul_t(block[...], gate[tile, :])
            second = mul_t(block[...], up[tile, :])
            act, slope = gelu_parts(value)
            inner = low(act * second)
            inner_block[:, tile] = inner
            pair.write(act_ref, tile, low(act))
            pair.write(slope_ref, tile, low(slope * second))
            pair.write(inner_ref, tile, inner)

        tile_loop(units // TILE, TILE, into)

        def out(tile):
            pair.write(part, tile, low(dot(inner_block[...], down[:, tile])))

        tile_loop(width // (2 * TILE), 2 * TILE, out)

    ring.send(0)
    all_ref[span(index * rows, rows), :] = own_ref[...]
    for copy in loads:
        copy.wait()
    compute(0)
    for step in range(1, HEADS):
        if step < RING_STEPS:
            ring.send(step)
        else:
            ring.arrive(step)
        compute(step)
        sums.send(step - 1)
    for lane in range(4):
        sum_ref[pl.ds(lane_offset(lane, rows), piece), :] = sums.last(index, lane)
    ring.sent()
    sums.sent()


def ffn_forward(own, gate, up, down, number):
    rows, width = own.shape
    units = gate.shape[0]
    near, anywhere = pl.BlockSpec(memory_space=pltpu.VMEM), pl.BlockSpec(memory_space=pl.ANY)
    total = rows * HEADS
    steps = 4 * RING_STEPS
    bf16 = jnp.bfloat16
    inner = jax.ShapeDtypeStruct((total, units), bf16)
    return pl.pallas_call(
        ffn_kernel,
        out_shape=[
            jax.ShapeDtypeStruct((rows, width), jnp.float32),
            jax.ShapeDtypeStruct((total, width), bf16),
            inner,
            inner,
            inner,
        ],
        in_specs=[near] + [anywhere] * 3,
        out_specs=[near] * 5,
        scratch_shapes=[pltpu.VMEM((units, width), bf16)] * 3
        + [
            pltpu.VMEM((rows, width), bf16),
            pltpu.VMEM((rows, units), bf16),
            pltpu.VMEM((total, width), bf16),
            pltpu.VMEM((steps + 4, rows // 4, width), bf16),
            pltpu.SemaphoreType.DMA((3,)),
        ]
        + [pltpu.SemaphoreType.DMA((steps,))] * 4,
        compiler_params=pltpu.CompilerParams(
            collective_id=number, has_side_effects=True, vmem_limit_bytes=VMEM_BYTES
        ),
    )(own, gate, up, down)


def ffn_back_kernel(
    first_ref,
    ffw_ref,
    extra_ref,
    seed_ref,
    gains_ref,
    small_any,
    pl_proj_any,
    all_any,
    act_any,
    slope_any,
    inner_any,
    gate_any,
    up_any,
    down_any,
    sum_ref,
    result_ref,
    d_extra_ref,
    d_second_ref,
    gain_grads,
    down_out,
    gate_out,
    up_out,
    far_down,
    theirs_any,
    gate_sum,
    proj_sum,
    d_all,
    tokens,
    d_up,
    d_gate,
    inner,
    gate,
    up,
    down,
    block,
    inner_block,
    part,
    held,
    turned,
    give,
    keep,
    theirs,
    own_ref,
    pl_gate,
    pl_proj,
    gate_blocks,
    gate_folded,
    gate_far,
    gate_held,
    proj_blocks,
    proj_folded,
    proj_far,
    proj_held,
    load_sems,
    store_sems,
    *sems,
):
    ring_sems, sum_sems, fold_sems, far_sems, gate_sems, proj_sems, pl_fold_sems, pl_far_sems = [
        sems[i : i + 2] for i in range(0, 16, 2)
    ]
    rows, width = first_ref.shape
    units = gate.shape[0]
    piece = rows // 4
    index = lax.axis_index("fsdp")
    place = ring_place(index)
    ends = ring_ends(place)
    unused_chip, core, sibling, across = neighbours()
    per_layer = pl_gate.shape[1]
    (
        load_pl_gate,
        load_pl_proj,
        load_down,
        load_act,
        load_slope,
        load_gate,
        load_up,
        load_inner,
        load_tokens,
    ) = start_loads(
        (
            (small_any.at[:, pl.ds(0, per_layer)], pl_gate),
            (pl_proj_any, pl_proj),
            (down_any, down),
            (act_any, d_up),
            (slope_any, d_gate),
            (gate_any, gate),
            (up_any, up),
            (inner_any, inner),
            (all_any, tokens),
        ),
        load_sems,
    )
    greet(ends + (sibling, across))
    ring = Ring(
        place,
        ends,
        4,
        ring_sems,
        lambda lane: own_ref.at[pl.ds(lane_offset(lane, rows), piece)],
        lambda owner, lane: d_all.at[span(owner * rows + lane_offset(lane, rows), piece)],
    )

    def own(owner, lane):
        return part[span(owner * rows + lane_offset(lane, rows), piece), :].astype(jnp.float32)

    chip = neighbours()[0]
    mine, yours = 2 * chip + core, 2 * (1 - chip) + core

    def block_ring(block_sems, block_held, blocks):
        low_rows = blocks.shape[2] // 2
        return RingSum(
            place,
            ends,
            2,
            block_sems,
            block_held,
            lambda owner, lane: blocks[owner, mine, pl.ds(lane * low_rows, low_rows), :].astype(
                jnp.float32
            ),
        )

    sums = RingSum(place, ends, 4, sum_sems, held, own)
    pl_rings = (
        block_ring(gate_sems, gate_held, gate_blocks),
        block_ring(proj_sems, proj_held, proj_blocks),
    )
    pl_arrays = (
        (gate_blocks, gate_folded, gate_far),
        (proj_blocks, proj_folded, proj_far),
    )
    pl_folds, pl_sends = [], []

    def per_layer_branch():
        def after_ffw(tile):
            value = ffw_ref[tile, :]
            total = first_ref[tile, :] + value * root_of(value) * gains_ref[0:1, :]
            sum_ref[tile, :] = total
            block[tile, :] = low(total)

        tile_loop(rows // 32, 32, after_ffw)
        load_pl_gate.wait()
        load_pl_proj.wait()
        extra = extra_ref[...].astype(jnp.float32)
        act, slope = gelu_parts(dot(block[...], pl_gate[...]))
        mix = low(act * extra)
        d_second_ref[...] = dot(mix, pl_proj[...])

        def back_out(tile):
            value = d_second_ref[tile, :]
            result_ref[tile, :] = low(sum_ref[tile, :] + value * root_of(value) * gains_ref[1:2, :])
            grad, gain_grad = norm_pull(
                value, gains_ref[1:2, :], seed_ref[tile, :].astype(jnp.float32)
            )
            own_ref[tile, :] = low(grad)
            gain_grads[1:2, :] += gain_grad

        tile_loop(rows // 32, 32, back_out)
        d_mix = mul_t(own_ref[...], pl_proj[...])
        d_extra_ref[...] = low(d_mix * act)
        d_pre = low(d_mix * extra * slope)
        turned_mix = mix.T
        deep = proj_blocks.shape[2]
        for step in range(QUARTERS):
            wide = proj_blocks.shape[3]
            value = low(dot(turned_mix, own_ref[:, step * wide : (step + 1) * wide]))
            for owner in range(HEADS):
                proj_blocks[owner, step] = value[owner * deep : (owner + 1) * deep]
        shard = width // HEADS
        for owner in range(HEADS):
            value = low(dot(block[:, owner * shard : (owner + 1) * shard].T, d_pre))
            for step in range(QUARTERS):
                gate_blocks[owner, step] = value[
                    step * (shard // QUARTERS) : (step + 1) * (shard // QUARTERS)
                ]
        d_second_ref[...] = mul_t(d_pre, pl_gate[...])

        def back_ffw(tile):
            grad = seed_ref[tile, :].astype(jnp.float32) + d_second_ref[tile, :]
            d_second_ref[tile, :] = grad
            grad, gain_grad = norm_pull(ffw_ref[tile, :], gains_ref[0:1, :], grad)
            own_ref[tile, :] = low(grad)
            gain_grads[0:1, :] += gain_grad

        tile_loop(rows // 32, 32, back_ffw)

    def pl_fold():
        for number, (blocks, folded, far) in enumerate(pl_arrays):
            for side in range(2):
                pl_folds[2 * number + side].wait_recv()
            for owner in range(HEADS):
                blocks[owner, yours] = add_low(blocks[owner, yours], folded[1 - chip, owner])
            pl_sends.append(remote(blocks.at[:, yours], far, pl_far_sems, number, across))
            for owner in range(HEADS):
                blocks[owner, mine] = add_low(blocks[owner, mine], folded[chip, owner])

    def pl_join():
        for number, (blocks, folded, far) in enumerate(pl_arrays):
            pl_sends[number].wait_recv()
            for owner in range(HEADS):
                blocks[owner, mine] = add_low(blocks[owner, mine], far[owner])

    def compute(step):
        pair = Pair(place, step, rows)
        block[...] = pair.read(d_all)

        def into(tile):
            grad = mul_t(block[...], down[tile, :])
            first = low(grad * pair.read(d_gate, tile).astype(jnp.float32))
            second = low(grad * pair.read(d_up, tile).astype(jnp.float32))
            pair.write(d_gate, tile, first)
            pair.write(d_up, tile, second)
            inner_block[0, :, tile] = first
            inner_block[1, :, tile] = second

        tile_loop(units // TILE, TILE, into)
        if step == 0:
            load_gate.wait()
            load_up.wait()

        def out(tile):
            total = dot(inner_block[0], gate[:, tile]) + dot(inner_block[1], up[:, tile])
            pair.write(part, tile, low(total))

        tile_loop(width // (2 * TILE), 2 * TILE, out)

    half = units // 2
    folds, stores, swaps = [], [], []
    jobs = (
        (inner, d_all, down_out),
        (d_gate, tokens, gate_out),
        (d_up, tokens, up_out),
    )

    def outer_half(number, side, target):
        left, right, unused_out = jobs[number]
        turned[...] = left[:, span(side * half, half)].T

        def tile_step(tile):
            target[:, tile] = low(dot(turned[...], right[:, tile]))

        tile_loop(width // (2 * TILE), 2 * TILE, tile_step)

    def grads_give(number):
        if number:
            folds[number - 1].wait_send()
        outer_half(number, 1 - core, give)
        folds.append(remote(give, theirs_any.at[number], fold_sems, number, sibling))

    def grads_keep(number):
        if number > 1:
            stores[number - 1].wait()
        outer_half(number, core, keep)
        folds[number].wait_recv()
        load = pltpu.make_async_copy(theirs_any.at[number], theirs, load_sems.at[9])
        load.start()
        load.wait()

        def add(tile):
            keep[tile, :] = add_low(keep[tile, :], theirs[tile, :])

        tile_loop(half // 64, 64, add)
        store = pltpu.make_async_copy(keep, jobs[number][2], store_sems.at[number])
        store.start()
        stores.append(store)
        if not number:
            store.wait()
            swaps.append(remote(down_out, far_down, far_sems, 0, across))

    gain_grads[...] = jnp.zeros_like(gain_grads)
    per_layer_branch()
    ring.send(0)
    for number, (blocks, folded, unused_far) in enumerate(pl_arrays):
        for side in range(2):
            pl_folds.append(
                remote(
                    blocks.at[:, 2 * side + 1 - core],
                    folded.at[side],
                    pl_fold_sems,
                    2 * number + side,
                    sibling,
                )
            )
    d_all[span(index * rows, rows), :] = own_ref[...]
    for copy in (load_down, load_act, load_slope):
        copy.wait()
    compute(0)
    for step in range(1, HEADS):
        if step < RING_STEPS:
            ring.send(step)
        else:
            ring.arrive(step)
        if step >= RING_STEPS - 1:
            sums.send(step - RING_STEPS + 1)
        compute(step)
        if step == 2:
            pl_fold()
        if step == 4:
            pl_join()
    load_inner.wait()
    load_tokens.wait()
    for step in range(RING_STEPS):
        if step >= 2:
            sums.send(step)
        for item in pl_rings:
            item.send(step)
        if step < 6:
            if step % 2:
                grads_keep(step // 2)
            else:
                grads_give(step // 2)
    for lane in range(4):
        sum_ref[pl.ds(lane_offset(lane, rows), piece), :] = sums.last(index, lane)
    for item, target in zip(pl_rings, (gate_sum, proj_sum)):
        low_rows = target.shape[0] // 2
        for lane in range(2):
            target[pl.ds(lane * low_rows, low_rows), :] = low(item.last(index, lane))
    for item in (ring, sums) + pl_rings:
        item.sent()
    for copy in pl_folds + pl_sends:
        copy.wait_send()
    folds[-1].wait_send()
    stores[-1].wait()
    swaps[0].wait()


def ffn_back(local, gains, small, pl_proj, arrays, weights, number):
    rows, width = local[0].shape
    units = weights[0].shape[0]
    near, anywhere = pl.BlockSpec(memory_space=pltpu.VMEM), pl.BlockSpec(memory_space=pl.ANY)
    total = rows * HEADS
    steps = 4 * RING_STEPS
    bf16, f32 = jnp.bfloat16, jnp.float32
    low_steps = 2 * RING_STEPS
    counts = [steps, steps, 3, 1, low_steps, low_steps, 4, 2]
    half = (units // 2, width)
    deep, per_layer = pl_proj.shape[0] // HEADS, local[2].shape[1]
    gate_block = (width // HEADS // QUARTERS, per_layer)
    proj_block = (deep, width // QUARTERS)

    def block_scratch(shape):
        return [
            pltpu.VMEM((HEADS, QUARTERS) + shape, bf16),
            pltpu.VMEM((2, HEADS) + shape, bf16),
            pltpu.VMEM((HEADS,) + shape, bf16),
            pltpu.VMEM((low_steps + 2, shape[0] // 2, shape[1]), bf16),
        ]

    return pl.pallas_call(
        ffn_back_kernel,
        out_shape=[
            jax.ShapeDtypeStruct((rows, width), f32),
            jax.ShapeDtypeStruct((rows, width), bf16),
            jax.ShapeDtypeStruct((rows, per_layer), bf16),
            jax.ShapeDtypeStruct((rows, width), f32),
            jax.ShapeDtypeStruct(gains.shape, f32),
        ]
        + [jax.ShapeDtypeStruct(half, bf16)] * 4
        + [jax.ShapeDtypeStruct((3,) + half, bf16)]
        + [jax.ShapeDtypeStruct(gate_block, bf16), jax.ShapeDtypeStruct(proj_block, bf16)],
        in_specs=[near] * 5 + [anywhere] * 9,
        out_specs=[near] * 5 + [anywhere] * 5 + [near] * 2,
        scratch_shapes=[pltpu.VMEM((total, width), bf16)] * 2
        + [pltpu.VMEM((total, units), bf16)] * 3
        + [pltpu.VMEM((units, width), bf16)] * 3
        + [
            pltpu.VMEM((rows, width), bf16),
            pltpu.VMEM((2, rows, units), bf16),
            pltpu.VMEM((total, width), bf16),
            pltpu.VMEM((steps + 4, rows // 4, width), bf16),
            pltpu.VMEM((units // 2, total), bf16),
            pltpu.VMEM(half, bf16),
            pltpu.VMEM(half, bf16),
            pltpu.VMEM(half, bf16),
            pltpu.VMEM((rows, width), bf16),
            pltpu.VMEM((width, per_layer), bf16),
            pltpu.VMEM(pl_proj.shape, bf16),
        ]
        + block_scratch(gate_block)
        + block_scratch(proj_block)
        + [pltpu.SemaphoreType.DMA((10,)), pltpu.SemaphoreType.DMA((3,))]
        + [pltpu.SemaphoreType.DMA((count,)) for count in counts for unused_side in range(2)],
        compiler_params=pltpu.CompilerParams(
            collective_id=number, has_side_effects=True, vmem_limit_bytes=58 << 20
        ),
    )(*local, gains, small, pl_proj, *arrays, *weights)


def head_back(grad, raw, gain, cosine, sine):
    half = raw.shape[1] // 2
    first, second = grad[:, :half], grad[:, half:]
    turned = jnp.concatenate(
        [first * cosine + second * sine, second * cosine - first * sine], axis=1
    )
    root = lax.rsqrt(jnp.mean(raw * raw, axis=1, keepdims=True) + EPS)
    gain_grad = jnp.sum(turned * raw * root, axis=0, keepdims=True)
    turned = turned * gain
    along = jnp.mean(turned * raw, axis=1, keepdims=True)
    return (root * turned - raw * (root * root * root * along), gain_grad)


def attention_back_kernel(
    hidden_ref,
    first_ref,
    d_ffwin_ref,
    d_second_ref,
    branch_ref,
    low_rank_ref,
    left_low_ref,
    gains_ref,
    ffw_gains_ref,
    o_any,
    q_any,
    k_any,
    v_any,
    att_any,
    probs_any,
    normed_any,
    weights_any,
    q_raw_any,
    k_raw_any,
    cosine_any,
    sine_any,
    small_any,
    pl_gate_ref,
    pl_proj_ref,
    own_down,
    far_down,
    own_gate,
    own_up,
    source_ref,
    owned_ref,
    early_ref,
    pl_proj_all,
    gain_sums,
    total_down,
    total_gate,
    total_up,
    far_gate,
    far_up,
    o_proj,
    q_low,
    k_low,
    v_low,
    att,
    probs,
    normed,
    weights,
    q_raw,
    k_raw,
    cosine,
    sine,
    d_all,
    block,
    att_block,
    q_block,
    dq_block,
    d_q,
    d_k,
    d_v,
    d_qkv,
    turned,
    part,
    held,
    blocks,
    folded,
    far,
    near_sum,
    key_held,
    o_grad,
    o_folded,
    o_far,
    sum_own,
    sum_far,
    own_ref,
    laurel,
    d_low_rank,
    d_scaled,
    sum_ref,
    gain_rows,
    gain_parts,
    gain_landed,
    gain_totals,
    load_sems,
    final_sems,
    *sems,
):
    pairs = [sems[i : i + 2] for i in range(0, len(sems), 2)]
    ring_sems, sum_sems, fold_sems, far_sems, swap_sems, key_sems = pairs[:6]
    mirror_sems, early_sems, o_fold_sems, o_far_sems, cross_sems, total_sems, proj_sems = pairs[6:13]
    gain_sems, twin_sems = pairs[13:]
    rows, width = own_ref.shape
    total_rows = rows * HEADS
    half = rows // 2
    piece = rows // 4
    index = lax.axis_index("fsdp")
    chip, core, sibling, across = neighbours()
    place = ring_place(index)
    ends = ring_ends(place)
    others = [lax.rem(index + step, HEADS) for step in range(1, HEADS)]
    quarter = 2 * chip + core
    quarter_rows = blocks.shape[2]
    own_rows = span(quarter * quarter_rows, quarter_rows)
    other_rows = span((2 * (1 - chip) + core) * quarter_rows, quarter_rows)
    groups = HEADS // KV_HEADS
    scale = HEAD_DIM ** (-0.5)
    head_columns = 3 * HEAD_DIM
    loads = start_loads(
        (
            (o_any, o_proj),
            (q_any, q_low),
            (k_any, k_low),
            (v_any, v_low),
            (att_any, att),
            (probs_any, probs),
            (q_raw_any, q_raw),
            (k_raw_any, k_raw),
            (cosine_any, cosine),
            (sine_any, sine),
            (weights_any, weights),
            (normed_any, normed),
            (small_any.at[:, span(small_any.shape[1] - laurel.shape[1], laurel.shape[1])], laurel),
        ),
        load_sems,
    )
    rep = lax.axis_index("rep")
    twins = [lax.rem(rep + step, QUARTERS) for step in range(1, QUARTERS)]
    greet([{"fsdp": other} for other in others] + [{"rep": twin} for twin in twins])
    early_rows = far_up.shape[0] // 4
    late_rows = far_up.shape[0] - early_rows
    crossings = [
        remote(own_gate, far_gate, cross_sems, 0, across),
        remote(
            own_up.at[pl.ds(0, early_rows)], far_up.at[pl.ds(0, early_rows)], cross_sems, 1, across
        ),
    ]
    ring = Ring(
        place,
        ends,
        4,
        ring_sems,
        lambda lane: own_ref.at[pl.ds(lane_offset(lane, rows), piece)],
        lambda owner, lane: d_all.at[span(owner * rows + lane_offset(lane, rows), piece)],
    )
    sums = RingSum(
        place,
        ends,
        4,
        sum_sems,
        held,
        lambda owner, lane: part[pl.ds(lane_offset(lane, rows), piece), :],
    )
    key_tiles = total_rows // TILE
    rank = laurel.shape[1] // 2

    def before(tile):
        grad, part_sum = norm_pull(first_ref[tile, :], gains_ref[3:4, :], d_ffwin_ref[tile, :])
        gain_rows[3:4, :] += part_sum
        scaled = (d_second_ref[tile, :] + grad) * HALF_ROOT
        d_scaled[tile, :] = scaled
        grad, part_sum = norm_pull(branch_ref[tile, :], gains_ref[1:2, :], scaled)
        gain_rows[1:2, :] += part_sum
        own_ref[tile, :] = low(grad)
        grad, part_sum = norm_pull(low_rank_ref[tile, :], gains_ref[2:3, :], scaled)
        gain_rows[2:3, :] += part_sum
        d_low_rank[tile, :] = low(grad)

    def low_rank_grads():
        d_left = low(dot(d_low_rank[...], laurel[...])[:, rank:])
        source = hidden_ref[...].astype(jnp.float32)
        block[...] = low(source * root_of(source) * gains_ref[0:1, :])
        shard = width // HEADS
        for owner in range(HEADS):
            columns = slice(owner * shard, (owner + 1) * shard)
            value = jnp.concatenate(
                [
                    dot(block[:, columns].T, d_left),
                    dot(d_low_rank[:, columns].T, left_low_ref[...]),
                ],
                axis=1,
            )
            value = low(value)
            for step in range(QUARTERS):
                blocks[owner, step, :, head_columns:] = value[
                    step * quarter_rows : (step + 1) * quarter_rows
                ]
        return d_left

    def after(tile):
        grad = d_scaled[tile, :] + sum_ref[tile, :]
        grad, part_sum = norm_pull(
            hidden_ref[tile, :].astype(jnp.float32), gains_ref[0:1, :], grad
        )
        gain_rows[0:1, :] += part_sum
        source_ref[tile, :] = low(d_scaled[tile, :] + grad)

    def compute(step):
        pair = Pair(place, step, rows)
        block[...] = pair.read(d_all)
        d_att = low(mul_t(block[...], o_proj[...]))
        att_block[...] = d_att
        q_block[...] = pair.read(q_low)
        delta = jnp.sum(
            d_att.astype(jnp.float32) * pair.read(att).astype(jnp.float32), axis=1, keepdims=True
        )
        dq_block[...] = jnp.zeros_like(dq_block)

        def keys(tile):
            chance = pair.read(probs, tile)
            d_chance = mul_t(att_block[...], v_low[tile, :])
            d_score = low(chance.astype(jnp.float32) * (d_chance - delta) * scale)
            dq_block[...] += dot(d_score, k_low[tile, :])
            d_k[tile, :] += dot(d_score.T, q_block[...])
            d_v[tile, :] += dot(chance.T, att_block[...])

        tile_loop(key_tiles, TILE, keys)
        pair.write(d_q, slice(None), dq_block[...])

    finals = (
        (own_down, far_down, total_down),
        (own_gate, far_gate, total_gate),
        (own_up, far_up, total_up),
    )
    final_loads, final_sends, final_stores = [], [], []
    half_units = far_up.shape[0]

    def load_final(number):
        if number:
            final_sends[number - 1].wait_send()
            final_stores[number - 1].wait()
        for side, (ref, target) in enumerate(zip(finals[number], (sum_own, sum_far))):
            copy = pltpu.make_async_copy(ref, target, final_sems.at[side])
            copy.start()
            final_loads.append(copy)

    def add_final(number):
        for copy in final_loads[2 * number :]:
            copy.wait()

        def add(tile):
            sum_own[tile, :] = add_low(sum_own[tile, :], sum_far[tile, :])

        tile_loop(half_units // 64, 64, add)
        target = finals[number][2].at[span(core * half_units, half_units)]
        final_sends.append(remote(sum_own, target, total_sems, number, sibling))
        store = pltpu.make_async_copy(sum_own, target, final_sems.at[2])
        store.start()
        final_stores.append(store)

    d_k[...] = jnp.zeros_like(d_k)
    d_v[...] = jnp.zeros_like(d_v)
    gain_rows[...] = jnp.zeros_like(gain_rows)
    tile_loop(rows // 32, 32, before)
    ring.send(0)
    d_all[span(index * rows, rows), :] = own_ref[...]
    loads[12].wait()
    d_left = low_rank_grads()
    for copy in loads[:6]:
        copy.wait()
    compute(0)
    for step in range(1, HEADS):
        if step < RING_STEPS:
            ring.send(step)
        else:
            ring.arrive(step)
        compute(step)
        if step == 2:
            load_final(0)
        if step == 4:
            add_final(0)
    for copy in loads[6:12]:
        copy.wait()

    def raw_tile(tile):
        for side, (grad, raw) in enumerate(((d_q, q_raw), (d_k, k_raw))):
            value, gain_grad = head_back(
                grad[tile, :],
                raw[tile, :],
                gains_ref[6 + side : 7 + side, :HEAD_DIM],
                cosine[tile, :],
                sine[tile, :],
            )
            d_qkv[tile, side * HEAD_DIM : (side + 1) * HEAD_DIM] = low(value)
            gain_rows[6 + side : 7 + side, :HEAD_DIM] += gain_grad
        d_qkv[tile, 2 * HEAD_DIM :] = low(d_v[tile, :])

    tile_loop(total_rows // 128, 128, raw_tile)

    def owner_at(step, way):
        return ring_index(lax.rem(place + (step + 1 if way else HEADS - 1 - step), HEADS))

    def part_of(step):
        tops = [
            d_qkv[span(owner_at(step, way) * rows + way * half, half), :] for way in range(2)
        ]
        part[...] = mul_t(jnp.concatenate(tops, axis=0), weights[...])

    def head_grads(number, carry):
        turned[...] = normed[:, span(number * TILE, TILE)].T
        value = low(dot(turned[...], d_qkv[...]))
        for step in range(QUARTERS):
            blocks[number, step, :, :head_columns] = value[
                step * quarter_rows : (step + 1) * quarter_rows
            ]
        return carry

    def o_tile(tile):
        value = low(dot(turned[...], d_all[:, tile]))
        for step in range(QUARTERS):
            o_grad[step, :, tile] = value[step * quarter_rows : (step + 1) * quarter_rows]

    part_of(0)
    sums.send(0)
    lax.fori_loop(0, width // TILE, head_grads, 0)
    folds, o_folds, across_sends, swaps, key_swaps = [], [], [], [], []
    for side in range(2):
        folds.append(
            remote(blocks.at[:, 2 * side + 1 - core], folded.at[side], fold_sems, side, sibling)
        )
    part_of(1)
    sums.send(1)
    turned[...] = att[...].T
    tile_loop(width // (2 * TILE), 2 * TILE, o_tile)
    for side in range(2):
        o_folds.append(
            remote(o_grad.at[2 * side + 1 - core], o_folded.at[side], o_fold_sems, side, sibling)
        )
    mirror, early, pl_mirror = Mirror(1, mirror_sems), Mirror(1, early_sems), Mirror(1, proj_sems)
    wide = pl_proj_ref.shape[1]
    own_columns = span(quarter * wide, wide)
    other_columns = span((2 * (1 - chip) + core) * wide, wide)
    rest = blocks.shape[3] - HEAD_DIM
    q_columns = HEADS * HEAD_DIM
    mine, yours = 2 * chip + core, 2 * (1 - chip) + core

    def fold_step():
        for side in range(2):
            folds[side].wait_recv()
            o_folds[side].wait_recv()
        for number in range(HEADS):
            blocks[number, yours] = add_low(blocks[number, yours], folded[1 - chip, number])
        across_sends.append(remote(blocks.at[:, yours], far, far_sems, 0, across))
        o_grad[yours] = add_low(o_grad[yours], o_folded[1 - chip])
        across_sends.append(remote(o_grad.at[yours], o_far, o_far_sems, 0, across))
        crossings.append(
            remote(
                own_up.at[pl.ds(early_rows, late_rows)],
                far_up.at[pl.ds(early_rows, late_rows)],
                cross_sems,
                2,
                across,
            )
        )
        for number in range(HEADS):
            blocks[number, mine] = add_low(blocks[number, mine], folded[chip, number])
        o_grad[mine] = add_low(o_grad[mine], o_folded[chip])

    def swap_step():
        across_sends[0].wait_recv()
        for number in range(HEADS):
            near_sum[number] = add_low(blocks[number, mine], far[number])
        here = span(index * HEAD_DIM, HEAD_DIM)
        for step, other in enumerate(others):
            swaps.append(
                remote(
                    near_sum.at[other, :, pl.ds(0, HEAD_DIM)],
                    owned_ref.at[own_rows, here],
                    swap_sems,
                    step,
                    {"fsdp": other},
                )
            )
            key_swaps.append(
                remote(
                    near_sum.at[other, :, pl.ds(HEAD_DIM, rest)],
                    key_held.at[index],
                    key_sems,
                    step,
                    {"fsdp": other},
                )
            )
        owned_ref[own_rows, here] = near_sum[index, :, :HEAD_DIM]
        key_held[index] = near_sum[index, :, HEAD_DIM:]
        across_sends[1].wait_recv()
        early_ref[own_rows, :width] = add_low(o_grad[mine], o_far[...])
        early_ref[own_rows, width:] = pl_gate_ref[...]
        early.give(0, early_ref.at[own_rows])
        pl_proj_all[:, own_columns] = pl_proj_ref[...]
        pl_mirror.give(0, pl_proj_all.at[:, own_columns])

    for step in range(2, RING_STEPS):
        part_of(step)
        sums.send(step)
        if step == 2:
            fold_step()
        if step == 3:
            crossings[0].wait_recv()
            load_final(1)
        if step == 4:
            swap_step()
        if step == 5:
            add_final(1)
        if step == 6:
            early.relay(0, early_ref.at[other_rows])
            pl_mirror.relay(0, pl_proj_all.at[:, other_columns])
    part[...] = mul_t(d_qkv[span(index * rows, rows), :], weights[...])
    for lane in range(4):
        sum_ref[pl.ds(lane_offset(lane, rows), piece), :] = sums.last(index, lane)
    for copy in swaps + key_swaps:
        copy.wait_recv()
    for head in range(KV_HEADS):
        total = key_held[head * groups].astype(jnp.float32)
        for step in range(1, groups):
            total = total + key_held[head * groups + step].astype(jnp.float32)
        total = low(total)
        for side in range(2):
            base = q_columns + (side * KV_HEADS + head) * HEAD_DIM
            owned_ref[own_rows, pl.ds(base, HEAD_DIM)] = total[
                :, side * HEAD_DIM : (side + 1) * HEAD_DIM
            ]
    extra = key_held[0, :, 2 * HEAD_DIM :].astype(jnp.float32)
    for step in range(1, HEADS):
        extra = extra + key_held[step, :, 2 * HEAD_DIM :].astype(jnp.float32)
    base = q_columns + 2 * KV_HEADS * HEAD_DIM
    owned_ref[own_rows, pl.ds(base, rest - 2 * HEAD_DIM)] = low(extra)
    mirror.give(0, owned_ref.at[own_rows])
    sum_ref[...] += mul_t(d_left, laurel[:, :rank])
    tile_loop(rows // 32, 32, after)
    gain_rows[4:6, :] = ffw_gains_ref[...]
    shard = width // HEADS
    for owner in range(HEADS):
        gain_parts[owner, :6] = gain_rows[:6, owner * shard : (owner + 1) * shard]
        gain_parts[owner, 6:] = gain_rows[6:, :HEAD_DIM]
    gain_sends = [
        remote(gain_parts.at[other], gain_landed.at[index], gain_sems, step, {"fsdp": other})
        for step, other in enumerate(others)
    ]
    gain_landed[index] = gain_parts[index]
    for copy in gain_sends:
        copy.wait_recv()
    total = gain_landed[0]
    for step in range(1, HEADS):
        total = total + gain_landed[step]
    gain_totals[rep] = total
    twin_sends = [
        remote(gain_totals.at[rep], gain_totals.at[rep], twin_sems, step, {"rep": twin})
        for step, twin in enumerate(twins)
    ]
    crossings[1].wait_recv()
    crossings[2].wait_recv()
    load_final(2)
    mirror.relay(0, owned_ref.at[other_rows])
    for copy in twin_sends:
        copy.wait_recv()
    total = gain_totals[0]
    for step in range(1, QUARTERS):
        total = total + gain_totals[step]
    gain_sums[...] = total
    add_final(2)
    mirror.finish()
    early.finish()
    pl_mirror.finish()
    ring.sent()
    sums.sent()
    for copy in (
        folds + o_folds + across_sends + swaps + key_swaps + crossings + gain_sends + twin_sends
    ):
        copy.wait_send()
    final_sends[2].wait_send()
    final_stores[2].wait()
    for copy in final_sends:
        copy.wait_recv()


def attention_back(local, arrays, small, pl_sums, chip_grads, far_down, number):
    rows, width = local[0].shape
    total = rows * HEADS
    shard = width // HEADS
    quarter = shard // QUARTERS
    steps = 4 * RING_STEPS
    pl_gate, pl_proj = pl_sums
    laurel = 2 * local[6].shape[1]
    columns = 3 * HEAD_DIM + laurel
    half = chip_grads[0].shape
    near, anywhere = pl.BlockSpec(memory_space=pltpu.VMEM), pl.BlockSpec(memory_space=pl.ANY)
    bf16, f32 = jnp.bfloat16, jnp.float32
    owned = (HEADS + 2 * KV_HEADS) * HEAD_DIM + laurel
    counts = [steps, steps, 2, 1, HEADS - 1, HEADS - 1, 3, 3, 2, 1, 3, 3, 3]
    counts += [HEADS - 1, QUARTERS - 1]
    down, gate, up = chip_grads
    whole = jax.ShapeDtypeStruct((2 * half[0], half[1]), bf16)
    part = jax.ShapeDtypeStruct(half, bf16)
    return pl.pallas_call(
        attention_back_kernel,
        out_shape=[
            jax.ShapeDtypeStruct((rows, width), bf16),
            jax.ShapeDtypeStruct((shard, owned), bf16),
            jax.ShapeDtypeStruct((shard, width + pl_gate.shape[1]), bf16),
            jax.ShapeDtypeStruct((pl_proj.shape[0], width), bf16),
            jax.ShapeDtypeStruct((8, shard), f32),
            whole,
            whole,
            whole,
            part,
            part,
        ],
        in_specs=[near] * len(local) + [anywhere] * (len(arrays) + 1) + [near] * 2 + [anywhere] * 4,
        out_specs=[near] * 5 + [anywhere] * 5,
        scratch_shapes=[pltpu.VMEM(item.shape, item.dtype) for item in arrays]
        + [
            pltpu.VMEM((total, width), bf16),
            pltpu.VMEM((rows, width), bf16),
            pltpu.VMEM((rows, HEAD_DIM), bf16),
            pltpu.VMEM((rows, HEAD_DIM), bf16),
            pltpu.VMEM((rows, HEAD_DIM), f32),
            pltpu.VMEM((total, HEAD_DIM), f32),
            pltpu.VMEM((total, HEAD_DIM), f32),
            pltpu.VMEM((total, HEAD_DIM), f32),
            pltpu.VMEM((total, 3 * HEAD_DIM), bf16),
            pltpu.VMEM((HEAD_DIM, total), bf16),
            pltpu.VMEM((rows, width), f32),
            pltpu.VMEM((steps + 4, rows // 4, width), bf16),
            pltpu.VMEM((HEADS, QUARTERS, quarter, columns), bf16),
            pltpu.VMEM((2, HEADS, quarter, columns), bf16),
            pltpu.VMEM((HEADS, quarter, columns), bf16),
            pltpu.VMEM((HEADS, quarter, columns), bf16),
            pltpu.VMEM((HEADS, quarter, columns - HEAD_DIM), bf16),
            pltpu.VMEM((QUARTERS, quarter, width), bf16),
            pltpu.VMEM((2, quarter, width), bf16),
            pltpu.VMEM((quarter, width), bf16),
            pltpu.VMEM(half, bf16),
            pltpu.VMEM(half, bf16),
            pltpu.VMEM((rows, width), bf16),
            pltpu.VMEM((width, laurel), bf16),
            pltpu.VMEM((rows, width), bf16),
            pltpu.VMEM((rows, width), f32),
            pltpu.VMEM((rows, width), f32),
            pltpu.VMEM((8, width), f32),
            pltpu.VMEM((HEADS, 8, shard), f32),
            pltpu.VMEM((HEADS, 8, shard), f32),
            pltpu.VMEM((QUARTERS, 8, shard), f32),
            pltpu.SemaphoreType.DMA((len(arrays) + 1,)),
            pltpu.SemaphoreType.DMA((3,)),
        ]
        + [pltpu.SemaphoreType.DMA((count,)) for count in counts for unused_side in range(2)],
        compiler_params=pltpu.CompilerParams(
            collective_id=number, has_side_effects=True, vmem_limit_bytes=58 << 20
        ),
    )(*local, *arrays, small, pl_gate, pl_proj, down, far_down, gate, up)


def head_plan(
    hidden_in,
    layer_input,
    out_grad,
    seg_lengths,
    seg_parents,
    attn_norm,
    q_proj,
    k_proj,
    v_proj,
    q_norm,
    k_norm,
    o_proj,
    attn_post_norm,
    laurel_left,
    laurel_right,
    laurel_norm,
    ffw_norm,
    gate_proj,
    up_proj,
    down_proj,
    ffw_post_norm,
    pl_gate,
    pl_proj,
    pl_post_norm,
):
    index = lax.axis_index("fsdp")
    rows, width = hidden_in.shape
    shard = width // HEADS
    total = rows * HEADS
    rank = laurel_left.shape[1]
    per_layer = pl_gate.shape[1]

    piece = HEAD_DIM // HEADS
    gains = (attn_norm, attn_post_norm, laurel_norm, ffw_norm, ffw_post_norm, pl_post_norm)
    lanes = jnp.arange(HEAD_DIM, dtype=jnp.int32) // piece == index
    gains += tuple(jnp.where(lanes, jnp.tile(item, HEADS), 0) for item in (q_norm, k_norm))
    packed = jnp.concatenate([item.astype(jnp.float32) for item in gains]).reshape(8, shard)
    segments = jnp.stack([seg_lengths[0], seg_parents[0]]).astype(jnp.float32)
    segments = jnp.pad(segments, ((0, 6), (0, 128 - segments.shape[1])))
    (
        branch,
        wide_gains,
        small_all,
        full_plproj,
        normed_all,
        qkv_head,
        q_raw,
        k_raw,
        q_low,
        k_low,
        v_low,
        attended_low,
        probs_low,
        cosine,
        sine,
    ) = attention_forward(
        hidden_in,
        packed,
        segments,
        seg_lengths.shape[1],
        q_proj,
        jnp.concatenate([k_proj, v_proj], axis=1),
        jnp.concatenate([pl_gate, laurel_left, laurel_right], axis=1),
        pl_proj,
        o_proj,
        0,
    )
    gain_anorm, gain_apost, gain_lnorm, gain_fnorm = wide_gains[:4]
    full_left = small_all[:, per_layer : per_layer + rank]
    full_right = small_all[:, per_layer + rank :]

    source = hidden_in.astype(jnp.float32)
    normed = norm_rows(source, gain_anorm)
    normed_low = low(normed)
    left_low = low(dot(normed_low, full_left))
    low_rank = mul_t(left_low, full_right)
    first_sum = (
        source + norm_rows(branch, gain_apost) + normed + norm_rows(low_rank, gain_lnorm)
    ) * HALF_ROOT
    ffw_low = low(norm_rows(first_sum, gain_fnorm))

    ffw_out, ffw_all, act, slope, inner_low = ffn_forward(
        ffw_low, gate_proj, up_proj, down_proj, 7
    )
    d_ffwin, result, d_extra, d_second, ffw_gains, *rest = ffn_back(
        (first_sum, ffw_out, layer_input, out_grad),
        wide_gains[4:6],
        small_all,
        full_plproj,
        (ffw_all, act, slope, inner_low),
        (gate_proj, up_proj, down_proj),
        9,
    )
    chip_grads, far_down, pl_sums = rest[:3], rest[3], rest[5:]

    d_source, owned, early, sum_plproj, gain_sums, *totals = attention_back(
        (
            hidden_in,
            first_sum,
            d_ffwin,
            d_second,
            branch,
            low_rank,
            left_low,
            wide_gains,
            ffw_gains,
        ),
        (
            o_proj,
            q_low,
            k_low,
            v_low,
            attended_low,
            probs_low,
            normed_all,
            qkv_head,
            q_raw,
            k_raw,
            cosine,
            sine,
        ),
        small_all,
        pl_sums,
        chip_grads,
        far_down,
        12,
    )
    sum_down, sum_gate, sum_up = [item.astype(jnp.float32) for item in totals[:3]]
    sum_anorm, sum_apost, sum_lnorm, sum_fnorm, sum_fpost, sum_plpost = gain_sums[:6]
    sum_qnorm, sum_knorm = [
        lax.dynamic_slice_in_dim(item, index * piece, piece) for item in gain_sums[6:]
    ]

    def owned_part(start, size):
        return owned[:, start : start + size].astype(jnp.float32)

    keys = KV_HEADS * HEAD_DIM
    value_at = width + keys
    left_at = value_at + keys
    return (
        result,
        d_source,
        d_extra,
        sum_anorm,
        owned_part(0, width),
        owned_part(width, keys),
        owned_part(value_at, keys),
        sum_qnorm,
        sum_knorm,
        early[:, :width].astype(jnp.float32),
        sum_apost,
        owned_part(left_at, rank),
        owned_part(left_at + rank, rank),
        sum_lnorm,
        sum_fnorm,
        sum_gate,
        sum_up,
        sum_down,
        sum_fpost,
        early[:, width:].astype(jnp.float32),
        sum_plproj.astype(jnp.float32),
        sum_plpost,
    )


def gather_plan(
    hidden_in,
    layer_input,
    out_grad,
    seg_lengths,
    seg_parents,
    attn_norm,
    q_proj,
    k_proj,
    v_proj,
    q_norm,
    k_norm,
    o_proj,
    attn_post_norm,
    laurel_left,
    laurel_right,
    laurel_norm,
    ffw_norm,
    gate_proj,
    up_proj,
    down_proj,
    ffw_post_norm,
    pl_gate,
    pl_proj,
    pl_post_norm,
):
    shards = lax.axis_size("fsdp")
    rank_index = lax.axis_index("fsdp")
    rows = hidden_in.shape[0]
    total = rows * shards
    groups = HEADS // KV_HEADS
    scale = HEAD_DIM ** (-0.5)
    tokens, member, reach, position = tree_tables(seg_lengths[0], seg_parents[0], total)
    first_row = rank_index * rows
    my_tokens = first_row + jnp.arange(rows, dtype=jnp.int32)
    my_reach = lax.dynamic_slice_in_dim(reach, first_row, rows, 0)
    my_depth = lax.dynamic_slice_in_dim(position, first_row, rows, 0).astype(jnp.float32)
    seen = (jnp.dot(my_reach, member.T) > 0) & (tokens[None, :] <= my_tokens[:, None])
    (
        full_anorm,
        full_q,
        full_k,
        full_v,
        full_qnorm,
        full_knorm,
        full_o,
        full_apost,
        full_left,
        full_right,
        full_lnorm,
        full_fnorm,
        full_fpost,
        full_plgate,
        full_plproj,
        full_plpost,
    ) = (
        lax.all_gather(attn_norm, "fsdp", axis=0, tiled=True),
        lax.all_gather(q_proj, "fsdp", axis=0, tiled=True),
        lax.all_gather(k_proj, "fsdp", axis=0, tiled=True),
        lax.all_gather(v_proj, "fsdp", axis=0, tiled=True),
        lax.all_gather(q_norm, "fsdp", axis=0, tiled=True),
        lax.all_gather(k_norm, "fsdp", axis=0, tiled=True),
        lax.all_gather(o_proj, "fsdp", axis=0, tiled=True),
        lax.all_gather(attn_post_norm, "fsdp", axis=0, tiled=True),
        lax.all_gather(laurel_left, "fsdp", axis=0, tiled=True),
        lax.all_gather(laurel_right, "fsdp", axis=0, tiled=True),
        lax.all_gather(laurel_norm, "fsdp", axis=0, tiled=True),
        lax.all_gather(ffw_norm, "fsdp", axis=0, tiled=True),
        lax.all_gather(ffw_post_norm, "fsdp", axis=0, tiled=True),
        lax.all_gather(pl_gate, "fsdp", axis=0, tiled=True),
        lax.all_gather(pl_proj, "fsdp", axis=0, tiled=True),
        lax.all_gather(pl_post_norm, "fsdp", axis=0, tiled=True),
    )
    gain_anorm = full_anorm.astype(jnp.float32)
    gain_qnorm = full_qnorm.astype(jnp.float32)
    gain_knorm = full_knorm.astype(jnp.float32)
    gain_apost = full_apost.astype(jnp.float32)
    gain_lnorm = full_lnorm.astype(jnp.float32)
    gain_fnorm = full_fnorm.astype(jnp.float32)
    gain_fpost = full_fpost.astype(jnp.float32)
    gain_plpost = full_plpost.astype(jnp.float32)
    source = hidden_in.astype(jnp.float32)
    extra = layer_input.astype(jnp.float32)
    normed = norm_rows(source, gain_anorm)
    normed_low = normed.astype(jnp.bfloat16)
    q_raw = jnp.dot(normed_low, full_q, preferred_element_type=jnp.float32)
    k_raw = jnp.dot(normed_low, full_k, preferred_element_type=jnp.float32)
    v_raw = jnp.dot(normed_low, full_v, preferred_element_type=jnp.float32)

    def head_path(raw, gain):
        return rotate(norm_rows(raw.reshape(rows, -1, HEAD_DIM), gain), my_depth)

    q_low = head_path(q_raw, gain_qnorm).astype(jnp.bfloat16)
    k_low = head_path(k_raw, gain_knorm).reshape(rows, -1).astype(jnp.bfloat16)
    v_low = v_raw.astype(jnp.bfloat16)
    keys_all, values_all = (
        lax.all_gather(k_low, "fsdp", axis=0, tiled=True),
        lax.all_gather(v_low, "fsdp", axis=0, tiled=True),
    )
    keys_heads = keys_all.reshape(total, KV_HEADS, HEAD_DIM)
    values_heads = values_all.reshape(total, KV_HEADS, HEAD_DIM)
    query_groups = q_low.reshape(rows, KV_HEADS, groups, HEAD_DIM)
    mixed_list = []
    log_list = []
    for head in range(KV_HEADS):
        scores = (
            jnp.einsum(
                "tgd,nd->gtn",
                query_groups[:, head],
                keys_heads[:, head],
                preferred_element_type=jnp.float32,
            )
            * scale
        )
        scores = jnp.where(seen[None], scores, MASKED)
        top = jnp.max(scores, axis=-1, keepdims=True)
        expo = jnp.exp(scores - top)
        sums = jnp.sum(expo, axis=-1, keepdims=True)
        weights = (expo / sums).astype(jnp.bfloat16)
        mixed_list.append(
            jnp.einsum(
                "gtn,nd->tgd", weights, values_heads[:, head], preferred_element_type=jnp.float32
            )
        )
        log_list.append(top[..., 0] + jnp.log(sums[..., 0]))
    attended = jnp.stack(mixed_list, axis=1)
    log_sums = jnp.stack(log_list, axis=0)
    attended_low = attended.reshape(rows, -1).astype(jnp.bfloat16)
    branch = jnp.dot(attended_low, full_o, preferred_element_type=jnp.float32)
    left_low = jnp.dot(normed_low, full_left, preferred_element_type=jnp.float32).astype(
        jnp.bfloat16
    )
    low_rank = mul_t(left_low, full_right)
    first_sum = (
        source + norm_rows(branch, gain_apost) + normed + norm_rows(low_rank, gain_lnorm)
    ) * HALF_ROOT
    ffw_low = norm_rows(first_sum, gain_fnorm).astype(jnp.bfloat16)
    full_gate, full_up, full_down = (
        lax.all_gather(gate_proj, "fsdp", axis=0, tiled=True),
        lax.all_gather(up_proj, "fsdp", axis=0, tiled=True),
        lax.all_gather(down_proj, "fsdp", axis=0, tiled=True),
    )
    gate_val = mul_t(ffw_low, full_gate)
    up_val = mul_t(ffw_low, full_up)
    inner_low = gelu_mix(gate_val, up_val).astype(jnp.bfloat16)
    ffw_out = jnp.dot(inner_low, full_down, preferred_element_type=jnp.float32)
    second_sum = first_sum + norm_rows(ffw_out, gain_fpost)
    second_low = second_sum.astype(jnp.bfloat16)
    pl_pre = jnp.dot(second_low, full_plgate, preferred_element_type=jnp.float32)
    pl_mix = gelu_mix(pl_pre, extra).astype(jnp.bfloat16)
    pl_out = jnp.dot(pl_mix, full_plproj, preferred_element_type=jnp.float32)
    result = second_sum + norm_rows(pl_out, gain_plpost)
    seed = out_grad.astype(jnp.float32)
    d_plout, grad_plpost = norm_back(pl_out, gain_plpost, seed)
    d_plout_low = d_plout.astype(jnp.bfloat16)
    grad_plproj = outer(pl_mix, d_plout_low)
    d_mix = mul_t(d_plout_low, full_plproj)
    d_pre, d_extra = mix_back(pl_pre, extra, d_mix)
    d_pre_low = d_pre.astype(jnp.bfloat16)
    grad_plgate = outer(second_low, d_pre_low)
    d_second = seed + mul_t(d_pre_low, full_plgate)
    d_ffwout, grad_fpost = norm_back(ffw_out, gain_fpost, d_second)
    d_ffw_low = d_ffwout.astype(jnp.bfloat16)
    d_inner = mul_t(d_ffw_low, full_down)
    d_gate, d_up = mix_back(gate_val, up_val, d_inner)
    d_gate_low = d_gate.astype(jnp.bfloat16)
    d_up_low = d_up.astype(jnp.bfloat16)
    d_ffwin = jnp.dot(d_gate_low, full_gate, preferred_element_type=jnp.float32) + jnp.dot(
        d_up_low, full_up, preferred_element_type=jnp.float32
    )
    width = ffw_low.shape[1]
    gate_part = outer(d_gate_low, ffw_low)
    up_part = outer(d_up_low, ffw_low)
    down_part = outer(inner_low, d_ffw_low)
    stacked = lax.psum_scatter(
        jnp.concatenate([gate_part, up_part, down_part], axis=1).astype(jnp.bfloat16),
        "fsdp",
        scatter_dimension=0,
        tiled=True,
    ).astype(jnp.float32)
    grad_gate = stacked[:, :width]
    grad_up = stacked[:, width : 2 * width]
    grad_down = stacked[:, 2 * width :]
    d_first_part, grad_fnorm = norm_back(first_sum, gain_fnorm, d_ffwin)
    d_first = d_second + d_first_part
    d_scaled = d_first * HALF_ROOT
    d_branch, grad_apost = norm_back(branch, gain_apost, d_scaled)
    d_branch_low = d_branch.astype(jnp.bfloat16)
    d_lowrank, grad_lnorm = norm_back(low_rank, gain_lnorm, d_scaled)
    d_lowrank_low = d_lowrank.astype(jnp.bfloat16)
    grad_o = outer(attended_low, d_branch_low)
    d_att_low = mul_t(d_branch_low, full_o).astype(jnp.bfloat16)
    grad_right = outer(d_lowrank_low, left_low)
    d_left_low = jnp.dot(d_lowrank_low, full_right, preferred_element_type=jnp.float32).astype(
        jnp.bfloat16
    )
    grad_left = outer(normed_low, d_left_low)
    d_att_heads = d_att_low.reshape(rows, KV_HEADS, groups, HEAD_DIM)
    delta = jnp.sum(d_att_heads.astype(jnp.float32) * attended, axis=-1).transpose(1, 2, 0)
    block = 512
    count = total // block
    key_blocks = keys_heads.reshape(count, block, KV_HEADS, HEAD_DIM)
    value_blocks = values_heads.reshape(count, block, KV_HEADS, HEAD_DIM)
    seen_blocks = seen.reshape(rows, count, block).transpose(1, 0, 2)

    def key_step(d_query, item):
        keys, values, shown = item
        scores = (
            jnp.einsum("tkgd,nkd->kgtn", query_groups, keys, preferred_element_type=jnp.float32)
            * scale
        )
        scores = jnp.where(shown[None, None], scores, MASKED)
        probs = jnp.exp(scores - log_sums[..., None])
        d_probs = jnp.einsum(
            "tkgd,nkd->kgtn", d_att_heads, values, preferred_element_type=jnp.float32
        )
        d_scores = (probs * (d_probs - delta[..., None]) * scale).astype(jnp.bfloat16)
        d_query = d_query + jnp.einsum(
            "kgtn,nkd->tkgd", d_scores, keys, preferred_element_type=jnp.float32
        )
        d_keys = jnp.einsum(
            "kgtn,tkgd->nkd", d_scores, query_groups, preferred_element_type=jnp.float32
        )
        d_values = jnp.einsum(
            "kgtn,tkgd->nkd",
            probs.astype(jnp.bfloat16),
            d_att_heads,
            preferred_element_type=jnp.float32,
        )
        return (d_query, (d_keys, d_values))

    zero_query = jnp.zeros((rows, KV_HEADS, groups, HEAD_DIM), jnp.float32)
    d_query, (d_key_blocks, d_value_blocks) = lax.scan(
        key_step, zero_query, (key_blocks, value_blocks, seen_blocks)
    )
    my_dkeys, my_dvalues = (
        lax.psum_scatter(
            d_key_blocks.reshape(total, -1).astype(jnp.bfloat16),
            "fsdp",
            scatter_dimension=0,
            tiled=True,
        ).astype(jnp.float32),
        lax.psum_scatter(
            d_value_blocks.reshape(total, -1).astype(jnp.bfloat16),
            "fsdp",
            scatter_dimension=0,
            tiled=True,
        ).astype(jnp.float32),
    )
    unused_q, q_pull = jax.vjp(head_path, q_raw, gain_qnorm)
    d_qraw, grad_qnorm = q_pull(d_query.reshape(rows, HEADS, HEAD_DIM))
    unused_k, k_pull = jax.vjp(head_path, k_raw, gain_knorm)
    d_kraw, grad_knorm = k_pull(my_dkeys.reshape(rows, KV_HEADS, HEAD_DIM))
    d_q_low = d_qraw.astype(jnp.bfloat16)
    d_k_low = d_kraw.astype(jnp.bfloat16)
    d_v_low = my_dvalues.astype(jnp.bfloat16)
    grad_q = outer(normed_low, d_q_low)
    grad_k = outer(normed_low, d_k_low)
    grad_v = outer(normed_low, d_v_low)
    d_normed = (
        d_scaled
        + mul_t(d_q_low, full_q)
        + mul_t(d_k_low, full_k)
        + mul_t(d_v_low, full_v)
        + mul_t(d_left_low, full_left)
    )
    d_source_part, grad_anorm = norm_back(source, gain_anorm, d_normed)
    d_source = d_scaled + d_source_part
    shard_grads = (
        lax.psum_scatter(
            grad_anorm.astype(jnp.bfloat16), "fsdp", scatter_dimension=0, tiled=True
        ).astype(jnp.float32),
        lax.psum_scatter(
            grad_q.astype(jnp.bfloat16), "fsdp", scatter_dimension=0, tiled=True
        ).astype(jnp.float32),
        lax.psum_scatter(
            grad_k.astype(jnp.bfloat16), "fsdp", scatter_dimension=0, tiled=True
        ).astype(jnp.float32),
        lax.psum_scatter(
            grad_v.astype(jnp.bfloat16), "fsdp", scatter_dimension=0, tiled=True
        ).astype(jnp.float32),
        lax.psum_scatter(
            grad_qnorm.astype(jnp.bfloat16), "fsdp", scatter_dimension=0, tiled=True
        ).astype(jnp.float32),
        lax.psum_scatter(
            grad_knorm.astype(jnp.bfloat16), "fsdp", scatter_dimension=0, tiled=True
        ).astype(jnp.float32),
        lax.psum_scatter(
            grad_o.astype(jnp.bfloat16), "fsdp", scatter_dimension=0, tiled=True
        ).astype(jnp.float32),
        lax.psum_scatter(
            grad_apost.astype(jnp.bfloat16), "fsdp", scatter_dimension=0, tiled=True
        ).astype(jnp.float32),
        lax.psum_scatter(
            grad_left.astype(jnp.bfloat16), "fsdp", scatter_dimension=0, tiled=True
        ).astype(jnp.float32),
        lax.psum_scatter(
            grad_right.astype(jnp.bfloat16), "fsdp", scatter_dimension=0, tiled=True
        ).astype(jnp.float32),
        lax.psum_scatter(
            grad_lnorm.astype(jnp.bfloat16), "fsdp", scatter_dimension=0, tiled=True
        ).astype(jnp.float32),
        lax.psum_scatter(
            grad_fnorm.astype(jnp.bfloat16), "fsdp", scatter_dimension=0, tiled=True
        ).astype(jnp.float32),
        lax.psum_scatter(
            grad_fpost.astype(jnp.bfloat16), "fsdp", scatter_dimension=0, tiled=True
        ).astype(jnp.float32),
        lax.psum_scatter(
            grad_plgate.astype(jnp.bfloat16), "fsdp", scatter_dimension=0, tiled=True
        ).astype(jnp.float32),
        lax.psum_scatter(
            grad_plproj.astype(jnp.bfloat16), "fsdp", scatter_dimension=0, tiled=True
        ).astype(jnp.float32),
        lax.psum_scatter(
            grad_plpost.astype(jnp.bfloat16), "fsdp", scatter_dimension=0, tiled=True
        ).astype(jnp.float32),
    )
    (
        sum_anorm,
        sum_q,
        sum_k,
        sum_v,
        sum_qnorm,
        sum_knorm,
        sum_o,
        sum_apost,
        sum_left,
        sum_right,
        sum_lnorm,
        sum_fnorm,
        sum_fpost,
        sum_plgate,
        sum_plproj,
        sum_plpost,
        sum_gate,
        sum_up,
        sum_down,
    ) = (
        lax.psum(shard_grads[0].astype(jnp.bfloat16), "rep").astype(jnp.float32),
        lax.psum(shard_grads[1].astype(jnp.bfloat16), "rep").astype(jnp.float32),
        lax.psum(shard_grads[2].astype(jnp.bfloat16), "rep").astype(jnp.float32),
        lax.psum(shard_grads[3].astype(jnp.bfloat16), "rep").astype(jnp.float32),
        lax.psum(shard_grads[4].astype(jnp.bfloat16), "rep").astype(jnp.float32),
        lax.psum(shard_grads[5].astype(jnp.bfloat16), "rep").astype(jnp.float32),
        lax.psum(shard_grads[6].astype(jnp.bfloat16), "rep").astype(jnp.float32),
        lax.psum(shard_grads[7].astype(jnp.bfloat16), "rep").astype(jnp.float32),
        lax.psum(shard_grads[8].astype(jnp.bfloat16), "rep").astype(jnp.float32),
        lax.psum(shard_grads[9].astype(jnp.bfloat16), "rep").astype(jnp.float32),
        lax.psum(shard_grads[10].astype(jnp.bfloat16), "rep").astype(jnp.float32),
        lax.psum(shard_grads[11].astype(jnp.bfloat16), "rep").astype(jnp.float32),
        lax.psum(shard_grads[12].astype(jnp.bfloat16), "rep").astype(jnp.float32),
        lax.psum(shard_grads[13].astype(jnp.bfloat16), "rep").astype(jnp.float32),
        lax.psum(shard_grads[14].astype(jnp.bfloat16), "rep").astype(jnp.float32),
        lax.psum(shard_grads[15].astype(jnp.bfloat16), "rep").astype(jnp.float32),
        lax.psum(grad_gate.astype(jnp.bfloat16), "rep").astype(jnp.float32),
        lax.psum(grad_up.astype(jnp.bfloat16), "rep").astype(jnp.float32),
        lax.psum(grad_down.astype(jnp.bfloat16), "rep").astype(jnp.float32),
    )
    return (
        result.astype(jnp.bfloat16),
        d_source.astype(jnp.bfloat16),
        d_extra.astype(jnp.bfloat16),
        sum_anorm,
        sum_q,
        sum_k,
        sum_v,
        sum_qnorm,
        sum_knorm,
        sum_o,
        sum_apost,
        sum_left,
        sum_right,
        sum_lnorm,
        sum_fnorm,
        sum_gate,
        sum_up,
        sum_down,
        sum_fpost,
        sum_plgate,
        sum_plproj,
        sum_plpost,
    )


def solution(mesh):
    placed = (
        P(("rep", "fsdp"), None),
        P(("rep", "fsdp"), None),
        P(("rep", "fsdp"), None),
        P("rep", None),
        P("rep", None),
        P("fsdp"),
        P("fsdp", None),
        P("fsdp", None),
        P("fsdp", None),
        P("fsdp"),
        P("fsdp"),
        P("fsdp", None),
        P("fsdp"),
        P("fsdp", None),
        P("fsdp", None),
        P("fsdp"),
        P("fsdp"),
        P("fsdp", None),
        P("fsdp", None),
        P("fsdp", None),
        P("fsdp"),
        P("fsdp", None),
        P("fsdp", None),
        P("fsdp"),
    )
    return jax.shard_map(
        head_plan if mesh.shape["fsdp"] == HEADS else gather_plan,
        mesh=mesh,
        in_specs=placed,
        out_specs=(
            P(("rep", "fsdp"), None),
            P(("rep", "fsdp"), None),
            P(("rep", "fsdp"), None),
            P("fsdp"),
            P("fsdp", None),
            P("fsdp", None),
            P("fsdp", None),
            P("fsdp"),
            P("fsdp"),
            P("fsdp", None),
            P("fsdp"),
            P("fsdp", None),
            P("fsdp", None),
            P("fsdp"),
            P("fsdp"),
            P("fsdp", None),
            P("fsdp", None),
            P("fsdp", None),
            P("fsdp"),
            P("fsdp", None),
            P("fsdp", None),
            P("fsdp"),
        ),
        check_vma=False,
    )
```

```python
import functools
import math

import jax
import jax.numpy as jnp
from jax import lax
from jax.experimental import pallas as pl
from jax.experimental.pallas import tpu as pltpu
from jax.sharding import PartitionSpec as P

HEADS = 8
KV_HEADS = 2
HEAD_DIM = 256


EPS = 1e-06
ROPE_BASE = 1000000.0
HALF_ROOT = 0.7071067811865476
MASKED = -1e30


def norm_rows(value, gain):
    return value * lax.rsqrt(jnp.mean(value * value, axis=-1, keepdims=True) + EPS) * gain


def norm_back(value, gain, grad):
    unused, pull = jax.vjp(norm_rows, value, gain)
    return pull(grad)


def rotate(value, position):
    half = value.shape[-1] // 2
    freqs = jnp.exp(
        jnp.arange(half, dtype=jnp.float32) * (-2.0 * math.log(ROPE_BASE) / value.shape[-1])
    )
    angle = position[:, None] * freqs[None, :]
    cosine = jnp.cos(angle)[:, None, :]
    sine = jnp.sin(angle)[:, None, :]
    first_half = value[..., :half]
    second_half = value[..., half:]
    return jnp.concatenate(
        [first_half * cosine - second_half * sine, second_half * cosine + first_half * sine],
        axis=-1,
    )


def tree_tables(lengths, parents, total):
    count = lengths.shape[0]
    labels = jnp.arange(count, dtype=jnp.int32)
    ends = jnp.cumsum(lengths)
    starts = ends - lengths
    tokens = jnp.arange(total, dtype=jnp.int32)
    segment = jnp.sum((ends[None, :] <= tokens[:, None]).astype(jnp.int32), axis=1)
    parent_hot = ((parents[:, None] == labels[None, :]) & (labels[:, None] > 0)).astype(jnp.int32)
    identity = (labels[:, None] == labels[None, :]).astype(jnp.int32)
    ancestors = lax.fori_loop(
        0, count, lambda step, held: jnp.minimum(1, identity + jnp.dot(parent_hot, held)), identity
    )
    offset = jnp.dot(ancestors - identity, lengths) - starts
    member = (segment[:, None] == labels[None, :]).astype(jnp.int32)
    reach = jnp.dot(member, ancestors)
    position = jnp.dot(member, offset) + tokens
    return (tokens, member, reach, position)


def outer(left, right):
    return lax.dot_general(
        left, right, (((0,), (0,)), ((), ())), preferred_element_type=jnp.float32
    )


def mul_t(left, right):
    return lax.dot_general(
        left, right, (((1,), (1,)), ((), ())), preferred_element_type=jnp.float32
    )


def gelu_mix(first, second):
    return jax.nn.gelu(first, approximate=True) * second


def mix_back(first, second, grad):
    unused, pull = jax.vjp(gelu_mix, first, second)
    return pull(grad)


MESH = pl.DeviceIdType.MESH
VMEM_BYTES = 58 << 20


def ring_place(index):
    side = lax.rem(index, 2)
    return index // 2 + side * (HEADS - 1 - 2 * (index // 2))


def ring_index(place):
    back = place // (HEADS // 2)
    return (1 - back) * 2 * place + back * (2 * HEADS - 1 - 2 * place)


def ring_ends(place):
    after = {"fsdp": ring_index(lax.rem(place + 1, HEADS))}
    before = {"fsdp": ring_index(lax.rem(place + HEADS - 1, HEADS))}
    return (after, before)


def greet(others):
    barrier = pltpu.get_barrier_semaphore()
    for other in others:
        pl.semaphore_signal(barrier, inc=1, device_id=other, device_id_type=MESH)
    pl.semaphore_wait(barrier, len(others))


def span(start, size):
    return pl.ds(pl.multiple_of(start, size), size)


def neighbours():
    rep = lax.axis_index("rep")
    chip = rep // 2
    core = lax.rem(rep, 2)
    return (chip, core, {"rep": 2 * chip + 1 - core}, {"rep": 2 * (1 - chip) + core})


def remote(source, target, sems, number, device):
    copy = pltpu.make_async_remote_copy(
        source,
        target,
        sems[0].at[number],
        sems[1].at[number],
        device_id=device,
        device_id_type=MESH,
    )
    copy.start()
    return copy


class Ring:
    def __init__(self, place, ends, lanes, sems, own, there):
        self.place, self.ends, self.lanes, self.sems = place, ends, lanes, sems
        self.own, self.there = own, there
        self.copies = []

    def owner(self, step, lane):
        ahead = step if lane % 2 else HEADS - step
        return ring_index(lax.rem(self.place + ahead, HEADS))

    def send(self, step):
        for lane in range(self.lanes):
            number = step * self.lanes + lane
            target = self.there(self.owner(step, lane), lane)
            if step:
                self.copies[number - self.lanes].wait_recv()
            source = target if step else self.own(lane)
            self.copies.append(remote(source, target, self.sems, number, self.ends[lane % 2]))

    def arrive(self, step):
        for lane in range(self.lanes):
            self.copies[(step - 1) * self.lanes + lane].wait_recv()

    def sent(self):
        for copy in self.copies:
            copy.wait_send()


class Mirror:
    def __init__(self, count, sems):
        unused_chip, unused_core, self.sibling, self.across = neighbours()
        self.count, self.sems = count, sems
        self.copies = [None] * (3 * count)

    def give(self, number, ref, source=None):
        source = ref if source is None else source
        self.copies[number] = remote(source, ref, self.sems, number, self.sibling)
        self.copies[self.count + number] = remote(
            source, ref, self.sems, self.count + number, self.across
        )

    def relay(self, number, ref):
        self.copies[self.count + number].wait_recv()
        self.copies[2 * self.count + number] = remote(
            ref, ref, self.sems, 2 * self.count + number, self.sibling
        )

    def arrive(self):
        for number, copy in enumerate(self.copies):
            if number // self.count != 1:
                copy.wait_recv()

    def sent(self):
        for copy in self.copies:
            copy.wait_send()

    def finish(self):
        self.arrive()
        self.sent()


RING_STEPS = HEADS - 1
QUARTERS = 4


def dot(left, right):
    return jnp.dot(left, right, preferred_element_type=jnp.float32)


def low(value):
    return value.astype(jnp.bfloat16)


def add_low(left, right):
    return (left.astype(jnp.float32) + right.astype(jnp.float32)).astype(jnp.bfloat16)


class RingSum:
    def __init__(self, place, ends, lanes, sems, held, own):
        self.place, self.ends, self.lanes, self.sems = place, ends, lanes, sems
        self.held, self.own = held, own
        self.copies = []

    def send(self, step):
        for lane in range(self.lanes):
            ahead = step + 1 if lane % 2 else HEADS - 1 - step
            owner = ring_index(lax.rem(self.place + ahead, HEADS))
            number = step * self.lanes + lane
            if step:
                slot = number - self.lanes
                self.copies[slot].wait_recv()
                value = self.held[slot].astype(jnp.float32) + self.own(owner, lane)
            else:
                slot = RING_STEPS * self.lanes + lane
                value = self.own(owner, lane)
            self.held[slot] = value.astype(jnp.bfloat16)
            self.copies.append(
                remote(self.held.at[slot], self.held.at[number], self.sems, number, self.ends[lane % 2])
            )

    def last(self, index, lane):
        number = (RING_STEPS - 1) * self.lanes + lane
        self.copies[number].wait_recv()
        return self.held[number].astype(jnp.float32) + self.own(index, lane)

    def sent(self):
        for copy in self.copies:
            copy.wait_send()


def lane_offset(lane, rows):
    return (lane % 2) * (rows // 2) + (lane // 2) * (rows // 4)


def tile_loop(count, size, body):
    def step(number, carry):
        body(span(number * size, size))
        return carry

    lax.fori_loop(0, count, step, 0)


class Pair:
    def __init__(self, place, step, rows):
        half = rows // 2
        behind = ring_index(lax.rem(place + HEADS - step, HEADS))
        ahead = ring_index(lax.rem(place + step, HEADS))
        self.half = half
        self.rows = (span(behind * rows, half), span(ahead * rows + half, half))

    def read(self, ref, columns=slice(None)):
        return jnp.concatenate([ref[rows, columns] for rows in self.rows], axis=0)

    def write(self, ref, columns, value):
        for side, rows in enumerate(self.rows):
            ref[rows, columns] = value[side * self.half : (side + 1) * self.half]


GELU_ROOT = math.sqrt(2.0 / math.pi)
GELU_CUBE = 0.044715
TILE = 256


def start_loads(pairs, sems):
    copies = []
    for number, (source, target) in enumerate(pairs):
        copy = pltpu.make_async_copy(source, target, sems.at[number])
        copy.start()
        copies.append(copy)
    return copies


def root_of(value):
    return lax.rsqrt(jnp.mean(value * value, axis=1, keepdims=True) + EPS)


def norm_pull(value, gain, grad):
    root = root_of(value)
    gain_grad = jnp.sum(grad * value * root, axis=0, keepdims=True)
    grad = grad * gain
    along = jnp.mean(grad * value, axis=1, keepdims=True)
    return (root * grad - value * (root * root * root * along), gain_grad)


def gelu_parts(value):
    square = value * value
    bent = jnp.tanh(GELU_ROOT * value * (1.0 + GELU_CUBE * square))
    share = 0.5 * (1.0 + bent)
    slope = share + (0.5 * GELU_ROOT) * value * (1.0 - bent * bent) * (
        1.0 + (3.0 * GELU_CUBE) * square
    )
    return (value * share, slope)


def tree_tables_near(segments, count, tables):
    member, reach, cosine, sine = tables
    lengths, parents = segments[0:1, :], segments[1:2, :]
    size = lengths.shape[1]
    row = lax.broadcasted_iota(jnp.int32, (size, size), 0)
    column = lax.broadcasted_iota(jnp.int32, (size, size), 1)
    same = row == column

    def upright(value):
        return jnp.sum(jnp.where(same, value, 0.0), axis=1, keepdims=True)

    parent = upright(parents) == column.astype(jnp.float32)
    reached = jnp.where(same | (parent & (row > 0)), 1.0, 0.0)
    for unused_step in range((count - 1).bit_length()):
        reached = jnp.where(dot(low(reached), low(reached)) > 0.5, 1.0, 0.0)
    ends = jnp.sum(jnp.where(row <= column, upright(lengths), 0.0), axis=0, keepdims=True)
    starts = ends - lengths
    above = jnp.sum(jnp.where(same, 0.0, reached * lengths), axis=1, keepdims=True)
    offset = jnp.sum(jnp.where(same, above, 0.0), axis=0, keepdims=True) - starts
    reached = low(reached)
    half = cosine.shape[1]
    place = lax.broadcasted_iota(jnp.int32, (1, half), 1).astype(jnp.float32)
    freqs = jnp.exp(place * (-math.log(ROPE_BASE) / half))

    def token_tile(number, carry):
        tile = span(number * size, size)
        token = (row + number * size).astype(jnp.float32)
        inside = jnp.where((token >= starts) & (token < ends), 1.0, 0.0)
        position = jnp.sum(inside * offset, axis=1, keepdims=True) + token[:, :1]
        angle = position * freqs
        cosine[tile, :] = jnp.cos(angle)
        sine[tile, :] = jnp.sin(angle)
        member[tile, :] = low(inside)
        reach[tile, :] = low(dot(low(inside), reached))
        return carry

    lax.fori_loop(0, member.shape[0] // size, token_tile, 0)


def attention_kernel(
    count,
    segments_ref,
    norm_refs,
    hidden_ref,
    q_ref,
    k_ref,
    v_ref,
    small_ref,
    pl_proj_ref,
    o_any,
    sum_ref,
    gains_ref,
    small_all,
    pl_proj_all,
    normed_any,
    weights_any,
    q_raw_any,
    k_raw_any,
    q_low_any,
    k_low_any,
    v_low_any,
    att_any,
    probs_any,
    cosine_any,
    sine_any,
    normed,
    weights,
    q_raw,
    k_raw,
    q_low,
    k_low,
    v_low,
    att,
    probs,
    cosine,
    sine,
    hidden_all,
    kv_all,
    gains_all,
    packed_ref,
    norm_held,
    o_proj,
    member,
    reach,
    part,
    held,
    load_sems,
    store_sems,
    *sems,
):
    pairs = [sems[i : i + 2] for i in range(0, len(sems), 2)]
    hidden_sems, gains_sems, q_sems, kv_sems, small_sems, pl_proj_sems, sum_sems = pairs[:7]
    q_mirror_sems, kv_mirror_sems, small_mirror_sems, pl_proj_mirror_sems = pairs[7:]
    rows, width = hidden_ref.shape
    total_rows = rows * HEADS
    half = rows // 2
    piece = rows // 4
    shard = q_ref.shape[0]
    deep = pl_proj_ref.shape[0]
    q_rows = shard // QUARTERS
    shard_part = q_rows // 2
    wide = pl_proj_ref.shape[1] // QUARTERS
    wide_part = wide // 2
    index = lax.axis_index("fsdp")
    chip, core, sibling, across = neighbours()
    quarter, other_quarter = 2 * chip + core, 2 * (1 - chip) + core
    place = ring_place(index)
    ends = ring_ends(place)
    others = [lax.rem(index + step, HEADS) for step in range(1, HEADS)]
    own_shard = span(index * shard, shard)
    loads = start_loads(
        (
            (q_ref.at[:, span(index * HEAD_DIM, HEAD_DIM)], weights.at[own_shard, pl.ds(0, HEAD_DIM)]),
            (k_ref, kv_all.at[own_shard, pl.ds(0, k_ref.shape[1])]),
            (v_ref, kv_all.at[own_shard, pl.ds(k_ref.shape[1], v_ref.shape[1])]),
            (o_any, o_proj),
            (small_ref, small_all.at[own_shard]),
            (pl_proj_ref, pl_proj_all.at[span(index * deep, deep)]),
            (hidden_ref, hidden_all.at[span(index * rows, rows)]),
        ),
        load_sems,
    )
    norm_loads = start_loads(zip(norm_refs, norm_held), load_sems.at[pl.ds(9, len(norm_refs))])
    shard_lanes = lax.broadcasted_iota(jnp.int32, (1, shard), 1)
    few = shard // HEADS
    spread = jnp.where(
        lax.broadcasted_iota(jnp.int32, (few, shard), 0)
        == lax.rem(lax.broadcasted_iota(jnp.int32, (few, shard), 1), few),
        1.0,
        0.0,
    )
    for copy in norm_loads:
        copy.wait()
    for number, ref in enumerate(norm_held):
        value = ref[...].astype(jnp.float32).reshape(1, ref.shape[0])
        if ref.shape[0] != shard:
            value = jnp.sum(value.reshape(few, 1) * spread, axis=0, keepdims=True)
            value = jnp.where(shard_lanes // few == index, value, 0.0)
        packed_ref[number : number + 1, :] = value
    greet([{"fsdp": other} for other in others] + [sibling, across])
    gain_copies = [
        remote(packed_ref, gains_all.at[index], gains_sems, step, {"fsdp": other})
        for step, other in enumerate(others)
    ]

    def shard_at(ref, part_of):
        return lambda owner, lane: ref.at[
            span(owner * shard + part_of * q_rows + lane * shard_part, shard_part)
        ]

    def pl_proj_at(part_of):
        return lambda owner, lane: pl_proj_all.at[
            span(owner * deep, deep), span(part_of * wide + lane * wide_part, wide_part)
        ]

    def shard_own(ref):
        return lambda lane: ref.at[span(quarter * q_rows + lane * shard_part, shard_part)]

    hidden = Ring(
        place,
        ends,
        4,
        hidden_sems,
        lambda lane: hidden_ref.at[pl.ds(lane_offset(lane, rows), piece)],
        lambda owner, lane: hidden_all.at[span(owner * rows + lane_offset(lane, rows), piece)],
    )
    kv_at = shard_at(kv_all, quarter)
    kv = Ring(place, ends, 2, kv_sems, lambda lane: kv_at(index, lane), kv_at)
    small = Ring(place, ends, 2, small_sems, shard_own(small_ref), shard_at(small_all, quarter))
    pl_proj = Ring(
        place,
        ends,
        2,
        pl_proj_sems,
        lambda lane: pl_proj_ref.at[:, span(quarter * wide + lane * wide_part, wide_part)],
        pl_proj_at(quarter),
    )
    lanes = 2 * RING_STEPS
    kv_mirror = Mirror(lanes, kv_mirror_sems)
    q_mirror = Mirror(HEADS - 1, q_mirror_sems)
    late = (
        (small, Mirror(lanes, small_mirror_sems), shard_at(small_all, other_quarter)),
        (pl_proj, Mirror(lanes, pl_proj_mirror_sems), pl_proj_at(other_quarter)),
    )
    kv_other = shard_at(kv_all, other_quarter)

    def pass_on(ring, mirror, step):
        for lane in range(2):
            mirror.give((step - 1) * 2 + lane, ring.there(ring.owner(step, lane), lane))

    def pass_again(ring, mirror, there, step):
        for lane in range(2):
            mirror.relay((step - 1) * 2 + lane, there(ring.owner(step, lane), lane))

    def late_step(step):
        for ring, mirror, there in late:
            if step < RING_STEPS:
                ring.send(step)
            elif step == RING_STEPS:
                ring.arrive(step)
            if 1 <= step <= RING_STEPS:
                pass_on(ring, mirror, step)
            if step >= 2:
                pass_again(ring, mirror, there, step - 1)

    def q_at(step, part_of):
        giver = lax.rem(index + HEADS - 1 - step, HEADS)
        return weights.at[span(giver * shard + part_of * q_rows, q_rows), pl.ds(0, HEAD_DIM)]

    loads[1].wait()
    loads[2].wait()
    kv.send(0)
    q_landing = weights.at[span(index * shard + quarter * q_rows, q_rows), pl.ds(0, HEAD_DIM)]
    q_copies = [
        remote(
            q_ref.at[span(quarter * q_rows, q_rows), span(other * HEAD_DIM, HEAD_DIM)],
            q_landing,
            q_sems,
            step,
            {"fsdp": other},
        )
        for step, other in enumerate(others)
    ]
    hidden.send(0)
    gains_all[index] = packed_ref[...]
    tree_tables_near(segments_ref, count, (member, reach, cosine, sine))

    def project(step):
        pair = Pair(place, step, rows)
        source = pair.read(hidden_all).astype(jnp.float32)
        value = low(source * root_of(source) * gains_ref[0:1, :])
        pair.write(normed, slice(None), value)
        raw = dot(value, weights[...])
        cos_rows, sin_rows = pair.read(cosine), pair.read(sine)
        for side, (raw_ref, low_ref) in enumerate(((q_raw, q_low), (k_raw, k_low))):
            item = raw[:, side * HEAD_DIM : (side + 1) * HEAD_DIM]
            pair.write(raw_ref, slice(None), item)
            item = item * root_of(item) * gains_ref[6 + side : 7 + side, :HEAD_DIM]
            first, second = item[:, : HEAD_DIM // 2], item[:, HEAD_DIM // 2 :]
            turned = jnp.concatenate(
                [first * cos_rows - second * sin_rows, second * cos_rows + first * sin_rows],
                axis=1,
            )
            pair.write(low_ref, slice(None), low(turned))
        pair.write(v_low, slice(None), low(raw[:, 2 * HEAD_DIM :]))

    for step in range(1, RING_STEPS):
        if step <= 3:
            for kv_step in (2 * step - 1, 2 * step):
                kv.send(kv_step)
                pass_on(kv, kv_mirror, kv_step)
        hidden.send(step)
        if step in (2, 3):
            for kv_step in (2 * step - 3, 2 * step - 2):
                pass_again(kv, kv_mirror, kv_other, kv_step)
        if step == 2:
            for number, copy in enumerate(q_copies):
                copy.wait_recv()
                q_mirror.give(number, q_at(number, quarter))
        if step == 3:
            for number in range(HEADS - 1):
                q_mirror.relay(number, q_at(number, other_quarter))
        if step == 4:
            kv.arrive(RING_STEPS)
            pass_on(kv, kv_mirror, RING_STEPS)
            for kv_step in (5, 6, 7):
                pass_again(kv, kv_mirror, kv_other, kv_step)
            for copy in gain_copies:
                copy.wait_recv()
            for owner in range(HEADS):
                gains_ref[:, owner * shard : (owner + 1) * shard] = gains_all[owner]
            total = gains_all[0, 6:, :]
            for owner in range(1, HEADS):
                total = total + gains_all[owner, 6:, :]
            gains_ref[6:, :shard] = total
        if step == 5:
            late_step(0)
            kv_mirror.arrive()
            q_mirror.arrive()
            loads[0].wait()
            loads[6].wait()
            key_at = (index // (HEADS // KV_HEADS)) * HEAD_DIM
            turns = start_loads(
                [
                    (
                        kv_all.at[:, span(key_at + side * KV_HEADS * HEAD_DIM, HEAD_DIM)],
                        weights.at[:, pl.ds((1 + side) * HEAD_DIM, HEAD_DIM)],
                    )
                    for side in range(2)
                ],
                load_sems.at[pl.ds(7, 2)],
            )
            for copy in turns:
                copy.wait()
            for number in range(3):
                project(number)
        if step == 6:
            late_step(1)
            for number in range(3, 6):
                project(number)
    late_step(2)
    project(6)
    hidden.arrive(RING_STEPS)
    project(7)
    stores = start_loads(
        (
            (normed, normed_any),
            (weights, weights_any),
            (q_raw, q_raw_any),
            (k_raw, k_raw_any),
            (q_low, q_low_any),
            (k_low, k_low_any),
            (v_low, v_low_any),
            (cosine, cosine_any),
            (sine, sine_any),
        ),
        store_sems,
    )
    loads[3].wait()
    scale = HEAD_DIM ** (-0.5)

    def attend(first_owner, second_owner):
        starts = (first_owner * rows, second_owner * rows + half)
        spans = [span(start, half) for start in starts]

        def read(ref):
            return jnp.concatenate([ref[rows_of, :] for rows_of in spans], axis=0)

        query = lax.broadcasted_iota(jnp.int32, (half, total_rows), 0)
        query = jnp.concatenate([query + start for start in starts], axis=0)
        key = lax.broadcasted_iota(jnp.int32, (rows, total_rows), 1)
        scores = mul_t(read(q_low), k_low[...]) * scale
        seen = (mul_t(read(reach), member[...]) > 0.5) & (key <= query)
        scores = jnp.where(seen, scores, MASKED)
        expo = jnp.exp(scores - jnp.max(scores, axis=1, keepdims=True))
        chance = low(expo / jnp.sum(expo, axis=1, keepdims=True))
        mixed = low(dot(chance, v_low[...]))
        for side, rows_of in enumerate(spans):
            probs[rows_of, :] = chance[side * half : (side + 1) * half]
            att[rows_of, :] = mixed[side * half : (side + 1) * half]
        part[...] = dot(mixed, o_proj[...])

    sums = RingSum(
        place,
        ends,
        4,
        sum_sems,
        held,
        lambda owner, lane: part[pl.ds(lane_offset(lane, rows), piece), :],
    )
    for step in range(RING_STEPS):
        attend(
            ring_index(lax.rem(place + HEADS - 1 - step, HEADS)),
            ring_index(lax.rem(place + step + 1, HEADS)),
        )
        sums.send(step)
        if step + 3 <= HEADS:
            late_step(step + 3)
    attend(index, index)
    stores += start_loads(((att, att_any), (probs, probs_any)), store_sems.at[pl.ds(9, 2)])
    for lane in range(4):
        sum_ref[pl.ds(lane_offset(lane, rows), piece), :] = sums.last(index, lane)
    for item in (hidden, kv, small, pl_proj, sums, kv_mirror, q_mirror):
        item.sent()
    for unused_ring, mirror, unused_there in late:
        mirror.finish()
    for copy in q_copies + gain_copies:
        copy.wait_send()
    for copy in loads[4:6] + stores:
        copy.wait()


def attention_forward(
    segments, norms, count, hidden, q_proj, k_proj, v_proj, small, pl_proj, o_proj, number
):
    rows, width = hidden.shape
    total = rows * HEADS
    shard = q_proj.shape[0]
    steps = 4 * RING_STEPS
    near, anywhere = pl.BlockSpec(memory_space=pltpu.VMEM), pl.BlockSpec(memory_space=pltpu.HBM)
    bf16, f32 = jnp.bfloat16, jnp.float32
    head = (total, HEAD_DIM)
    table = (total, HEAD_DIM // 2)
    kept = [
        ((total, width), bf16),
        ((width, 3 * HEAD_DIM), bf16),
        (head, f32),
        (head, f32),
        (head, bf16),
        (head, bf16),
        (head, bf16),
        (head, bf16),
        ((total, total), bf16),
        (table, f32),
        (table, f32),
    ]
    grown = [((shard * HEADS, small.shape[1]), bf16), ((pl_proj.shape[0] * HEADS, width), bf16)]
    low_steps = 2 * RING_STEPS
    counts = [steps, HEADS - 1, HEADS - 1] + [low_steps] * 3 + [steps]
    counts += [3 * (HEADS - 1)] + [3 * low_steps] * 3
    return pl.pallas_call(
        functools.partial(attention_kernel, count),
        out_shape=[
            jax.ShapeDtypeStruct((rows, width), f32),
            jax.ShapeDtypeStruct((8, width), f32),
        ]
        + [jax.ShapeDtypeStruct(shape, dtype) for shape, dtype in grown + kept],
        in_specs=[near, (anywhere,) * len(norms)] + [anywhere] * 7,
        out_specs=[near] * 2 + [anywhere] * (len(grown) + len(kept)),
        scratch_shapes=[pltpu.VMEM(shape, dtype) for shape, dtype in kept]
        + [
            pltpu.VMEM((total, width), bf16),
            pltpu.VMEM((width, 2 * k_proj.shape[1]), bf16),
            pltpu.VMEM((HEADS, 8, shard), f32),
            pltpu.VMEM((8, shard), f32),
            tuple(pltpu.VMEM(item.shape, bf16) for item in norms),
            pltpu.VMEM(o_proj.shape, bf16),
            pltpu.VMEM((total, segments.shape[1]), bf16),
            pltpu.VMEM((total, segments.shape[1]), bf16),
            pltpu.VMEM((rows, width), f32),
            pltpu.VMEM((steps + 4, rows // 4, width), bf16),
            pltpu.SemaphoreType.DMA((9 + len(norms),)),
            pltpu.SemaphoreType.DMA((11,)),
        ]
        + [pltpu.SemaphoreType.DMA((item,)) for item in counts for unused_side in range(2)],
        compiler_params=pltpu.CompilerParams(
            collective_id=number, has_side_effects=True, vmem_limit_bytes=VMEM_BYTES
        ),
    )(segments, norms, hidden, q_proj, k_proj, v_proj, small, pl_proj, o_proj)


def ffn_kernel(
    own_ref,
    gate_any,
    up_any,
    down_any,
    sum_ref,
    all_ref,
    act_ref,
    slope_ref,
    inner_ref,
    far_any,
    gate,
    up,
    down,
    block,
    inner_block,
    part,
    held,
    load_sems,
    send_sem,
    recv_sem,
    sum_send,
    sum_recv,
    far_send,
    far_recv,
):
    rows, width = own_ref.shape
    units = gate.shape[0]
    piece = rows // 4
    index = lax.axis_index("fsdp")
    place = ring_place(index)
    ends = ring_ends(place)
    loads = start_loads(((gate_any, gate), (up_any, up), (down_any, down)), load_sems)
    across = neighbours()[3]
    greet(ends + (across,))
    ring = Ring(
        place,
        ends,
        4,
        (send_sem, recv_sem),
        lambda lane: own_ref.at[pl.ds(lane_offset(lane, rows), piece)],
        lambda owner, lane: all_ref.at[span(owner * rows + lane_offset(lane, rows), piece)],
    )

    def own(owner, lane):
        return part[span(owner * rows + lane_offset(lane, rows), piece), :].astype(jnp.float32)

    sums = RingSum(place, ends, 4, (sum_send, sum_recv), held, own)

    def compute(step):
        pair = Pair(place, step, rows)
        block[...] = pair.read(all_ref)

        def into(tile):
            value = mul_t(block[...], gate[tile, :])
            second = mul_t(block[...], up[tile, :])
            act, slope = gelu_parts(value)
            inner = low(act * second)
            inner_block[:, tile] = inner
            pair.write(act_ref, tile, low(act))
            pair.write(slope_ref, tile, low(slope * second))
            pair.write(inner_ref, tile, inner)

        tile_loop(units // TILE, TILE, into)

        def out(tile):
            pair.write(part, tile, low(dot(inner_block[...], down[:, tile])))

        tile_loop(width // (2 * TILE), 2 * TILE, out)

    crossings = []

    def cross(step):
        for rows_of in Pair(place, step, rows).rows:
            crossings.append(
                remote(
                    all_ref.at[rows_of],
                    far_any.at[rows_of],
                    (far_send, far_recv),
                    len(crossings),
                    across,
                )
            )

    ring.send(0)
    all_ref[span(index * rows, rows), :] = own_ref[...]
    cross(0)
    for copy in loads:
        copy.wait()
    compute(0)
    for step in range(1, HEADS):
        if step < RING_STEPS:
            ring.send(step)
            cross(step)
        else:
            ring.arrive(step)
        compute(step)
        sums.send(step - 1)
    for lane in range(4):
        sum_ref[pl.ds(lane_offset(lane, rows), piece), :] = sums.last(index, lane)
    ring.sent()
    sums.sent()
    for copy in crossings:
        copy.wait()


def ffn_forward(own, gate, up, down, number):
    rows, width = own.shape
    units = gate.shape[0]
    near, anywhere = pl.BlockSpec(memory_space=pltpu.VMEM), pl.BlockSpec(memory_space=pltpu.HBM)
    total = rows * HEADS
    steps = 4 * RING_STEPS
    bf16 = jnp.bfloat16
    inner = jax.ShapeDtypeStruct((total, units), bf16)
    return pl.pallas_call(
        ffn_kernel,
        out_shape=[
            jax.ShapeDtypeStruct((rows, width), jnp.float32),
            jax.ShapeDtypeStruct((total, width), bf16),
            inner,
            inner,
            inner,
            jax.ShapeDtypeStruct((total, width), bf16),
        ],
        in_specs=[near] + [anywhere] * 3,
        out_specs=[near] * 5 + [anywhere],
        scratch_shapes=[pltpu.VMEM((units, width), bf16)] * 3
        + [
            pltpu.VMEM((rows, width), bf16),
            pltpu.VMEM((rows, units), bf16),
            pltpu.VMEM((total, width), bf16),
            pltpu.VMEM((steps + 4, rows // 4, width), bf16),
            pltpu.SemaphoreType.DMA((3,)),
        ]
        + [pltpu.SemaphoreType.DMA((steps,))] * 4
        + [pltpu.SemaphoreType.DMA((2 * RING_STEPS,))] * 2,
        compiler_params=pltpu.CompilerParams(
            collective_id=number, has_side_effects=True, vmem_limit_bytes=VMEM_BYTES
        ),
    )(own, gate, up, down)


def ffn_back_kernel(
    first_ref,
    ffw_ref,
    extra_ref,
    seed_ref,
    gains_ref,
    small_any,
    pl_proj_any,
    all_any,
    far_all_any,
    act_any,
    slope_any,
    inner_any,
    gate_any,
    up_any,
    down_any,
    sum_ref,
    result_ref,
    d_extra_ref,
    d_second_ref,
    gain_grads,
    down_out,
    gate_out,
    up_out,
    far_down,
    theirs_any,
    joint_any,
    far_gate_any,
    far_up_any,
    far_rest_any,
    gate_sum,
    proj_sum,
    d_all,
    tokens,
    d_up,
    d_gate,
    inner,
    gate,
    up,
    down,
    block,
    inner_block,
    part,
    held,
    turned,
    give,
    keep,
    theirs,
    own_ref,
    pl_gate,
    pl_proj,
    gate_blocks,
    gate_folded,
    gate_far,
    gate_held,
    proj_blocks,
    proj_folded,
    proj_far,
    proj_held,
    load_sems,
    store_sems,
    *sems,
):
    pairs = [sems[i : i + 2] for i in range(0, len(sems), 2)]
    ring_sems, sum_sems, fold_sems, far_sems, gate_sems, proj_sems = pairs[:6]
    pl_fold_sems, pl_far_sems, cross_sems, rest_sems, joint_sems = pairs[6:]
    rows, width = first_ref.shape
    units = gate.shape[0]
    piece = rows // 4
    index = lax.axis_index("fsdp")
    place = ring_place(index)
    ends = ring_ends(place)
    unused_chip, core, sibling, across = neighbours()
    per_layer = pl_gate.shape[1]
    (
        load_pl_gate,
        load_pl_proj,
        load_down,
        load_act,
        load_slope,
        load_gate,
        load_up,
        load_inner,
        load_tokens,
    ) = start_loads(
        (
            (small_any.at[:, pl.ds(0, per_layer)], pl_gate),
            (pl_proj_any, pl_proj),
            (down_any, down),
            (act_any, d_up),
            (slope_any, d_gate),
            (gate_any, gate),
            (up_any, up),
            (inner_any, inner),
            (all_any, tokens),
        ),
        load_sems,
    )
    greet(ends + (sibling, across))
    last_pair = Pair(place, RING_STEPS, rows)
    rests = [
        remote(
            all_any.at[rows_of],
            far_rest_any.at[pl.ds(side * (rows // 2), rows // 2)],
            rest_sems,
            side,
            across,
        )
        for side, rows_of in enumerate(last_pair.rows)
    ]
    ring = Ring(
        place,
        ends,
        4,
        ring_sems,
        lambda lane: own_ref.at[pl.ds(lane_offset(lane, rows), piece)],
        lambda owner, lane: d_all.at[span(owner * rows + lane_offset(lane, rows), piece)],
    )

    def own(owner, lane):
        return part[span(owner * rows + lane_offset(lane, rows), piece), :].astype(jnp.float32)

    chip = neighbours()[0]
    mine, yours = 2 * chip + core, 2 * (1 - chip) + core

    def block_ring(block_sems, block_held, blocks):
        low_rows = blocks.shape[2] // 2
        return RingSum(
            place,
            ends,
            2,
            block_sems,
            block_held,
            lambda owner, lane: blocks[owner, mine, pl.ds(lane * low_rows, low_rows), :].astype(
                jnp.float32
            ),
        )

    sums = RingSum(place, ends, 4, sum_sems, held, own)
    pl_rings = (
        block_ring(gate_sems, gate_held, gate_blocks),
        block_ring(proj_sems, proj_held, proj_blocks),
    )
    pl_arrays = (
        (gate_blocks, gate_folded, gate_far),
        (proj_blocks, proj_folded, proj_far),
    )
    pl_folds, pl_sends = [], []

    def per_layer_branch():
        def after_ffw(tile):
            value = ffw_ref[tile, :]
            total = first_ref[tile, :] + value * root_of(value) * gains_ref[0:1, :]
            sum_ref[tile, :] = total
            block[tile, :] = low(total)

        tile_loop(rows // 32, 32, after_ffw)
        load_pl_gate.wait()
        load_pl_proj.wait()
        extra = extra_ref[...].astype(jnp.float32)
        act, slope = gelu_parts(dot(block[...], pl_gate[...]))
        mix = low(act * extra)
        d_second_ref[...] = dot(mix, pl_proj[...])

        def back_out(tile):
            value = d_second_ref[tile, :]
            result_ref[tile, :] = low(sum_ref[tile, :] + value * root_of(value) * gains_ref[1:2, :])
            grad, gain_grad = norm_pull(
                value, gains_ref[1:2, :], seed_ref[tile, :].astype(jnp.float32)
            )
            own_ref[tile, :] = low(grad)
            gain_grads[1:2, :] += gain_grad

        tile_loop(rows // 32, 32, back_out)
        d_mix = mul_t(own_ref[...], pl_proj[...])
        d_extra_ref[...] = low(d_mix * act)
        d_pre = low(d_mix * extra * slope)
        turned_mix = mix.T
        deep = proj_blocks.shape[2]
        for step in range(QUARTERS):
            wide = proj_blocks.shape[3]
            value = low(dot(turned_mix, own_ref[:, step * wide : (step + 1) * wide]))
            for owner in range(HEADS):
                proj_blocks[owner, step] = value[owner * deep : (owner + 1) * deep]
        shard = width // HEADS
        for owner in range(HEADS):
            value = low(dot(block[:, owner * shard : (owner + 1) * shard].T, d_pre))
            for step in range(QUARTERS):
                gate_blocks[owner, step] = value[
                    step * (shard // QUARTERS) : (step + 1) * (shard // QUARTERS)
                ]
        d_second_ref[...] = mul_t(d_pre, pl_gate[...])

        def back_ffw(tile):
            grad = seed_ref[tile, :].astype(jnp.float32) + d_second_ref[tile, :]
            d_second_ref[tile, :] = grad
            grad, gain_grad = norm_pull(ffw_ref[tile, :], gains_ref[0:1, :], grad)
            own_ref[tile, :] = low(grad)
            gain_grads[0:1, :] += gain_grad

        tile_loop(rows // 32, 32, back_ffw)

    def pl_fold():
        for number, (blocks, folded, far) in enumerate(pl_arrays):
            for side in range(2):
                pl_folds[2 * number + side].wait_recv()
            for owner in range(HEADS):
                blocks[owner, yours] = add_low(blocks[owner, yours], folded[1 - chip, owner])
            pl_sends.append(remote(blocks.at[:, yours], far, pl_far_sems, number, across))
            for owner in range(HEADS):
                blocks[owner, mine] = add_low(blocks[owner, mine], folded[chip, owner])

    def pl_join():
        for number, (blocks, folded, far) in enumerate(pl_arrays):
            pl_sends[number].wait_recv()
            for owner in range(HEADS):
                blocks[owner, mine] = add_low(blocks[owner, mine], far[owner])

    def compute(step):
        pair = Pair(place, step, rows)
        block[...] = pair.read(d_all)

        def into(tile):
            grad = mul_t(block[...], down[tile, :])
            first = low(grad * pair.read(d_gate, tile).astype(jnp.float32))
            second = low(grad * pair.read(d_up, tile).astype(jnp.float32))
            pair.write(d_gate, tile, first)
            pair.write(d_up, tile, second)
            inner_block[0, :, tile] = first
            inner_block[1, :, tile] = second

        tile_loop(units // TILE, TILE, into)
        if step == 0:
            load_gate.wait()
            load_up.wait()

        def out(tile):
            total = dot(inner_block[0], gate[:, tile]) + dot(inner_block[1], up[:, tile])
            pair.write(part, tile, low(total))

        tile_loop(width // (2 * TILE), 2 * TILE, out)

    half = units // 2
    crossings, swaps = [], []

    def cross(step):
        columns = span((1 - chip) * half, half)
        for rows_of in Pair(place, step, rows).rows:
            for source, target in ((d_gate, far_gate_any), (d_up, far_up_any)):
                crossings.append(
                    remote(
                        source.at[rows_of, columns],
                        target.at[rows_of],
                        cross_sems,
                        len(crossings),
                        across,
                    )
                )

    def outer_into(turn, right, target, add=False):
        turned[...] = turn.T

        def tile_step(tile):
            value = dot(turned[...], right[:, tile])
            if add:
                value = value + target[:, tile].astype(jnp.float32)
            target[:, tile] = low(value)

        tile_loop(width // (2 * TILE), 2 * TILE, tile_step)

    def add_from(landed, rows_of, target):
        count = landed.shape[0]
        copy = pltpu.make_async_copy(landed, theirs.at[pl.ds(0, count)], load_sems.at[10])
        copy.start()
        copy.wait()

        def add(tile):
            here = span(rows_of + tile.start, 64)
            target[here, :] = add_low(target[here, :], theirs[tile, :])

        tile_loop(count // 64, 64, add)

    early_rows = half * 3 // 4
    folds, stores, joints = [], [], []

    def grads_step(step):
        if step == 0:
            outer_into(inner[:, span((1 - core) * half, half)], d_all, give)
            folds.append(remote(give, theirs_any, fold_sems, 0, sibling))
        elif step == 1:
            outer_into(inner[:, span(core * half, half)], d_all, keep)
            folds[0].wait_recv()
            add_from(theirs_any, 0, keep)
            store = pltpu.make_async_copy(keep, down_out, store_sems.at[0])
            store.start()
            store.wait()
            early = pl.ds(0, early_rows)
            swaps.append(remote(down_out.at[early], far_down.at[early], far_sems, 0, across))
        elif step == 2:
            folds[0].wait_send()
            outer_into(d_gate[:, span(chip * half, half)], tokens, give)
        elif step == 3:
            outer_into(d_up[:, span(chip * half, half)], tokens, keep)
            for copy in rests + crossings:
                copy.wait()
            for copy in start_loads(
                (
                    (far_all_any, tokens),
                    (far_gate_any, d_gate.at[:, pl.ds(0, half)]),
                    (far_up_any, d_up.at[:, pl.ds(0, half)]),
                ),
                load_sems.at[pl.ds(11, 3)],
            ):
                copy.wait()
            for copy in start_loads(
                [
                    (far_rest_any.at[pl.ds(side * (rows // 2), rows // 2)], tokens.at[rows_of])
                    for side, rows_of in enumerate(last_pair.rows)
                ],
                load_sems.at[pl.ds(11, 2)],
            ):
                copy.wait()
        elif step in (4, 5):
            number = step - 4
            source, target = ((d_gate, give), (d_up, keep))[number]
            outer_into(source[:, :half], tokens, target, add=True)
            joints.append(
                remote(
                    target.at[span((1 - core) * (half // 2), half // 2)],
                    joint_any.at[number],
                    joint_sems,
                    number,
                    sibling,
                )
            )

    def join(number):
        target, out = ((give, gate_out), (keep, up_out))[number]
        joints[number].wait_recv()
        add_from(joint_any.at[number], core * (half // 2), target)
        store = pltpu.make_async_copy(
            target.at[span(core * (half // 2), half // 2)], out, store_sems.at[number]
        )
        store.start()
        stores.append(store)

    gain_grads[...] = jnp.zeros_like(gain_grads)
    per_layer_branch()
    ring.send(0)
    for number, (blocks, folded, unused_far) in enumerate(pl_arrays):
        for side in range(2):
            pl_folds.append(
                remote(
                    blocks.at[:, 2 * side + 1 - core],
                    folded.at[side],
                    pl_fold_sems,
                    2 * number + side,
                    sibling,
                )
            )
    d_all[span(index * rows, rows), :] = own_ref[...]
    for copy in (load_down, load_act, load_slope):
        copy.wait()
    compute(0)
    cross(0)
    for step in range(1, HEADS):
        if step < RING_STEPS:
            ring.send(step)
        else:
            ring.arrive(step)
        if step >= RING_STEPS - 1:
            sums.send(step - RING_STEPS + 1)
        compute(step)
        cross(step)
        if step == 2:
            pl_fold()
        if step == 4:
            pl_join()
    load_inner.wait()
    load_tokens.wait()
    for step in range(RING_STEPS):
        if step >= 2:
            sums.send(step)
        for item in pl_rings:
            item.send(step)
        if step < 6:
            grads_step(step)
        else:
            join(0)
    join(1)
    for lane in range(4):
        sum_ref[pl.ds(lane_offset(lane, rows), piece), :] = sums.last(index, lane)
    for item, target in zip(pl_rings, (gate_sum, proj_sum)):
        low_rows = target.shape[0] // 2
        for lane in range(2):
            target[pl.ds(lane * low_rows, low_rows), :] = low(item.last(index, lane))
    for item in (ring, sums) + pl_rings:
        item.sent()
    for copy in pl_folds + pl_sends:
        copy.wait_send()
    for copy in joints:
        copy.wait_send()
    for copy in stores + swaps:
        copy.wait()


def ffn_back(local, gains, small, pl_proj, arrays, weights, number):
    rows, width = local[0].shape
    units = weights[0].shape[0]
    near, anywhere = pl.BlockSpec(memory_space=pltpu.VMEM), pl.BlockSpec(memory_space=pltpu.HBM)
    total = rows * HEADS
    steps = 4 * RING_STEPS
    bf16, f32 = jnp.bfloat16, jnp.float32
    low_steps = 2 * RING_STEPS
    counts = [steps, steps, 1, 1, low_steps, low_steps, 4, 2, 4 * HEADS, 2, 2]
    half = (units // 2, width)
    quarter = (units // 4, width)
    deep, per_layer = pl_proj.shape[0] // HEADS, local[2].shape[1]
    gate_block = (width // HEADS // QUARTERS, per_layer)
    proj_block = (deep, width // QUARTERS)

    def block_scratch(shape):
        return [
            pltpu.VMEM((HEADS, QUARTERS) + shape, bf16),
            pltpu.VMEM((2, HEADS) + shape, bf16),
            pltpu.VMEM((HEADS,) + shape, bf16),
            pltpu.VMEM((low_steps + 2, shape[0] // 2, shape[1]), bf16),
        ]

    return pl.pallas_call(
        ffn_back_kernel,
        out_shape=[
            jax.ShapeDtypeStruct((rows, width), f32),
            jax.ShapeDtypeStruct((rows, width), bf16),
            jax.ShapeDtypeStruct((rows, per_layer), bf16),
            jax.ShapeDtypeStruct((rows, width), f32),
            jax.ShapeDtypeStruct(gains.shape, f32),
        ]
        + [jax.ShapeDtypeStruct(half, bf16)]
        + [jax.ShapeDtypeStruct(quarter, bf16)] * 2
        + [jax.ShapeDtypeStruct(half, bf16)] * 2
        + [jax.ShapeDtypeStruct((2,) + quarter, bf16)]
        + [jax.ShapeDtypeStruct((total, units // 2), bf16)] * 2
        + [jax.ShapeDtypeStruct((rows, width), bf16)]
        + [jax.ShapeDtypeStruct(gate_block, bf16), jax.ShapeDtypeStruct(proj_block, bf16)],
        in_specs=[near] * 5 + [anywhere] * 10,
        out_specs=[near] * 5 + [anywhere] * 9 + [near] * 2,
        scratch_shapes=[pltpu.VMEM((total, width), bf16)] * 2
        + [pltpu.VMEM((total, units), bf16)] * 3
        + [pltpu.VMEM((units, width), bf16)] * 3
        + [
            pltpu.VMEM((rows, width), bf16),
            pltpu.VMEM((2, rows, units), bf16),
            pltpu.VMEM((total, width), bf16),
            pltpu.VMEM((steps + 4, rows // 4, width), bf16),
            pltpu.VMEM((units // 2, total), bf16),
            pltpu.VMEM(half, bf16),
            pltpu.VMEM(half, bf16),
            pltpu.VMEM(half, bf16),
            pltpu.VMEM((rows, width), bf16),
            pltpu.VMEM((width, per_layer), bf16),
            pltpu.VMEM(pl_proj.shape, bf16),
        ]
        + block_scratch(gate_block)
        + block_scratch(proj_block)
        + [pltpu.SemaphoreType.DMA((14,)), pltpu.SemaphoreType.DMA((2,))]
        + [pltpu.SemaphoreType.DMA((count,)) for count in counts for unused_side in range(2)],
        compiler_params=pltpu.CompilerParams(
            collective_id=number, has_side_effects=True, vmem_limit_bytes=VMEM_BYTES
        ),
    )(*local, gains, small, pl_proj, *arrays, *weights)


def head_back(grad, raw, gain, cosine, sine):
    half = raw.shape[1] // 2
    first, second = grad[:, :half], grad[:, half:]
    turned = jnp.concatenate(
        [first * cosine + second * sine, second * cosine - first * sine], axis=1
    )
    root = lax.rsqrt(jnp.mean(raw * raw, axis=1, keepdims=True) + EPS)
    gain_grad = jnp.sum(turned * raw * root, axis=0, keepdims=True)
    turned = turned * gain
    along = jnp.mean(turned * raw, axis=1, keepdims=True)
    return (root * turned - raw * (root * root * root * along), gain_grad)


def attention_back_kernel(
    hidden_ref,
    first_ref,
    d_ffwin_ref,
    d_second_ref,
    branch_ref,
    low_rank_ref,
    left_low_ref,
    gains_ref,
    ffw_gains_ref,
    o_any,
    q_any,
    k_any,
    v_any,
    att_any,
    probs_any,
    normed_any,
    weights_any,
    q_raw_any,
    k_raw_any,
    cosine_any,
    sine_any,
    small_any,
    pl_gate_ref,
    pl_proj_ref,
    own_down,
    far_down,
    own_gate,
    own_up,
    source_ref,
    owned_any,
    early_any,
    pl_proj_all,
    gain_sums,
    total_down,
    total_gate,
    total_up,
    far_rest,
    o_proj,
    q_low,
    k_low,
    v_low,
    att,
    probs,
    normed,
    weights,
    q_raw,
    k_raw,
    cosine,
    sine,
    d_all,
    block,
    att_block,
    q_block,
    dq_block,
    d_q,
    d_k,
    d_v,
    d_qkv,
    turned,
    part,
    held,
    blocks,
    folded,
    far,
    near_sum,
    key_held,
    o_grad,
    o_folded,
    o_far,
    sum_own,
    sum_far,
    own_ref,
    laurel,
    d_low_rank,
    d_scaled,
    sum_ref,
    gain_rows,
    gain_parts,
    gain_landed,
    gain_totals,
    owned_ref,
    early_ref,
    load_sems,
    final_sems,
    *sems,
):
    pairs = [sems[i : i + 2] for i in range(0, len(sems), 2)]
    ring_sems, sum_sems, fold_sems, far_sems, swap_sems, key_sems = pairs[:6]
    mirror_sems, early_sems, o_fold_sems, o_far_sems, cross_sems, total_sems, proj_sems = pairs[6:13]
    gain_sems, twin_sems, units_sems = pairs[13:]
    rows, width = own_ref.shape
    total_rows = rows * HEADS
    half = rows // 2
    piece = rows // 4
    index = lax.axis_index("fsdp")
    chip, core, sibling, across = neighbours()
    place = ring_place(index)
    ends = ring_ends(place)
    others = [lax.rem(index + step, HEADS) for step in range(1, HEADS)]
    quarter = 2 * chip + core
    quarter_rows = blocks.shape[2]
    own_rows = span(quarter * quarter_rows, quarter_rows)
    other_rows = span((2 * (1 - chip) + core) * quarter_rows, quarter_rows)
    groups = HEADS // KV_HEADS
    scale = HEAD_DIM ** (-0.5)
    head_columns = 3 * HEAD_DIM
    loads = start_loads(
        (
            (o_any, o_proj),
            (q_any, q_low),
            (k_any, k_low),
            (v_any, v_low),
            (att_any, att),
            (probs_any, probs),
            (q_raw_any, q_raw),
            (k_raw_any, k_raw),
            (cosine_any, cosine),
            (sine_any, sine),
            (weights_any, weights),
            (normed_any, normed),
            (small_any.at[:, span(small_any.shape[1] - laurel.shape[1], laurel.shape[1])], laurel),
        ),
        load_sems,
    )
    rep = lax.axis_index("rep")
    twins = [lax.rem(rep + step, QUARTERS) for step in range(1, QUARTERS)]
    greet([{"fsdp": other} for other in others] + [{"rep": twin} for twin in twins])
    late_rows = far_rest.shape[0]
    early_rows = own_down.shape[0] - late_rows
    late = pl.ds(early_rows, late_rows)
    part_rows = own_gate.shape[0]
    unit_rows = span(quarter * part_rows, part_rows)
    other_unit_rows = span((2 * (1 - chip) + core) * part_rows, part_rows)
    units = Mirror(2, units_sems)
    units.give(0, total_gate.at[unit_rows], own_gate)
    crossings = [remote(own_down.at[late], far_rest, cross_sems, 0, across)]
    units.give(1, total_up.at[unit_rows], own_up)
    placed = start_loads(
        ((own_gate, total_gate.at[unit_rows]), (own_up, total_up.at[unit_rows])),
        final_sems.at[pl.ds(5, 2)],
    )
    ring = Ring(
        place,
        ends,
        4,
        ring_sems,
        lambda lane: own_ref.at[pl.ds(lane_offset(lane, rows), piece)],
        lambda owner, lane: d_all.at[span(owner * rows + lane_offset(lane, rows), piece)],
    )
    sums = RingSum(
        place,
        ends,
        4,
        sum_sems,
        held,
        lambda owner, lane: part[pl.ds(lane_offset(lane, rows), piece), :],
    )
    key_tiles = total_rows // TILE
    rank = laurel.shape[1] // 2

    def before(tile):
        grad, part_sum = norm_pull(first_ref[tile, :], gains_ref[3:4, :], d_ffwin_ref[tile, :])
        gain_rows[3:4, :] += part_sum
        scaled = (d_second_ref[tile, :] + grad) * HALF_ROOT
        d_scaled[tile, :] = scaled
        grad, part_sum = norm_pull(branch_ref[tile, :], gains_ref[1:2, :], scaled)
        gain_rows[1:2, :] += part_sum
        own_ref[tile, :] = low(grad)
        grad, part_sum = norm_pull(low_rank_ref[tile, :], gains_ref[2:3, :], scaled)
        gain_rows[2:3, :] += part_sum
        d_low_rank[tile, :] = low(grad)

    def low_rank_grads():
        d_left = low(dot(d_low_rank[...], laurel[...])[:, rank:])
        source = hidden_ref[...].astype(jnp.float32)
        block[...] = low(source * root_of(source) * gains_ref[0:1, :])
        shard = width // HEADS
        for owner in range(HEADS):
            columns = slice(owner * shard, (owner + 1) * shard)
            value = jnp.concatenate(
                [
                    dot(block[:, columns].T, d_left),
                    dot(d_low_rank[:, columns].T, left_low_ref[...]),
                ],
                axis=1,
            )
            value = low(value)
            for step in range(QUARTERS):
                blocks[owner, step, :, head_columns:] = value[
                    step * quarter_rows : (step + 1) * quarter_rows
                ]
        return d_left

    def after(tile):
        grad = d_scaled[tile, :] + sum_ref[tile, :]
        grad, part_sum = norm_pull(
            hidden_ref[tile, :].astype(jnp.float32), gains_ref[0:1, :], grad
        )
        gain_rows[0:1, :] += part_sum
        source_ref[tile, :] = low(d_scaled[tile, :] + grad)

    def compute(step):
        pair = Pair(place, step, rows)
        block[...] = pair.read(d_all)
        d_att = low(mul_t(block[...], o_proj[...]))
        att_block[...] = d_att
        q_block[...] = pair.read(q_low)
        delta = jnp.sum(
            d_att.astype(jnp.float32) * pair.read(att).astype(jnp.float32), axis=1, keepdims=True
        )
        dq_block[...] = jnp.zeros_like(dq_block)

        def keys(tile):
            chance = pair.read(probs, tile)
            d_chance = mul_t(att_block[...], v_low[tile, :])
            d_score = low(chance.astype(jnp.float32) * (d_chance - delta) * scale)
            dq_block[...] += dot(d_score, k_low[tile, :])
            d_k[tile, :] += dot(d_score.T, q_block[...])
            d_v[tile, :] += dot(chance.T, att_block[...])

        tile_loop(key_tiles, TILE, keys)
        pair.write(d_q, slice(None), dq_block[...])

    half_units = own_down.shape[0]
    final_loads, final_sends = [], []

    def load_final():
        crossings[0].wait_recv()
        early_part = pl.ds(0, early_rows)
        final_loads.extend(
            start_loads(
                (
                    (own_down, sum_own),
                    (far_down.at[early_part], sum_far.at[early_part]),
                    (far_rest, sum_far.at[late]),
                ),
                final_sems.at[pl.ds(0, 3)],
            )
        )

    def add_final():
        for copy in final_loads:
            copy.wait()

        def add(tile):
            sum_own[tile, :] = add_low(sum_own[tile, :], sum_far[tile, :])

        tile_loop(half_units // 64, 64, add)
        target = total_down.at[span(core * half_units, half_units)]
        final_sends.append(remote(sum_own, target, total_sems, 0, sibling))
        final_loads.extend(start_loads(((sum_own, target),), final_sems.at[pl.ds(0, 1)]))

    d_k[...] = jnp.zeros_like(d_k)
    d_v[...] = jnp.zeros_like(d_v)
    gain_rows[...] = jnp.zeros_like(gain_rows)
    tile_loop(rows // 32, 32, before)
    ring.send(0)
    d_all[span(index * rows, rows), :] = own_ref[...]
    loads[12].wait()
    d_left = low_rank_grads()
    for copy in loads[:6]:
        copy.wait()
    compute(0)
    for step in range(1, HEADS):
        if step < RING_STEPS:
            ring.send(step)
        else:
            ring.arrive(step)
        compute(step)
        if step == 6:
            units.relay(0, total_gate.at[other_unit_rows])
    for copy in loads[6:12]:
        copy.wait()

    def raw_tile(tile):
        for side, (grad, raw) in enumerate(((d_q, q_raw), (d_k, k_raw))):
            value, gain_grad = head_back(
                grad[tile, :],
                raw[tile, :],
                gains_ref[6 + side : 7 + side, :HEAD_DIM],
                cosine[tile, :],
                sine[tile, :],
            )
            d_qkv[tile, side * HEAD_DIM : (side + 1) * HEAD_DIM] = low(value)
            gain_rows[6 + side : 7 + side, :HEAD_DIM] += gain_grad
        d_qkv[tile, 2 * HEAD_DIM :] = low(d_v[tile, :])

    tile_loop(total_rows // 128, 128, raw_tile)

    def owner_at(step, way):
        return ring_index(lax.rem(place + (step + 1 if way else HEADS - 1 - step), HEADS))

    def part_of(step):
        tops = [
            d_qkv[span(owner_at(step, way) * rows + way * half, half), :] for way in range(2)
        ]
        part[...] = mul_t(jnp.concatenate(tops, axis=0), weights[...])

    def head_grads(number, carry):
        turned[...] = normed[:, span(number * TILE, TILE)].T
        value = low(dot(turned[...], d_qkv[...]))
        for step in range(QUARTERS):
            blocks[number, step, :, :head_columns] = value[
                step * quarter_rows : (step + 1) * quarter_rows
            ]
        return carry

    def o_tile(tile):
        value = low(dot(turned[...], d_all[:, tile]))
        for step in range(QUARTERS):
            o_grad[step, :, tile] = value[step * quarter_rows : (step + 1) * quarter_rows]

    part_of(0)
    sums.send(0)
    lax.fori_loop(0, width // TILE, head_grads, 0)
    folds, o_folds, across_sends, swaps, key_swaps = [], [], [], [], []
    for side in range(2):
        folds.append(
            remote(blocks.at[:, 2 * side + 1 - core], folded.at[side], fold_sems, side, sibling)
        )
    part_of(1)
    sums.send(1)
    turned[...] = att[...].T
    tile_loop(width // (2 * TILE), 2 * TILE, o_tile)
    for side in range(2):
        o_folds.append(
            remote(o_grad.at[2 * side + 1 - core], o_folded.at[side], o_fold_sems, side, sibling)
        )
    mirror, early, pl_mirror = Mirror(1, mirror_sems), Mirror(1, early_sems), Mirror(1, proj_sems)
    wide = pl_proj_ref.shape[1]
    own_columns = span(quarter * wide, wide)
    other_columns = span((2 * (1 - chip) + core) * wide, wide)
    rest = blocks.shape[3] - HEAD_DIM
    q_columns = HEADS * HEAD_DIM
    mine, yours = 2 * chip + core, 2 * (1 - chip) + core

    def fold_step():
        for side in range(2):
            folds[side].wait_recv()
            o_folds[side].wait_recv()
        for number in range(HEADS):
            blocks[number, yours] = add_low(blocks[number, yours], folded[1 - chip, number])
        across_sends.append(remote(blocks.at[:, yours], far, far_sems, 0, across))
        o_grad[yours] = add_low(o_grad[yours], o_folded[1 - chip])
        across_sends.append(remote(o_grad.at[yours], o_far, o_far_sems, 0, across))
        for number in range(HEADS):
            blocks[number, mine] = add_low(blocks[number, mine], folded[chip, number])
        o_grad[mine] = add_low(o_grad[mine], o_folded[chip])

    def swap_step():
        across_sends[0].wait_recv()
        for number in range(HEADS):
            near_sum[number] = add_low(blocks[number, mine], far[number])
        here = span(index * HEAD_DIM, HEAD_DIM)
        for step, other in enumerate(others):
            swaps.append(
                remote(
                    near_sum.at[other, :, pl.ds(0, HEAD_DIM)],
                    owned_ref.at[own_rows, here],
                    swap_sems,
                    step,
                    {"fsdp": other},
                )
            )
            key_swaps.append(
                remote(
                    near_sum.at[other, :, pl.ds(HEAD_DIM, rest)],
                    key_held.at[index],
                    key_sems,
                    step,
                    {"fsdp": other},
                )
            )
        owned_ref[own_rows, here] = near_sum[index, :, :HEAD_DIM]
        key_held[index] = near_sum[index, :, HEAD_DIM:]
        across_sends[1].wait_recv()
        early_ref[own_rows, :width] = add_low(o_grad[mine], o_far[...])
        early_ref[own_rows, width:] = pl_gate_ref[...]
        early.give(0, early_ref.at[own_rows])
        pl_proj_all[:, own_columns] = pl_proj_ref[...]
        pl_mirror.give(0, pl_proj_all.at[:, own_columns])

    for step in range(2, RING_STEPS):
        part_of(step)
        sums.send(step)
        if step == 2:
            fold_step()
        if step == 3:
            load_final()
        if step == 4:
            swap_step()
        if step == 5:
            units.relay(1, total_up.at[other_unit_rows])
            add_final()
        if step == 6:
            early.relay(0, early_ref.at[other_rows])
            pl_mirror.relay(0, pl_proj_all.at[:, other_columns])
    part[...] = mul_t(d_qkv[span(index * rows, rows), :], weights[...])
    for lane in range(4):
        sum_ref[pl.ds(lane_offset(lane, rows), piece), :] = sums.last(index, lane)
    for copy in swaps + key_swaps:
        copy.wait_recv()
    for head in range(KV_HEADS):
        total = key_held[head * groups].astype(jnp.float32)
        for step in range(1, groups):
            total = total + key_held[head * groups + step].astype(jnp.float32)
        total = low(total)
        for side in range(2):
            base = q_columns + (side * KV_HEADS + head) * HEAD_DIM
            owned_ref[own_rows, pl.ds(base, HEAD_DIM)] = total[
                :, side * HEAD_DIM : (side + 1) * HEAD_DIM
            ]
    extra = key_held[0, :, 2 * HEAD_DIM :].astype(jnp.float32)
    for step in range(1, HEADS):
        extra = extra + key_held[step, :, 2 * HEAD_DIM :].astype(jnp.float32)
    base = q_columns + 2 * KV_HEADS * HEAD_DIM
    owned_ref[own_rows, pl.ds(base, rest - 2 * HEAD_DIM)] = low(extra)
    mirror.give(0, owned_ref.at[own_rows])
    sum_ref[...] += mul_t(d_left, laurel[:, :rank])
    tile_loop(rows // 32, 32, after)
    gain_rows[4:6, :] = ffw_gains_ref[...]
    shard = width // HEADS
    for owner in range(HEADS):
        gain_parts[owner, :6] = gain_rows[:6, owner * shard : (owner + 1) * shard]
        gain_parts[owner, 6:] = gain_rows[6:, :HEAD_DIM]
    gain_sends = [
        remote(gain_parts.at[other], gain_landed.at[index], gain_sems, step, {"fsdp": other})
        for step, other in enumerate(others)
    ]
    gain_landed[index] = gain_parts[index]
    for copy in gain_sends:
        copy.wait_recv()
    total = gain_landed[0]
    for step in range(1, HEADS):
        total = total + gain_landed[step]
    gain_totals[rep] = total
    twin_sends = [
        remote(gain_totals.at[rep], gain_totals.at[rep], twin_sems, step, {"rep": twin})
        for step, twin in enumerate(twins)
    ]
    mirror.relay(0, owned_ref.at[other_rows])
    for copy in twin_sends:
        copy.wait_recv()
    total = gain_totals[0]
    for step in range(1, QUARTERS):
        total = total + gain_totals[step]
    gain_sums[...] = total
    units.finish()
    early.finish()
    leaving = start_loads(((early_ref, early_any),), final_sems.at[pl.ds(3, 1)])
    mirror.finish()
    leaving += start_loads(((owned_ref, owned_any),), final_sems.at[pl.ds(4, 1)])
    pl_mirror.finish()
    ring.sent()
    sums.sent()
    for copy in (
        folds + o_folds + across_sends + swaps + key_swaps + crossings + gain_sends + twin_sends
    ):
        copy.wait_send()
    final_loads[3].wait()
    for copy in final_sends:
        copy.wait()
    for copy in leaving + placed:
        copy.wait()


def attention_back(local, arrays, small, pl_sums, chip_grads, far_down, number):
    rows, width = local[0].shape
    total = rows * HEADS
    shard = width // HEADS
    quarter = shard // QUARTERS
    steps = 4 * RING_STEPS
    pl_gate, pl_proj = pl_sums
    laurel = 2 * local[6].shape[1]
    columns = 3 * HEAD_DIM + laurel
    half = chip_grads[0].shape
    near, anywhere = pl.BlockSpec(memory_space=pltpu.VMEM), pl.BlockSpec(memory_space=pltpu.HBM)
    bf16, f32 = jnp.bfloat16, jnp.float32
    owned = (HEADS + 2 * KV_HEADS) * HEAD_DIM + laurel
    counts = [steps, steps, 2, 1, HEADS - 1, HEADS - 1, 3, 3, 2, 1, 1, 1, 3]
    counts += [HEADS - 1, QUARTERS - 1, 6]
    down, gate, up = chip_grads
    whole = jax.ShapeDtypeStruct((2 * half[0], half[1]), bf16)
    return pl.pallas_call(
        attention_back_kernel,
        out_shape=[
            jax.ShapeDtypeStruct((rows, width), bf16),
            jax.ShapeDtypeStruct((shard, owned), bf16),
            jax.ShapeDtypeStruct((shard, width + pl_gate.shape[1]), bf16),
            jax.ShapeDtypeStruct((pl_proj.shape[0], width), bf16),
            jax.ShapeDtypeStruct((8, shard), f32),
            whole,
            whole,
            whole,
            jax.ShapeDtypeStruct((half[0] // 4, half[1]), bf16),
        ],
        in_specs=[near] * len(local) + [anywhere] * (len(arrays) + 1) + [near] * 2 + [anywhere] * 4,
        out_specs=[near] + [anywhere] * 2 + [near] * 2 + [anywhere] * 4,
        scratch_shapes=[pltpu.VMEM(item.shape, item.dtype) for item in arrays]
        + [
            pltpu.VMEM((total, width), bf16),
            pltpu.VMEM((rows, width), bf16),
            pltpu.VMEM((rows, HEAD_DIM), bf16),
            pltpu.VMEM((rows, HEAD_DIM), bf16),
            pltpu.VMEM((rows, HEAD_DIM), f32),
            pltpu.VMEM((total, HEAD_DIM), f32),
            pltpu.VMEM((total, HEAD_DIM), f32),
            pltpu.VMEM((total, HEAD_DIM), f32),
            pltpu.VMEM((total, 3 * HEAD_DIM), bf16),
            pltpu.VMEM((HEAD_DIM, total), bf16),
            pltpu.VMEM((rows, width), f32),
            pltpu.VMEM((steps + 4, rows // 4, width), bf16),
            pltpu.VMEM((HEADS, QUARTERS, quarter, columns), bf16),
            pltpu.VMEM((2, HEADS, quarter, columns), bf16),
            pltpu.VMEM((HEADS, quarter, columns), bf16),
            pltpu.VMEM((HEADS, quarter, columns), bf16),
            pltpu.VMEM((HEADS, quarter, columns - HEAD_DIM), bf16),
            pltpu.VMEM((QUARTERS, quarter, width), bf16),
            pltpu.VMEM((2, quarter, width), bf16),
            pltpu.VMEM((quarter, width), bf16),
            pltpu.VMEM(half, bf16),
            pltpu.VMEM(half, bf16),
            pltpu.VMEM((rows, width), bf16),
            pltpu.VMEM((width, laurel), bf16),
            pltpu.VMEM((rows, width), bf16),
            pltpu.VMEM((rows, width), f32),
            pltpu.VMEM((rows, width), f32),
            pltpu.VMEM((8, width), f32),
            pltpu.VMEM((HEADS, 8, shard), f32),
            pltpu.VMEM((HEADS, 8, shard), f32),
            pltpu.VMEM((QUARTERS, 8, shard), f32),
            pltpu.VMEM((shard, owned), bf16),
            pltpu.VMEM((shard, width + pl_gate.shape[1]), bf16),
            pltpu.SemaphoreType.DMA((len(arrays) + 1,)),
            pltpu.SemaphoreType.DMA((7,)),
        ]
        + [pltpu.SemaphoreType.DMA((count,)) for count in counts for unused_side in range(2)],
        compiler_params=pltpu.CompilerParams(
            collective_id=number, has_side_effects=True, vmem_limit_bytes=VMEM_BYTES
        ),
    )(*local, *arrays, small, pl_gate, pl_proj, down, far_down, gate, up)


WRITE_STEPS = 8


def write_kernel(cuts, *refs):
    sources = refs[: len(cuts)]
    targets = iter(refs[len(cuts) :])
    for source, parts in zip(sources, cuts):
        for start, size in parts:
            target = next(targets)
            target[...] = source[:, start : start + size].astype(target.dtype)


def write_out(items):
    in_specs, out_specs, out_shape, cuts = [], [], [], []
    for array, parts in items:
        rows = array.shape[0] // WRITE_STEPS
        whole = rows % 16 != 0
        block_rows = array.shape[0] if whole else rows
        place = (lambda step: (0, 0)) if whole else (lambda step: (step, 0))
        in_specs.append(pl.BlockSpec((block_rows, array.shape[1]), place))
        cuts.append(tuple((start, size) for start, size, unused_dtype in parts))
        for unused_start, size, dtype in parts:
            out_specs.append(pl.BlockSpec((block_rows, size), place))
            out_shape.append(jax.ShapeDtypeStruct((array.shape[0], size), dtype))
    return pl.pallas_call(
        functools.partial(write_kernel, tuple(cuts)),
        grid=(WRITE_STEPS,),
        out_shape=out_shape,
        in_specs=in_specs,
        out_specs=out_specs,
        compiler_params=pltpu.CompilerParams(vmem_limit_bytes=VMEM_BYTES),
    )(*[array for array, unused_parts in items])


def head_plan(
    hidden_in,
    layer_input,
    out_grad,
    seg_lengths,
    seg_parents,
    attn_norm,
    q_proj,
    k_proj,
    v_proj,
    q_norm,
    k_norm,
    o_proj,
    attn_post_norm,
    laurel_left,
    laurel_right,
    laurel_norm,
    ffw_norm,
    gate_proj,
    up_proj,
    down_proj,
    ffw_post_norm,
    pl_gate,
    pl_proj,
    pl_post_norm,
):
    index = lax.axis_index("fsdp")
    rows, width = hidden_in.shape
    shard = width // HEADS
    total = rows * HEADS
    rank = laurel_left.shape[1]
    per_layer = pl_gate.shape[1]

    piece = HEAD_DIM // HEADS
    gains = (attn_norm, attn_post_norm, laurel_norm, ffw_norm, ffw_post_norm, pl_post_norm)
    segments = jnp.stack([seg_lengths[0], seg_parents[0]]).astype(jnp.float32)
    segments = jnp.pad(segments, ((0, 6), (0, 128 - segments.shape[1])))
    (
        branch,
        wide_gains,
        small_all,
        full_plproj,
        normed_all,
        qkv_head,
        q_raw,
        k_raw,
        q_low,
        k_low,
        v_low,
        attended_low,
        probs_low,
        cosine,
        sine,
    ) = attention_forward(
        segments,
        gains + (q_norm, k_norm),
        seg_lengths.shape[1],
        hidden_in,
        q_proj,
        k_proj,
        v_proj,
        jnp.concatenate([pl_gate, laurel_left, laurel_right], axis=1),
        pl_proj,
        o_proj,
        0,
    )
    gain_anorm, gain_apost, gain_lnorm, gain_fnorm = wide_gains[:4]
    full_left = small_all[:, per_layer : per_layer + rank]
    full_right = small_all[:, per_layer + rank :]

    source = hidden_in.astype(jnp.float32)
    normed = norm_rows(source, gain_anorm)
    normed_low = low(normed)
    left_low = low(dot(normed_low, full_left))
    low_rank = mul_t(left_low, full_right)
    first_sum = (
        source + norm_rows(branch, gain_apost) + normed + norm_rows(low_rank, gain_lnorm)
    ) * HALF_ROOT
    ffw_low = low(norm_rows(first_sum, gain_fnorm))

    ffw_out, ffw_all, act, slope, inner_low, far_all = ffn_forward(
        ffw_low, gate_proj, up_proj, down_proj, 7
    )
    d_ffwin, result, d_extra, d_second, ffw_gains, *rest = ffn_back(
        (first_sum, ffw_out, layer_input, out_grad),
        wide_gains[4:6],
        small_all,
        full_plproj,
        (ffw_all, far_all, act, slope, inner_low),
        (gate_proj, up_proj, down_proj),
        9,
    )
    chip_grads, far_down, pl_sums = rest[:3], rest[3], rest[-2:]

    d_source, owned, early, sum_plproj, gain_sums, *totals = attention_back(
        (
            hidden_in,
            first_sum,
            d_ffwin,
            d_second,
            branch,
            low_rank,
            left_low,
            wide_gains,
            ffw_gains,
        ),
        (
            o_proj,
            q_low,
            k_low,
            v_low,
            attended_low,
            probs_low,
            normed_all,
            qkv_head,
            q_raw,
            k_raw,
            cosine,
            sine,
        ),
        small_all,
        pl_sums,
        chip_grads,
        far_down,
        12,
    )
    sum_anorm, sum_apost, sum_lnorm, sum_fnorm, sum_fpost, sum_plpost = gain_sums[:6]
    sum_qnorm, sum_knorm = [
        lax.dynamic_slice_in_dim(item, index * piece, piece) for item in gain_sums[6:]
    ]

    keys = KV_HEADS * HEAD_DIM
    value_at = width + keys
    left_at = value_at + keys
    f32, bf16 = jnp.float32, jnp.bfloat16
    (
        sum_down,
        sum_gate,
        sum_up,
        sum_q,
        sum_k,
        sum_v,
        sum_laurel,
        sum_o,
        sum_plgate,
        sum_plproj,
        result,
        d_source,
        d_extra,
    ) = write_out(
        [(item, ((0, width, f32),)) for item in totals[:3]]
        + [
            (
                owned,
                (
                    (0, width, f32),
                    (width, keys, f32),
                    (value_at, keys, f32),
                    (left_at, 2 * rank, f32),
                ),
            ),
            (early, ((0, width, f32), (width, per_layer, f32))),
            (sum_plproj, ((0, width, f32),)),
            (result, ((0, width, bf16),)),
            (d_source, ((0, width, bf16),)),
            (d_extra, ((0, per_layer, bf16),)),
        ]
    )
    return (
        result,
        d_source,
        d_extra,
        sum_anorm,
        sum_q,
        sum_k,
        sum_v,
        sum_qnorm,
        sum_knorm,
        sum_o,
        sum_apost,
        sum_laurel[:, :rank],
        sum_laurel[:, rank:],
        sum_lnorm,
        sum_fnorm,
        sum_gate,
        sum_up,
        sum_down,
        sum_fpost,
        sum_plgate,
        sum_plproj,
        sum_plpost,
    )


def gather_plan(
    hidden_in,
    layer_input,
    out_grad,
    seg_lengths,
    seg_parents,
    attn_norm,
    q_proj,
    k_proj,
    v_proj,
    q_norm,
    k_norm,
    o_proj,
    attn_post_norm,
    laurel_left,
    laurel_right,
    laurel_norm,
    ffw_norm,
    gate_proj,
    up_proj,
    down_proj,
    ffw_post_norm,
    pl_gate,
    pl_proj,
    pl_post_norm,
):
    shards = lax.axis_size("fsdp")
    rank_index = lax.axis_index("fsdp")
    rows = hidden_in.shape[0]
    total = rows * shards
    groups = HEADS // KV_HEADS
    scale = HEAD_DIM ** (-0.5)
    tokens, member, reach, position = tree_tables(seg_lengths[0], seg_parents[0], total)
    first_row = rank_index * rows
    my_tokens = first_row + jnp.arange(rows, dtype=jnp.int32)
    my_reach = lax.dynamic_slice_in_dim(reach, first_row, rows, 0)
    my_depth = lax.dynamic_slice_in_dim(position, first_row, rows, 0).astype(jnp.float32)
    seen = (jnp.dot(my_reach, member.T) > 0) & (tokens[None, :] <= my_tokens[:, None])
    (
        full_anorm,
        full_q,
        full_k,
        full_v,
        full_qnorm,
        full_knorm,
        full_o,
        full_apost,
        full_left,
        full_right,
        full_lnorm,
        full_fnorm,
        full_fpost,
        full_plgate,
        full_plproj,
        full_plpost,
    ) = (
        lax.all_gather(attn_norm, "fsdp", axis=0, tiled=True),
        lax.all_gather(q_proj, "fsdp", axis=0, tiled=True),
        lax.all_gather(k_proj, "fsdp", axis=0, tiled=True),
        lax.all_gather(v_proj, "fsdp", axis=0, tiled=True),
        lax.all_gather(q_norm, "fsdp", axis=0, tiled=True),
        lax.all_gather(k_norm, "fsdp", axis=0, tiled=True),
        lax.all_gather(o_proj, "fsdp", axis=0, tiled=True),
        lax.all_gather(attn_post_norm, "fsdp", axis=0, tiled=True),
        lax.all_gather(laurel_left, "fsdp", axis=0, tiled=True),
        lax.all_gather(laurel_right, "fsdp", axis=0, tiled=True),
        lax.all_gather(laurel_norm, "fsdp", axis=0, tiled=True),
        lax.all_gather(ffw_norm, "fsdp", axis=0, tiled=True),
        lax.all_gather(ffw_post_norm, "fsdp", axis=0, tiled=True),
        lax.all_gather(pl_gate, "fsdp", axis=0, tiled=True),
        lax.all_gather(pl_proj, "fsdp", axis=0, tiled=True),
        lax.all_gather(pl_post_norm, "fsdp", axis=0, tiled=True),
    )
    gain_anorm = full_anorm.astype(jnp.float32)
    gain_qnorm = full_qnorm.astype(jnp.float32)
    gain_knorm = full_knorm.astype(jnp.float32)
    gain_apost = full_apost.astype(jnp.float32)
    gain_lnorm = full_lnorm.astype(jnp.float32)
    gain_fnorm = full_fnorm.astype(jnp.float32)
    gain_fpost = full_fpost.astype(jnp.float32)
    gain_plpost = full_plpost.astype(jnp.float32)
    source = hidden_in.astype(jnp.float32)
    extra = layer_input.astype(jnp.float32)
    normed = norm_rows(source, gain_anorm)
    normed_low = normed.astype(jnp.bfloat16)
    q_raw = jnp.dot(normed_low, full_q, preferred_element_type=jnp.float32)
    k_raw = jnp.dot(normed_low, full_k, preferred_element_type=jnp.float32)
    v_raw = jnp.dot(normed_low, full_v, preferred_element_type=jnp.float32)

    def head_path(raw, gain):
        return rotate(norm_rows(raw.reshape(rows, -1, HEAD_DIM), gain), my_depth)

    q_low = head_path(q_raw, gain_qnorm).astype(jnp.bfloat16)
    k_low = head_path(k_raw, gain_knorm).reshape(rows, -1).astype(jnp.bfloat16)
    v_low = v_raw.astype(jnp.bfloat16)
    keys_all, values_all = (
        lax.all_gather(k_low, "fsdp", axis=0, tiled=True),
        lax.all_gather(v_low, "fsdp", axis=0, tiled=True),
    )
    keys_heads = keys_all.reshape(total, KV_HEADS, HEAD_DIM)
    values_heads = values_all.reshape(total, KV_HEADS, HEAD_DIM)
    query_groups = q_low.reshape(rows, KV_HEADS, groups, HEAD_DIM)
    mixed_list = []
    log_list = []
    for head in range(KV_HEADS):
        scores = (
            jnp.einsum(
                "tgd,nd->gtn",
                query_groups[:, head],
                keys_heads[:, head],
                preferred_element_type=jnp.float32,
            )
            * scale
        )
        scores = jnp.where(seen[None], scores, MASKED)
        top = jnp.max(scores, axis=-1, keepdims=True)
        expo = jnp.exp(scores - top)
        sums = jnp.sum(expo, axis=-1, keepdims=True)
        weights = (expo / sums).astype(jnp.bfloat16)
        mixed_list.append(
            jnp.einsum(
                "gtn,nd->tgd", weights, values_heads[:, head], preferred_element_type=jnp.float32
            )
        )
        log_list.append(top[..., 0] + jnp.log(sums[..., 0]))
    attended = jnp.stack(mixed_list, axis=1)
    log_sums = jnp.stack(log_list, axis=0)
    attended_low = attended.reshape(rows, -1).astype(jnp.bfloat16)
    branch = jnp.dot(attended_low, full_o, preferred_element_type=jnp.float32)
    left_low = jnp.dot(normed_low, full_left, preferred_element_type=jnp.float32).astype(
        jnp.bfloat16
    )
    low_rank = mul_t(left_low, full_right)
    first_sum = (
        source + norm_rows(branch, gain_apost) + normed + norm_rows(low_rank, gain_lnorm)
    ) * HALF_ROOT
    ffw_low = norm_rows(first_sum, gain_fnorm).astype(jnp.bfloat16)
    full_gate, full_up, full_down = (
        lax.all_gather(gate_proj, "fsdp", axis=0, tiled=True),
        lax.all_gather(up_proj, "fsdp", axis=0, tiled=True),
        lax.all_gather(down_proj, "fsdp", axis=0, tiled=True),
    )
    gate_val = mul_t(ffw_low, full_gate)
    up_val = mul_t(ffw_low, full_up)
    inner_low = gelu_mix(gate_val, up_val).astype(jnp.bfloat16)
    ffw_out = jnp.dot(inner_low, full_down, preferred_element_type=jnp.float32)
    second_sum = first_sum + norm_rows(ffw_out, gain_fpost)
    second_low = second_sum.astype(jnp.bfloat16)
    pl_pre = jnp.dot(second_low, full_plgate, preferred_element_type=jnp.float32)
    pl_mix = gelu_mix(pl_pre, extra).astype(jnp.bfloat16)
    pl_out = jnp.dot(pl_mix, full_plproj, preferred_element_type=jnp.float32)
    result = second_sum + norm_rows(pl_out, gain_plpost)
    seed = out_grad.astype(jnp.float32)
    d_plout, grad_plpost = norm_back(pl_out, gain_plpost, seed)
    d_plout_low = d_plout.astype(jnp.bfloat16)
    grad_plproj = outer(pl_mix, d_plout_low)
    d_mix = mul_t(d_plout_low, full_plproj)
    d_pre, d_extra = mix_back(pl_pre, extra, d_mix)
    d_pre_low = d_pre.astype(jnp.bfloat16)
    grad_plgate = outer(second_low, d_pre_low)
    d_second = seed + mul_t(d_pre_low, full_plgate)
    d_ffwout, grad_fpost = norm_back(ffw_out, gain_fpost, d_second)
    d_ffw_low = d_ffwout.astype(jnp.bfloat16)
    d_inner = mul_t(d_ffw_low, full_down)
    d_gate, d_up = mix_back(gate_val, up_val, d_inner)
    d_gate_low = d_gate.astype(jnp.bfloat16)
    d_up_low = d_up.astype(jnp.bfloat16)
    d_ffwin = jnp.dot(d_gate_low, full_gate, preferred_element_type=jnp.float32) + jnp.dot(
        d_up_low, full_up, preferred_element_type=jnp.float32
    )
    width = ffw_low.shape[1]
    gate_part = outer(d_gate_low, ffw_low)
    up_part = outer(d_up_low, ffw_low)
    down_part = outer(inner_low, d_ffw_low)
    stacked = lax.psum_scatter(
        jnp.concatenate([gate_part, up_part, down_part], axis=1).astype(jnp.bfloat16),
        "fsdp",
        scatter_dimension=0,
        tiled=True,
    ).astype(jnp.float32)
    grad_gate = stacked[:, :width]
    grad_up = stacked[:, width : 2 * width]
    grad_down = stacked[:, 2 * width :]
    d_first_part, grad_fnorm = norm_back(first_sum, gain_fnorm, d_ffwin)
    d_first = d_second + d_first_part
    d_scaled = d_first * HALF_ROOT
    d_branch, grad_apost = norm_back(branch, gain_apost, d_scaled)
    d_branch_low = d_branch.astype(jnp.bfloat16)
    d_lowrank, grad_lnorm = norm_back(low_rank, gain_lnorm, d_scaled)
    d_lowrank_low = d_lowrank.astype(jnp.bfloat16)
    grad_o = outer(attended_low, d_branch_low)
    d_att_low = mul_t(d_branch_low, full_o).astype(jnp.bfloat16)
    grad_right = outer(d_lowrank_low, left_low)
    d_left_low = jnp.dot(d_lowrank_low, full_right, preferred_element_type=jnp.float32).astype(
        jnp.bfloat16
    )
    grad_left = outer(normed_low, d_left_low)
    d_att_heads = d_att_low.reshape(rows, KV_HEADS, groups, HEAD_DIM)
    delta = jnp.sum(d_att_heads.astype(jnp.float32) * attended, axis=-1).transpose(1, 2, 0)
    block = 512
    count = total // block
    key_blocks = keys_heads.reshape(count, block, KV_HEADS, HEAD_DIM)
    value_blocks = values_heads.reshape(count, block, KV_HEADS, HEAD_DIM)
    seen_blocks = seen.reshape(rows, count, block).transpose(1, 0, 2)

    def key_step(d_query, item):
        keys, values, shown = item
        scores = (
            jnp.einsum("tkgd,nkd->kgtn", query_groups, keys, preferred_element_type=jnp.float32)
            * scale
        )
        scores = jnp.where(shown[None, None], scores, MASKED)
        probs = jnp.exp(scores - log_sums[..., None])
        d_probs = jnp.einsum(
            "tkgd,nkd->kgtn", d_att_heads, values, preferred_element_type=jnp.float32
        )
        d_scores = (probs * (d_probs - delta[..., None]) * scale).astype(jnp.bfloat16)
        d_query = d_query + jnp.einsum(
            "kgtn,nkd->tkgd", d_scores, keys, preferred_element_type=jnp.float32
        )
        d_keys = jnp.einsum(
            "kgtn,tkgd->nkd", d_scores, query_groups, preferred_element_type=jnp.float32
        )
        d_values = jnp.einsum(
            "kgtn,tkgd->nkd",
            probs.astype(jnp.bfloat16),
            d_att_heads,
            preferred_element_type=jnp.float32,
        )
        return (d_query, (d_keys, d_values))

    zero_query = jnp.zeros((rows, KV_HEADS, groups, HEAD_DIM), jnp.float32)
    d_query, (d_key_blocks, d_value_blocks) = lax.scan(
        key_step, zero_query, (key_blocks, value_blocks, seen_blocks)
    )
    my_dkeys, my_dvalues = (
        lax.psum_scatter(
            d_key_blocks.reshape(total, -1).astype(jnp.bfloat16),
            "fsdp",
            scatter_dimension=0,
            tiled=True,
        ).astype(jnp.float32),
        lax.psum_scatter(
            d_value_blocks.reshape(total, -1).astype(jnp.bfloat16),
            "fsdp",
            scatter_dimension=0,
            tiled=True,
        ).astype(jnp.float32),
    )
    unused_q, q_pull = jax.vjp(head_path, q_raw, gain_qnorm)
    d_qraw, grad_qnorm = q_pull(d_query.reshape(rows, HEADS, HEAD_DIM))
    unused_k, k_pull = jax.vjp(head_path, k_raw, gain_knorm)
    d_kraw, grad_knorm = k_pull(my_dkeys.reshape(rows, KV_HEADS, HEAD_DIM))
    d_q_low = d_qraw.astype(jnp.bfloat16)
    d_k_low = d_kraw.astype(jnp.bfloat16)
    d_v_low = my_dvalues.astype(jnp.bfloat16)
    grad_q = outer(normed_low, d_q_low)
    grad_k = outer(normed_low, d_k_low)
    grad_v = outer(normed_low, d_v_low)
    d_normed = (
        d_scaled
        + mul_t(d_q_low, full_q)
        + mul_t(d_k_low, full_k)
        + mul_t(d_v_low, full_v)
        + mul_t(d_left_low, full_left)
    )
    d_source_part, grad_anorm = norm_back(source, gain_anorm, d_normed)
    d_source = d_scaled + d_source_part
    shard_grads = (
        lax.psum_scatter(
            grad_anorm.astype(jnp.bfloat16), "fsdp", scatter_dimension=0, tiled=True
        ).astype(jnp.float32),
        lax.psum_scatter(
            grad_q.astype(jnp.bfloat16), "fsdp", scatter_dimension=0, tiled=True
        ).astype(jnp.float32),
        lax.psum_scatter(
            grad_k.astype(jnp.bfloat16), "fsdp", scatter_dimension=0, tiled=True
        ).astype(jnp.float32),
        lax.psum_scatter(
            grad_v.astype(jnp.bfloat16), "fsdp", scatter_dimension=0, tiled=True
        ).astype(jnp.float32),
        lax.psum_scatter(
            grad_qnorm.astype(jnp.bfloat16), "fsdp", scatter_dimension=0, tiled=True
        ).astype(jnp.float32),
        lax.psum_scatter(
            grad_knorm.astype(jnp.bfloat16), "fsdp", scatter_dimension=0, tiled=True
        ).astype(jnp.float32),
        lax.psum_scatter(
            grad_o.astype(jnp.bfloat16), "fsdp", scatter_dimension=0, tiled=True
        ).astype(jnp.float32),
        lax.psum_scatter(
            grad_apost.astype(jnp.bfloat16), "fsdp", scatter_dimension=0, tiled=True
        ).astype(jnp.float32),
        lax.psum_scatter(
            grad_left.astype(jnp.bfloat16), "fsdp", scatter_dimension=0, tiled=True
        ).astype(jnp.float32),
        lax.psum_scatter(
            grad_right.astype(jnp.bfloat16), "fsdp", scatter_dimension=0, tiled=True
        ).astype(jnp.float32),
        lax.psum_scatter(
            grad_lnorm.astype(jnp.bfloat16), "fsdp", scatter_dimension=0, tiled=True
        ).astype(jnp.float32),
        lax.psum_scatter(
            grad_fnorm.astype(jnp.bfloat16), "fsdp", scatter_dimension=0, tiled=True
        ).astype(jnp.float32),
        lax.psum_scatter(
            grad_fpost.astype(jnp.bfloat16), "fsdp", scatter_dimension=0, tiled=True
        ).astype(jnp.float32),
        lax.psum_scatter(
            grad_plgate.astype(jnp.bfloat16), "fsdp", scatter_dimension=0, tiled=True
        ).astype(jnp.float32),
        lax.psum_scatter(
            grad_plproj.astype(jnp.bfloat16), "fsdp", scatter_dimension=0, tiled=True
        ).astype(jnp.float32),
        lax.psum_scatter(
            grad_plpost.astype(jnp.bfloat16), "fsdp", scatter_dimension=0, tiled=True
        ).astype(jnp.float32),
    )
    (
        sum_anorm,
        sum_q,
        sum_k,
        sum_v,
        sum_qnorm,
        sum_knorm,
        sum_o,
        sum_apost,
        sum_left,
        sum_right,
        sum_lnorm,
        sum_fnorm,
        sum_fpost,
        sum_plgate,
        sum_plproj,
        sum_plpost,
        sum_gate,
        sum_up,
        sum_down,
    ) = (
        lax.psum(shard_grads[0].astype(jnp.bfloat16), "rep").astype(jnp.float32),
        lax.psum(shard_grads[1].astype(jnp.bfloat16), "rep").astype(jnp.float32),
        lax.psum(shard_grads[2].astype(jnp.bfloat16), "rep").astype(jnp.float32),
        lax.psum(shard_grads[3].astype(jnp.bfloat16), "rep").astype(jnp.float32),
        lax.psum(shard_grads[4].astype(jnp.bfloat16), "rep").astype(jnp.float32),
        lax.psum(shard_grads[5].astype(jnp.bfloat16), "rep").astype(jnp.float32),
        lax.psum(shard_grads[6].astype(jnp.bfloat16), "rep").astype(jnp.float32),
        lax.psum(shard_grads[7].astype(jnp.bfloat16), "rep").astype(jnp.float32),
        lax.psum(shard_grads[8].astype(jnp.bfloat16), "rep").astype(jnp.float32),
        lax.psum(shard_grads[9].astype(jnp.bfloat16), "rep").astype(jnp.float32),
        lax.psum(shard_grads[10].astype(jnp.bfloat16), "rep").astype(jnp.float32),
        lax.psum(shard_grads[11].astype(jnp.bfloat16), "rep").astype(jnp.float32),
        lax.psum(shard_grads[12].astype(jnp.bfloat16), "rep").astype(jnp.float32),
        lax.psum(shard_grads[13].astype(jnp.bfloat16), "rep").astype(jnp.float32),
        lax.psum(shard_grads[14].astype(jnp.bfloat16), "rep").astype(jnp.float32),
        lax.psum(shard_grads[15].astype(jnp.bfloat16), "rep").astype(jnp.float32),
        lax.psum(grad_gate.astype(jnp.bfloat16), "rep").astype(jnp.float32),
        lax.psum(grad_up.astype(jnp.bfloat16), "rep").astype(jnp.float32),
        lax.psum(grad_down.astype(jnp.bfloat16), "rep").astype(jnp.float32),
    )
    return (
        result.astype(jnp.bfloat16),
        d_source.astype(jnp.bfloat16),
        d_extra.astype(jnp.bfloat16),
        sum_anorm,
        sum_q,
        sum_k,
        sum_v,
        sum_qnorm,
        sum_knorm,
        sum_o,
        sum_apost,
        sum_left,
        sum_right,
        sum_lnorm,
        sum_fnorm,
        sum_gate,
        sum_up,
        sum_down,
        sum_fpost,
        sum_plgate,
        sum_plproj,
        sum_plpost,
    )


def solution(mesh):
    placed = (
        P(("rep", "fsdp"), None),
        P(("rep", "fsdp"), None),
        P(("rep", "fsdp"), None),
        P("rep", None),
        P("rep", None),
        P("fsdp"),
        P("fsdp", None),
        P("fsdp", None),
        P("fsdp", None),
        P("fsdp"),
        P("fsdp"),
        P("fsdp", None),
        P("fsdp"),
        P("fsdp", None),
        P("fsdp", None),
        P("fsdp"),
        P("fsdp"),
        P("fsdp", None),
        P("fsdp", None),
        P("fsdp", None),
        P("fsdp"),
        P("fsdp", None),
        P("fsdp", None),
        P("fsdp"),
    )
    return jax.shard_map(
        head_plan if mesh.shape["fsdp"] == HEADS else gather_plan,
        mesh=mesh,
        in_specs=placed,
        out_specs=(
            P(("rep", "fsdp"), None),
            P(("rep", "fsdp"), None),
            P(("rep", "fsdp"), None),
            P("fsdp"),
            P("fsdp", None),
            P("fsdp", None),
            P("fsdp", None),
            P("fsdp"),
            P("fsdp"),
            P("fsdp", None),
            P("fsdp"),
            P("fsdp", None),
            P("fsdp", None),
            P("fsdp"),
            P("fsdp"),
            P("fsdp", None),
            P("fsdp", None),
            P("fsdp", None),
            P("fsdp"),
            P("fsdp", None),
            P("fsdp", None),
            P("fsdp"),
        ),
        check_vma=False,
    )
```

```python
import functools
import math

import jax
import jax.numpy as jnp
from jax import lax
from jax.experimental import pallas as pl
from jax.experimental.pallas import tpu as pltpu
from jax.sharding import PartitionSpec as P

HEADS = 8
KV_HEADS = 2
HEAD_DIM = 256


EPS = 1e-06
ROPE_BASE = 1000000.0
HALF_ROOT = 0.7071067811865476
MASKED = -1e30


def norm_rows(value, gain):
    return value * lax.rsqrt(jnp.mean(value * value, axis=-1, keepdims=True) + EPS) * gain


def norm_back(value, gain, grad):
    unused, pull = jax.vjp(norm_rows, value, gain)
    return pull(grad)


def rotate(value, position):
    half = value.shape[-1] // 2
    freqs = jnp.exp(
        jnp.arange(half, dtype=jnp.float32) * (-2.0 * math.log(ROPE_BASE) / value.shape[-1])
    )
    angle = position[:, None] * freqs[None, :]
    cosine = jnp.cos(angle)[:, None, :]
    sine = jnp.sin(angle)[:, None, :]
    first_half = value[..., :half]
    second_half = value[..., half:]
    return jnp.concatenate(
        [first_half * cosine - second_half * sine, second_half * cosine + first_half * sine],
        axis=-1,
    )


def tree_tables(lengths, parents, total):
    count = lengths.shape[0]
    labels = jnp.arange(count, dtype=jnp.int32)
    ends = jnp.cumsum(lengths)
    starts = ends - lengths
    tokens = jnp.arange(total, dtype=jnp.int32)
    segment = jnp.sum((ends[None, :] <= tokens[:, None]).astype(jnp.int32), axis=1)
    parent_hot = ((parents[:, None] == labels[None, :]) & (labels[:, None] > 0)).astype(jnp.int32)
    identity = (labels[:, None] == labels[None, :]).astype(jnp.int32)
    ancestors = lax.fori_loop(
        0, count, lambda step, held: jnp.minimum(1, identity + jnp.dot(parent_hot, held)), identity
    )
    offset = jnp.dot(ancestors - identity, lengths) - starts
    member = (segment[:, None] == labels[None, :]).astype(jnp.int32)
    reach = jnp.dot(member, ancestors)
    position = jnp.dot(member, offset) + tokens
    return (tokens, member, reach, position)


def outer(left, right):
    return lax.dot_general(
        left, right, (((0,), (0,)), ((), ())), preferred_element_type=jnp.float32
    )


def mul_t(left, right):
    return lax.dot_general(
        left, right, (((1,), (1,)), ((), ())), preferred_element_type=jnp.float32
    )


def gelu_mix(first, second):
    return jax.nn.gelu(first, approximate=True) * second


def mix_back(first, second, grad):
    unused, pull = jax.vjp(gelu_mix, first, second)
    return pull(grad)


MESH = pl.DeviceIdType.MESH
VMEM_BYTES = 58 << 20


def ring_place(index):
    side = lax.rem(index, 2)
    return index // 2 + side * (HEADS - 1 - 2 * (index // 2))


def ring_index(place):
    back = place // (HEADS // 2)
    return (1 - back) * 2 * place + back * (2 * HEADS - 1 - 2 * place)


def ring_ends(place):
    after = {"fsdp": ring_index(lax.rem(place + 1, HEADS))}
    before = {"fsdp": ring_index(lax.rem(place + HEADS - 1, HEADS))}
    return (after, before)


def announce(others):
    barrier = pltpu.get_barrier_semaphore()
    for other in others:
        pl.semaphore_signal(barrier, inc=1, device_id=other, device_id_type=MESH)


def await_all(others):
    pl.semaphore_wait(pltpu.get_barrier_semaphore(), len(others))


def greet(others):
    announce(others)
    await_all(others)


def span(start, size):
    return pl.ds(pl.multiple_of(start, size), size)


def neighbours():
    rep = lax.axis_index("rep")
    chip = rep // 2
    core = lax.rem(rep, 2)
    return (chip, core, {"rep": 2 * chip + 1 - core}, {"rep": 2 * (1 - chip) + core})


def remote(source, target, sems, number, device):
    copy = pltpu.make_async_remote_copy(
        source,
        target,
        sems[0].at[number],
        sems[1].at[number],
        device_id=device,
        device_id_type=MESH,
    )
    copy.start()
    return copy


class Ring:
    def __init__(self, place, ends, lanes, sems, own, there):
        self.place, self.ends, self.lanes, self.sems = place, ends, lanes, sems
        self.own, self.there = own, there
        self.copies = []

    def owner(self, step, lane):
        ahead = step if lane % 2 else HEADS - step
        return ring_index(lax.rem(self.place + ahead, HEADS))

    def send(self, step):
        for lane in range(self.lanes):
            number = step * self.lanes + lane
            target = self.there(self.owner(step, lane), lane)
            if step:
                self.copies[number - self.lanes].wait_recv()
            source = target if step else self.own(lane)
            self.copies.append(remote(source, target, self.sems, number, self.ends[lane % 2]))

    def arrive(self, step):
        for lane in range(self.lanes):
            self.copies[(step - 1) * self.lanes + lane].wait_recv()

    def sent(self):
        for copy in self.copies:
            copy.wait_send()


class Mirror:
    def __init__(self, count, sems):
        unused_chip, unused_core, self.sibling, self.across = neighbours()
        self.count, self.sems = count, sems
        self.copies = [None] * (3 * count)

    def give(self, number, ref, source=None):
        source = ref if source is None else source
        self.copies[number] = remote(source, ref, self.sems, number, self.sibling)
        self.copies[self.count + number] = remote(
            source, ref, self.sems, self.count + number, self.across
        )

    def relay(self, number, ref):
        self.copies[self.count + number].wait_recv()
        self.copies[2 * self.count + number] = remote(
            ref, ref, self.sems, 2 * self.count + number, self.sibling
        )

    def arrive(self):
        for number, copy in enumerate(self.copies):
            if number // self.count != 1:
                copy.wait_recv()

    def sent(self):
        for copy in self.copies:
            copy.wait_send()

    def finish(self):
        self.arrive()
        self.sent()


RING_STEPS = HEADS - 1
QUARTERS = 4


def dot(left, right):
    return jnp.dot(left, right, preferred_element_type=jnp.float32)


def low(value):
    return value.astype(jnp.bfloat16)


def add_low(left, right):
    return (left.astype(jnp.float32) + right.astype(jnp.float32)).astype(jnp.bfloat16)


class RingSum:
    def __init__(self, place, ends, lanes, sems, held, own):
        self.place, self.ends, self.lanes, self.sems = place, ends, lanes, sems
        self.held, self.own = held, own
        self.copies = []

    def send(self, step, lanes=None):
        for lane in lanes or range(self.lanes):
            ahead = step + 1 if lane % 2 else HEADS - 1 - step
            owner = ring_index(lax.rem(self.place + ahead, HEADS))
            number = step * self.lanes + lane
            if step:
                slot = number - self.lanes
                self.copies[slot].wait_recv()
                value = self.held[slot].astype(jnp.float32) + self.own(owner, lane)
            else:
                slot = RING_STEPS * self.lanes + lane
                value = self.own(owner, lane)
            self.held[slot] = value.astype(jnp.bfloat16)
            self.copies.append(
                remote(self.held.at[slot], self.held.at[number], self.sems, number, self.ends[lane % 2])
            )

    def last(self, index, lane):
        number = (RING_STEPS - 1) * self.lanes + lane
        self.copies[number].wait_recv()
        return self.held[number].astype(jnp.float32) + self.own(index, lane)

    def sent(self):
        for copy in self.copies:
            copy.wait_send()


def lane_offset(lane, rows):
    return (lane % 2) * (rows // 2) + (lane // 2) * (rows // 4)


def tile_loop(count, size, body):
    def step(number, carry):
        body(span(number * size, size))
        return carry

    lax.fori_loop(0, count, step, 0)


class Pair:
    def __init__(self, place, step, rows):
        half = rows // 2
        behind = ring_index(lax.rem(place + HEADS - step, HEADS))
        ahead = ring_index(lax.rem(place + step, HEADS))
        self.half = half
        self.rows = (span(behind * rows, half), span(ahead * rows + half, half))

    def read(self, ref, columns=slice(None)):
        return jnp.concatenate([ref[rows, columns] for rows in self.rows], axis=0)

    def write(self, ref, columns, value):
        for side, rows in enumerate(self.rows):
            ref[rows, columns] = value[side * self.half : (side + 1) * self.half]


GELU_ROOT = math.sqrt(2.0 / math.pi)
GELU_CUBE = 0.044715
TILE = 256


def start_loads(pairs, sems):
    copies = []
    for number, (source, target) in enumerate(pairs):
        copy = pltpu.make_async_copy(source, target, sems.at[number])
        copy.start()
        copies.append(copy)
    return copies


def root_of(value):
    return lax.rsqrt(jnp.mean(value * value, axis=1, keepdims=True) + EPS)


def norm_pull(value, gain, grad):
    root = root_of(value)
    gain_grad = jnp.sum(grad * value * root, axis=0, keepdims=True)
    grad = grad * gain
    along = jnp.mean(grad * value, axis=1, keepdims=True)
    return (root * grad - value * (root * root * root * along), gain_grad)


def gelu_parts(value):
    square = value * value
    bent = jnp.tanh(GELU_ROOT * value * (1.0 + GELU_CUBE * square))
    share = 0.5 * (1.0 + bent)
    slope = share + (0.5 * GELU_ROOT) * value * (1.0 - bent * bent) * (
        1.0 + (3.0 * GELU_CUBE) * square
    )
    return (value * share, slope)


def tree_tables_near(segments, count, tables):
    member, reach, cosine, sine = tables
    lengths, parents = segments[0:1, :], segments[1:2, :]
    size = lengths.shape[1]
    row = lax.broadcasted_iota(jnp.int32, (size, size), 0)
    column = lax.broadcasted_iota(jnp.int32, (size, size), 1)
    same = row == column

    def upright(value):
        return jnp.sum(jnp.where(same, value, 0.0), axis=1, keepdims=True)

    parent = upright(parents) == column.astype(jnp.float32)
    reached = jnp.where(same | (parent & (row > 0)), 1.0, 0.0)
    for unused_step in range((count - 1).bit_length()):
        reached = jnp.where(dot(low(reached), low(reached)) > 0.5, 1.0, 0.0)
    ends = jnp.sum(jnp.where(row <= column, upright(lengths), 0.0), axis=0, keepdims=True)
    starts = ends - lengths
    above = jnp.sum(jnp.where(same, 0.0, reached * lengths), axis=1, keepdims=True)
    offset = jnp.sum(jnp.where(same, above, 0.0), axis=0, keepdims=True) - starts
    reached = low(reached)
    half = cosine.shape[1]
    place = lax.broadcasted_iota(jnp.int32, (1, half), 1).astype(jnp.float32)
    freqs = jnp.exp(place * (-math.log(ROPE_BASE) / half))

    def token_tile(number, carry):
        tile = span(number * size, size)
        token = (row + number * size).astype(jnp.float32)
        inside = jnp.where((token >= starts) & (token < ends), 1.0, 0.0)
        position = jnp.sum(inside * offset, axis=1, keepdims=True) + token[:, :1]
        angle = position * freqs
        cosine[tile, :] = jnp.cos(angle)
        sine[tile, :] = jnp.sin(angle)
        member[tile, :] = low(inside)
        reach[tile, :] = low(dot(low(inside), reached))
        return carry

    lax.fori_loop(0, member.shape[0] // size, token_tile, 0)


def attention_kernel(
    count,
    segments_ref,
    norm_refs,
    hidden_ref,
    q_ref,
    k_ref,
    v_ref,
    small_ref,
    pl_proj_ref,
    o_any,
    sum_ref,
    gains_ref,
    small_all,
    pl_proj_all,
    normed_any,
    weights_any,
    q_raw_any,
    k_raw_any,
    q_low_any,
    k_low_any,
    v_low_any,
    att_any,
    probs_any,
    cosine_any,
    sine_any,
    normed,
    weights,
    q_raw,
    k_raw,
    q_low,
    k_low,
    v_low,
    att,
    probs,
    cosine,
    sine,
    hidden_all,
    kv_all,
    gains_all,
    packed_ref,
    norm_held,
    o_proj,
    member,
    reach,
    part,
    held,
    load_sems,
    store_sems,
    *sems,
):
    pairs = [sems[i : i + 2] for i in range(0, len(sems), 2)]
    hidden_sems, gains_sems, q_sems, kv_sems, small_sems, pl_proj_sems, sum_sems = pairs[:7]
    q_mirror_sems, kv_mirror_sems, small_mirror_sems, pl_proj_mirror_sems = pairs[7:]
    rows, width = hidden_ref.shape
    total_rows = rows * HEADS
    half = rows // 2
    piece = rows // 4
    shard = q_ref.shape[0]
    deep = pl_proj_ref.shape[0]
    q_rows = shard // QUARTERS
    shard_part = q_rows // 2
    wide = pl_proj_ref.shape[1] // QUARTERS
    wide_part = wide // 2
    index = lax.axis_index("fsdp")
    chip, core, sibling, across = neighbours()
    quarter, other_quarter = 2 * chip + core, 2 * (1 - chip) + core
    place = ring_place(index)
    ends = ring_ends(place)
    others = [lax.rem(index + step, HEADS) for step in range(1, HEADS)]
    own_shard = span(index * shard, shard)
    loads = start_loads(
        (
            (q_ref.at[:, span(index * HEAD_DIM, HEAD_DIM)], weights.at[own_shard, pl.ds(0, HEAD_DIM)]),
            (k_ref, kv_all.at[own_shard, pl.ds(0, k_ref.shape[1])]),
            (v_ref, kv_all.at[own_shard, pl.ds(k_ref.shape[1], v_ref.shape[1])]),
            (o_any, o_proj),
            (small_ref, small_all.at[own_shard]),
            (pl_proj_ref, pl_proj_all.at[span(index * deep, deep)]),
            (hidden_ref, hidden_all.at[span(index * rows, rows)]),
        ),
        load_sems,
    )
    norm_loads = start_loads(zip(norm_refs, norm_held), load_sems.at[pl.ds(9, len(norm_refs))])
    shard_lanes = lax.broadcasted_iota(jnp.int32, (1, shard), 1)
    few = shard // HEADS
    spread = jnp.where(
        lax.broadcasted_iota(jnp.int32, (few, shard), 0)
        == lax.rem(lax.broadcasted_iota(jnp.int32, (few, shard), 1), few),
        1.0,
        0.0,
    )
    for copy in norm_loads:
        copy.wait()
    for number, ref in enumerate(norm_held):
        value = ref[...].astype(jnp.float32).reshape(1, ref.shape[0])
        if ref.shape[0] != shard:
            value = jnp.sum(value.reshape(few, 1) * spread, axis=0, keepdims=True)
            value = jnp.where(shard_lanes // few == index, value, 0.0)
        packed_ref[number : number + 1, :] = value
    greet([{"fsdp": other} for other in others] + [sibling, across])
    gain_copies = [
        remote(packed_ref, gains_all.at[index], gains_sems, step, {"fsdp": other})
        for step, other in enumerate(others)
    ]

    def shard_at(ref, part_of):
        return lambda owner, lane: ref.at[
            span(owner * shard + part_of * q_rows + lane * shard_part, shard_part)
        ]

    def pl_proj_at(part_of):
        return lambda owner, lane: pl_proj_all.at[
            span(owner * deep, deep), span(part_of * wide + lane * wide_part, wide_part)
        ]

    def shard_own(ref):
        return lambda lane: ref.at[span(quarter * q_rows + lane * shard_part, shard_part)]

    hidden = Ring(
        place,
        ends,
        4,
        hidden_sems,
        lambda lane: hidden_ref.at[pl.ds(lane_offset(lane, rows), piece)],
        lambda owner, lane: hidden_all.at[span(owner * rows + lane_offset(lane, rows), piece)],
    )
    kv_at = shard_at(kv_all, quarter)
    kv = Ring(place, ends, 2, kv_sems, lambda lane: kv_at(index, lane), kv_at)
    small = Ring(place, ends, 2, small_sems, shard_own(small_ref), shard_at(small_all, quarter))
    pl_proj = Ring(
        place,
        ends,
        2,
        pl_proj_sems,
        lambda lane: pl_proj_ref.at[:, span(quarter * wide + lane * wide_part, wide_part)],
        pl_proj_at(quarter),
    )
    lanes = 2 * RING_STEPS
    kv_mirror = Mirror(lanes, kv_mirror_sems)
    q_mirror = Mirror(HEADS - 1, q_mirror_sems)
    late = (
        (small, Mirror(lanes, small_mirror_sems), shard_at(small_all, other_quarter)),
        (pl_proj, Mirror(lanes, pl_proj_mirror_sems), pl_proj_at(other_quarter)),
    )
    kv_other = shard_at(kv_all, other_quarter)

    def pass_on(ring, mirror, step):
        for lane in range(2):
            mirror.give((step - 1) * 2 + lane, ring.there(ring.owner(step, lane), lane))

    def pass_again(ring, mirror, there, step):
        for lane in range(2):
            mirror.relay((step - 1) * 2 + lane, there(ring.owner(step, lane), lane))

    def late_step(step):
        for ring, mirror, there in late:
            if step < RING_STEPS:
                ring.send(step)
            elif step == RING_STEPS:
                ring.arrive(step)
            if 1 <= step <= RING_STEPS:
                pass_on(ring, mirror, step)
            if step >= 2:
                pass_again(ring, mirror, there, step - 1)

    def q_at(step, part_of):
        giver = lax.rem(index + HEADS - 1 - step, HEADS)
        return weights.at[span(giver * shard + part_of * q_rows, q_rows), pl.ds(0, HEAD_DIM)]

    loads[1].wait()
    loads[2].wait()
    kv.send(0)
    q_landing = weights.at[span(index * shard + quarter * q_rows, q_rows), pl.ds(0, HEAD_DIM)]
    q_copies = [
        remote(
            q_ref.at[span(quarter * q_rows, q_rows), span(other * HEAD_DIM, HEAD_DIM)],
            q_landing,
            q_sems,
            step,
            {"fsdp": other},
        )
        for step, other in enumerate(others)
    ]
    hidden.send(0)
    gains_all[index] = packed_ref[...]
    tree_tables_near(segments_ref, count, (member, reach, cosine, sine))

    def project(step):
        pair = Pair(place, step, rows)
        source = pair.read(hidden_all).astype(jnp.float32)
        value = low(source * root_of(source) * gains_ref[0:1, :])
        pair.write(normed, slice(None), value)
        raw = dot(value, weights[...])
        cos_rows, sin_rows = pair.read(cosine), pair.read(sine)
        for side, (raw_ref, low_ref) in enumerate(((q_raw, q_low), (k_raw, k_low))):
            item = raw[:, side * HEAD_DIM : (side + 1) * HEAD_DIM]
            pair.write(raw_ref, slice(None), item)
            item = item * root_of(item) * gains_ref[6 + side : 7 + side, :HEAD_DIM]
            first, second = item[:, : HEAD_DIM // 2], item[:, HEAD_DIM // 2 :]
            turned = jnp.concatenate(
                [first * cos_rows - second * sin_rows, second * cos_rows + first * sin_rows],
                axis=1,
            )
            pair.write(low_ref, slice(None), low(turned))
        pair.write(v_low, slice(None), low(raw[:, 2 * HEAD_DIM :]))

    for step in range(1, RING_STEPS):
        if step <= 3:
            for kv_step in (2 * step - 1, 2 * step):
                kv.send(kv_step)
                pass_on(kv, kv_mirror, kv_step)
        hidden.send(step)
        if step in (2, 3):
            for kv_step in (2 * step - 3, 2 * step - 2):
                pass_again(kv, kv_mirror, kv_other, kv_step)
        if step == 2:
            for number, copy in enumerate(q_copies):
                copy.wait_recv()
                q_mirror.give(number, q_at(number, quarter))
        if step == 3:
            for number in range(HEADS - 1):
                q_mirror.relay(number, q_at(number, other_quarter))
        if step == 4:
            kv.arrive(RING_STEPS)
            pass_on(kv, kv_mirror, RING_STEPS)
            for kv_step in (5, 6, 7):
                pass_again(kv, kv_mirror, kv_other, kv_step)
            for copy in gain_copies:
                copy.wait_recv()
            for owner in range(HEADS):
                gains_ref[:, owner * shard : (owner + 1) * shard] = gains_all[owner]
            total = gains_all[0, 6:, :]
            for owner in range(1, HEADS):
                total = total + gains_all[owner, 6:, :]
            gains_ref[6:, :shard] = total
        if step == 5:
            late_step(0)
            kv_mirror.arrive()
            q_mirror.arrive()
            loads[0].wait()
            loads[6].wait()
            key_at = (index // (HEADS // KV_HEADS)) * HEAD_DIM
            turns = start_loads(
                [
                    (
                        kv_all.at[:, span(key_at + side * KV_HEADS * HEAD_DIM, HEAD_DIM)],
                        weights.at[:, pl.ds((1 + side) * HEAD_DIM, HEAD_DIM)],
                    )
                    for side in range(2)
                ],
                load_sems.at[pl.ds(7, 2)],
            )
            for copy in turns:
                copy.wait()
            for number in range(3):
                project(number)
        if step == 6:
            late_step(1)
            for number in range(3, 6):
                project(number)
    late_step(2)
    project(6)
    hidden.arrive(RING_STEPS)
    project(7)
    stores = start_loads(
        (
            (normed, normed_any),
            (weights, weights_any),
            (q_raw, q_raw_any),
            (k_raw, k_raw_any),
            (q_low, q_low_any),
            (k_low, k_low_any),
            (v_low, v_low_any),
            (cosine, cosine_any),
            (sine, sine_any),
        ),
        store_sems,
    )
    loads[3].wait()
    scale = HEAD_DIM ** (-0.5)

    def attend(first_owner, second_owner):
        starts = (first_owner * rows, second_owner * rows + half)
        spans = [span(start, half) for start in starts]

        def read(ref):
            return jnp.concatenate([ref[rows_of, :] for rows_of in spans], axis=0)

        query = lax.broadcasted_iota(jnp.int32, (half, total_rows), 0)
        query = jnp.concatenate([query + start for start in starts], axis=0)
        key = lax.broadcasted_iota(jnp.int32, (rows, total_rows), 1)
        scores = mul_t(read(q_low), k_low[...]) * scale
        seen = (mul_t(read(reach), member[...]) > 0.5) & (key <= query)
        scores = jnp.where(seen, scores, MASKED)
        expo = jnp.exp(scores - jnp.max(scores, axis=1, keepdims=True))
        chance = low(expo / jnp.sum(expo, axis=1, keepdims=True))
        mixed = low(dot(chance, v_low[...]))
        for side, rows_of in enumerate(spans):
            probs[rows_of, :] = chance[side * half : (side + 1) * half]
            att[rows_of, :] = mixed[side * half : (side + 1) * half]
        part[...] = dot(mixed, o_proj[...])

    sums = RingSum(
        place,
        ends,
        4,
        sum_sems,
        held,
        lambda owner, lane: part[pl.ds(lane_offset(lane, rows), piece), :],
    )
    for step in range(RING_STEPS):
        attend(
            ring_index(lax.rem(place + HEADS - 1 - step, HEADS)),
            ring_index(lax.rem(place + step + 1, HEADS)),
        )
        sums.send(step)
        if step + 3 <= HEADS:
            late_step(step + 3)
    attend(index, index)
    stores += start_loads(((att, att_any), (probs, probs_any)), store_sems.at[pl.ds(9, 2)])
    for lane in range(4):
        sum_ref[pl.ds(lane_offset(lane, rows), piece), :] = sums.last(index, lane)
    for item in (hidden, kv, small, pl_proj, sums, kv_mirror, q_mirror):
        item.sent()
    for unused_ring, mirror, unused_there in late:
        mirror.finish()
    for copy in q_copies + gain_copies:
        copy.wait_send()
    for copy in loads[4:6] + stores:
        copy.wait()


def attention_forward(
    segments, norms, count, hidden, q_proj, k_proj, v_proj, small, pl_proj, o_proj, number
):
    rows, width = hidden.shape
    total = rows * HEADS
    shard = q_proj.shape[0]
    steps = 4 * RING_STEPS
    near, anywhere = pl.BlockSpec(memory_space=pltpu.VMEM), pl.BlockSpec(memory_space=pltpu.HBM)
    bf16, f32 = jnp.bfloat16, jnp.float32
    head = (total, HEAD_DIM)
    table = (total, HEAD_DIM // 2)
    kept = [
        ((total, width), bf16),
        ((width, 3 * HEAD_DIM), bf16),
        (head, f32),
        (head, f32),
        (head, bf16),
        (head, bf16),
        (head, bf16),
        (head, bf16),
        ((total, total), bf16),
        (table, f32),
        (table, f32),
    ]
    grown = [((shard * HEADS, small.shape[1]), bf16), ((pl_proj.shape[0] * HEADS, width), bf16)]
    low_steps = 2 * RING_STEPS
    counts = [steps, HEADS - 1, HEADS - 1] + [low_steps] * 3 + [steps]
    counts += [3 * (HEADS - 1)] + [3 * low_steps] * 3
    return pl.pallas_call(
        functools.partial(attention_kernel, count),
        out_shape=[
            jax.ShapeDtypeStruct((rows, width), f32),
            jax.ShapeDtypeStruct((8, width), f32),
        ]
        + [jax.ShapeDtypeStruct(shape, dtype) for shape, dtype in grown + kept],
        in_specs=[near, (anywhere,) * len(norms)] + [anywhere] * 7,
        out_specs=[near] * 2 + [anywhere] * (len(grown) + len(kept)),
        scratch_shapes=[pltpu.VMEM(shape, dtype) for shape, dtype in kept]
        + [
            pltpu.VMEM((total, width), bf16),
            pltpu.VMEM((width, 2 * k_proj.shape[1]), bf16),
            pltpu.VMEM((HEADS, 8, shard), f32),
            pltpu.VMEM((8, shard), f32),
            tuple(pltpu.VMEM(item.shape, bf16) for item in norms),
            pltpu.VMEM(o_proj.shape, bf16),
            pltpu.VMEM((total, segments.shape[1]), bf16),
            pltpu.VMEM((total, segments.shape[1]), bf16),
            pltpu.VMEM((rows, width), f32),
            pltpu.VMEM((steps + 4, rows // 4, width), bf16),
            pltpu.SemaphoreType.DMA((9 + len(norms),)),
            pltpu.SemaphoreType.DMA((11,)),
        ]
        + [pltpu.SemaphoreType.DMA((item,)) for item in counts for unused_side in range(2)],
        compiler_params=pltpu.CompilerParams(
            collective_id=number, has_side_effects=True, vmem_limit_bytes=VMEM_BYTES
        ),
    )(segments, norms, hidden, q_proj, k_proj, v_proj, small, pl_proj, o_proj)


def ffn_kernel(
    hidden_ref,
    branch_ref,
    gains_ref,
    small_any,
    gate_any,
    up_any,
    down_any,
    sum_ref,
    all_ref,
    act_ref,
    slope_ref,
    inner_ref,
    far_any,
    first_ref,
    low_rank_ref,
    left_low_ref,
    own_ref,
    laurel,
    gate,
    up,
    down,
    block,
    inner_block,
    part,
    held,
    load_sems,
    send_sem,
    recv_sem,
    sum_send,
    sum_recv,
    far_send,
    far_recv,
):
    rows, width = hidden_ref.shape
    units = gate.shape[0]
    piece = rows // 4
    index = lax.axis_index("fsdp")
    place = ring_place(index)
    ends = ring_ends(place)
    across = neighbours()[3]
    everyone = ends + (across,)
    announce(everyone)
    columns = laurel.shape[1]
    loads = start_loads(
        (
            (small_any.at[:, pl.ds(small_any.shape[1] - columns, columns)], laurel),
            (gate_any, gate),
            (up_any, up),
            (down_any, down),
        ),
        load_sems,
    )
    ring = Ring(
        place,
        ends,
        4,
        (send_sem, recv_sem),
        lambda lane: own_ref.at[pl.ds(lane_offset(lane, rows), piece)],
        lambda owner, lane: all_ref.at[span(owner * rows + lane_offset(lane, rows), piece)],
    )

    def own(owner, lane):
        return part[span(owner * rows + lane_offset(lane, rows), piece), :].astype(jnp.float32)

    sums = RingSum(place, ends, 4, (sum_send, sum_recv), held, own)

    def compute(step):
        pair = Pair(place, step, rows)
        block[...] = pair.read(all_ref)

        def into(tile):
            value = mul_t(block[...], gate[tile, :])
            second = mul_t(block[...], up[tile, :])
            act, slope = gelu_parts(value)
            inner = low(act * second)
            inner_block[:, tile] = inner
            pair.write(act_ref, tile, low(act))
            pair.write(slope_ref, tile, low(slope * second))
            pair.write(inner_ref, tile, inner)

        tile_loop(units // TILE, TILE, into)

        def out(tile):
            pair.write(part, tile, low(dot(inner_block[...], down[:, tile])))

        tile_loop(width // (2 * TILE), 2 * TILE, out)

    crossings = []

    def cross(step):
        for rows_of in Pair(place, step, rows).rows:
            crossings.append(
                remote(
                    all_ref.at[rows_of],
                    far_any.at[rows_of],
                    (far_send, far_recv),
                    len(crossings),
                    across,
                )
            )

    def normed_tile(tile):
        source = hidden_ref[tile, :].astype(jnp.float32)
        block[tile, :] = low(source * root_of(source) * gains_ref[0:1, :])

    def first_tile(tile):
        source = hidden_ref[tile, :].astype(jnp.float32)
        total = source + source * root_of(source) * gains_ref[0:1, :]
        for number, ref in ((1, branch_ref), (2, low_rank_ref)):
            value = ref[tile, :]
            total = total + value * root_of(value) * gains_ref[number : number + 1, :]
        total = total * HALF_ROOT
        first_ref[tile, :] = total
        own_ref[tile, :] = low(total * root_of(total) * gains_ref[3:4, :])

    rank = columns // 2
    tile_loop(rows // 32, 32, normed_tile)
    loads[0].wait()
    left_low = low(dot(block[...], laurel[...])[:, :rank])
    left_low_ref[...] = left_low
    low_rank_ref[...] = mul_t(left_low, laurel[:, rank:])
    tile_loop(rows // 32, 32, first_tile)
    await_all(everyone)
    ring.send(0)
    all_ref[span(index * rows, rows), :] = own_ref[...]
    cross(0)
    for copy in loads[1:]:
        copy.wait()
    compute(0)
    for step in range(1, HEADS):
        if step < RING_STEPS:
            ring.send(step)
            cross(step)
        else:
            ring.arrive(step)
        compute(step)
        sums.send(step - 1)
    for lane in range(4):
        sum_ref[pl.ds(lane_offset(lane, rows), piece), :] = sums.last(index, lane)
    ring.sent()
    sums.sent()
    for copy in crossings:
        copy.wait()


def ffn_forward(hidden, branch, gains, small, rank, gate, up, down, number):
    rows, width = hidden.shape
    units = gate.shape[0]
    near, anywhere = pl.BlockSpec(memory_space=pltpu.VMEM), pl.BlockSpec(memory_space=pltpu.HBM)
    total = rows * HEADS
    steps = 4 * RING_STEPS
    bf16 = jnp.bfloat16
    inner = jax.ShapeDtypeStruct((total, units), bf16)
    return pl.pallas_call(
        ffn_kernel,
        out_shape=[
            jax.ShapeDtypeStruct((rows, width), jnp.float32),
            jax.ShapeDtypeStruct((total, width), bf16),
            inner,
            inner,
            inner,
            jax.ShapeDtypeStruct((total, width), bf16),
            jax.ShapeDtypeStruct((rows, width), jnp.float32),
            jax.ShapeDtypeStruct((rows, width), jnp.float32),
            jax.ShapeDtypeStruct((rows, rank), bf16),
        ],
        in_specs=[near] * 3 + [anywhere] * 4,
        out_specs=[near] * 5 + [anywhere] + [near] * 3,
        scratch_shapes=[pltpu.VMEM((rows, width), bf16), pltpu.VMEM((width, 2 * rank), bf16)]
        + [pltpu.VMEM((units, width), bf16)] * 3
        + [
            pltpu.VMEM((rows, width), bf16),
            pltpu.VMEM((rows, units), bf16),
            pltpu.VMEM((total, width), bf16),
            pltpu.VMEM((steps + 4, rows // 4, width), bf16),
            pltpu.SemaphoreType.DMA((4,)),
        ]
        + [pltpu.SemaphoreType.DMA((steps,))] * 4
        + [pltpu.SemaphoreType.DMA((2 * RING_STEPS,))] * 2,
        compiler_params=pltpu.CompilerParams(
            collective_id=number, has_side_effects=True, vmem_limit_bytes=VMEM_BYTES
        ),
    )(hidden, branch, gains, small, gate, up, down)


def ffn_back_kernel(
    first_ref,
    ffw_ref,
    extra_ref,
    seed_ref,
    gains_ref,
    small_any,
    pl_proj_any,
    all_any,
    far_all_any,
    act_any,
    slope_any,
    inner_any,
    gate_any,
    up_any,
    down_any,
    sum_ref,
    result_ref,
    d_extra_ref,
    d_second_ref,
    gain_grads,
    down_out,
    gate_out,
    up_out,
    far_down,
    theirs_any,
    joint_any,
    far_gate_any,
    far_up_any,
    far_rest_any,
    gate_sum,
    proj_sum,
    d_all,
    tokens,
    d_up,
    d_gate,
    inner,
    gate,
    up,
    down,
    block,
    inner_block,
    part,
    held,
    turned,
    give,
    keep,
    theirs,
    own_ref,
    pl_gate,
    pl_proj,
    crossed,
    d_pl_out,
    gate_blocks,
    gate_folded,
    gate_far,
    gate_held,
    proj_blocks,
    proj_folded,
    proj_far,
    proj_held,
    load_sems,
    store_sems,
    *sems,
):
    pairs = [sems[i : i + 2] for i in range(0, len(sems), 2)]
    ring_sems, sum_sems, fold_sems, far_sems, gate_sems, proj_sems = pairs[:6]
    pl_fold_sems, pl_far_sems, cross_sems, rest_sems, joint_sems = pairs[6:]
    rows, width = first_ref.shape
    units = gate.shape[0]
    piece = rows // 4
    index = lax.axis_index("fsdp")
    place = ring_place(index)
    ends = ring_ends(place)
    unused_chip, core, sibling, across = neighbours()
    per_layer = pl_gate.shape[1]
    (
        load_pl_gate,
        load_pl_proj,
        load_down,
        load_act,
        load_slope,
        load_gate,
        load_up,
        load_inner,
        load_tokens,
    ) = start_loads(
        (
            (small_any.at[:, pl.ds(0, per_layer)], pl_gate),
            (pl_proj_any, pl_proj),
            (down_any, down),
            (act_any, d_up),
            (slope_any, d_gate),
            (gate_any, gate),
            (up_any, up),
            (inner_any, inner),
            (all_any, tokens),
        ),
        load_sems,
    )
    everyone = ends + (sibling, across)
    announce(everyone)
    ring = Ring(
        place,
        ends,
        4,
        ring_sems,
        lambda lane: own_ref.at[pl.ds(lane_offset(lane, rows), piece)],
        lambda owner, lane: d_all.at[span(owner * rows + lane_offset(lane, rows), piece)],
    )

    def own(owner, lane):
        return part[span(owner * rows + lane_offset(lane, rows), piece), :].astype(jnp.float32)

    chip = neighbours()[0]
    mine, yours = 2 * chip + core, 2 * (1 - chip) + core

    def block_ring(block_sems, block_held, blocks):
        low_rows = blocks.shape[2] // 2
        return RingSum(
            place,
            ends,
            2,
            block_sems,
            block_held,
            lambda owner, lane: blocks[owner, mine, pl.ds(lane * low_rows, low_rows), :].astype(
                jnp.float32
            ),
        )

    sums = RingSum(place, ends, 4, sum_sems, held, own)
    pl_rings = (
        block_ring(gate_sems, gate_held, gate_blocks),
        block_ring(proj_sems, proj_held, proj_blocks),
    )
    pl_arrays = (
        (gate_blocks, gate_folded, gate_far),
        (proj_blocks, proj_folded, proj_far),
    )
    pl_folds, pl_sends = [], []

    def per_layer_branch():
        def after_ffw(tile):
            value = ffw_ref[tile, :]
            total = first_ref[tile, :] + value * root_of(value) * gains_ref[0:1, :]
            sum_ref[tile, :] = total
            block[tile, :] = low(total)

        tile_loop(rows // 32, 32, after_ffw)
        load_pl_gate.wait()
        load_pl_proj.wait()
        extra = extra_ref[...].astype(jnp.float32)
        act, slope = gelu_parts(dot(block[...], pl_gate[...]))
        mix = low(act * extra)
        d_second_ref[...] = dot(mix, pl_proj[...])

        def back_out(tile):
            value = d_second_ref[tile, :]
            result_ref[tile, :] = low(sum_ref[tile, :] + value * root_of(value) * gains_ref[1:2, :])
            grad, gain_grad = norm_pull(
                value, gains_ref[1:2, :], seed_ref[tile, :].astype(jnp.float32)
            )
            d_pl_out[tile, :] = low(grad)
            gain_grads[1:2, :] += gain_grad

        tile_loop(rows // 32, 32, back_out)
        d_mix = mul_t(d_pl_out[...], pl_proj[...])
        d_extra_ref[...] = low(d_mix * act)
        d_pre = low(d_mix * extra * slope)
        d_second_ref[...] = mul_t(d_pre, pl_gate[...])

        def back_ffw(tile):
            grad = seed_ref[tile, :].astype(jnp.float32) + d_second_ref[tile, :]
            d_second_ref[tile, :] = grad
            grad, gain_grad = norm_pull(ffw_ref[tile, :], gains_ref[0:1, :], grad)
            own_ref[tile, :] = low(grad)
            gain_grads[0:1, :] += gain_grad

        tile_loop(rows // 32, 32, back_ffw)
        return (mix, d_pre)

    def per_layer_grads(mix, d_pre):
        turned_mix = mix.T
        deep = proj_blocks.shape[2]
        for step in range(QUARTERS):
            wide = proj_blocks.shape[3]
            value = low(dot(turned_mix, d_pl_out[:, step * wide : (step + 1) * wide]))
            for owner in range(HEADS):
                proj_blocks[owner, step] = value[owner * deep : (owner + 1) * deep]
        shard = width // HEADS
        for owner in range(HEADS):
            value = low(dot(block[:, owner * shard : (owner + 1) * shard].T, d_pre))
            for step in range(QUARTERS):
                gate_blocks[owner, step] = value[
                    step * (shard // QUARTERS) : (step + 1) * (shard // QUARTERS)
                ]

    def pl_fold():
        for number, (blocks, folded, far) in enumerate(pl_arrays):
            for side in range(2):
                pl_folds[2 * number + side].wait_recv()
            for owner in range(HEADS):
                blocks[owner, yours] = add_low(blocks[owner, yours], folded[1 - chip, owner])
            pl_sends.append(remote(blocks.at[:, yours], far, pl_far_sems, number, across))
            for owner in range(HEADS):
                blocks[owner, mine] = add_low(blocks[owner, mine], folded[chip, owner])

    def pl_join():
        for number, (blocks, folded, far) in enumerate(pl_arrays):
            pl_sends[number].wait_recv()
            for owner in range(HEADS):
                blocks[owner, mine] = add_low(blocks[owner, mine], far[owner])

    def compute(step):
        pair = Pair(place, step, rows)
        block[...] = pair.read(d_all)

        def into(tile):
            grad = mul_t(block[...], down[tile, :])
            first = low(grad * pair.read(d_gate, tile).astype(jnp.float32))
            second = low(grad * pair.read(d_up, tile).astype(jnp.float32))
            pair.write(d_gate, tile, first)
            pair.write(d_up, tile, second)
            inner_block[0, :, tile] = first
            inner_block[1, :, tile] = second

        tile_loop(units // TILE, TILE, into)
        if step == 0:
            load_gate.wait()
            load_up.wait()

        def out(tile):
            total = dot(inner_block[0], gate[:, tile]) + dot(inner_block[1], up[:, tile])
            pair.write(part, tile, low(total))

        tile_loop(width // (2 * TILE), 2 * TILE, out)

    half = units // 2
    crossings, swaps = [], []

    def cross(step):
        slot = step % 2
        if step >= 2:
            for copy in crossings[2 * step - 4 : 2 * step - 2]:
                copy.wait_send()
        columns = span((1 - chip) * half, half)
        for number, target in enumerate((far_gate_any, far_up_any)):
            crossed[slot, number] = inner_block[number, :, columns]
            crossings.append(
                remote(
                    crossed.at[slot, number], target.at[step], cross_sems, len(crossings), across
                )
            )

    def outer_into(side, turn, right, target, add=False):
        if not side:
            turned[...] = turn().T
        wide = width // 2

        def tile_step(number, carry):
            tile = span(side * wide + number * 2 * TILE, 2 * TILE)
            value = dot(turned[...], right[:, tile])
            if add:
                value = value + target[:, tile].astype(jnp.float32)
            target[:, tile] = low(value)
            return carry

        lax.fori_loop(0, wide // (2 * TILE), tile_step, 0)

    def add_from(landed, rows_of, target):
        count = landed.shape[0]
        copy = pltpu.make_async_copy(landed, theirs.at[pl.ds(0, count)], load_sems.at[10])
        copy.start()
        copy.wait()

        def add(tile):
            here = span(rows_of + tile.start, 64)
            target[here, :] = add_low(target[here, :], theirs[tile, :])

        tile_loop(count // 64, 64, add)

    early_rows = half // 2
    folds, stores, joints, far_parts = [], [], [], []

    def down_give(side):
        outer_into(side, lambda: inner[:, span((1 - core) * half, half)], d_all, give)
        if side:
            folds.append(remote(give, theirs_any, fold_sems, 0, sibling))

    def down_keep(side):
        outer_into(side, lambda: inner[:, span(core * half, half)], d_all, keep)

    def down_fold():
        folds[0].wait_recv()
        add_from(theirs_any, 0, keep)
        stores.extend(start_loads(((keep, down_out),), store_sems.at[pl.ds(0, 1)]))

    def down_swap():
        stores.pop().wait()
        early = pl.ds(0, early_rows)
        swaps.append(remote(down_out.at[early], far_down.at[early], far_sems, 0, across))
        folds[0].wait_send()

    def near_grads(number, side):
        source, target = ((d_gate, give), (d_up, keep))[number]
        outer_into(side, lambda: source[:, span(chip * half, half)], tokens, target)

    def far_loads():
        for copy in rests + crossings:
            copy.wait_recv()
        for copy in rests + crossings[-4:]:
            copy.wait_send()
        parts = [(far_all_any, tokens)]
        for step in range(HEADS):
            for side, rows_of in enumerate(Pair(place, step, rows).rows):
                here = pl.ds(side * (rows // 2), rows // 2)
                parts.append((far_gate_any.at[step, here], d_gate.at[rows_of, pl.ds(0, half)]))
                parts.append((far_up_any.at[step, here], d_up.at[rows_of, pl.ds(0, half)]))
        far_parts.extend(start_loads(parts, load_sems.at[pl.ds(11, len(parts))]))

    def far_rest_loads():
        for copy in far_parts:
            copy.wait()
        for copy in start_loads(
            [
                (far_rest_any.at[pl.ds(side * (rows // 2), rows // 2)], tokens.at[rows_of])
                for side, rows_of in enumerate(last_pair.rows)
            ],
            load_sems.at[pl.ds(11, 2)],
        ):
            copy.wait()

    def far_grads(number, side):
        source, target = ((d_gate, give), (d_up, keep))[number]
        outer_into(side, lambda: source[:, :half], tokens, target, add=True)
        if side:
            joints.append(
                remote(
                    target.at[span((1 - core) * (half // 2), half // 2)],
                    joint_any.at[number],
                    joint_sems,
                    number,
                    sibling,
                )
            )

    def join(number):
        target, out = ((give, gate_out), (keep, up_out))[number]
        joints[number].wait_recv()
        add_from(joint_any.at[number], core * (half // 2), target)
        store = pltpu.make_async_copy(
            target.at[span(core * (half // 2), half // 2)], out, store_sems.at[number]
        )
        store.start()
        stores.append(store)

    gain_grads[...] = jnp.zeros_like(gain_grads)
    mix, d_pre = per_layer_branch()
    await_all(everyone)
    ring.send(0)
    last_pair = Pair(place, RING_STEPS, rows)
    rests = [
        remote(
            all_any.at[rows_of],
            far_rest_any.at[pl.ds(side * (rows // 2), rows // 2)],
            rest_sems,
            side,
            across,
        )
        for side, rows_of in enumerate(last_pair.rows)
    ]
    per_layer_grads(mix, d_pre)
    for number, (blocks, folded, unused_far) in enumerate(pl_arrays):
        for side in range(2):
            pl_folds.append(
                remote(
                    blocks.at[:, 2 * side + 1 - core],
                    folded.at[side],
                    pl_fold_sems,
                    2 * number + side,
                    sibling,
                )
            )
    d_all[span(index * rows, rows), :] = own_ref[...]
    for copy in (load_down, load_act, load_slope):
        copy.wait()
    compute(0)
    cross(0)
    for step in range(1, HEADS):
        if step < RING_STEPS:
            ring.send(step)
        else:
            ring.arrive(step)
        if step >= RING_STEPS - 1:
            sums.send(step - RING_STEPS + 1)
            for item in pl_rings:
                item.send(step - RING_STEPS + 1)
        compute(step)
        cross(step)
        if step == 2:
            pl_fold()
        if step == 4:
            pl_join()
    load_inner.wait()
    load_tokens.wait()
    down_give(0)
    down_give(1)
    tasks = (
        (lambda: down_keep(0),),
        (lambda: down_keep(1),),
        (down_fold,),
        (down_swap, lambda: near_grads(0, 0)),
        (lambda: near_grads(0, 1), lambda: near_grads(1, 0)),
        (lambda: near_grads(1, 1), far_loads),
        (far_rest_loads, lambda: far_grads(0, 0), lambda: far_grads(0, 1)),
        (lambda: far_grads(1, 0),),
        (lambda: far_grads(1, 1),),
        (lambda: join(0),),
    )
    for number, group in enumerate(tasks):
        step = 2 + number // 2
        first = 2 * (number % 2)
        sums.send(step, (first, first + 1))
        if not first:
            for item in pl_rings:
                item.send(step)
        for task in group:
            task()
    for lane in range(4):
        sum_ref[pl.ds(lane_offset(lane, rows), piece), :] = sums.last(index, lane)
    join(1)
    for item, target in zip(pl_rings, (gate_sum, proj_sum)):
        low_rows = target.shape[0] // 2
        for lane in range(2):
            target[pl.ds(lane * low_rows, low_rows), :] = low(item.last(index, lane))
    for item in (ring, sums) + pl_rings:
        item.sent()
    for copy in pl_folds + pl_sends:
        copy.wait_send()
    for copy in joints:
        copy.wait_send()
    for copy in stores + swaps:
        copy.wait()


def ffn_back(local, gains, small, pl_proj, arrays, weights, number):
    rows, width = local[0].shape
    units = weights[0].shape[0]
    near, anywhere = pl.BlockSpec(memory_space=pltpu.VMEM), pl.BlockSpec(memory_space=pltpu.HBM)
    total = rows * HEADS
    steps = 4 * RING_STEPS
    bf16, f32 = jnp.bfloat16, jnp.float32
    low_steps = 2 * RING_STEPS
    counts = [steps, steps, 1, 1, low_steps, low_steps, 4, 2, 2 * HEADS, 2, 2]
    half = (units // 2, width)
    quarter = (units // 4, width)
    deep, per_layer = pl_proj.shape[0] // HEADS, local[2].shape[1]
    gate_block = (width // HEADS // QUARTERS, per_layer)
    proj_block = (deep, width // QUARTERS)

    def block_scratch(shape):
        return [
            pltpu.VMEM((HEADS, QUARTERS) + shape, bf16),
            pltpu.VMEM((2, HEADS) + shape, bf16),
            pltpu.VMEM((HEADS,) + shape, bf16),
            pltpu.VMEM((low_steps + 2, shape[0] // 2, shape[1]), bf16),
        ]

    return pl.pallas_call(
        ffn_back_kernel,
        out_shape=[
            jax.ShapeDtypeStruct((rows, width), f32),
            jax.ShapeDtypeStruct((rows, width), bf16),
            jax.ShapeDtypeStruct((rows, per_layer), bf16),
            jax.ShapeDtypeStruct((rows, width), f32),
            jax.ShapeDtypeStruct(gains.shape, f32),
        ]
        + [jax.ShapeDtypeStruct(half, bf16)]
        + [jax.ShapeDtypeStruct(quarter, bf16)] * 2
        + [jax.ShapeDtypeStruct(half, bf16)] * 2
        + [jax.ShapeDtypeStruct((2,) + quarter, bf16)]
        + [jax.ShapeDtypeStruct((HEADS, rows, units // 2), bf16)] * 2
        + [jax.ShapeDtypeStruct((rows, width), bf16)]
        + [jax.ShapeDtypeStruct(gate_block, bf16), jax.ShapeDtypeStruct(proj_block, bf16)],
        in_specs=[near] * 5 + [anywhere] * 10,
        out_specs=[near] * 5 + [anywhere] * 9 + [near] * 2,
        scratch_shapes=[pltpu.VMEM((total, width), bf16)] * 2
        + [pltpu.VMEM((total, units), bf16)] * 3
        + [pltpu.VMEM((units, width), bf16)] * 3
        + [
            pltpu.VMEM((rows, width), bf16),
            pltpu.VMEM((2, rows, units), bf16),
            pltpu.VMEM((total, width), bf16),
            pltpu.VMEM((steps + 4, rows // 4, width), bf16),
            pltpu.VMEM((units // 2, total), bf16),
            pltpu.VMEM(half, bf16),
            pltpu.VMEM(half, bf16),
            pltpu.VMEM(half, bf16),
            pltpu.VMEM((rows, width), bf16),
            pltpu.VMEM((width, per_layer), bf16),
            pltpu.VMEM(pl_proj.shape, bf16),
            pltpu.VMEM((2, 2, rows, units // 2), bf16),
            pltpu.VMEM((rows, width), bf16),
        ]
        + block_scratch(gate_block)
        + block_scratch(proj_block)
        + [pltpu.SemaphoreType.DMA((12 + 4 * HEADS,)), pltpu.SemaphoreType.DMA((2,))]
        + [pltpu.SemaphoreType.DMA((count,)) for count in counts for unused_side in range(2)],
        compiler_params=pltpu.CompilerParams(
            collective_id=number, has_side_effects=True, vmem_limit_bytes=VMEM_BYTES
        ),
    )(*local, gains, small, pl_proj, *arrays, *weights)


def head_back(grad, raw, gain, cosine, sine):
    half = raw.shape[1] // 2
    first, second = grad[:, :half], grad[:, half:]
    turned = jnp.concatenate(
        [first * cosine + second * sine, second * cosine - first * sine], axis=1
    )
    root = lax.rsqrt(jnp.mean(raw * raw, axis=1, keepdims=True) + EPS)
    gain_grad = jnp.sum(turned * raw * root, axis=0, keepdims=True)
    turned = turned * gain
    along = jnp.mean(turned * raw, axis=1, keepdims=True)
    return (root * turned - raw * (root * root * root * along), gain_grad)


def attention_back_kernel(
    hidden_ref,
    first_ref,
    d_ffwin_ref,
    d_second_ref,
    branch_ref,
    low_rank_ref,
    left_low_ref,
    gains_ref,
    ffw_gains_ref,
    o_any,
    q_any,
    k_any,
    v_any,
    att_any,
    probs_any,
    normed_any,
    weights_any,
    q_raw_any,
    k_raw_any,
    cosine_any,
    sine_any,
    small_any,
    pl_gate_ref,
    pl_proj_ref,
    own_down,
    far_down,
    own_gate,
    own_up,
    source_ref,
    owned_any,
    early_any,
    pl_proj_all,
    gain_sums,
    total_down,
    total_gate,
    total_up,
    far_rest,
    o_proj,
    q_low,
    k_low,
    v_low,
    att,
    probs,
    normed,
    weights,
    q_raw,
    k_raw,
    cosine,
    sine,
    d_all,
    block,
    att_block,
    q_block,
    dq_block,
    d_q,
    d_k,
    d_v,
    d_qkv,
    turned,
    part,
    held,
    blocks,
    folded,
    far,
    near_sum,
    key_held,
    o_grad,
    o_folded,
    o_far,
    sum_own,
    sum_far,
    own_ref,
    laurel,
    d_low_rank,
    d_scaled,
    sum_ref,
    gain_rows,
    gain_parts,
    gain_landed,
    gain_totals,
    owned_ref,
    early_ref,
    load_sems,
    final_sems,
    *sems,
):
    pairs = [sems[i : i + 2] for i in range(0, len(sems), 2)]
    ring_sems, sum_sems, fold_sems, far_sems, swap_sems, key_sems = pairs[:6]
    mirror_sems, early_sems, o_fold_sems, o_far_sems, cross_sems, total_sems, proj_sems = pairs[6:13]
    gain_sems, twin_sems, units_sems = pairs[13:]
    rows, width = own_ref.shape
    total_rows = rows * HEADS
    half = rows // 2
    piece = rows // 4
    index = lax.axis_index("fsdp")
    chip, core, sibling, across = neighbours()
    place = ring_place(index)
    ends = ring_ends(place)
    others = [lax.rem(index + step, HEADS) for step in range(1, HEADS)]
    quarter = 2 * chip + core
    quarter_rows = blocks.shape[2]
    own_rows = span(quarter * quarter_rows, quarter_rows)
    other_rows = span((2 * (1 - chip) + core) * quarter_rows, quarter_rows)
    groups = HEADS // KV_HEADS
    scale = HEAD_DIM ** (-0.5)
    head_columns = 3 * HEAD_DIM
    loads = start_loads(
        (
            (o_any, o_proj),
            (q_any, q_low),
            (k_any, k_low),
            (v_any, v_low),
            (att_any, att),
            (probs_any, probs),
            (q_raw_any, q_raw),
            (k_raw_any, k_raw),
            (cosine_any, cosine),
            (sine_any, sine),
            (weights_any, weights),
            (normed_any, normed),
            (small_any.at[:, span(small_any.shape[1] - laurel.shape[1], laurel.shape[1])], laurel),
        ),
        load_sems,
    )
    rep = lax.axis_index("rep")
    twins = [lax.rem(rep + step, QUARTERS) for step in range(1, QUARTERS)]
    everyone = [{"fsdp": other} for other in others] + [{"rep": twin} for twin in twins]
    announce(everyone)
    late_rows = far_rest.shape[0]
    early_rows = own_down.shape[0] - late_rows
    late = pl.ds(early_rows, late_rows)
    part_rows = own_gate.shape[0]
    unit_rows = span(quarter * part_rows, part_rows)
    other_unit_rows = span((2 * (1 - chip) + core) * part_rows, part_rows)
    units = Mirror(2, units_sems)
    ring = Ring(
        place,
        ends,
        4,
        ring_sems,
        lambda lane: own_ref.at[pl.ds(lane_offset(lane, rows), piece)],
        lambda owner, lane: d_all.at[span(owner * rows + lane_offset(lane, rows), piece)],
    )
    sums = RingSum(
        place,
        ends,
        4,
        sum_sems,
        held,
        lambda owner, lane: part[pl.ds(lane_offset(lane, rows), piece), :],
    )
    key_tiles = total_rows // TILE
    rank = laurel.shape[1] // 2

    def before(tile):
        grad, part_sum = norm_pull(first_ref[tile, :], gains_ref[3:4, :], d_ffwin_ref[tile, :])
        gain_rows[3:4, :] += part_sum
        scaled = (d_second_ref[tile, :] + grad) * HALF_ROOT
        d_scaled[tile, :] = scaled
        grad, part_sum = norm_pull(branch_ref[tile, :], gains_ref[1:2, :], scaled)
        gain_rows[1:2, :] += part_sum
        own_ref[tile, :] = low(grad)
        grad, part_sum = norm_pull(low_rank_ref[tile, :], gains_ref[2:3, :], scaled)
        gain_rows[2:3, :] += part_sum
        d_low_rank[tile, :] = low(grad)

    def low_rank_grads():
        d_left = low(dot(d_low_rank[...], laurel[...])[:, rank:])
        source = hidden_ref[...].astype(jnp.float32)
        block[...] = low(source * root_of(source) * gains_ref[0:1, :])
        shard = width // HEADS
        for owner in range(HEADS):
            columns = slice(owner * shard, (owner + 1) * shard)
            value = jnp.concatenate(
                [
                    dot(block[:, columns].T, d_left),
                    dot(d_low_rank[:, columns].T, left_low_ref[...]),
                ],
                axis=1,
            )
            value = low(value)
            for step in range(QUARTERS):
                blocks[owner, step, :, head_columns:] = value[
                    step * quarter_rows : (step + 1) * quarter_rows
                ]
        return d_left

    def after(tile):
        grad = d_scaled[tile, :] + sum_ref[tile, :]
        grad, part_sum = norm_pull(
            hidden_ref[tile, :].astype(jnp.float32), gains_ref[0:1, :], grad
        )
        gain_rows[0:1, :] += part_sum
        source_ref[tile, :] = low(d_scaled[tile, :] + grad)

    def compute(step):
        pair = Pair(place, step, rows)
        block[...] = pair.read(d_all)
        d_att = low(mul_t(block[...], o_proj[...]))
        att_block[...] = d_att
        q_block[...] = pair.read(q_low)
        delta = jnp.sum(
            d_att.astype(jnp.float32) * pair.read(att).astype(jnp.float32), axis=1, keepdims=True
        )
        dq_block[...] = jnp.zeros_like(dq_block)

        def keys(tile):
            chance = pair.read(probs, tile)
            d_chance = mul_t(att_block[...], v_low[tile, :])
            d_score = low(chance.astype(jnp.float32) * (d_chance - delta) * scale)
            dq_block[...] += dot(d_score, k_low[tile, :])
            d_k[tile, :] += dot(d_score.T, q_block[...])
            d_v[tile, :] += dot(chance.T, att_block[...])

        tile_loop(key_tiles, TILE, keys)
        pair.write(d_q, slice(None), dq_block[...])

    half_units = own_down.shape[0]
    final_loads, final_sends = [], []

    def load_final():
        crossings[0].wait_recv()
        early_part = pl.ds(0, early_rows)
        final_loads.extend(
            start_loads(
                (
                    (own_down, sum_own),
                    (far_down.at[early_part], sum_far.at[early_part]),
                    (far_rest, sum_far.at[late]),
                ),
                final_sems.at[pl.ds(0, 3)],
            )
        )

    def add_final():
        for copy in final_loads:
            copy.wait()

        def add(tile):
            sum_own[tile, :] = add_low(sum_own[tile, :], sum_far[tile, :])

        tile_loop(half_units // 64, 64, add)
        target = total_down.at[span(core * half_units, half_units)]
        final_sends.append(remote(sum_own, target, total_sems, 0, sibling))
        final_loads.extend(start_loads(((sum_own, target),), final_sems.at[pl.ds(0, 1)]))

    d_k[...] = jnp.zeros_like(d_k)
    d_v[...] = jnp.zeros_like(d_v)
    gain_rows[...] = jnp.zeros_like(gain_rows)
    tile_loop(rows // 32, 32, before)
    await_all(everyone)
    ring.send(0)
    units.give(0, total_gate.at[unit_rows], own_gate)
    crossings = [remote(own_down.at[late], far_rest, cross_sems, 0, across)]
    units.give(1, total_up.at[unit_rows], own_up)
    placed = start_loads(
        ((own_gate, total_gate.at[unit_rows]), (own_up, total_up.at[unit_rows])),
        final_sems.at[pl.ds(5, 2)],
    )
    d_all[span(index * rows, rows), :] = own_ref[...]
    loads[12].wait()
    d_left = low_rank_grads()
    for copy in loads[:6]:
        copy.wait()
    compute(0)
    for step in range(1, HEADS):
        if step < RING_STEPS:
            ring.send(step)
        else:
            ring.arrive(step)
        compute(step)
        if step == 6:
            units.relay(0, total_gate.at[other_unit_rows])
    for copy in loads[6:12]:
        copy.wait()

    def raw_tile(tile):
        for side, (grad, raw) in enumerate(((d_q, q_raw), (d_k, k_raw))):
            value, gain_grad = head_back(
                grad[tile, :],
                raw[tile, :],
                gains_ref[6 + side : 7 + side, :HEAD_DIM],
                cosine[tile, :],
                sine[tile, :],
            )
            d_qkv[tile, side * HEAD_DIM : (side + 1) * HEAD_DIM] = low(value)
            gain_rows[6 + side : 7 + side, :HEAD_DIM] += gain_grad
        d_qkv[tile, 2 * HEAD_DIM :] = low(d_v[tile, :])

    tile_loop(total_rows // 128, 128, raw_tile)

    def owner_at(step, way):
        return ring_index(lax.rem(place + (step + 1 if way else HEADS - 1 - step), HEADS))

    def part_of(step):
        tops = [
            d_qkv[span(owner_at(step, way) * rows + way * half, half), :] for way in range(2)
        ]
        part[...] = mul_t(jnp.concatenate(tops, axis=0), weights[...])

    def head_grads(number, carry):
        turned[...] = normed[:, span(number * TILE, TILE)].T
        value = low(dot(turned[...], d_qkv[...]))
        for step in range(QUARTERS):
            blocks[number, step, :, :head_columns] = value[
                step * quarter_rows : (step + 1) * quarter_rows
            ]
        return carry

    def o_tile(tile):
        value = low(dot(turned[...], d_all[:, tile]))
        for step in range(QUARTERS):
            o_grad[step, :, tile] = value[step * quarter_rows : (step + 1) * quarter_rows]

    folds, o_folds, across_sends, swaps, key_swaps = [], [], [], [], []
    mirror, early, pl_mirror = Mirror(2, mirror_sems), Mirror(1, early_sems), Mirror(1, proj_sems)
    wide = pl_proj_ref.shape[1]
    own_columns = span(quarter * wide, wide)
    other_columns = span((2 * (1 - chip) + core) * wide, wide)
    rest = blocks.shape[3] - HEAD_DIM
    q_columns = HEADS * HEAD_DIM
    mine, yours = 2 * chip + core, 2 * (1 - chip) + core
    cut_rows = quarter_rows // 2
    cuts = [pl.ds(cut * cut_rows, cut_rows) for cut in range(2)]

    def fold_sends():
        for side in range(2):
            folds.append(
                remote(blocks.at[:, 2 * side + 1 - core], folded.at[side], fold_sems, side, sibling)
            )

    def fold_far(cut):
        if not cut:
            folds[0].wait_recv()
            folds[1].wait_recv()
        rows_of = cuts[cut]
        for number in range(HEADS):
            blocks[number, yours, rows_of, :] = add_low(
                blocks[number, yours, rows_of, :], folded[1 - chip, number, rows_of, :]
            )
        across_sends.append(
            remote(blocks.at[:, yours, rows_of], far.at[:, rows_of], far_sems, cut, across)
        )

    def fold_near():
        for number in range(HEADS):
            blocks[number, mine] = add_low(blocks[number, mine], folded[chip, number])

    def o_half(side):
        if not side:
            turned[...] = att[...].T
        for number in range(2):
            tile = pl.ds((2 * side + number) * (width // 4), width // 4)
            o_tile(tile)
        if side:
            for item in range(2):
                o_folds.append(
                    remote(
                        o_grad.at[2 * item + 1 - core], o_folded.at[item], o_fold_sems, item, sibling
                    )
                )

    def o_fold():
        for copy in o_folds:
            copy.wait_recv()
        o_grad[yours] = add_low(o_grad[yours], o_folded[1 - chip])
        across_sends.append(remote(o_grad.at[yours], o_far, o_far_sems, 0, across))
        o_grad[mine] = add_low(o_grad[mine], o_folded[chip])

    def swap_cut(cut):
        across_sends[cut].wait_recv()
        rows_of = cuts[cut]
        for number in range(HEADS):
            near_sum[number, rows_of, :] = add_low(
                blocks[number, mine, rows_of, :], far[number, rows_of, :]
            )
        landing = span(quarter * quarter_rows + cut * cut_rows, cut_rows)
        here = span(index * HEAD_DIM, HEAD_DIM)
        for step, other in enumerate(others):
            number = cut * (HEADS - 1) + step
            swaps.append(
                remote(
                    near_sum.at[other, rows_of, pl.ds(0, HEAD_DIM)],
                    owned_ref.at[landing, here],
                    swap_sems,
                    number,
                    {"fsdp": other},
                )
            )
            key_swaps.append(
                remote(
                    near_sum.at[other, rows_of, pl.ds(HEAD_DIM, rest)],
                    key_held.at[index, rows_of],
                    key_sems,
                    number,
                    {"fsdp": other},
                )
            )
        owned_ref[landing, here] = near_sum[index, rows_of, :HEAD_DIM]
        key_held[index, rows_of, :] = near_sum[index, rows_of, HEAD_DIM:]

    def early_give():
        across_sends[2].wait_recv()
        early_ref[own_rows, :width] = add_low(o_grad[mine], o_far[...])
        early_ref[own_rows, width:] = pl_gate_ref[...]
        early.give(0, early_ref.at[own_rows])
        pl_proj_all[:, own_columns] = pl_proj_ref[...]
        pl_mirror.give(0, pl_proj_all.at[:, own_columns])

    def early_relay():
        early.relay(0, early_ref.at[other_rows])
        pl_mirror.relay(0, pl_proj_all.at[:, other_columns])

    part_of(0)
    sums.send(0)
    lax.fori_loop(0, width // TILE, head_grads, 0)
    fold_sends()
    tasks = (
        (lambda: o_half(0),),
        (lambda: o_half(1), lambda: fold_far(0)),
        (lambda: fold_far(1),),
        (fold_near,),
        (o_fold,),
        (load_final,),
        (lambda: swap_cut(0),),
        (add_final,),
        (lambda: swap_cut(1), lambda: units.relay(1, total_up.at[other_unit_rows])),
        (),
        (early_give,),
        (),
    )
    for number, group in enumerate(tasks):
        step = 1 + number // 2
        first = 2 * (number % 2)
        if not first:
            part_of(step)
        sums.send(step, (first, first + 1))
        for task in group:
            task()
    part[...] = mul_t(d_qkv[span(index * rows, rows), :], weights[...])
    for lane in range(4):
        sum_ref[pl.ds(lane_offset(lane, rows), piece), :] = sums.last(index, lane)

    def finish_cut(cut):
        here = slice(cut * (HEADS - 1), (cut + 1) * (HEADS - 1))
        for copy in swaps[here] + key_swaps[here]:
            copy.wait_recv()
        rows_of = cuts[cut]
        landing = span(quarter * quarter_rows + cut * cut_rows, cut_rows)
        for head in range(KV_HEADS):
            total = key_held[head * groups, rows_of, :].astype(jnp.float32)
            for step in range(1, groups):
                total = total + key_held[head * groups + step, rows_of, :].astype(jnp.float32)
            total = low(total)
            for side in range(2):
                base = q_columns + (side * KV_HEADS + head) * HEAD_DIM
                owned_ref[landing, pl.ds(base, HEAD_DIM)] = total[
                    :, side * HEAD_DIM : (side + 1) * HEAD_DIM
                ]
        extra = key_held[0, rows_of, 2 * HEAD_DIM :].astype(jnp.float32)
        for step in range(1, HEADS):
            extra = extra + key_held[step, rows_of, 2 * HEAD_DIM :].astype(jnp.float32)
        base = q_columns + 2 * KV_HEADS * HEAD_DIM
        owned_ref[landing, pl.ds(base, rest - 2 * HEAD_DIM)] = low(extra)
        mirror.give(cut, owned_ref.at[landing])

    def relay_cut(cut):
        start = (2 * (1 - chip) + core) * quarter_rows + cut * cut_rows
        mirror.relay(cut, owned_ref.at[span(start, cut_rows)])

    finish_cut(0)
    sum_ref[...] += mul_t(d_left, laurel[:, :rank])
    tile_loop(rows // 32, 32, after)
    gain_rows[4:6, :] = ffw_gains_ref[...]
    shard = width // HEADS
    for owner in range(HEADS):
        gain_parts[owner, :6] = gain_rows[:6, owner * shard : (owner + 1) * shard]
        gain_parts[owner, 6:] = gain_rows[6:, :HEAD_DIM]
    gain_sends = [
        remote(gain_parts.at[other], gain_landed.at[index], gain_sems, step, {"fsdp": other})
        for step, other in enumerate(others)
    ]
    gain_landed[index] = gain_parts[index]
    finish_cut(1)
    for copy in gain_sends:
        copy.wait_recv()
    total = gain_landed[0]
    for step in range(1, HEADS):
        total = total + gain_landed[step]
    gain_totals[rep] = total
    twin_sends = [
        remote(gain_totals.at[rep], gain_totals.at[rep], twin_sems, step, {"rep": twin})
        for step, twin in enumerate(twins)
    ]
    early_relay()
    relay_cut(0)
    relay_cut(1)
    for copy in twin_sends:
        copy.wait_recv()
    total = gain_totals[0]
    for step in range(1, QUARTERS):
        total = total + gain_totals[step]
    gain_sums[...] = total
    units.finish()
    early.finish()
    leaving = start_loads(((early_ref, early_any),), final_sems.at[pl.ds(3, 1)])
    mirror.finish()
    leaving += start_loads(((owned_ref, owned_any),), final_sems.at[pl.ds(4, 1)])
    pl_mirror.finish()
    ring.sent()
    sums.sent()
    for copy in (
        folds + o_folds + across_sends + swaps + key_swaps + crossings + gain_sends + twin_sends
    ):
        copy.wait_send()
    final_loads[3].wait()
    for copy in final_sends:
        copy.wait()
    for copy in leaving + placed:
        copy.wait()


def attention_back(local, arrays, small, pl_sums, chip_grads, far_down, number):
    rows, width = local[0].shape
    total = rows * HEADS
    shard = width // HEADS
    quarter = shard // QUARTERS
    steps = 4 * RING_STEPS
    pl_gate, pl_proj = pl_sums
    laurel = 2 * local[6].shape[1]
    columns = 3 * HEAD_DIM + laurel
    half = chip_grads[0].shape
    near, anywhere = pl.BlockSpec(memory_space=pltpu.VMEM), pl.BlockSpec(memory_space=pltpu.HBM)
    bf16, f32 = jnp.bfloat16, jnp.float32
    owned = (HEADS + 2 * KV_HEADS) * HEAD_DIM + laurel
    counts = [steps, steps, 2, 2, 2 * HEADS - 2, 2 * HEADS - 2, 6, 3, 2, 1, 1, 1, 3]
    counts += [HEADS - 1, QUARTERS - 1, 6]
    down, gate, up = chip_grads
    whole = jax.ShapeDtypeStruct((2 * half[0], half[1]), bf16)
    return pl.pallas_call(
        attention_back_kernel,
        out_shape=[
            jax.ShapeDtypeStruct((rows, width), bf16),
            jax.ShapeDtypeStruct((shard, owned), bf16),
            jax.ShapeDtypeStruct((shard, width + pl_gate.shape[1]), bf16),
            jax.ShapeDtypeStruct((pl_proj.shape[0], width), bf16),
            jax.ShapeDtypeStruct((8, shard), f32),
            whole,
            whole,
            whole,
            jax.ShapeDtypeStruct((half[0] // 2, half[1]), bf16),
        ],
        in_specs=[near] * len(local) + [anywhere] * (len(arrays) + 1) + [near] * 2 + [anywhere] * 4,
        out_specs=[near] + [anywhere] * 2 + [near] * 2 + [anywhere] * 4,
        scratch_shapes=[pltpu.VMEM(item.shape, item.dtype) for item in arrays]
        + [
            pltpu.VMEM((total, width), bf16),
            pltpu.VMEM((rows, width), bf16),
            pltpu.VMEM((rows, HEAD_DIM), bf16),
            pltpu.VMEM((rows, HEAD_DIM), bf16),
            pltpu.VMEM((rows, HEAD_DIM), f32),
            pltpu.VMEM((total, HEAD_DIM), f32),
            pltpu.VMEM((total, HEAD_DIM), f32),
            pltpu.VMEM((total, HEAD_DIM), f32),
            pltpu.VMEM((total, 3 * HEAD_DIM), bf16),
            pltpu.VMEM((HEAD_DIM, total), bf16),
            pltpu.VMEM((rows, width), f32),
            pltpu.VMEM((steps + 4, rows // 4, width), bf16),
            pltpu.VMEM((HEADS, QUARTERS, quarter, columns), bf16),
            pltpu.VMEM((2, HEADS, quarter, columns), bf16),
            pltpu.VMEM((HEADS, quarter, columns), bf16),
            pltpu.VMEM((HEADS, quarter, columns), bf16),
            pltpu.VMEM((HEADS, quarter, columns - HEAD_DIM), bf16),
            pltpu.VMEM((QUARTERS, quarter, width), bf16),
            pltpu.VMEM((2, quarter, width), bf16),
            pltpu.VMEM((quarter, width), bf16),
            pltpu.VMEM(half, bf16),
            pltpu.VMEM(half, bf16),
            pltpu.VMEM((rows, width), bf16),
            pltpu.VMEM((width, laurel), bf16),
            pltpu.VMEM((rows, width), bf16),
            pltpu.VMEM((rows, width), f32),
            pltpu.VMEM((rows, width), f32),
            pltpu.VMEM((8, width), f32),
            pltpu.VMEM((HEADS, 8, shard), f32),
            pltpu.VMEM((HEADS, 8, shard), f32),
            pltpu.VMEM((QUARTERS, 8, shard), f32),
            pltpu.VMEM((shard, owned), bf16),
            pltpu.VMEM((shard, width + pl_gate.shape[1]), bf16),
            pltpu.SemaphoreType.DMA((len(arrays) + 1,)),
            pltpu.SemaphoreType.DMA((7,)),
        ]
        + [pltpu.SemaphoreType.DMA((count,)) for count in counts for unused_side in range(2)],
        compiler_params=pltpu.CompilerParams(
            collective_id=number, has_side_effects=True, vmem_limit_bytes=VMEM_BYTES
        ),
    )(*local, *arrays, small, pl_gate, pl_proj, down, far_down, gate, up)


WRITE_STEPS = 8


def write_kernel(cuts, *refs):
    sources = refs[: len(cuts)]
    targets = iter(refs[len(cuts) :])
    for source, parts in zip(sources, cuts):
        for start, size in parts:
            target = next(targets)
            target[...] = source[:, start : start + size].astype(target.dtype)


def write_out(items):
    in_specs, out_specs, out_shape, cuts = [], [], [], []
    for array, parts in items:
        rows = array.shape[0] // WRITE_STEPS
        whole = rows % 16 != 0
        block_rows = array.shape[0] if whole else rows
        place = (lambda step: (0, 0)) if whole else (lambda step: (step, 0))
        in_specs.append(pl.BlockSpec((block_rows, array.shape[1]), place))
        cuts.append(tuple((start, size) for start, size, unused_dtype in parts))
        for unused_start, size, dtype in parts:
            out_specs.append(pl.BlockSpec((block_rows, size), place))
            out_shape.append(jax.ShapeDtypeStruct((array.shape[0], size), dtype))
    return pl.pallas_call(
        functools.partial(write_kernel, tuple(cuts)),
        grid=(WRITE_STEPS,),
        out_shape=out_shape,
        in_specs=in_specs,
        out_specs=out_specs,
        compiler_params=pltpu.CompilerParams(vmem_limit_bytes=VMEM_BYTES),
    )(*[array for array, unused_parts in items])


def head_plan(
    hidden_in,
    layer_input,
    out_grad,
    seg_lengths,
    seg_parents,
    attn_norm,
    q_proj,
    k_proj,
    v_proj,
    q_norm,
    k_norm,
    o_proj,
    attn_post_norm,
    laurel_left,
    laurel_right,
    laurel_norm,
    ffw_norm,
    gate_proj,
    up_proj,
    down_proj,
    ffw_post_norm,
    pl_gate,
    pl_proj,
    pl_post_norm,
):
    index = lax.axis_index("fsdp")
    rows, width = hidden_in.shape
    shard = width // HEADS
    total = rows * HEADS
    rank = laurel_left.shape[1]
    per_layer = pl_gate.shape[1]

    piece = HEAD_DIM // HEADS
    gains = (attn_norm, attn_post_norm, laurel_norm, ffw_norm, ffw_post_norm, pl_post_norm)
    segments = jnp.stack([seg_lengths[0], seg_parents[0]]).astype(jnp.float32)
    segments = jnp.pad(segments, ((0, 6), (0, 128 - segments.shape[1])))
    (
        branch,
        wide_gains,
        small_all,
        full_plproj,
        normed_all,
        qkv_head,
        q_raw,
        k_raw,
        q_low,
        k_low,
        v_low,
        attended_low,
        probs_low,
        cosine,
        sine,
    ) = attention_forward(
        segments,
        gains + (q_norm, k_norm),
        seg_lengths.shape[1],
        hidden_in,
        q_proj,
        k_proj,
        v_proj,
        jnp.concatenate([pl_gate, laurel_left, laurel_right], axis=1),
        pl_proj,
        o_proj,
        0,
    )
    (
        ffw_out,
        ffw_all,
        act,
        slope,
        inner_low,
        far_all,
        first_sum,
        low_rank,
        left_low,
    ) = ffn_forward(
        hidden_in, branch, wide_gains, small_all, rank, gate_proj, up_proj, down_proj, 7
    )
    d_ffwin, result, d_extra, d_second, ffw_gains, *rest = ffn_back(
        (first_sum, ffw_out, layer_input, out_grad),
        wide_gains[4:6],
        small_all,
        full_plproj,
        (ffw_all, far_all, act, slope, inner_low),
        (gate_proj, up_proj, down_proj),
        9,
    )
    chip_grads, far_down, pl_sums = rest[:3], rest[3], rest[-2:]

    d_source, owned, early, sum_plproj, gain_sums, *totals = attention_back(
        (
            hidden_in,
            first_sum,
            d_ffwin,
            d_second,
            branch,
            low_rank,
            left_low,
            wide_gains,
            ffw_gains,
        ),
        (
            o_proj,
            q_low,
            k_low,
            v_low,
            attended_low,
            probs_low,
            normed_all,
            qkv_head,
            q_raw,
            k_raw,
            cosine,
            sine,
        ),
        small_all,
        pl_sums,
        chip_grads,
        far_down,
        12,
    )
    sum_anorm, sum_apost, sum_lnorm, sum_fnorm, sum_fpost, sum_plpost = gain_sums[:6]
    sum_qnorm, sum_knorm = [
        lax.dynamic_slice_in_dim(item, index * piece, piece) for item in gain_sums[6:]
    ]

    keys = KV_HEADS * HEAD_DIM
    value_at = width + keys
    left_at = value_at + keys
    f32, bf16 = jnp.float32, jnp.bfloat16
    (
        sum_down,
        sum_gate,
        sum_up,
        sum_q,
        sum_k,
        sum_v,
        sum_laurel,
        sum_o,
        sum_plgate,
        sum_plproj,
        result,
        d_source,
        d_extra,
    ) = write_out(
        [(item, ((0, width, f32),)) for item in totals[:3]]
        + [
            (
                owned,
                (
                    (0, width, f32),
                    (width, keys, f32),
                    (value_at, keys, f32),
                    (left_at, 2 * rank, f32),
                ),
            ),
            (early, ((0, width, f32), (width, per_layer, f32))),
            (sum_plproj, ((0, width, f32),)),
            (result, ((0, width, bf16),)),
            (d_source, ((0, width, bf16),)),
            (d_extra, ((0, per_layer, bf16),)),
        ]
    )
    return (
        result,
        d_source,
        d_extra,
        sum_anorm,
        sum_q,
        sum_k,
        sum_v,
        sum_qnorm,
        sum_knorm,
        sum_o,
        sum_apost,
        sum_laurel[:, :rank],
        sum_laurel[:, rank:],
        sum_lnorm,
        sum_fnorm,
        sum_gate,
        sum_up,
        sum_down,
        sum_fpost,
        sum_plgate,
        sum_plproj,
        sum_plpost,
    )


def gather_plan(
    hidden_in,
    layer_input,
    out_grad,
    seg_lengths,
    seg_parents,
    attn_norm,
    q_proj,
    k_proj,
    v_proj,
    q_norm,
    k_norm,
    o_proj,
    attn_post_norm,
    laurel_left,
    laurel_right,
    laurel_norm,
    ffw_norm,
    gate_proj,
    up_proj,
    down_proj,
    ffw_post_norm,
    pl_gate,
    pl_proj,
    pl_post_norm,
):
    shards = lax.axis_size("fsdp")
    rank_index = lax.axis_index("fsdp")
    rows = hidden_in.shape[0]
    total = rows * shards
    groups = HEADS // KV_HEADS
    scale = HEAD_DIM ** (-0.5)
    tokens, member, reach, position = tree_tables(seg_lengths[0], seg_parents[0], total)
    first_row = rank_index * rows
    my_tokens = first_row + jnp.arange(rows, dtype=jnp.int32)
    my_reach = lax.dynamic_slice_in_dim(reach, first_row, rows, 0)
    my_depth = lax.dynamic_slice_in_dim(position, first_row, rows, 0).astype(jnp.float32)
    seen = (jnp.dot(my_reach, member.T) > 0) & (tokens[None, :] <= my_tokens[:, None])
    (
        full_anorm,
        full_q,
        full_k,
        full_v,
        full_qnorm,
        full_knorm,
        full_o,
        full_apost,
        full_left,
        full_right,
        full_lnorm,
        full_fnorm,
        full_fpost,
        full_plgate,
        full_plproj,
        full_plpost,
    ) = (
        lax.all_gather(attn_norm, "fsdp", axis=0, tiled=True),
        lax.all_gather(q_proj, "fsdp", axis=0, tiled=True),
        lax.all_gather(k_proj, "fsdp", axis=0, tiled=True),
        lax.all_gather(v_proj, "fsdp", axis=0, tiled=True),
        lax.all_gather(q_norm, "fsdp", axis=0, tiled=True),
        lax.all_gather(k_norm, "fsdp", axis=0, tiled=True),
        lax.all_gather(o_proj, "fsdp", axis=0, tiled=True),
        lax.all_gather(attn_post_norm, "fsdp", axis=0, tiled=True),
        lax.all_gather(laurel_left, "fsdp", axis=0, tiled=True),
        lax.all_gather(laurel_right, "fsdp", axis=0, tiled=True),
        lax.all_gather(laurel_norm, "fsdp", axis=0, tiled=True),
        lax.all_gather(ffw_norm, "fsdp", axis=0, tiled=True),
        lax.all_gather(ffw_post_norm, "fsdp", axis=0, tiled=True),
        lax.all_gather(pl_gate, "fsdp", axis=0, tiled=True),
        lax.all_gather(pl_proj, "fsdp", axis=0, tiled=True),
        lax.all_gather(pl_post_norm, "fsdp", axis=0, tiled=True),
    )
    gain_anorm = full_anorm.astype(jnp.float32)
    gain_qnorm = full_qnorm.astype(jnp.float32)
    gain_knorm = full_knorm.astype(jnp.float32)
    gain_apost = full_apost.astype(jnp.float32)
    gain_lnorm = full_lnorm.astype(jnp.float32)
    gain_fnorm = full_fnorm.astype(jnp.float32)
    gain_fpost = full_fpost.astype(jnp.float32)
    gain_plpost = full_plpost.astype(jnp.float32)
    source = hidden_in.astype(jnp.float32)
    extra = layer_input.astype(jnp.float32)
    normed = norm_rows(source, gain_anorm)
    normed_low = normed.astype(jnp.bfloat16)
    q_raw = jnp.dot(normed_low, full_q, preferred_element_type=jnp.float32)
    k_raw = jnp.dot(normed_low, full_k, preferred_element_type=jnp.float32)
    v_raw = jnp.dot(normed_low, full_v, preferred_element_type=jnp.float32)

    def head_path(raw, gain):
        return rotate(norm_rows(raw.reshape(rows, -1, HEAD_DIM), gain), my_depth)

    q_low = head_path(q_raw, gain_qnorm).astype(jnp.bfloat16)
    k_low = head_path(k_raw, gain_knorm).reshape(rows, -1).astype(jnp.bfloat16)
    v_low = v_raw.astype(jnp.bfloat16)
    keys_all, values_all = (
        lax.all_gather(k_low, "fsdp", axis=0, tiled=True),
        lax.all_gather(v_low, "fsdp", axis=0, tiled=True),
    )
    keys_heads = keys_all.reshape(total, KV_HEADS, HEAD_DIM)
    values_heads = values_all.reshape(total, KV_HEADS, HEAD_DIM)
    query_groups = q_low.reshape(rows, KV_HEADS, groups, HEAD_DIM)
    mixed_list = []
    log_list = []
    for head in range(KV_HEADS):
        scores = (
            jnp.einsum(
                "tgd,nd->gtn",
                query_groups[:, head],
                keys_heads[:, head],
                preferred_element_type=jnp.float32,
            )
            * scale
        )
        scores = jnp.where(seen[None], scores, MASKED)
        top = jnp.max(scores, axis=-1, keepdims=True)
        expo = jnp.exp(scores - top)
        sums = jnp.sum(expo, axis=-1, keepdims=True)
        weights = (expo / sums).astype(jnp.bfloat16)
        mixed_list.append(
            jnp.einsum(
                "gtn,nd->tgd", weights, values_heads[:, head], preferred_element_type=jnp.float32
            )
        )
        log_list.append(top[..., 0] + jnp.log(sums[..., 0]))
    attended = jnp.stack(mixed_list, axis=1)
    log_sums = jnp.stack(log_list, axis=0)
    attended_low = attended.reshape(rows, -1).astype(jnp.bfloat16)
    branch = jnp.dot(attended_low, full_o, preferred_element_type=jnp.float32)
    left_low = jnp.dot(normed_low, full_left, preferred_element_type=jnp.float32).astype(
        jnp.bfloat16
    )
    low_rank = mul_t(left_low, full_right)
    first_sum = (
        source + norm_rows(branch, gain_apost) + normed + norm_rows(low_rank, gain_lnorm)
    ) * HALF_ROOT
    ffw_low = norm_rows(first_sum, gain_fnorm).astype(jnp.bfloat16)
    full_gate, full_up, full_down = (
        lax.all_gather(gate_proj, "fsdp", axis=0, tiled=True),
        lax.all_gather(up_proj, "fsdp", axis=0, tiled=True),
        lax.all_gather(down_proj, "fsdp", axis=0, tiled=True),
    )
    gate_val = mul_t(ffw_low, full_gate)
    up_val = mul_t(ffw_low, full_up)
    inner_low = gelu_mix(gate_val, up_val).astype(jnp.bfloat16)
    ffw_out = jnp.dot(inner_low, full_down, preferred_element_type=jnp.float32)
    second_sum = first_sum + norm_rows(ffw_out, gain_fpost)
    second_low = second_sum.astype(jnp.bfloat16)
    pl_pre = jnp.dot(second_low, full_plgate, preferred_element_type=jnp.float32)
    pl_mix = gelu_mix(pl_pre, extra).astype(jnp.bfloat16)
    pl_out = jnp.dot(pl_mix, full_plproj, preferred_element_type=jnp.float32)
    result = second_sum + norm_rows(pl_out, gain_plpost)
    seed = out_grad.astype(jnp.float32)
    d_plout, grad_plpost = norm_back(pl_out, gain_plpost, seed)
    d_plout_low = d_plout.astype(jnp.bfloat16)
    grad_plproj = outer(pl_mix, d_plout_low)
    d_mix = mul_t(d_plout_low, full_plproj)
    d_pre, d_extra = mix_back(pl_pre, extra, d_mix)
    d_pre_low = d_pre.astype(jnp.bfloat16)
    grad_plgate = outer(second_low, d_pre_low)
    d_second = seed + mul_t(d_pre_low, full_plgate)
    d_ffwout, grad_fpost = norm_back(ffw_out, gain_fpost, d_second)
    d_ffw_low = d_ffwout.astype(jnp.bfloat16)
    d_inner = mul_t(d_ffw_low, full_down)
    d_gate, d_up = mix_back(gate_val, up_val, d_inner)
    d_gate_low = d_gate.astype(jnp.bfloat16)
    d_up_low = d_up.astype(jnp.bfloat16)
    d_ffwin = jnp.dot(d_gate_low, full_gate, preferred_element_type=jnp.float32) + jnp.dot(
        d_up_low, full_up, preferred_element_type=jnp.float32
    )
    width = ffw_low.shape[1]
    gate_part = outer(d_gate_low, ffw_low)
    up_part = outer(d_up_low, ffw_low)
    down_part = outer(inner_low, d_ffw_low)
    stacked = lax.psum_scatter(
        jnp.concatenate([gate_part, up_part, down_part], axis=1).astype(jnp.bfloat16),
        "fsdp",
        scatter_dimension=0,
        tiled=True,
    ).astype(jnp.float32)
    grad_gate = stacked[:, :width]
    grad_up = stacked[:, width : 2 * width]
    grad_down = stacked[:, 2 * width :]
    d_first_part, grad_fnorm = norm_back(first_sum, gain_fnorm, d_ffwin)
    d_first = d_second + d_first_part
    d_scaled = d_first * HALF_ROOT
    d_branch, grad_apost = norm_back(branch, gain_apost, d_scaled)
    d_branch_low = d_branch.astype(jnp.bfloat16)
    d_lowrank, grad_lnorm = norm_back(low_rank, gain_lnorm, d_scaled)
    d_lowrank_low = d_lowrank.astype(jnp.bfloat16)
    grad_o = outer(attended_low, d_branch_low)
    d_att_low = mul_t(d_branch_low, full_o).astype(jnp.bfloat16)
    grad_right = outer(d_lowrank_low, left_low)
    d_left_low = jnp.dot(d_lowrank_low, full_right, preferred_element_type=jnp.float32).astype(
        jnp.bfloat16
    )
    grad_left = outer(normed_low, d_left_low)
    d_att_heads = d_att_low.reshape(rows, KV_HEADS, groups, HEAD_DIM)
    delta = jnp.sum(d_att_heads.astype(jnp.float32) * attended, axis=-1).transpose(1, 2, 0)
    block = 512
    count = total // block
    key_blocks = keys_heads.reshape(count, block, KV_HEADS, HEAD_DIM)
    value_blocks = values_heads.reshape(count, block, KV_HEADS, HEAD_DIM)
    seen_blocks = seen.reshape(rows, count, block).transpose(1, 0, 2)

    def key_step(d_query, item):
        keys, values, shown = item
        scores = (
            jnp.einsum("tkgd,nkd->kgtn", query_groups, keys, preferred_element_type=jnp.float32)
            * scale
        )
        scores = jnp.where(shown[None, None], scores, MASKED)
        probs = jnp.exp(scores - log_sums[..., None])
        d_probs = jnp.einsum(
            "tkgd,nkd->kgtn", d_att_heads, values, preferred_element_type=jnp.float32
        )
        d_scores = (probs * (d_probs - delta[..., None]) * scale).astype(jnp.bfloat16)
        d_query = d_query + jnp.einsum(
            "kgtn,nkd->tkgd", d_scores, keys, preferred_element_type=jnp.float32
        )
        d_keys = jnp.einsum(
            "kgtn,tkgd->nkd", d_scores, query_groups, preferred_element_type=jnp.float32
        )
        d_values = jnp.einsum(
            "kgtn,tkgd->nkd",
            probs.astype(jnp.bfloat16),
            d_att_heads,
            preferred_element_type=jnp.float32,
        )
        return (d_query, (d_keys, d_values))

    zero_query = jnp.zeros((rows, KV_HEADS, groups, HEAD_DIM), jnp.float32)
    d_query, (d_key_blocks, d_value_blocks) = lax.scan(
        key_step, zero_query, (key_blocks, value_blocks, seen_blocks)
    )
    my_dkeys, my_dvalues = (
        lax.psum_scatter(
            d_key_blocks.reshape(total, -1).astype(jnp.bfloat16),
            "fsdp",
            scatter_dimension=0,
            tiled=True,
        ).astype(jnp.float32),
        lax.psum_scatter(
            d_value_blocks.reshape(total, -1).astype(jnp.bfloat16),
            "fsdp",
            scatter_dimension=0,
            tiled=True,
        ).astype(jnp.float32),
    )
    unused_q, q_pull = jax.vjp(head_path, q_raw, gain_qnorm)
    d_qraw, grad_qnorm = q_pull(d_query.reshape(rows, HEADS, HEAD_DIM))
    unused_k, k_pull = jax.vjp(head_path, k_raw, gain_knorm)
    d_kraw, grad_knorm = k_pull(my_dkeys.reshape(rows, KV_HEADS, HEAD_DIM))
    d_q_low = d_qraw.astype(jnp.bfloat16)
    d_k_low = d_kraw.astype(jnp.bfloat16)
    d_v_low = my_dvalues.astype(jnp.bfloat16)
    grad_q = outer(normed_low, d_q_low)
    grad_k = outer(normed_low, d_k_low)
    grad_v = outer(normed_low, d_v_low)
    d_normed = (
        d_scaled
        + mul_t(d_q_low, full_q)
        + mul_t(d_k_low, full_k)
        + mul_t(d_v_low, full_v)
        + mul_t(d_left_low, full_left)
    )
    d_source_part, grad_anorm = norm_back(source, gain_anorm, d_normed)
    d_source = d_scaled + d_source_part
    shard_grads = (
        lax.psum_scatter(
            grad_anorm.astype(jnp.bfloat16), "fsdp", scatter_dimension=0, tiled=True
        ).astype(jnp.float32),
        lax.psum_scatter(
            grad_q.astype(jnp.bfloat16), "fsdp", scatter_dimension=0, tiled=True
        ).astype(jnp.float32),
        lax.psum_scatter(
            grad_k.astype(jnp.bfloat16), "fsdp", scatter_dimension=0, tiled=True
        ).astype(jnp.float32),
        lax.psum_scatter(
            grad_v.astype(jnp.bfloat16), "fsdp", scatter_dimension=0, tiled=True
        ).astype(jnp.float32),
        lax.psum_scatter(
            grad_qnorm.astype(jnp.bfloat16), "fsdp", scatter_dimension=0, tiled=True
        ).astype(jnp.float32),
        lax.psum_scatter(
            grad_knorm.astype(jnp.bfloat16), "fsdp", scatter_dimension=0, tiled=True
        ).astype(jnp.float32),
        lax.psum_scatter(
            grad_o.astype(jnp.bfloat16), "fsdp", scatter_dimension=0, tiled=True
        ).astype(jnp.float32),
        lax.psum_scatter(
            grad_apost.astype(jnp.bfloat16), "fsdp", scatter_dimension=0, tiled=True
        ).astype(jnp.float32),
        lax.psum_scatter(
            grad_left.astype(jnp.bfloat16), "fsdp", scatter_dimension=0, tiled=True
        ).astype(jnp.float32),
        lax.psum_scatter(
            grad_right.astype(jnp.bfloat16), "fsdp", scatter_dimension=0, tiled=True
        ).astype(jnp.float32),
        lax.psum_scatter(
            grad_lnorm.astype(jnp.bfloat16), "fsdp", scatter_dimension=0, tiled=True
        ).astype(jnp.float32),
        lax.psum_scatter(
            grad_fnorm.astype(jnp.bfloat16), "fsdp", scatter_dimension=0, tiled=True
        ).astype(jnp.float32),
        lax.psum_scatter(
            grad_fpost.astype(jnp.bfloat16), "fsdp", scatter_dimension=0, tiled=True
        ).astype(jnp.float32),
        lax.psum_scatter(
            grad_plgate.astype(jnp.bfloat16), "fsdp", scatter_dimension=0, tiled=True
        ).astype(jnp.float32),
        lax.psum_scatter(
            grad_plproj.astype(jnp.bfloat16), "fsdp", scatter_dimension=0, tiled=True
        ).astype(jnp.float32),
        lax.psum_scatter(
            grad_plpost.astype(jnp.bfloat16), "fsdp", scatter_dimension=0, tiled=True
        ).astype(jnp.float32),
    )
    (
        sum_anorm,
        sum_q,
        sum_k,
        sum_v,
        sum_qnorm,
        sum_knorm,
        sum_o,
        sum_apost,
        sum_left,
        sum_right,
        sum_lnorm,
        sum_fnorm,
        sum_fpost,
        sum_plgate,
        sum_plproj,
        sum_plpost,
        sum_gate,
        sum_up,
        sum_down,
    ) = (
        lax.psum(shard_grads[0].astype(jnp.bfloat16), "rep").astype(jnp.float32),
        lax.psum(shard_grads[1].astype(jnp.bfloat16), "rep").astype(jnp.float32),
        lax.psum(shard_grads[2].astype(jnp.bfloat16), "rep").astype(jnp.float32),
        lax.psum(shard_grads[3].astype(jnp.bfloat16), "rep").astype(jnp.float32),
        lax.psum(shard_grads[4].astype(jnp.bfloat16), "rep").astype(jnp.float32),
        lax.psum(shard_grads[5].astype(jnp.bfloat16), "rep").astype(jnp.float32),
        lax.psum(shard_grads[6].astype(jnp.bfloat16), "rep").astype(jnp.float32),
        lax.psum(shard_grads[7].astype(jnp.bfloat16), "rep").astype(jnp.float32),
        lax.psum(shard_grads[8].astype(jnp.bfloat16), "rep").astype(jnp.float32),
        lax.psum(shard_grads[9].astype(jnp.bfloat16), "rep").astype(jnp.float32),
        lax.psum(shard_grads[10].astype(jnp.bfloat16), "rep").astype(jnp.float32),
        lax.psum(shard_grads[11].astype(jnp.bfloat16), "rep").astype(jnp.float32),
        lax.psum(shard_grads[12].astype(jnp.bfloat16), "rep").astype(jnp.float32),
        lax.psum(shard_grads[13].astype(jnp.bfloat16), "rep").astype(jnp.float32),
        lax.psum(shard_grads[14].astype(jnp.bfloat16), "rep").astype(jnp.float32),
        lax.psum(shard_grads[15].astype(jnp.bfloat16), "rep").astype(jnp.float32),
        lax.psum(grad_gate.astype(jnp.bfloat16), "rep").astype(jnp.float32),
        lax.psum(grad_up.astype(jnp.bfloat16), "rep").astype(jnp.float32),
        lax.psum(grad_down.astype(jnp.bfloat16), "rep").astype(jnp.float32),
    )
    return (
        result.astype(jnp.bfloat16),
        d_source.astype(jnp.bfloat16),
        d_extra.astype(jnp.bfloat16),
        sum_anorm,
        sum_q,
        sum_k,
        sum_v,
        sum_qnorm,
        sum_knorm,
        sum_o,
        sum_apost,
        sum_left,
        sum_right,
        sum_lnorm,
        sum_fnorm,
        sum_gate,
        sum_up,
        sum_down,
        sum_fpost,
        sum_plgate,
        sum_plproj,
        sum_plpost,
    )


def solution(mesh):
    placed = (
        P(("rep", "fsdp"), None),
        P(("rep", "fsdp"), None),
        P(("rep", "fsdp"), None),
        P("rep", None),
        P("rep", None),
        P("fsdp"),
        P("fsdp", None),
        P("fsdp", None),
        P("fsdp", None),
        P("fsdp"),
        P("fsdp"),
        P("fsdp", None),
        P("fsdp"),
        P("fsdp", None),
        P("fsdp", None),
        P("fsdp"),
        P("fsdp"),
        P("fsdp", None),
        P("fsdp", None),
        P("fsdp", None),
        P("fsdp"),
        P("fsdp", None),
        P("fsdp", None),
        P("fsdp"),
    )
    return jax.shard_map(
        head_plan if mesh.shape["fsdp"] == HEADS else gather_plan,
        mesh=mesh,
        in_specs=placed,
        out_specs=(
            P(("rep", "fsdp"), None),
            P(("rep", "fsdp"), None),
            P(("rep", "fsdp"), None),
            P("fsdp"),
            P("fsdp", None),
            P("fsdp", None),
            P("fsdp", None),
            P("fsdp"),
            P("fsdp"),
            P("fsdp", None),
            P("fsdp"),
            P("fsdp", None),
            P("fsdp", None),
            P("fsdp"),
            P("fsdp"),
            P("fsdp", None),
            P("fsdp", None),
            P("fsdp", None),
            P("fsdp"),
            P("fsdp", None),
            P("fsdp", None),
            P("fsdp"),
        ),
        check_vma=False,
    )
```

```python
import functools
import math

import jax
import jax.numpy as jnp
from jax import lax
from jax.experimental import pallas as pl
from jax.experimental.pallas import tpu as pltpu
from jax.sharding import PartitionSpec as P

HEADS = 8
KV_HEADS = 2
HEAD_DIM = 256


EPS = 1e-06
ROPE_BASE = 1000000.0
HALF_ROOT = 0.7071067811865476
MASKED = -1e30


def norm_rows(value, gain):
    return value * lax.rsqrt(jnp.mean(value * value, axis=-1, keepdims=True) + EPS) * gain


def norm_back(value, gain, grad):
    unused, pull = jax.vjp(norm_rows, value, gain)
    return pull(grad)


def rotate(value, position):
    half = value.shape[-1] // 2
    freqs = jnp.exp(
        jnp.arange(half, dtype=jnp.float32) * (-2.0 * math.log(ROPE_BASE) / value.shape[-1])
    )
    angle = position[:, None] * freqs[None, :]
    cosine = jnp.cos(angle)[:, None, :]
    sine = jnp.sin(angle)[:, None, :]
    first_half = value[..., :half]
    second_half = value[..., half:]
    return jnp.concatenate(
        [first_half * cosine - second_half * sine, second_half * cosine + first_half * sine],
        axis=-1,
    )


def tree_tables(lengths, parents, total):
    count = lengths.shape[0]
    labels = jnp.arange(count, dtype=jnp.int32)
    ends = jnp.cumsum(lengths)
    starts = ends - lengths
    tokens = jnp.arange(total, dtype=jnp.int32)
    segment = jnp.sum((ends[None, :] <= tokens[:, None]).astype(jnp.int32), axis=1)
    parent_hot = ((parents[:, None] == labels[None, :]) & (labels[:, None] > 0)).astype(jnp.int32)
    identity = (labels[:, None] == labels[None, :]).astype(jnp.int32)
    ancestors = lax.fori_loop(
        0, count, lambda step, held: jnp.minimum(1, identity + jnp.dot(parent_hot, held)), identity
    )
    offset = jnp.dot(ancestors - identity, lengths) - starts
    member = (segment[:, None] == labels[None, :]).astype(jnp.int32)
    reach = jnp.dot(member, ancestors)
    position = jnp.dot(member, offset) + tokens
    return (tokens, member, reach, position)


def outer(left, right):
    return lax.dot_general(
        left, right, (((0,), (0,)), ((), ())), preferred_element_type=jnp.float32
    )


def mul_t(left, right):
    return lax.dot_general(
        left, right, (((1,), (1,)), ((), ())), preferred_element_type=jnp.float32
    )


def gelu_mix(first, second):
    return jax.nn.gelu(first, approximate=True) * second


def mix_back(first, second, grad):
    unused, pull = jax.vjp(gelu_mix, first, second)
    return pull(grad)


MESH = pl.DeviceIdType.MESH
VMEM_BYTES = 58 << 20


def ring_place(index):
    side = lax.rem(index, 2)
    return index // 2 + side * (HEADS - 1 - 2 * (index // 2))


def ring_index(place):
    back = place // (HEADS // 2)
    return (1 - back) * 2 * place + back * (2 * HEADS - 1 - 2 * place)


def ring_ends(place):
    after = {"fsdp": ring_index(lax.rem(place + 1, HEADS))}
    before = {"fsdp": ring_index(lax.rem(place + HEADS - 1, HEADS))}
    return (after, before)


def announce(others):
    barrier = pltpu.get_barrier_semaphore()
    for other in others:
        pl.semaphore_signal(barrier, inc=1, device_id=other, device_id_type=MESH)


def await_all(others):
    pl.semaphore_wait(pltpu.get_barrier_semaphore(), len(others))


def greet(others):
    announce(others)
    await_all(others)


def span(start, size):
    return pl.ds(pl.multiple_of(start, size), size)


def neighbours():
    rep = lax.axis_index("rep")
    chip = rep // 2
    core = lax.rem(rep, 2)
    return (chip, core, {"rep": 2 * chip + 1 - core}, {"rep": 2 * (1 - chip) + core})


def remote(source, target, sems, number, device):
    copy = pltpu.make_async_remote_copy(
        source,
        target,
        sems[0].at[number],
        sems[1].at[number],
        device_id=device,
        device_id_type=MESH,
    )
    copy.start()
    return copy


class Ring:
    def __init__(self, place, ends, lanes, sems, own, there):
        self.place, self.ends, self.lanes, self.sems = place, ends, lanes, sems
        self.own, self.there = own, there
        self.copies = []

    def owner(self, step, lane):
        ahead = step if lane % 2 else HEADS - step
        return ring_index(lax.rem(self.place + ahead, HEADS))

    def send(self, step):
        for lane in range(self.lanes):
            number = step * self.lanes + lane
            target = self.there(self.owner(step, lane), lane)
            if step:
                self.copies[number - self.lanes].wait_recv()
            source = target if step else self.own(lane)
            self.copies.append(remote(source, target, self.sems, number, self.ends[lane % 2]))

    def arrive(self, step):
        for lane in range(self.lanes):
            self.copies[(step - 1) * self.lanes + lane].wait_recv()

    def sent(self):
        for copy in self.copies:
            copy.wait_send()


class Mirror:
    def __init__(self, count, sems):
        unused_chip, unused_core, self.sibling, self.across = neighbours()
        self.count, self.sems = count, sems
        self.copies = [None] * (3 * count)

    def give(self, number, ref, source=None):
        source = ref if source is None else source
        self.copies[number] = remote(source, ref, self.sems, number, self.sibling)
        self.copies[self.count + number] = remote(
            source, ref, self.sems, self.count + number, self.across
        )

    def relay(self, number, ref):
        self.copies[self.count + number].wait_recv()
        self.copies[2 * self.count + number] = remote(
            ref, ref, self.sems, 2 * self.count + number, self.sibling
        )

    def arrive(self):
        for number, copy in enumerate(self.copies):
            if number // self.count != 1:
                copy.wait_recv()

    def sent(self):
        for copy in self.copies:
            copy.wait_send()

    def finish(self):
        self.arrive()
        self.sent()


RING_STEPS = HEADS - 1
QUARTERS = 4


def dot(left, right):
    return jnp.dot(left, right, preferred_element_type=jnp.float32)


def low(value):
    return value.astype(jnp.bfloat16)


def add_low(left, right):
    return (left.astype(jnp.float32) + right.astype(jnp.float32)).astype(jnp.bfloat16)


class RingSum:
    def __init__(self, place, ends, lanes, sems, held, own):
        self.place, self.ends, self.lanes, self.sems = place, ends, lanes, sems
        self.held, self.own = held, own
        self.copies = []

    def send(self, step, lanes=None):
        for lane in lanes or range(self.lanes):
            ahead = step + 1 if lane % 2 else HEADS - 1 - step
            owner = ring_index(lax.rem(self.place + ahead, HEADS))
            number = step * self.lanes + lane
            if step:
                slot = number - self.lanes
                self.copies[slot].wait_recv()
                value = self.held[slot].astype(jnp.float32) + self.own(owner, lane)
            else:
                slot = RING_STEPS * self.lanes + lane
                value = self.own(owner, lane)
            self.held[slot] = value.astype(jnp.bfloat16)
            self.copies.append(
                remote(self.held.at[slot], self.held.at[number], self.sems, number, self.ends[lane % 2])
            )

    def last(self, index, lane):
        number = (RING_STEPS - 1) * self.lanes + lane
        self.copies[number].wait_recv()
        return self.held[number].astype(jnp.float32) + self.own(index, lane)

    def sent(self):
        for copy in self.copies:
            copy.wait_send()


def lane_offset(lane, rows):
    return (lane % 2) * (rows // 2) + (lane // 2) * (rows // 4)


def tile_loop(count, size, body):
    def step(number, carry):
        body(span(number * size, size))
        return carry

    lax.fori_loop(0, count, step, 0)


class Pair:
    def __init__(self, place, step, rows):
        half = rows // 2
        behind = ring_index(lax.rem(place + HEADS - step, HEADS))
        ahead = ring_index(lax.rem(place + step, HEADS))
        self.half = half
        self.rows = (span(behind * rows, half), span(ahead * rows + half, half))

    def read(self, ref, columns=slice(None)):
        return jnp.concatenate([ref[rows, columns] for rows in self.rows], axis=0)

    def write(self, ref, columns, value):
        for side, rows in enumerate(self.rows):
            ref[rows, columns] = value[side * self.half : (side + 1) * self.half]


GELU_ROOT = math.sqrt(2.0 / math.pi)
GELU_CUBE = 0.044715
TILE = 256


def start_loads(pairs, sems):
    copies = []
    for number, (source, target) in enumerate(pairs):
        copy = pltpu.make_async_copy(source, target, sems.at[number])
        copy.start()
        copies.append(copy)
    return copies


def root_of(value):
    return lax.rsqrt(jnp.mean(value * value, axis=1, keepdims=True) + EPS)


def norm_pull(value, gain, grad):
    root = root_of(value)
    gain_grad = jnp.sum(grad * value * root, axis=0, keepdims=True)
    grad = grad * gain
    along = jnp.mean(grad * value, axis=1, keepdims=True)
    return (root * grad - value * (root * root * root * along), gain_grad)


def gelu_parts(value):
    square = value * value
    bent = jnp.tanh(GELU_ROOT * value * (1.0 + GELU_CUBE * square))
    share = 0.5 * (1.0 + bent)
    slope = share + (0.5 * GELU_ROOT) * value * (1.0 - bent * bent) * (
        1.0 + (3.0 * GELU_CUBE) * square
    )
    return (value * share, slope)


def tree_tables_near(segments, count, tables):
    member, reach, cosine, sine = tables
    lengths, parents = segments[0:1, :], segments[1:2, :]
    size = lengths.shape[1]
    row = lax.broadcasted_iota(jnp.int32, (size, size), 0)
    column = lax.broadcasted_iota(jnp.int32, (size, size), 1)
    same = row == column

    def upright(value):
        return jnp.sum(jnp.where(same, value, 0.0), axis=1, keepdims=True)

    parent = upright(parents) == column.astype(jnp.float32)
    reached = jnp.where(same | (parent & (row > 0)), 1.0, 0.0)
    for unused_step in range((count - 1).bit_length()):
        reached = jnp.where(dot(low(reached), low(reached)) > 0.5, 1.0, 0.0)
    ends = jnp.sum(jnp.where(row <= column, upright(lengths), 0.0), axis=0, keepdims=True)
    starts = ends - lengths
    above = jnp.sum(jnp.where(same, 0.0, reached * lengths), axis=1, keepdims=True)
    offset = jnp.sum(jnp.where(same, above, 0.0), axis=0, keepdims=True) - starts
    reached = low(reached)
    half = cosine.shape[1]
    place = lax.broadcasted_iota(jnp.int32, (1, half), 1).astype(jnp.float32)
    freqs = jnp.exp(place * (-math.log(ROPE_BASE) / half))

    def token_tile(number, carry):
        tile = span(number * size, size)
        token = (row + number * size).astype(jnp.float32)
        inside = jnp.where((token >= starts) & (token < ends), 1.0, 0.0)
        position = jnp.sum(inside * offset, axis=1, keepdims=True) + token[:, :1]
        angle = position * freqs
        cosine[tile, :] = jnp.cos(angle)
        sine[tile, :] = jnp.sin(angle)
        member[tile, :] = low(inside)
        reach[tile, :] = low(dot(low(inside), reached))
        return carry

    lax.fori_loop(0, member.shape[0] // size, token_tile, 0)


def attention_kernel(
    count,
    segments_ref,
    norm_refs,
    hidden_ref,
    q_ref,
    k_ref,
    v_ref,
    small_ref,
    pl_proj_ref,
    o_any,
    sum_ref,
    gains_ref,
    small_all,
    pl_proj_all,
    normed_any,
    weights_any,
    q_raw_any,
    k_raw_any,
    q_low_any,
    k_low_any,
    v_low_any,
    att_any,
    probs_any,
    cosine_any,
    sine_any,
    normed,
    weights,
    q_raw,
    k_raw,
    q_low,
    k_low,
    v_low,
    att,
    probs,
    cosine,
    sine,
    hidden_all,
    kv_all,
    gains_all,
    packed_ref,
    norm_held,
    o_proj,
    member,
    reach,
    part,
    held,
    load_sems,
    store_sems,
    *sems,
):
    pairs = [sems[i : i + 2] for i in range(0, len(sems), 2)]
    hidden_sems, gains_sems, q_sems, kv_sems, small_sems, pl_proj_sems, sum_sems = pairs[:7]
    q_mirror_sems, kv_mirror_sems, small_mirror_sems, pl_proj_mirror_sems = pairs[7:]
    rows, width = hidden_ref.shape
    total_rows = rows * HEADS
    half = rows // 2
    piece = rows // 4
    shard = q_ref.shape[0]
    deep = pl_proj_ref.shape[0]
    q_rows = shard // QUARTERS
    shard_part = q_rows // 2
    wide = pl_proj_ref.shape[1] // QUARTERS
    wide_part = wide // 2
    index = lax.axis_index("fsdp")
    chip, core, sibling, across = neighbours()
    quarter, other_quarter = 2 * chip + core, 2 * (1 - chip) + core
    place = ring_place(index)
    ends = ring_ends(place)
    others = [lax.rem(index + step, HEADS) for step in range(1, HEADS)]
    own_shard = span(index * shard, shard)
    loads = start_loads(
        (
            (q_ref.at[:, span(index * HEAD_DIM, HEAD_DIM)], weights.at[own_shard, pl.ds(0, HEAD_DIM)]),
            (k_ref, kv_all.at[own_shard, pl.ds(0, k_ref.shape[1])]),
            (v_ref, kv_all.at[own_shard, pl.ds(k_ref.shape[1], v_ref.shape[1])]),
            (o_any, o_proj),
            (small_ref, small_all.at[own_shard]),
            (pl_proj_ref, pl_proj_all.at[span(index * deep, deep)]),
            (hidden_ref, hidden_all.at[span(index * rows, rows)]),
        ),
        load_sems,
    )
    norm_loads = start_loads(zip(norm_refs, norm_held), load_sems.at[pl.ds(9, len(norm_refs))])
    shard_lanes = lax.broadcasted_iota(jnp.int32, (1, shard), 1)
    few = shard // HEADS
    spread = jnp.where(
        lax.broadcasted_iota(jnp.int32, (few, shard), 0)
        == lax.rem(lax.broadcasted_iota(jnp.int32, (few, shard), 1), few),
        1.0,
        0.0,
    )
    for copy in norm_loads:
        copy.wait()
    for number, ref in enumerate(norm_held):
        value = ref[...].astype(jnp.float32).reshape(1, ref.shape[0])
        if ref.shape[0] != shard:
            value = jnp.sum(value.reshape(few, 1) * spread, axis=0, keepdims=True)
            value = jnp.where(shard_lanes // few == index, value, 0.0)
        packed_ref[number : number + 1, :] = value
    greet([{"fsdp": other} for other in others] + [sibling, across])
    gain_copies = [
        remote(packed_ref, gains_all.at[index], gains_sems, step, {"fsdp": other})
        for step, other in enumerate(others)
    ]

    def shard_at(ref, part_of):
        return lambda owner, lane: ref.at[
            span(owner * shard + part_of * q_rows + lane * shard_part, shard_part)
        ]

    def pl_proj_at(part_of):
        return lambda owner, lane: pl_proj_all.at[
            span(owner * deep, deep), span(part_of * wide + lane * wide_part, wide_part)
        ]

    def shard_own(ref):
        return lambda lane: ref.at[span(quarter * q_rows + lane * shard_part, shard_part)]

    hidden = Ring(
        place,
        ends,
        4,
        hidden_sems,
        lambda lane: hidden_ref.at[pl.ds(lane_offset(lane, rows), piece)],
        lambda owner, lane: hidden_all.at[span(owner * rows + lane_offset(lane, rows), piece)],
    )
    kv_at = shard_at(kv_all, quarter)
    kv = Ring(place, ends, 2, kv_sems, lambda lane: kv_at(index, lane), kv_at)
    small = Ring(place, ends, 2, small_sems, shard_own(small_ref), shard_at(small_all, quarter))
    pl_proj = Ring(
        place,
        ends,
        2,
        pl_proj_sems,
        lambda lane: pl_proj_ref.at[:, span(quarter * wide + lane * wide_part, wide_part)],
        pl_proj_at(quarter),
    )
    lanes = 2 * RING_STEPS
    kv_mirror = Mirror(lanes, kv_mirror_sems)
    q_mirror = Mirror(HEADS - 1, q_mirror_sems)
    late = (
        (small, Mirror(lanes, small_mirror_sems), shard_at(small_all, other_quarter)),
        (pl_proj, Mirror(lanes, pl_proj_mirror_sems), pl_proj_at(other_quarter)),
    )
    kv_other = shard_at(kv_all, other_quarter)

    def pass_on(ring, mirror, step):
        for lane in range(2):
            mirror.give((step - 1) * 2 + lane, ring.there(ring.owner(step, lane), lane))

    def pass_again(ring, mirror, there, step):
        for lane in range(2):
            mirror.relay((step - 1) * 2 + lane, there(ring.owner(step, lane), lane))

    def late_step(step):
        for ring, mirror, there in late:
            if step < RING_STEPS:
                ring.send(step)
            elif step == RING_STEPS:
                ring.arrive(step)
            if 1 <= step <= RING_STEPS:
                pass_on(ring, mirror, step)
            if step >= 2:
                pass_again(ring, mirror, there, step - 1)

    def q_at(step, part_of):
        giver = lax.rem(index + HEADS - 1 - step, HEADS)
        return weights.at[span(giver * shard + part_of * q_rows, q_rows), pl.ds(0, HEAD_DIM)]

    loads[1].wait()
    loads[2].wait()
    kv.send(0)
    q_landing = weights.at[span(index * shard + quarter * q_rows, q_rows), pl.ds(0, HEAD_DIM)]
    q_copies = [
        remote(
            q_ref.at[span(quarter * q_rows, q_rows), span(other * HEAD_DIM, HEAD_DIM)],
            q_landing,
            q_sems,
            step,
            {"fsdp": other},
        )
        for step, other in enumerate(others)
    ]
    hidden.send(0)
    gains_all[index] = packed_ref[...]
    tree_tables_near(segments_ref, count, (member, reach, cosine, sine))

    def project(step):
        pair = Pair(place, step, rows)
        source = pair.read(hidden_all).astype(jnp.float32)
        value = low(source * root_of(source) * gains_ref[0:1, :])
        pair.write(normed, slice(None), value)
        raw = dot(value, weights[...])
        cos_rows, sin_rows = pair.read(cosine), pair.read(sine)
        for side, (raw_ref, low_ref) in enumerate(((q_raw, q_low), (k_raw, k_low))):
            item = raw[:, side * HEAD_DIM : (side + 1) * HEAD_DIM]
            pair.write(raw_ref, slice(None), item)
            item = item * root_of(item) * gains_ref[6 + side : 7 + side, :HEAD_DIM]
            first, second = item[:, : HEAD_DIM // 2], item[:, HEAD_DIM // 2 :]
            turned = jnp.concatenate(
                [first * cos_rows - second * sin_rows, second * cos_rows + first * sin_rows],
                axis=1,
            )
            pair.write(low_ref, slice(None), low(turned))
        pair.write(v_low, slice(None), low(raw[:, 2 * HEAD_DIM :]))

    for step in range(1, RING_STEPS):
        if step <= 3:
            for kv_step in (2 * step - 1, 2 * step):
                kv.send(kv_step)
                pass_on(kv, kv_mirror, kv_step)
        hidden.send(step)
        if step in (2, 3):
            for kv_step in (2 * step - 3, 2 * step - 2):
                pass_again(kv, kv_mirror, kv_other, kv_step)
        if step == 2:
            for number, copy in enumerate(q_copies):
                copy.wait_recv()
                q_mirror.give(number, q_at(number, quarter))
        if step == 3:
            for number in range(HEADS - 1):
                q_mirror.relay(number, q_at(number, other_quarter))
        if step == 4:
            kv.arrive(RING_STEPS)
            pass_on(kv, kv_mirror, RING_STEPS)
            for kv_step in (5, 6, 7):
                pass_again(kv, kv_mirror, kv_other, kv_step)
            for copy in gain_copies:
                copy.wait_recv()
            for owner in range(HEADS):
                gains_ref[:, owner * shard : (owner + 1) * shard] = gains_all[owner]
            total = gains_all[0, 6:, :]
            for owner in range(1, HEADS):
                total = total + gains_all[owner, 6:, :]
            gains_ref[6:, :shard] = total
        if step == 5:
            late_step(0)
            kv_mirror.arrive()
            q_mirror.arrive()
            loads[0].wait()
            loads[6].wait()
            key_at = (index // (HEADS // KV_HEADS)) * HEAD_DIM
            turns = start_loads(
                [
                    (
                        kv_all.at[:, span(key_at + side * KV_HEADS * HEAD_DIM, HEAD_DIM)],
                        weights.at[:, pl.ds((1 + side) * HEAD_DIM, HEAD_DIM)],
                    )
                    for side in range(2)
                ],
                load_sems.at[pl.ds(7, 2)],
            )
            for copy in turns:
                copy.wait()
            for number in range(3):
                project(number)
        if step == 6:
            late_step(1)
            for number in range(3, 6):
                project(number)
    late_step(2)
    project(6)
    hidden.arrive(RING_STEPS)
    project(7)
    stores = start_loads(
        (
            (normed, normed_any),
            (weights, weights_any),
            (q_raw, q_raw_any),
            (k_raw, k_raw_any),
            (q_low, q_low_any),
            (k_low, k_low_any),
            (v_low, v_low_any),
            (cosine, cosine_any),
            (sine, sine_any),
        ),
        store_sems,
    )
    loads[3].wait()
    scale = HEAD_DIM ** (-0.5)

    def attend(first_owner, second_owner):
        starts = (first_owner * rows, second_owner * rows + half)
        spans = [span(start, half) for start in starts]

        def read(ref):
            return jnp.concatenate([ref[rows_of, :] for rows_of in spans], axis=0)

        query = lax.broadcasted_iota(jnp.int32, (half, total_rows), 0)
        query = jnp.concatenate([query + start for start in starts], axis=0)
        key = lax.broadcasted_iota(jnp.int32, (rows, total_rows), 1)
        scores = mul_t(read(q_low), k_low[...]) * scale
        seen = (mul_t(read(reach), member[...]) > 0.5) & (key <= query)
        scores = jnp.where(seen, scores, MASKED)
        expo = jnp.exp(scores - jnp.max(scores, axis=1, keepdims=True))
        chance = low(expo / jnp.sum(expo, axis=1, keepdims=True))
        mixed = low(dot(chance, v_low[...]))
        for side, rows_of in enumerate(spans):
            probs[rows_of, :] = chance[side * half : (side + 1) * half]
            att[rows_of, :] = mixed[side * half : (side + 1) * half]
        part[...] = dot(mixed, o_proj[...])

    sums = RingSum(
        place,
        ends,
        4,
        sum_sems,
        held,
        lambda owner, lane: part[pl.ds(lane_offset(lane, rows), piece), :],
    )
    for step in range(RING_STEPS):
        attend(
            ring_index(lax.rem(place + HEADS - 1 - step, HEADS)),
            ring_index(lax.rem(place + step + 1, HEADS)),
        )
        sums.send(step)
        if step + 3 <= HEADS:
            late_step(step + 3)
    attend(index, index)
    stores += start_loads(((att, att_any), (probs, probs_any)), store_sems.at[pl.ds(9, 2)])
    for lane in range(4):
        sum_ref[pl.ds(lane_offset(lane, rows), piece), :] = sums.last(index, lane)
    for item in (hidden, kv, small, pl_proj, sums, kv_mirror, q_mirror):
        item.sent()
    for unused_ring, mirror, unused_there in late:
        mirror.finish()
    for copy in q_copies + gain_copies:
        copy.wait_send()
    for copy in loads[4:6] + stores:
        copy.wait()


def attention_forward(
    segments, norms, count, hidden, q_proj, k_proj, v_proj, small, pl_proj, o_proj, number
):
    rows, width = hidden.shape
    total = rows * HEADS
    shard = q_proj.shape[0]
    steps = 4 * RING_STEPS
    near, anywhere = pl.BlockSpec(memory_space=pltpu.VMEM), pl.BlockSpec(memory_space=pltpu.HBM)
    bf16, f32 = jnp.bfloat16, jnp.float32
    head = (total, HEAD_DIM)
    table = (total, HEAD_DIM // 2)
    kept = [
        ((total, width), bf16),
        ((width, 3 * HEAD_DIM), bf16),
        (head, f32),
        (head, f32),
        (head, bf16),
        (head, bf16),
        (head, bf16),
        (head, bf16),
        ((total, total), bf16),
        (table, f32),
        (table, f32),
    ]
    grown = [((shard * HEADS, small.shape[1]), bf16), ((pl_proj.shape[0] * HEADS, width), bf16)]
    low_steps = 2 * RING_STEPS
    counts = [steps, HEADS - 1, HEADS - 1] + [low_steps] * 3 + [steps]
    counts += [3 * (HEADS - 1)] + [3 * low_steps] * 3
    return pl.pallas_call(
        functools.partial(attention_kernel, count),
        out_shape=[
            jax.ShapeDtypeStruct((rows, width), f32),
            jax.ShapeDtypeStruct((8, width), f32),
        ]
        + [jax.ShapeDtypeStruct(shape, dtype) for shape, dtype in grown + kept],
        in_specs=[near, (anywhere,) * len(norms)] + [anywhere] * 7,
        out_specs=[near] * 2 + [anywhere] * (len(grown) + len(kept)),
        scratch_shapes=[pltpu.VMEM(shape, dtype) for shape, dtype in kept]
        + [
            pltpu.VMEM((total, width), bf16),
            pltpu.VMEM((width, 2 * k_proj.shape[1]), bf16),
            pltpu.VMEM((HEADS, 8, shard), f32),
            pltpu.VMEM((8, shard), f32),
            tuple(pltpu.VMEM(item.shape, bf16) for item in norms),
            pltpu.VMEM(o_proj.shape, bf16),
            pltpu.VMEM((total, segments.shape[1]), bf16),
            pltpu.VMEM((total, segments.shape[1]), bf16),
            pltpu.VMEM((rows, width), f32),
            pltpu.VMEM((steps + 4, rows // 4, width), bf16),
            pltpu.SemaphoreType.DMA((9 + len(norms),)),
            pltpu.SemaphoreType.DMA((11,)),
        ]
        + [pltpu.SemaphoreType.DMA((item,)) for item in counts for unused_side in range(2)],
        compiler_params=pltpu.CompilerParams(
            collective_id=number, has_side_effects=True, vmem_limit_bytes=VMEM_BYTES
        ),
    )(segments, norms, hidden, q_proj, k_proj, v_proj, small, pl_proj, o_proj)


def ffn_kernel(
    hidden_ref,
    branch_ref,
    gains_ref,
    small_any,
    gate_any,
    up_any,
    down_any,
    sum_ref,
    all_ref,
    act_ref,
    slope_ref,
    inner_ref,
    far_any,
    first_ref,
    low_rank_ref,
    left_low_ref,
    own_ref,
    laurel,
    gate,
    up,
    down,
    block,
    inner_block,
    part,
    held,
    load_sems,
    send_sem,
    recv_sem,
    sum_send,
    sum_recv,
    far_send,
    far_recv,
):
    rows, width = hidden_ref.shape
    units = gate.shape[0]
    piece = rows // 4
    index = lax.axis_index("fsdp")
    place = ring_place(index)
    ends = ring_ends(place)
    across = neighbours()[3]
    everyone = ends + (across,)
    announce(everyone)
    columns = laurel.shape[1]
    loads = start_loads(
        (
            (small_any.at[:, pl.ds(small_any.shape[1] - columns, columns)], laurel),
            (gate_any, gate),
            (up_any, up),
            (down_any, down),
        ),
        load_sems,
    )
    ring = Ring(
        place,
        ends,
        4,
        (send_sem, recv_sem),
        lambda lane: own_ref.at[pl.ds(lane_offset(lane, rows), piece)],
        lambda owner, lane: all_ref.at[span(owner * rows + lane_offset(lane, rows), piece)],
    )

    def own(owner, lane):
        return part[span(owner * rows + lane_offset(lane, rows), piece), :].astype(jnp.float32)

    sums = RingSum(place, ends, 4, (sum_send, sum_recv), held, own)

    def compute(step):
        pair = Pair(place, step, rows)
        block[...] = pair.read(all_ref)

        def into(tile):
            value = mul_t(block[...], gate[tile, :])
            second = mul_t(block[...], up[tile, :])
            act, slope = gelu_parts(value)
            inner = low(act * second)
            inner_block[:, tile] = inner
            pair.write(act_ref, tile, low(act))
            pair.write(slope_ref, tile, low(slope * second))
            pair.write(inner_ref, tile, inner)

        tile_loop(units // TILE, TILE, into)

        def out(tile):
            pair.write(part, tile, low(dot(inner_block[...], down[:, tile])))

        tile_loop(width // (2 * TILE), 2 * TILE, out)

    crossings = []

    def cross(step):
        for rows_of in Pair(place, step, rows).rows:
            crossings.append(
                remote(
                    all_ref.at[rows_of],
                    far_any.at[rows_of],
                    (far_send, far_recv),
                    len(crossings),
                    across,
                )
            )

    def normed_tile(tile):
        source = hidden_ref[tile, :].astype(jnp.float32)
        block[tile, :] = low(source * root_of(source) * gains_ref[0:1, :])

    def first_tile(tile):
        source = hidden_ref[tile, :].astype(jnp.float32)
        total = source + source * root_of(source) * gains_ref[0:1, :]
        for number, ref in ((1, branch_ref), (2, low_rank_ref)):
            value = ref[tile, :]
            total = total + value * root_of(value) * gains_ref[number : number + 1, :]
        total = total * HALF_ROOT
        first_ref[tile, :] = total
        own_ref[tile, :] = low(total * root_of(total) * gains_ref[3:4, :])

    rank = columns // 2
    tile_loop(rows // 32, 32, normed_tile)
    loads[0].wait()
    left_low = low(dot(block[...], laurel[...])[:, :rank])
    left_low_ref[...] = left_low
    low_rank_ref[...] = mul_t(left_low, laurel[:, rank:])
    tile_loop(rows // 32, 32, first_tile)
    await_all(everyone)
    ring.send(0)
    all_ref[span(index * rows, rows), :] = own_ref[...]
    cross(0)
    for copy in loads[1:]:
        copy.wait()
    compute(0)
    for step in range(1, HEADS):
        if step < RING_STEPS:
            ring.send(step)
            cross(step)
        else:
            ring.arrive(step)
        compute(step)
        sums.send(step - 1)
    for lane in range(4):
        sum_ref[pl.ds(lane_offset(lane, rows), piece), :] = sums.last(index, lane)
    ring.sent()
    sums.sent()
    for copy in crossings:
        copy.wait()


def ffn_forward(hidden, branch, gains, small, rank, gate, up, down, number):
    rows, width = hidden.shape
    units = gate.shape[0]
    near, anywhere = pl.BlockSpec(memory_space=pltpu.VMEM), pl.BlockSpec(memory_space=pltpu.HBM)
    total = rows * HEADS
    steps = 4 * RING_STEPS
    bf16 = jnp.bfloat16
    inner = jax.ShapeDtypeStruct((total, units), bf16)
    return pl.pallas_call(
        ffn_kernel,
        out_shape=[
            jax.ShapeDtypeStruct((rows, width), jnp.float32),
            jax.ShapeDtypeStruct((total, width), bf16),
            inner,
            inner,
            inner,
            jax.ShapeDtypeStruct((total, width), bf16),
            jax.ShapeDtypeStruct((rows, width), jnp.float32),
            jax.ShapeDtypeStruct((rows, width), jnp.float32),
            jax.ShapeDtypeStruct((rows, rank), bf16),
        ],
        in_specs=[near] * 3 + [anywhere] * 4,
        out_specs=[near] * 5 + [anywhere] + [near] * 3,
        scratch_shapes=[pltpu.VMEM((rows, width), bf16), pltpu.VMEM((width, 2 * rank), bf16)]
        + [pltpu.VMEM((units, width), bf16)] * 3
        + [
            pltpu.VMEM((rows, width), bf16),
            pltpu.VMEM((rows, units), bf16),
            pltpu.VMEM((total, width), bf16),
            pltpu.VMEM((steps + 4, rows // 4, width), bf16),
            pltpu.SemaphoreType.DMA((4,)),
        ]
        + [pltpu.SemaphoreType.DMA((steps,))] * 4
        + [pltpu.SemaphoreType.DMA((2 * RING_STEPS,))] * 2,
        compiler_params=pltpu.CompilerParams(
            collective_id=number, has_side_effects=True, vmem_limit_bytes=VMEM_BYTES
        ),
    )(hidden, branch, gains, small, gate, up, down)


def ffn_back_kernel(
    first_ref,
    ffw_ref,
    extra_ref,
    seed_ref,
    gains_ref,
    small_any,
    pl_proj_any,
    all_any,
    far_all_any,
    act_any,
    slope_any,
    inner_any,
    gate_any,
    up_any,
    down_any,
    sum_ref,
    result_ref,
    d_extra_ref,
    d_second_ref,
    gain_grads,
    down_out,
    gate_out,
    up_out,
    far_down,
    theirs_any,
    joint_any,
    far_gate_any,
    far_up_any,
    far_rest_any,
    gate_sum,
    proj_sum,
    d_all,
    tokens,
    d_up,
    d_gate,
    inner,
    gate,
    up,
    down,
    block,
    inner_block,
    part,
    held,
    turned,
    give,
    keep,
    theirs,
    own_ref,
    pl_gate,
    pl_proj,
    crossed,
    d_pl_out,
    gate_blocks,
    gate_folded,
    gate_far,
    gate_held,
    proj_blocks,
    proj_folded,
    proj_far,
    proj_held,
    load_sems,
    store_sems,
    *sems,
):
    pairs = [sems[i : i + 2] for i in range(0, len(sems), 2)]
    ring_sems, sum_sems, fold_sems, far_sems, gate_sems, proj_sems = pairs[:6]
    pl_fold_sems, pl_far_sems, cross_sems, rest_sems, joint_sems = pairs[6:]
    rows, width = first_ref.shape
    units = gate.shape[0]
    piece = rows // 4
    index = lax.axis_index("fsdp")
    place = ring_place(index)
    ends = ring_ends(place)
    unused_chip, core, sibling, across = neighbours()
    per_layer = pl_gate.shape[1]
    (
        load_pl_gate,
        load_pl_proj,
        load_down,
        load_act,
        load_slope,
        load_gate,
        load_up,
        load_inner,
        load_tokens,
    ) = start_loads(
        (
            (small_any.at[:, pl.ds(0, per_layer)], pl_gate),
            (pl_proj_any, pl_proj),
            (down_any, down),
            (act_any, d_up),
            (slope_any, d_gate),
            (gate_any, gate),
            (up_any, up),
            (inner_any, inner),
            (all_any, tokens),
        ),
        load_sems,
    )
    everyone = ends + (sibling, across)
    announce(everyone)
    ring = Ring(
        place,
        ends,
        4,
        ring_sems,
        lambda lane: own_ref.at[pl.ds(lane_offset(lane, rows), piece)],
        lambda owner, lane: d_all.at[span(owner * rows + lane_offset(lane, rows), piece)],
    )

    def own(owner, lane):
        return part[span(owner * rows + lane_offset(lane, rows), piece), :].astype(jnp.float32)

    chip = neighbours()[0]
    mine, yours = 2 * chip + core, 2 * (1 - chip) + core

    def block_ring(block_sems, block_held, blocks):
        low_rows = blocks.shape[2] // 2
        return RingSum(
            place,
            ends,
            2,
            block_sems,
            block_held,
            lambda owner, lane: blocks[owner, mine, pl.ds(lane * low_rows, low_rows), :].astype(
                jnp.float32
            ),
        )

    sums = RingSum(place, ends, 4, sum_sems, held, own)
    pl_rings = (
        block_ring(gate_sems, gate_held, gate_blocks),
        block_ring(proj_sems, proj_held, proj_blocks),
    )
    pl_arrays = (
        (gate_blocks, gate_folded, gate_far),
        (proj_blocks, proj_folded, proj_far),
    )
    pl_folds, pl_sends = [], []

    def per_layer_branch():
        def after_ffw(tile):
            value = ffw_ref[tile, :]
            total = first_ref[tile, :] + value * root_of(value) * gains_ref[0:1, :]
            sum_ref[tile, :] = total
            block[tile, :] = low(total)

        tile_loop(rows // 32, 32, after_ffw)
        load_pl_gate.wait()
        load_pl_proj.wait()
        extra = extra_ref[...].astype(jnp.float32)
        act, slope = gelu_parts(dot(block[...], pl_gate[...]))
        mix = low(act * extra)
        d_second_ref[...] = dot(mix, pl_proj[...])

        def back_out(tile):
            value = d_second_ref[tile, :]
            result_ref[tile, :] = low(sum_ref[tile, :] + value * root_of(value) * gains_ref[1:2, :])
            grad, gain_grad = norm_pull(
                value, gains_ref[1:2, :], seed_ref[tile, :].astype(jnp.float32)
            )
            d_pl_out[tile, :] = low(grad)
            gain_grads[1:2, :] += gain_grad

        tile_loop(rows // 32, 32, back_out)
        d_mix = mul_t(d_pl_out[...], pl_proj[...])
        d_extra_ref[...] = low(d_mix * act)
        d_pre = low(d_mix * extra * slope)
        d_second_ref[...] = mul_t(d_pre, pl_gate[...])

        def back_ffw(tile):
            grad = seed_ref[tile, :].astype(jnp.float32) + d_second_ref[tile, :]
            d_second_ref[tile, :] = grad
            grad, gain_grad = norm_pull(ffw_ref[tile, :], gains_ref[0:1, :], grad)
            own_ref[tile, :] = low(grad)
            gain_grads[0:1, :] += gain_grad

        tile_loop(rows // 32, 32, back_ffw)
        return (mix, d_pre)

    def per_layer_grads(mix, d_pre):
        turned_mix = mix.T
        deep = proj_blocks.shape[2]
        for step in range(QUARTERS):
            wide = proj_blocks.shape[3]
            value = low(dot(turned_mix, d_pl_out[:, step * wide : (step + 1) * wide]))
            for owner in range(HEADS):
                proj_blocks[owner, step] = value[owner * deep : (owner + 1) * deep]
        shard = width // HEADS
        for owner in range(HEADS):
            value = low(dot(block[:, owner * shard : (owner + 1) * shard].T, d_pre))
            for step in range(QUARTERS):
                gate_blocks[owner, step] = value[
                    step * (shard // QUARTERS) : (step + 1) * (shard // QUARTERS)
                ]

    def pl_fold():
        for number, (blocks, folded, far) in enumerate(pl_arrays):
            for side in range(2):
                pl_folds[2 * number + side].wait_recv()
            for owner in range(HEADS):
                blocks[owner, yours] = add_low(blocks[owner, yours], folded[1 - chip, owner])
            pl_sends.append(remote(blocks.at[:, yours], far, pl_far_sems, number, across))
            for owner in range(HEADS):
                blocks[owner, mine] = add_low(blocks[owner, mine], folded[chip, owner])

    def pl_join():
        for number, (blocks, folded, far) in enumerate(pl_arrays):
            pl_sends[number].wait_recv()
            for owner in range(HEADS):
                blocks[owner, mine] = add_low(blocks[owner, mine], far[owner])

    def compute(step):
        pair = Pair(place, step, rows)
        block[...] = pair.read(d_all)

        def into(tile):
            grad = mul_t(block[...], down[tile, :])
            first = low(grad * pair.read(d_gate, tile).astype(jnp.float32))
            second = low(grad * pair.read(d_up, tile).astype(jnp.float32))
            pair.write(d_gate, tile, first)
            pair.write(d_up, tile, second)
            inner_block[0, :, tile] = first
            inner_block[1, :, tile] = second

        tile_loop(units // TILE, TILE, into)
        if step == 0:
            load_gate.wait()
            load_up.wait()

        def out(tile):
            total = dot(inner_block[0], gate[:, tile]) + dot(inner_block[1], up[:, tile])
            pair.write(part, tile, low(total))

        tile_loop(width // (2 * TILE), 2 * TILE, out)

    half = units // 2
    crossings, swaps = [], []

    def cross(step):
        slot = step % 2
        if step >= 2:
            for copy in crossings[2 * step - 4 : 2 * step - 2]:
                copy.wait_send()
        columns = span((1 - chip) * half, half)
        for number, target in enumerate((far_gate_any, far_up_any)):
            crossed[slot, number] = inner_block[number, :, columns]
            crossings.append(
                remote(
                    crossed.at[slot, number], target.at[step], cross_sems, len(crossings), across
                )
            )

    def outer_into(side, turn, right, target, add=False):
        if not side:
            turned[...] = turn().T
        wide = width // 2

        def tile_step(number, carry):
            tile = span(side * wide + number * 2 * TILE, 2 * TILE)
            value = dot(turned[...], right[:, tile])
            if add:
                value = value + target[:, tile].astype(jnp.float32)
            target[:, tile] = low(value)
            return carry

        lax.fori_loop(0, wide // (2 * TILE), tile_step, 0)

    def add_from(landed, rows_of, target):
        count = landed.shape[0]
        copy = pltpu.make_async_copy(landed, theirs.at[pl.ds(0, count)], load_sems.at[10])
        copy.start()
        copy.wait()

        def add(tile):
            here = span(rows_of + tile.start, 64)
            target[here, :] = add_low(target[here, :], theirs[tile, :])

        tile_loop(count // 64, 64, add)

    early_rows = half * 5 // 8
    folds, stores, joints, far_parts = [], [], [], []

    def down_give(side):
        outer_into(side, lambda: inner[:, span((1 - core) * half, half)], d_all, give)
        if side:
            folds.append(remote(give, theirs_any, fold_sems, 0, sibling))

    def down_keep(side):
        outer_into(side, lambda: inner[:, span(core * half, half)], d_all, keep)

    def down_fold():
        folds[0].wait_recv()
        add_from(theirs_any, 0, keep)
        stores.extend(start_loads(((keep, down_out),), store_sems.at[pl.ds(0, 1)]))

    def down_swap():
        stores.pop().wait()
        early = pl.ds(0, early_rows)
        swaps.append(remote(down_out.at[early], far_down.at[early], far_sems, 0, across))
        folds[0].wait_send()

    def near_grads(number, side):
        source, target = ((d_gate, give), (d_up, keep))[number]
        outer_into(side, lambda: source[:, span(chip * half, half)], tokens, target)

    def far_loads():
        for copy in rests + crossings:
            copy.wait_recv()
        for copy in rests + crossings[-4:]:
            copy.wait_send()
        parts = [(far_all_any, tokens)]
        for step in range(HEADS):
            for side, rows_of in enumerate(Pair(place, step, rows).rows):
                here = pl.ds(side * (rows // 2), rows // 2)
                parts.append((far_gate_any.at[step, here], d_gate.at[rows_of, pl.ds(0, half)]))
                parts.append((far_up_any.at[step, here], d_up.at[rows_of, pl.ds(0, half)]))
        far_parts.extend(start_loads(parts, load_sems.at[pl.ds(11, len(parts))]))

    def far_rest_loads():
        for copy in far_parts:
            copy.wait()
        for copy in start_loads(
            [
                (far_rest_any.at[pl.ds(side * (rows // 2), rows // 2)], tokens.at[rows_of])
                for side, rows_of in enumerate(last_pair.rows)
            ],
            load_sems.at[pl.ds(11, 2)],
        ):
            copy.wait()

    def far_grads(number, side):
        source, target = ((d_gate, give), (d_up, keep))[number]
        outer_into(side, lambda: source[:, :half], tokens, target, add=True)
        if side:
            joints.append(
                remote(
                    target.at[span((1 - core) * (half // 2), half // 2)],
                    joint_any.at[number],
                    joint_sems,
                    number,
                    sibling,
                )
            )

    def join(number):
        target, out = ((give, gate_out), (keep, up_out))[number]
        joints[number].wait_recv()
        add_from(joint_any.at[number], core * (half // 2), target)
        store = pltpu.make_async_copy(
            target.at[span(core * (half // 2), half // 2)], out, store_sems.at[number]
        )
        store.start()
        stores.append(store)

    gain_grads[...] = jnp.zeros_like(gain_grads)
    mix, d_pre = per_layer_branch()
    await_all(everyone)
    ring.send(0)
    last_pair = Pair(place, RING_STEPS, rows)
    rests = [
        remote(
            all_any.at[rows_of],
            far_rest_any.at[pl.ds(side * (rows // 2), rows // 2)],
            rest_sems,
            side,
            across,
        )
        for side, rows_of in enumerate(last_pair.rows)
    ]
    per_layer_grads(mix, d_pre)
    for number, (blocks, folded, unused_far) in enumerate(pl_arrays):
        for side in range(2):
            pl_folds.append(
                remote(
                    blocks.at[:, 2 * side + 1 - core],
                    folded.at[side],
                    pl_fold_sems,
                    2 * number + side,
                    sibling,
                )
            )
    d_all[span(index * rows, rows), :] = own_ref[...]
    for copy in (load_down, load_act, load_slope):
        copy.wait()
    compute(0)
    cross(0)
    for step in range(1, HEADS):
        if step < RING_STEPS:
            ring.send(step)
        else:
            ring.arrive(step)
        if step >= RING_STEPS - 1:
            sums.send(step - RING_STEPS + 1)
            for item in pl_rings:
                item.send(step - RING_STEPS + 1)
        compute(step)
        cross(step)
        if step == 2:
            pl_fold()
        if step == 4:
            pl_join()
    load_inner.wait()
    load_tokens.wait()
    down_give(0)
    down_give(1)
    tasks = (
        (lambda: down_keep(0),),
        (lambda: down_keep(1),),
        (down_fold,),
        (down_swap, lambda: near_grads(0, 0)),
        (lambda: near_grads(0, 1), lambda: near_grads(1, 0)),
        (lambda: near_grads(1, 1), far_loads),
        (far_rest_loads, lambda: far_grads(0, 0), lambda: far_grads(0, 1)),
        (lambda: far_grads(1, 0),),
        (lambda: far_grads(1, 1),),
        (lambda: join(0),),
    )
    for number, group in enumerate(tasks):
        step = 2 + number // 2
        first = 2 * (number % 2)
        sums.send(step, (first, first + 1))
        if not first:
            for item in pl_rings:
                item.send(step)
        for task in group:
            task()
    for lane in range(4):
        sum_ref[pl.ds(lane_offset(lane, rows), piece), :] = sums.last(index, lane)
    join(1)
    for item, target in zip(pl_rings, (gate_sum, proj_sum)):
        low_rows = target.shape[0] // 2
        for lane in range(2):
            target[pl.ds(lane * low_rows, low_rows), :] = low(item.last(index, lane))
    for item in (ring, sums) + pl_rings:
        item.sent()
    for copy in pl_folds + pl_sends:
        copy.wait_send()
    for copy in joints:
        copy.wait_send()
    for copy in stores + swaps:
        copy.wait()


def ffn_back(local, gains, small, pl_proj, arrays, weights, number):
    rows, width = local[0].shape
    units = weights[0].shape[0]
    near, anywhere = pl.BlockSpec(memory_space=pltpu.VMEM), pl.BlockSpec(memory_space=pltpu.HBM)
    total = rows * HEADS
    steps = 4 * RING_STEPS
    bf16, f32 = jnp.bfloat16, jnp.float32
    low_steps = 2 * RING_STEPS
    counts = [steps, steps, 1, 1, low_steps, low_steps, 4, 2, 2 * HEADS, 2, 2]
    half = (units // 2, width)
    quarter = (units // 4, width)
    deep, per_layer = pl_proj.shape[0] // HEADS, local[2].shape[1]
    gate_block = (width // HEADS // QUARTERS, per_layer)
    proj_block = (deep, width // QUARTERS)

    def block_scratch(shape):
        return [
            pltpu.VMEM((HEADS, QUARTERS) + shape, bf16),
            pltpu.VMEM((2, HEADS) + shape, bf16),
            pltpu.VMEM((HEADS,) + shape, bf16),
            pltpu.VMEM((low_steps + 2, shape[0] // 2, shape[1]), bf16),
        ]

    return pl.pallas_call(
        ffn_back_kernel,
        out_shape=[
            jax.ShapeDtypeStruct((rows, width), f32),
            jax.ShapeDtypeStruct((rows, width), bf16),
            jax.ShapeDtypeStruct((rows, per_layer), bf16),
            jax.ShapeDtypeStruct((rows, width), f32),
            jax.ShapeDtypeStruct(gains.shape, f32),
        ]
        + [jax.ShapeDtypeStruct(half, bf16)]
        + [jax.ShapeDtypeStruct(quarter, bf16)] * 2
        + [jax.ShapeDtypeStruct(half, bf16)] * 2
        + [jax.ShapeDtypeStruct((2,) + quarter, bf16)]
        + [jax.ShapeDtypeStruct((HEADS, rows, units // 2), bf16)] * 2
        + [jax.ShapeDtypeStruct((rows, width), bf16)]
        + [jax.ShapeDtypeStruct(gate_block, bf16), jax.ShapeDtypeStruct(proj_block, bf16)],
        in_specs=[near] * 5 + [anywhere] * 10,
        out_specs=[near] * 5 + [anywhere] * 9 + [near] * 2,
        scratch_shapes=[pltpu.VMEM((total, width), bf16)] * 2
        + [pltpu.VMEM((total, units), bf16)] * 3
        + [pltpu.VMEM((units, width), bf16)] * 3
        + [
            pltpu.VMEM((rows, width), bf16),
            pltpu.VMEM((2, rows, units), bf16),
            pltpu.VMEM((total, width), bf16),
            pltpu.VMEM((steps + 4, rows // 4, width), bf16),
            pltpu.VMEM((units // 2, total), bf16),
            pltpu.VMEM(half, bf16),
            pltpu.VMEM(half, bf16),
            pltpu.VMEM(half, bf16),
            pltpu.VMEM((rows, width), bf16),
            pltpu.VMEM((width, per_layer), bf16),
            pltpu.VMEM(pl_proj.shape, bf16),
            pltpu.VMEM((2, 2, rows, units // 2), bf16),
            pltpu.VMEM((rows, width), bf16),
        ]
        + block_scratch(gate_block)
        + block_scratch(proj_block)
        + [pltpu.SemaphoreType.DMA((12 + 4 * HEADS,)), pltpu.SemaphoreType.DMA((2,))]
        + [pltpu.SemaphoreType.DMA((count,)) for count in counts for unused_side in range(2)],
        compiler_params=pltpu.CompilerParams(
            collective_id=number, has_side_effects=True, vmem_limit_bytes=VMEM_BYTES
        ),
    )(*local, gains, small, pl_proj, *arrays, *weights)


def head_back(grad, raw, gain, cosine, sine):
    half = raw.shape[1] // 2
    first, second = grad[:, :half], grad[:, half:]
    turned = jnp.concatenate(
        [first * cosine + second * sine, second * cosine - first * sine], axis=1
    )
    root = lax.rsqrt(jnp.mean(raw * raw, axis=1, keepdims=True) + EPS)
    gain_grad = jnp.sum(turned * raw * root, axis=0, keepdims=True)
    turned = turned * gain
    along = jnp.mean(turned * raw, axis=1, keepdims=True)
    return (root * turned - raw * (root * root * root * along), gain_grad)


def attention_back_kernel(
    hidden_ref,
    first_ref,
    d_ffwin_ref,
    d_second_ref,
    branch_ref,
    low_rank_ref,
    left_low_ref,
    gains_ref,
    ffw_gains_ref,
    o_any,
    q_any,
    k_any,
    v_any,
    att_any,
    probs_any,
    normed_any,
    weights_any,
    q_raw_any,
    k_raw_any,
    cosine_any,
    sine_any,
    small_any,
    pl_gate_ref,
    pl_proj_ref,
    own_down,
    far_down,
    own_gate,
    own_up,
    source_ref,
    owned_any,
    early_any,
    pl_proj_all,
    gain_sums,
    total_down,
    total_gate,
    total_up,
    far_rest,
    o_proj,
    q_low,
    k_low,
    v_low,
    att,
    probs,
    normed,
    weights,
    q_raw,
    k_raw,
    cosine,
    sine,
    d_all,
    block,
    att_block,
    q_block,
    dq_block,
    d_q,
    d_k,
    d_v,
    d_qkv,
    turned,
    part,
    held,
    blocks,
    folded,
    far,
    near_sum,
    key_held,
    o_grad,
    o_folded,
    o_far,
    sum_own,
    sum_far,
    own_ref,
    laurel,
    d_low_rank,
    d_scaled,
    sum_ref,
    gain_rows,
    gain_parts,
    gain_landed,
    gain_totals,
    owned_ref,
    early_ref,
    load_sems,
    final_sems,
    *sems,
):
    pairs = [sems[i : i + 2] for i in range(0, len(sems), 2)]
    ring_sems, sum_sems, fold_sems, far_sems, swap_sems, key_sems = pairs[:6]
    mirror_sems, early_sems, o_fold_sems, o_far_sems, cross_sems, total_sems, proj_sems = pairs[6:13]
    gain_sems, twin_sems, units_sems = pairs[13:]
    rows, width = own_ref.shape
    total_rows = rows * HEADS
    half = rows // 2
    piece = rows // 4
    index = lax.axis_index("fsdp")
    chip, core, sibling, across = neighbours()
    place = ring_place(index)
    ends = ring_ends(place)
    others = [lax.rem(index + step, HEADS) for step in range(1, HEADS)]
    quarter = 2 * chip + core
    quarter_rows = blocks.shape[2]
    own_rows = span(quarter * quarter_rows, quarter_rows)
    other_rows = span((2 * (1 - chip) + core) * quarter_rows, quarter_rows)
    groups = HEADS // KV_HEADS
    scale = HEAD_DIM ** (-0.5)
    head_columns = 3 * HEAD_DIM
    loads = start_loads(
        (
            (o_any, o_proj),
            (q_any, q_low),
            (k_any, k_low),
            (v_any, v_low),
            (att_any, att),
            (probs_any, probs),
            (q_raw_any, q_raw),
            (k_raw_any, k_raw),
            (cosine_any, cosine),
            (sine_any, sine),
            (weights_any, weights),
            (normed_any, normed),
            (small_any.at[:, span(small_any.shape[1] - laurel.shape[1], laurel.shape[1])], laurel),
        ),
        load_sems,
    )
    rep = lax.axis_index("rep")
    twins = [lax.rem(rep + step, QUARTERS) for step in range(1, QUARTERS)]
    everyone = [{"fsdp": other} for other in others] + [{"rep": twin} for twin in twins]
    greet(everyone)
    late_rows = far_rest.shape[0]
    early_rows = own_down.shape[0] - late_rows
    late = pl.ds(early_rows, late_rows)
    part_rows = own_gate.shape[0]
    unit_rows = span(quarter * part_rows, part_rows)
    other_unit_rows = span((2 * (1 - chip) + core) * part_rows, part_rows)
    units = Mirror(2, units_sems)
    units.give(0, total_gate.at[unit_rows], own_gate)
    crossings = [remote(own_down.at[late], far_rest, cross_sems, 0, across)]
    units.give(1, total_up.at[unit_rows], own_up)
    placed = start_loads(
        ((own_gate, total_gate.at[unit_rows]), (own_up, total_up.at[unit_rows])),
        final_sems.at[pl.ds(5, 2)],
    )
    ring = Ring(
        place,
        ends,
        4,
        ring_sems,
        lambda lane: own_ref.at[pl.ds(lane_offset(lane, rows), piece)],
        lambda owner, lane: d_all.at[span(owner * rows + lane_offset(lane, rows), piece)],
    )
    sums = RingSum(
        place,
        ends,
        4,
        sum_sems,
        held,
        lambda owner, lane: part[pl.ds(lane_offset(lane, rows), piece), :],
    )
    key_tiles = total_rows // TILE
    rank = laurel.shape[1] // 2

    def before(tile):
        grad, part_sum = norm_pull(first_ref[tile, :], gains_ref[3:4, :], d_ffwin_ref[tile, :])
        gain_rows[3:4, :] += part_sum
        scaled = (d_second_ref[tile, :] + grad) * HALF_ROOT
        d_scaled[tile, :] = scaled
        grad, part_sum = norm_pull(branch_ref[tile, :], gains_ref[1:2, :], scaled)
        gain_rows[1:2, :] += part_sum
        own_ref[tile, :] = low(grad)
        grad, part_sum = norm_pull(low_rank_ref[tile, :], gains_ref[2:3, :], scaled)
        gain_rows[2:3, :] += part_sum
        d_low_rank[tile, :] = low(grad)

    def low_rank_grads():
        d_left = low(dot(d_low_rank[...], laurel[...])[:, rank:])
        source = hidden_ref[...].astype(jnp.float32)
        block[...] = low(source * root_of(source) * gains_ref[0:1, :])
        shard = width // HEADS
        for owner in range(HEADS):
            columns = slice(owner * shard, (owner + 1) * shard)
            value = jnp.concatenate(
                [
                    dot(block[:, columns].T, d_left),
                    dot(d_low_rank[:, columns].T, left_low_ref[...]),
                ],
                axis=1,
            )
            value = low(value)
            for step in range(QUARTERS):
                blocks[owner, step, :, head_columns:] = value[
                    step * quarter_rows : (step + 1) * quarter_rows
                ]
        return d_left

    def after(tile):
        grad = d_scaled[tile, :] + sum_ref[tile, :]
        grad, part_sum = norm_pull(
            hidden_ref[tile, :].astype(jnp.float32), gains_ref[0:1, :], grad
        )
        gain_rows[0:1, :] += part_sum
        source_ref[tile, :] = low(d_scaled[tile, :] + grad)

    def compute(step):
        pair = Pair(place, step, rows)
        block[...] = pair.read(d_all)
        d_att = low(mul_t(block[...], o_proj[...]))
        att_block[...] = d_att
        q_block[...] = pair.read(q_low)
        delta = jnp.sum(
            d_att.astype(jnp.float32) * pair.read(att).astype(jnp.float32), axis=1, keepdims=True
        )
        dq_block[...] = jnp.zeros_like(dq_block)

        def keys(tile):
            chance = pair.read(probs, tile)
            d_chance = mul_t(att_block[...], v_low[tile, :])
            d_score = low(chance.astype(jnp.float32) * (d_chance - delta) * scale)
            dq_block[...] += dot(d_score, k_low[tile, :])
            d_k[tile, :] += dot(d_score.T, q_block[...])
            d_v[tile, :] += dot(chance.T, att_block[...])

        tile_loop(key_tiles, TILE, keys)
        pair.write(d_q, slice(None), dq_block[...])

    half_units = own_down.shape[0]
    final_loads, final_sends = [], []

    def load_final():
        crossings[0].wait_recv()
        early_part = pl.ds(0, early_rows)
        final_loads.extend(
            start_loads(
                (
                    (own_down, sum_own),
                    (far_down.at[early_part], sum_far.at[early_part]),
                    (far_rest, sum_far.at[late]),
                ),
                final_sems.at[pl.ds(0, 3)],
            )
        )

    def add_final():
        for copy in final_loads:
            copy.wait()

        def add(tile):
            sum_own[tile, :] = add_low(sum_own[tile, :], sum_far[tile, :])

        tile_loop(half_units // 64, 64, add)
        target = total_down.at[span(core * half_units, half_units)]
        final_sends.append(remote(sum_own, target, total_sems, 0, sibling))
        final_loads.extend(start_loads(((sum_own, target),), final_sems.at[pl.ds(0, 1)]))

    d_k[...] = jnp.zeros_like(d_k)
    d_v[...] = jnp.zeros_like(d_v)
    gain_rows[...] = jnp.zeros_like(gain_rows)
    tile_loop(rows // 32, 32, before)
    ring.send(0)
    d_all[span(index * rows, rows), :] = own_ref[...]
    loads[12].wait()
    d_left = low_rank_grads()
    for copy in loads[:6]:
        copy.wait()
    compute(0)
    for step in range(1, HEADS):
        if step < RING_STEPS:
            ring.send(step)
        else:
            ring.arrive(step)
        compute(step)
        if step == 6:
            units.relay(0, total_gate.at[other_unit_rows])
    for copy in loads[6:12]:
        copy.wait()

    def raw_tile(tile):
        for side, (grad, raw) in enumerate(((d_q, q_raw), (d_k, k_raw))):
            value, gain_grad = head_back(
                grad[tile, :],
                raw[tile, :],
                gains_ref[6 + side : 7 + side, :HEAD_DIM],
                cosine[tile, :],
                sine[tile, :],
            )
            d_qkv[tile, side * HEAD_DIM : (side + 1) * HEAD_DIM] = low(value)
            gain_rows[6 + side : 7 + side, :HEAD_DIM] += gain_grad
        d_qkv[tile, 2 * HEAD_DIM :] = low(d_v[tile, :])

    tile_loop(total_rows // 128, 128, raw_tile)

    def owner_at(step, way):
        return ring_index(lax.rem(place + (step + 1 if way else HEADS - 1 - step), HEADS))

    def part_of(step):
        tops = [
            d_qkv[span(owner_at(step, way) * rows + way * half, half), :] for way in range(2)
        ]
        part[...] = mul_t(jnp.concatenate(tops, axis=0), weights[...])

    def head_grads(number, carry):
        turned[...] = normed[:, span(number * TILE, TILE)].T
        value = low(dot(turned[...], d_qkv[...]))
        for step in range(QUARTERS):
            blocks[number, step, :, :head_columns] = value[
                step * quarter_rows : (step + 1) * quarter_rows
            ]
        return carry

    def o_tile(tile):
        value = low(dot(turned[...], d_all[:, tile]))
        for step in range(QUARTERS):
            o_grad[step, :, tile] = value[step * quarter_rows : (step + 1) * quarter_rows]

    folds, o_folds, across_sends, swaps, key_swaps = [], [], [], [], []
    mirror, early, pl_mirror = Mirror(2, mirror_sems), Mirror(1, early_sems), Mirror(1, proj_sems)
    wide = pl_proj_ref.shape[1]
    own_columns = span(quarter * wide, wide)
    other_columns = span((2 * (1 - chip) + core) * wide, wide)
    rest = blocks.shape[3] - HEAD_DIM
    q_columns = HEADS * HEAD_DIM
    mine, yours = 2 * chip + core, 2 * (1 - chip) + core
    cut_rows = quarter_rows // 2
    cuts = [pl.ds(cut * cut_rows, cut_rows) for cut in range(2)]

    def fold_sends():
        for side in range(2):
            folds.append(
                remote(blocks.at[:, 2 * side + 1 - core], folded.at[side], fold_sems, side, sibling)
            )

    def fold_far(cut):
        if not cut:
            folds[0].wait_recv()
            folds[1].wait_recv()
        rows_of = cuts[cut]
        for number in range(HEADS):
            blocks[number, yours, rows_of, :] = add_low(
                blocks[number, yours, rows_of, :], folded[1 - chip, number, rows_of, :]
            )
        across_sends.append(
            remote(blocks.at[:, yours, rows_of], far.at[:, rows_of], far_sems, cut, across)
        )

    def fold_near():
        for number in range(HEADS):
            blocks[number, mine] = add_low(blocks[number, mine], folded[chip, number])

    def o_half(side):
        if not side:
            turned[...] = att[...].T
        for number in range(2):
            tile = pl.ds((2 * side + number) * (width // 4), width // 4)
            o_tile(tile)
        if side:
            for item in range(2):
                o_folds.append(
                    remote(
                        o_grad.at[2 * item + 1 - core], o_folded.at[item], o_fold_sems, item, sibling
                    )
                )

    def o_fold():
        for copy in o_folds:
            copy.wait_recv()
        o_grad[yours] = add_low(o_grad[yours], o_folded[1 - chip])
        across_sends.append(remote(o_grad.at[yours], o_far, o_far_sems, 0, across))
        o_grad[mine] = add_low(o_grad[mine], o_folded[chip])

    def swap_cut(cut):
        across_sends[cut].wait_recv()
        rows_of = cuts[cut]
        for number in range(HEADS):
            near_sum[number, rows_of, :] = add_low(
                blocks[number, mine, rows_of, :], far[number, rows_of, :]
            )
        landing = span(quarter * quarter_rows + cut * cut_rows, cut_rows)
        here = span(index * HEAD_DIM, HEAD_DIM)
        for step, other in enumerate(others):
            number = cut * (HEADS - 1) + step
            swaps.append(
                remote(
                    near_sum.at[other, rows_of, pl.ds(0, HEAD_DIM)],
                    owned_ref.at[landing, here],
                    swap_sems,
                    number,
                    {"fsdp": other},
                )
            )
            key_swaps.append(
                remote(
                    near_sum.at[other, rows_of, pl.ds(HEAD_DIM, rest)],
                    key_held.at[index, rows_of],
                    key_sems,
                    number,
                    {"fsdp": other},
                )
            )
        owned_ref[landing, here] = near_sum[index, rows_of, :HEAD_DIM]
        key_held[index, rows_of, :] = near_sum[index, rows_of, HEAD_DIM:]

    def early_give():
        across_sends[2].wait_recv()
        early_ref[own_rows, :width] = add_low(o_grad[mine], o_far[...])
        early_ref[own_rows, width:] = pl_gate_ref[...]
        early.give(0, early_ref.at[own_rows])
        pl_proj_all[:, own_columns] = pl_proj_ref[...]
        pl_mirror.give(0, pl_proj_all.at[:, own_columns])

    def early_relay():
        early.relay(0, early_ref.at[other_rows])
        pl_mirror.relay(0, pl_proj_all.at[:, other_columns])

    part_of(0)
    sums.send(0)
    lax.fori_loop(0, width // TILE, head_grads, 0)
    fold_sends()
    tasks = (
        (lambda: o_half(0),),
        (lambda: o_half(1), lambda: fold_far(0)),
        (lambda: fold_far(1),),
        (fold_near,),
        (o_fold,),
        (load_final,),
        (lambda: swap_cut(0),),
        (add_final,),
        (lambda: swap_cut(1), lambda: units.relay(1, total_up.at[other_unit_rows])),
        (),
        (early_give,),
        (),
    )
    for number, group in enumerate(tasks):
        step = 1 + number // 2
        first = 2 * (number % 2)
        if not first:
            part_of(step)
        sums.send(step, (first, first + 1))
        for task in group:
            task()
    part[...] = mul_t(d_qkv[span(index * rows, rows), :], weights[...])
    for lane in range(4):
        sum_ref[pl.ds(lane_offset(lane, rows), piece), :] = sums.last(index, lane)

    def finish_cut(cut):
        here = slice(cut * (HEADS - 1), (cut + 1) * (HEADS - 1))
        for copy in swaps[here] + key_swaps[here]:
            copy.wait_recv()
        rows_of = cuts[cut]
        landing = span(quarter * quarter_rows + cut * cut_rows, cut_rows)
        for head in range(KV_HEADS):
            total = key_held[head * groups, rows_of, :].astype(jnp.float32)
            for step in range(1, groups):
                total = total + key_held[head * groups + step, rows_of, :].astype(jnp.float32)
            total = low(total)
            for side in range(2):
                base = q_columns + (side * KV_HEADS + head) * HEAD_DIM
                owned_ref[landing, pl.ds(base, HEAD_DIM)] = total[
                    :, side * HEAD_DIM : (side + 1) * HEAD_DIM
                ]
        extra = key_held[0, rows_of, 2 * HEAD_DIM :].astype(jnp.float32)
        for step in range(1, HEADS):
            extra = extra + key_held[step, rows_of, 2 * HEAD_DIM :].astype(jnp.float32)
        base = q_columns + 2 * KV_HEADS * HEAD_DIM
        owned_ref[landing, pl.ds(base, rest - 2 * HEAD_DIM)] = low(extra)
        mirror.give(cut, owned_ref.at[landing])

    def relay_cut(cut):
        start = (2 * (1 - chip) + core) * quarter_rows + cut * cut_rows
        mirror.relay(cut, owned_ref.at[span(start, cut_rows)])

    finish_cut(0)
    sum_ref[...] += mul_t(d_left, laurel[:, :rank])
    tile_loop(rows // 32, 32, after)
    gain_rows[4:6, :] = ffw_gains_ref[...]
    shard = width // HEADS
    for owner in range(HEADS):
        gain_parts[owner, :6] = gain_rows[:6, owner * shard : (owner + 1) * shard]
        gain_parts[owner, 6:] = gain_rows[6:, :HEAD_DIM]
    gain_sends = [
        remote(gain_parts.at[other], gain_landed.at[index], gain_sems, step, {"fsdp": other})
        for step, other in enumerate(others)
    ]
    gain_landed[index] = gain_parts[index]
    finish_cut(1)
    for copy in gain_sends:
        copy.wait_recv()
    total = gain_landed[0]
    for step in range(1, HEADS):
        total = total + gain_landed[step]
    gain_totals[rep] = total
    twin_sends = [
        remote(gain_totals.at[rep], gain_totals.at[rep], twin_sems, step, {"rep": twin})
        for step, twin in enumerate(twins)
    ]
    early_relay()
    relay_cut(0)
    relay_cut(1)
    for copy in twin_sends:
        copy.wait_recv()
    total = gain_totals[0]
    for step in range(1, QUARTERS):
        total = total + gain_totals[step]
    gain_sums[...] = total
    units.finish()
    early.finish()
    leaving = start_loads(((early_ref, early_any),), final_sems.at[pl.ds(3, 1)])
    mirror.finish()
    leaving += start_loads(((owned_ref, owned_any),), final_sems.at[pl.ds(4, 1)])
    pl_mirror.finish()
    ring.sent()
    sums.sent()
    for copy in (
        folds + o_folds + across_sends + swaps + key_swaps + crossings + gain_sends + twin_sends
    ):
        copy.wait_send()
    final_loads[3].wait()
    for copy in final_sends:
        copy.wait()
    for copy in leaving + placed:
        copy.wait()


def attention_back(local, arrays, small, pl_sums, chip_grads, far_down, number):
    rows, width = local[0].shape
    total = rows * HEADS
    shard = width // HEADS
    quarter = shard // QUARTERS
    steps = 4 * RING_STEPS
    pl_gate, pl_proj = pl_sums
    laurel = 2 * local[6].shape[1]
    columns = 3 * HEAD_DIM + laurel
    half = chip_grads[0].shape
    near, anywhere = pl.BlockSpec(memory_space=pltpu.VMEM), pl.BlockSpec(memory_space=pltpu.HBM)
    bf16, f32 = jnp.bfloat16, jnp.float32
    owned = (HEADS + 2 * KV_HEADS) * HEAD_DIM + laurel
    counts = [steps, steps, 2, 2, 2 * HEADS - 2, 2 * HEADS - 2, 6, 3, 2, 1, 1, 1, 3]
    counts += [HEADS - 1, QUARTERS - 1, 6]
    down, gate, up = chip_grads
    whole = jax.ShapeDtypeStruct((2 * half[0], half[1]), bf16)
    return pl.pallas_call(
        attention_back_kernel,
        out_shape=[
            jax.ShapeDtypeStruct((rows, width), bf16),
            jax.ShapeDtypeStruct((shard, owned), bf16),
            jax.ShapeDtypeStruct((shard, width + pl_gate.shape[1]), bf16),
            jax.ShapeDtypeStruct((pl_proj.shape[0], width), bf16),
            jax.ShapeDtypeStruct((8, shard), f32),
            whole,
            whole,
            whole,
            jax.ShapeDtypeStruct((half[0] * 3 // 8, half[1]), bf16),
        ],
        in_specs=[near] * len(local) + [anywhere] * (len(arrays) + 1) + [near] * 2 + [anywhere] * 4,
        out_specs=[near] + [anywhere] * 2 + [near] * 2 + [anywhere] * 4,
        scratch_shapes=[pltpu.VMEM(item.shape, item.dtype) for item in arrays]
        + [
            pltpu.VMEM((total, width), bf16),
            pltpu.VMEM((rows, width), bf16),
            pltpu.VMEM((rows, HEAD_DIM), bf16),
            pltpu.VMEM((rows, HEAD_DIM), bf16),
            pltpu.VMEM((rows, HEAD_DIM), f32),
            pltpu.VMEM((total, HEAD_DIM), f32),
            pltpu.VMEM((total, HEAD_DIM), f32),
            pltpu.VMEM((total, HEAD_DIM), f32),
            pltpu.VMEM((total, 3 * HEAD_DIM), bf16),
            pltpu.VMEM((HEAD_DIM, total), bf16),
            pltpu.VMEM((rows, width), f32),
            pltpu.VMEM((steps + 4, rows // 4, width), bf16),
            pltpu.VMEM((HEADS, QUARTERS, quarter, columns), bf16),
            pltpu.VMEM((2, HEADS, quarter, columns), bf16),
            pltpu.VMEM((HEADS, quarter, columns), bf16),
            pltpu.VMEM((HEADS, quarter, columns), bf16),
            pltpu.VMEM((HEADS, quarter, columns - HEAD_DIM), bf16),
            pltpu.VMEM((QUARTERS, quarter, width), bf16),
            pltpu.VMEM((2, quarter, width), bf16),
            pltpu.VMEM((quarter, width), bf16),
            pltpu.VMEM(half, bf16),
            pltpu.VMEM(half, bf16),
            pltpu.VMEM((rows, width), bf16),
            pltpu.VMEM((width, laurel), bf16),
            pltpu.VMEM((rows, width), bf16),
            pltpu.VMEM((rows, width), f32),
            pltpu.VMEM((rows, width), f32),
            pltpu.VMEM((8, width), f32),
            pltpu.VMEM((HEADS, 8, shard), f32),
            pltpu.VMEM((HEADS, 8, shard), f32),
            pltpu.VMEM((QUARTERS, 8, shard), f32),
            pltpu.VMEM((shard, owned), bf16),
            pltpu.VMEM((shard, width + pl_gate.shape[1]), bf16),
            pltpu.SemaphoreType.DMA((len(arrays) + 1,)),
            pltpu.SemaphoreType.DMA((7,)),
        ]
        + [pltpu.SemaphoreType.DMA((count,)) for count in counts for unused_side in range(2)],
        compiler_params=pltpu.CompilerParams(
            collective_id=number, has_side_effects=True, vmem_limit_bytes=VMEM_BYTES
        ),
    )(*local, *arrays, small, pl_gate, pl_proj, down, far_down, gate, up)


WRITE_STEPS = 16


def write_kernel(cuts, *refs):
    sources = refs[: len(cuts)]
    targets = iter(refs[len(cuts) :])
    for source, parts in zip(sources, cuts):
        for start, size in parts:
            target = next(targets)
            target[...] = source[:, start : start + size].astype(target.dtype)


def write_out(items):
    in_specs, out_specs, out_shape, cuts = [], [], [], []
    for array, parts in items:
        rows = array.shape[0] // WRITE_STEPS
        whole = rows % 16 != 0
        block_rows = array.shape[0] if whole else rows
        place = (lambda step: (0, 0)) if whole else (lambda step: (step, 0))
        in_specs.append(pl.BlockSpec((block_rows, array.shape[1]), place))
        cuts.append(tuple((start, size) for start, size, unused_dtype in parts))
        for unused_start, size, dtype in parts:
            out_specs.append(pl.BlockSpec((block_rows, size), place))
            out_shape.append(jax.ShapeDtypeStruct((array.shape[0], size), dtype))
    return pl.pallas_call(
        functools.partial(write_kernel, tuple(cuts)),
        grid=(WRITE_STEPS,),
        out_shape=out_shape,
        in_specs=in_specs,
        out_specs=out_specs,
        compiler_params=pltpu.CompilerParams(vmem_limit_bytes=VMEM_BYTES),
    )(*[array for array, unused_parts in items])


def head_plan(
    hidden_in,
    layer_input,
    out_grad,
    seg_lengths,
    seg_parents,
    attn_norm,
    q_proj,
    k_proj,
    v_proj,
    q_norm,
    k_norm,
    o_proj,
    attn_post_norm,
    laurel_left,
    laurel_right,
    laurel_norm,
    ffw_norm,
    gate_proj,
    up_proj,
    down_proj,
    ffw_post_norm,
    pl_gate,
    pl_proj,
    pl_post_norm,
):
    index = lax.axis_index("fsdp")
    rows, width = hidden_in.shape
    shard = width // HEADS
    total = rows * HEADS
    rank = laurel_left.shape[1]
    per_layer = pl_gate.shape[1]

    piece = HEAD_DIM // HEADS
    gains = (attn_norm, attn_post_norm, laurel_norm, ffw_norm, ffw_post_norm, pl_post_norm)
    segments = jnp.stack([seg_lengths[0], seg_parents[0]]).astype(jnp.float32)
    segments = jnp.pad(segments, ((0, 6), (0, 128 - segments.shape[1])))
    (
        branch,
        wide_gains,
        small_all,
        full_plproj,
        normed_all,
        qkv_head,
        q_raw,
        k_raw,
        q_low,
        k_low,
        v_low,
        attended_low,
        probs_low,
        cosine,
        sine,
    ) = attention_forward(
        segments,
        gains + (q_norm, k_norm),
        seg_lengths.shape[1],
        hidden_in,
        q_proj,
        k_proj,
        v_proj,
        jnp.concatenate([pl_gate, laurel_left, laurel_right], axis=1),
        pl_proj,
        o_proj,
        0,
    )
    (
        ffw_out,
        ffw_all,
        act,
        slope,
        inner_low,
        far_all,
        first_sum,
        low_rank,
        left_low,
    ) = ffn_forward(
        hidden_in, branch, wide_gains, small_all, rank, gate_proj, up_proj, down_proj, 7
    )
    d_ffwin, result, d_extra, d_second, ffw_gains, *rest = ffn_back(
        (first_sum, ffw_out, layer_input, out_grad),
        wide_gains[4:6],
        small_all,
        full_plproj,
        (ffw_all, far_all, act, slope, inner_low),
        (gate_proj, up_proj, down_proj),
        9,
    )
    chip_grads, far_down, pl_sums = rest[:3], rest[3], rest[-2:]

    d_source, owned, early, sum_plproj, gain_sums, *totals = attention_back(
        (
            hidden_in,
            first_sum,
            d_ffwin,
            d_second,
            branch,
            low_rank,
            left_low,
            wide_gains,
            ffw_gains,
        ),
        (
            o_proj,
            q_low,
            k_low,
            v_low,
            attended_low,
            probs_low,
            normed_all,
            qkv_head,
            q_raw,
            k_raw,
            cosine,
            sine,
        ),
        small_all,
        pl_sums,
        chip_grads,
        far_down,
        12,
    )
    sum_anorm, sum_apost, sum_lnorm, sum_fnorm, sum_fpost, sum_plpost = gain_sums[:6]
    sum_qnorm, sum_knorm = [
        lax.dynamic_slice_in_dim(item, index * piece, piece) for item in gain_sums[6:]
    ]

    keys = KV_HEADS * HEAD_DIM
    value_at = width + keys
    left_at = value_at + keys
    f32, bf16 = jnp.float32, jnp.bfloat16
    (
        sum_down,
        sum_gate,
        sum_up,
        sum_q,
        sum_k,
        sum_v,
        sum_laurel,
        sum_o,
        sum_plgate,
        sum_plproj,
        result,
        d_source,
        d_extra,
    ) = write_out(
        [(item, ((0, width, f32),)) for item in totals[:3]]
        + [
            (
                owned,
                (
                    (0, width, f32),
                    (width, keys, f32),
                    (value_at, keys, f32),
                    (left_at, 2 * rank, f32),
                ),
            ),
            (early, ((0, width, f32), (width, per_layer, f32))),
            (sum_plproj, ((0, width, f32),)),
            (result, ((0, width, bf16),)),
            (d_source, ((0, width, bf16),)),
            (d_extra, ((0, per_layer, bf16),)),
        ]
    )
    return (
        result,
        d_source,
        d_extra,
        sum_anorm,
        sum_q,
        sum_k,
        sum_v,
        sum_qnorm,
        sum_knorm,
        sum_o,
        sum_apost,
        sum_laurel[:, :rank],
        sum_laurel[:, rank:],
        sum_lnorm,
        sum_fnorm,
        sum_gate,
        sum_up,
        sum_down,
        sum_fpost,
        sum_plgate,
        sum_plproj,
        sum_plpost,
    )


def gather_plan(
    hidden_in,
    layer_input,
    out_grad,
    seg_lengths,
    seg_parents,
    attn_norm,
    q_proj,
    k_proj,
    v_proj,
    q_norm,
    k_norm,
    o_proj,
    attn_post_norm,
    laurel_left,
    laurel_right,
    laurel_norm,
    ffw_norm,
    gate_proj,
    up_proj,
    down_proj,
    ffw_post_norm,
    pl_gate,
    pl_proj,
    pl_post_norm,
):
    shards = lax.axis_size("fsdp")
    rank_index = lax.axis_index("fsdp")
    rows = hidden_in.shape[0]
    total = rows * shards
    groups = HEADS // KV_HEADS
    scale = HEAD_DIM ** (-0.5)
    tokens, member, reach, position = tree_tables(seg_lengths[0], seg_parents[0], total)
    first_row = rank_index * rows
    my_tokens = first_row + jnp.arange(rows, dtype=jnp.int32)
    my_reach = lax.dynamic_slice_in_dim(reach, first_row, rows, 0)
    my_depth = lax.dynamic_slice_in_dim(position, first_row, rows, 0).astype(jnp.float32)
    seen = (jnp.dot(my_reach, member.T) > 0) & (tokens[None, :] <= my_tokens[:, None])
    (
        full_anorm,
        full_q,
        full_k,
        full_v,
        full_qnorm,
        full_knorm,
        full_o,
        full_apost,
        full_left,
        full_right,
        full_lnorm,
        full_fnorm,
        full_fpost,
        full_plgate,
        full_plproj,
        full_plpost,
    ) = (
        lax.all_gather(attn_norm, "fsdp", axis=0, tiled=True),
        lax.all_gather(q_proj, "fsdp", axis=0, tiled=True),
        lax.all_gather(k_proj, "fsdp", axis=0, tiled=True),
        lax.all_gather(v_proj, "fsdp", axis=0, tiled=True),
        lax.all_gather(q_norm, "fsdp", axis=0, tiled=True),
        lax.all_gather(k_norm, "fsdp", axis=0, tiled=True),
        lax.all_gather(o_proj, "fsdp", axis=0, tiled=True),
        lax.all_gather(attn_post_norm, "fsdp", axis=0, tiled=True),
        lax.all_gather(laurel_left, "fsdp", axis=0, tiled=True),
        lax.all_gather(laurel_right, "fsdp", axis=0, tiled=True),
        lax.all_gather(laurel_norm, "fsdp", axis=0, tiled=True),
        lax.all_gather(ffw_norm, "fsdp", axis=0, tiled=True),
        lax.all_gather(ffw_post_norm, "fsdp", axis=0, tiled=True),
        lax.all_gather(pl_gate, "fsdp", axis=0, tiled=True),
        lax.all_gather(pl_proj, "fsdp", axis=0, tiled=True),
        lax.all_gather(pl_post_norm, "fsdp", axis=0, tiled=True),
    )
    gain_anorm = full_anorm.astype(jnp.float32)
    gain_qnorm = full_qnorm.astype(jnp.float32)
    gain_knorm = full_knorm.astype(jnp.float32)
    gain_apost = full_apost.astype(jnp.float32)
    gain_lnorm = full_lnorm.astype(jnp.float32)
    gain_fnorm = full_fnorm.astype(jnp.float32)
    gain_fpost = full_fpost.astype(jnp.float32)
    gain_plpost = full_plpost.astype(jnp.float32)
    source = hidden_in.astype(jnp.float32)
    extra = layer_input.astype(jnp.float32)
    normed = norm_rows(source, gain_anorm)
    normed_low = normed.astype(jnp.bfloat16)
    q_raw = jnp.dot(normed_low, full_q, preferred_element_type=jnp.float32)
    k_raw = jnp.dot(normed_low, full_k, preferred_element_type=jnp.float32)
    v_raw = jnp.dot(normed_low, full_v, preferred_element_type=jnp.float32)

    def head_path(raw, gain):
        return rotate(norm_rows(raw.reshape(rows, -1, HEAD_DIM), gain), my_depth)

    q_low = head_path(q_raw, gain_qnorm).astype(jnp.bfloat16)
    k_low = head_path(k_raw, gain_knorm).reshape(rows, -1).astype(jnp.bfloat16)
    v_low = v_raw.astype(jnp.bfloat16)
    keys_all, values_all = (
        lax.all_gather(k_low, "fsdp", axis=0, tiled=True),
        lax.all_gather(v_low, "fsdp", axis=0, tiled=True),
    )
    keys_heads = keys_all.reshape(total, KV_HEADS, HEAD_DIM)
    values_heads = values_all.reshape(total, KV_HEADS, HEAD_DIM)
    query_groups = q_low.reshape(rows, KV_HEADS, groups, HEAD_DIM)
    mixed_list = []
    log_list = []
    for head in range(KV_HEADS):
        scores = (
            jnp.einsum(
                "tgd,nd->gtn",
                query_groups[:, head],
                keys_heads[:, head],
                preferred_element_type=jnp.float32,
            )
            * scale
        )
        scores = jnp.where(seen[None], scores, MASKED)
        top = jnp.max(scores, axis=-1, keepdims=True)
        expo = jnp.exp(scores - top)
        sums = jnp.sum(expo, axis=-1, keepdims=True)
        weights = (expo / sums).astype(jnp.bfloat16)
        mixed_list.append(
            jnp.einsum(
                "gtn,nd->tgd", weights, values_heads[:, head], preferred_element_type=jnp.float32
            )
        )
        log_list.append(top[..., 0] + jnp.log(sums[..., 0]))
    attended = jnp.stack(mixed_list, axis=1)
    log_sums = jnp.stack(log_list, axis=0)
    attended_low = attended.reshape(rows, -1).astype(jnp.bfloat16)
    branch = jnp.dot(attended_low, full_o, preferred_element_type=jnp.float32)
    left_low = jnp.dot(normed_low, full_left, preferred_element_type=jnp.float32).astype(
        jnp.bfloat16
    )
    low_rank = mul_t(left_low, full_right)
    first_sum = (
        source + norm_rows(branch, gain_apost) + normed + norm_rows(low_rank, gain_lnorm)
    ) * HALF_ROOT
    ffw_low = norm_rows(first_sum, gain_fnorm).astype(jnp.bfloat16)
    full_gate, full_up, full_down = (
        lax.all_gather(gate_proj, "fsdp", axis=0, tiled=True),
        lax.all_gather(up_proj, "fsdp", axis=0, tiled=True),
        lax.all_gather(down_proj, "fsdp", axis=0, tiled=True),
    )
    gate_val = mul_t(ffw_low, full_gate)
    up_val = mul_t(ffw_low, full_up)
    inner_low = gelu_mix(gate_val, up_val).astype(jnp.bfloat16)
    ffw_out = jnp.dot(inner_low, full_down, preferred_element_type=jnp.float32)
    second_sum = first_sum + norm_rows(ffw_out, gain_fpost)
    second_low = second_sum.astype(jnp.bfloat16)
    pl_pre = jnp.dot(second_low, full_plgate, preferred_element_type=jnp.float32)
    pl_mix = gelu_mix(pl_pre, extra).astype(jnp.bfloat16)
    pl_out = jnp.dot(pl_mix, full_plproj, preferred_element_type=jnp.float32)
    result = second_sum + norm_rows(pl_out, gain_plpost)
    seed = out_grad.astype(jnp.float32)
    d_plout, grad_plpost = norm_back(pl_out, gain_plpost, seed)
    d_plout_low = d_plout.astype(jnp.bfloat16)
    grad_plproj = outer(pl_mix, d_plout_low)
    d_mix = mul_t(d_plout_low, full_plproj)
    d_pre, d_extra = mix_back(pl_pre, extra, d_mix)
    d_pre_low = d_pre.astype(jnp.bfloat16)
    grad_plgate = outer(second_low, d_pre_low)
    d_second = seed + mul_t(d_pre_low, full_plgate)
    d_ffwout, grad_fpost = norm_back(ffw_out, gain_fpost, d_second)
    d_ffw_low = d_ffwout.astype(jnp.bfloat16)
    d_inner = mul_t(d_ffw_low, full_down)
    d_gate, d_up = mix_back(gate_val, up_val, d_inner)
    d_gate_low = d_gate.astype(jnp.bfloat16)
    d_up_low = d_up.astype(jnp.bfloat16)
    d_ffwin = jnp.dot(d_gate_low, full_gate, preferred_element_type=jnp.float32) + jnp.dot(
        d_up_low, full_up, preferred_element_type=jnp.float32
    )
    width = ffw_low.shape[1]
    gate_part = outer(d_gate_low, ffw_low)
    up_part = outer(d_up_low, ffw_low)
    down_part = outer(inner_low, d_ffw_low)
    stacked = lax.psum_scatter(
        jnp.concatenate([gate_part, up_part, down_part], axis=1).astype(jnp.bfloat16),
        "fsdp",
        scatter_dimension=0,
        tiled=True,
    ).astype(jnp.float32)
    grad_gate = stacked[:, :width]
    grad_up = stacked[:, width : 2 * width]
    grad_down = stacked[:, 2 * width :]
    d_first_part, grad_fnorm = norm_back(first_sum, gain_fnorm, d_ffwin)
    d_first = d_second + d_first_part
    d_scaled = d_first * HALF_ROOT
    d_branch, grad_apost = norm_back(branch, gain_apost, d_scaled)
    d_branch_low = d_branch.astype(jnp.bfloat16)
    d_lowrank, grad_lnorm = norm_back(low_rank, gain_lnorm, d_scaled)
    d_lowrank_low = d_lowrank.astype(jnp.bfloat16)
    grad_o = outer(attended_low, d_branch_low)
    d_att_low = mul_t(d_branch_low, full_o).astype(jnp.bfloat16)
    grad_right = outer(d_lowrank_low, left_low)
    d_left_low = jnp.dot(d_lowrank_low, full_right, preferred_element_type=jnp.float32).astype(
        jnp.bfloat16
    )
    grad_left = outer(normed_low, d_left_low)
    d_att_heads = d_att_low.reshape(rows, KV_HEADS, groups, HEAD_DIM)
    delta = jnp.sum(d_att_heads.astype(jnp.float32) * attended, axis=-1).transpose(1, 2, 0)
    block = 512
    count = total // block
    key_blocks = keys_heads.reshape(count, block, KV_HEADS, HEAD_DIM)
    value_blocks = values_heads.reshape(count, block, KV_HEADS, HEAD_DIM)
    seen_blocks = seen.reshape(rows, count, block).transpose(1, 0, 2)

    def key_step(d_query, item):
        keys, values, shown = item
        scores = (
            jnp.einsum("tkgd,nkd->kgtn", query_groups, keys, preferred_element_type=jnp.float32)
            * scale
        )
        scores = jnp.where(shown[None, None], scores, MASKED)
        probs = jnp.exp(scores - log_sums[..., None])
        d_probs = jnp.einsum(
            "tkgd,nkd->kgtn", d_att_heads, values, preferred_element_type=jnp.float32
        )
        d_scores = (probs * (d_probs - delta[..., None]) * scale).astype(jnp.bfloat16)
        d_query = d_query + jnp.einsum(
            "kgtn,nkd->tkgd", d_scores, keys, preferred_element_type=jnp.float32
        )
        d_keys = jnp.einsum(
            "kgtn,tkgd->nkd", d_scores, query_groups, preferred_element_type=jnp.float32
        )
        d_values = jnp.einsum(
            "kgtn,tkgd->nkd",
            probs.astype(jnp.bfloat16),
            d_att_heads,
            preferred_element_type=jnp.float32,
        )
        return (d_query, (d_keys, d_values))

    zero_query = jnp.zeros((rows, KV_HEADS, groups, HEAD_DIM), jnp.float32)
    d_query, (d_key_blocks, d_value_blocks) = lax.scan(
        key_step, zero_query, (key_blocks, value_blocks, seen_blocks)
    )
    my_dkeys, my_dvalues = (
        lax.psum_scatter(
            d_key_blocks.reshape(total, -1).astype(jnp.bfloat16),
            "fsdp",
            scatter_dimension=0,
            tiled=True,
        ).astype(jnp.float32),
        lax.psum_scatter(
            d_value_blocks.reshape(total, -1).astype(jnp.bfloat16),
            "fsdp",
            scatter_dimension=0,
            tiled=True,
        ).astype(jnp.float32),
    )
    unused_q, q_pull = jax.vjp(head_path, q_raw, gain_qnorm)
    d_qraw, grad_qnorm = q_pull(d_query.reshape(rows, HEADS, HEAD_DIM))
    unused_k, k_pull = jax.vjp(head_path, k_raw, gain_knorm)
    d_kraw, grad_knorm = k_pull(my_dkeys.reshape(rows, KV_HEADS, HEAD_DIM))
    d_q_low = d_qraw.astype(jnp.bfloat16)
    d_k_low = d_kraw.astype(jnp.bfloat16)
    d_v_low = my_dvalues.astype(jnp.bfloat16)
    grad_q = outer(normed_low, d_q_low)
    grad_k = outer(normed_low, d_k_low)
    grad_v = outer(normed_low, d_v_low)
    d_normed = (
        d_scaled
        + mul_t(d_q_low, full_q)
        + mul_t(d_k_low, full_k)
        + mul_t(d_v_low, full_v)
        + mul_t(d_left_low, full_left)
    )
    d_source_part, grad_anorm = norm_back(source, gain_anorm, d_normed)
    d_source = d_scaled + d_source_part
    shard_grads = (
        lax.psum_scatter(
            grad_anorm.astype(jnp.bfloat16), "fsdp", scatter_dimension=0, tiled=True
        ).astype(jnp.float32),
        lax.psum_scatter(
            grad_q.astype(jnp.bfloat16), "fsdp", scatter_dimension=0, tiled=True
        ).astype(jnp.float32),
        lax.psum_scatter(
            grad_k.astype(jnp.bfloat16), "fsdp", scatter_dimension=0, tiled=True
        ).astype(jnp.float32),
        lax.psum_scatter(
            grad_v.astype(jnp.bfloat16), "fsdp", scatter_dimension=0, tiled=True
        ).astype(jnp.float32),
        lax.psum_scatter(
            grad_qnorm.astype(jnp.bfloat16), "fsdp", scatter_dimension=0, tiled=True
        ).astype(jnp.float32),
        lax.psum_scatter(
            grad_knorm.astype(jnp.bfloat16), "fsdp", scatter_dimension=0, tiled=True
        ).astype(jnp.float32),
        lax.psum_scatter(
            grad_o.astype(jnp.bfloat16), "fsdp", scatter_dimension=0, tiled=True
        ).astype(jnp.float32),
        lax.psum_scatter(
            grad_apost.astype(jnp.bfloat16), "fsdp", scatter_dimension=0, tiled=True
        ).astype(jnp.float32),
        lax.psum_scatter(
            grad_left.astype(jnp.bfloat16), "fsdp", scatter_dimension=0, tiled=True
        ).astype(jnp.float32),
        lax.psum_scatter(
            grad_right.astype(jnp.bfloat16), "fsdp", scatter_dimension=0, tiled=True
        ).astype(jnp.float32),
        lax.psum_scatter(
            grad_lnorm.astype(jnp.bfloat16), "fsdp", scatter_dimension=0, tiled=True
        ).astype(jnp.float32),
        lax.psum_scatter(
            grad_fnorm.astype(jnp.bfloat16), "fsdp", scatter_dimension=0, tiled=True
        ).astype(jnp.float32),
        lax.psum_scatter(
            grad_fpost.astype(jnp.bfloat16), "fsdp", scatter_dimension=0, tiled=True
        ).astype(jnp.float32),
        lax.psum_scatter(
            grad_plgate.astype(jnp.bfloat16), "fsdp", scatter_dimension=0, tiled=True
        ).astype(jnp.float32),
        lax.psum_scatter(
            grad_plproj.astype(jnp.bfloat16), "fsdp", scatter_dimension=0, tiled=True
        ).astype(jnp.float32),
        lax.psum_scatter(
            grad_plpost.astype(jnp.bfloat16), "fsdp", scatter_dimension=0, tiled=True
        ).astype(jnp.float32),
    )
    (
        sum_anorm,
        sum_q,
        sum_k,
        sum_v,
        sum_qnorm,
        sum_knorm,
        sum_o,
        sum_apost,
        sum_left,
        sum_right,
        sum_lnorm,
        sum_fnorm,
        sum_fpost,
        sum_plgate,
        sum_plproj,
        sum_plpost,
        sum_gate,
        sum_up,
        sum_down,
    ) = (
        lax.psum(shard_grads[0].astype(jnp.bfloat16), "rep").astype(jnp.float32),
        lax.psum(shard_grads[1].astype(jnp.bfloat16), "rep").astype(jnp.float32),
        lax.psum(shard_grads[2].astype(jnp.bfloat16), "rep").astype(jnp.float32),
        lax.psum(shard_grads[3].astype(jnp.bfloat16), "rep").astype(jnp.float32),
        lax.psum(shard_grads[4].astype(jnp.bfloat16), "rep").astype(jnp.float32),
        lax.psum(shard_grads[5].astype(jnp.bfloat16), "rep").astype(jnp.float32),
        lax.psum(shard_grads[6].astype(jnp.bfloat16), "rep").astype(jnp.float32),
        lax.psum(shard_grads[7].astype(jnp.bfloat16), "rep").astype(jnp.float32),
        lax.psum(shard_grads[8].astype(jnp.bfloat16), "rep").astype(jnp.float32),
        lax.psum(shard_grads[9].astype(jnp.bfloat16), "rep").astype(jnp.float32),
        lax.psum(shard_grads[10].astype(jnp.bfloat16), "rep").astype(jnp.float32),
        lax.psum(shard_grads[11].astype(jnp.bfloat16), "rep").astype(jnp.float32),
        lax.psum(shard_grads[12].astype(jnp.bfloat16), "rep").astype(jnp.float32),
        lax.psum(shard_grads[13].astype(jnp.bfloat16), "rep").astype(jnp.float32),
        lax.psum(shard_grads[14].astype(jnp.bfloat16), "rep").astype(jnp.float32),
        lax.psum(shard_grads[15].astype(jnp.bfloat16), "rep").astype(jnp.float32),
        lax.psum(grad_gate.astype(jnp.bfloat16), "rep").astype(jnp.float32),
        lax.psum(grad_up.astype(jnp.bfloat16), "rep").astype(jnp.float32),
        lax.psum(grad_down.astype(jnp.bfloat16), "rep").astype(jnp.float32),
    )
    return (
        result.astype(jnp.bfloat16),
        d_source.astype(jnp.bfloat16),
        d_extra.astype(jnp.bfloat16),
        sum_anorm,
        sum_q,
        sum_k,
        sum_v,
        sum_qnorm,
        sum_knorm,
        sum_o,
        sum_apost,
        sum_left,
        sum_right,
        sum_lnorm,
        sum_fnorm,
        sum_gate,
        sum_up,
        sum_down,
        sum_fpost,
        sum_plgate,
        sum_plproj,
        sum_plpost,
    )


def solution(mesh):
    placed = (
        P(("rep", "fsdp"), None),
        P(("rep", "fsdp"), None),
        P(("rep", "fsdp"), None),
        P("rep", None),
        P("rep", None),
        P("fsdp"),
        P("fsdp", None),
        P("fsdp", None),
        P("fsdp", None),
        P("fsdp"),
        P("fsdp"),
        P("fsdp", None),
        P("fsdp"),
        P("fsdp", None),
        P("fsdp", None),
        P("fsdp"),
        P("fsdp"),
        P("fsdp", None),
        P("fsdp", None),
        P("fsdp", None),
        P("fsdp"),
        P("fsdp", None),
        P("fsdp", None),
        P("fsdp"),
    )
    return jax.shard_map(
        head_plan if mesh.shape["fsdp"] == HEADS else gather_plan,
        mesh=mesh,
        in_specs=placed,
        out_specs=(
            P(("rep", "fsdp"), None),
            P(("rep", "fsdp"), None),
            P(("rep", "fsdp"), None),
            P("fsdp"),
            P("fsdp", None),
            P("fsdp", None),
            P("fsdp", None),
            P("fsdp"),
            P("fsdp"),
            P("fsdp", None),
            P("fsdp"),
            P("fsdp", None),
            P("fsdp", None),
            P("fsdp"),
            P("fsdp"),
            P("fsdp", None),
            P("fsdp", None),
            P("fsdp", None),
            P("fsdp"),
            P("fsdp", None),
            P("fsdp", None),
            P("fsdp"),
        ),
        check_vma=False,
    )
```
